32 devices in a mesh: img: 8 (over z, x), band: 4 (over y, core).
Axes of the slice: x: 2, y: 2, z: 4, core: 2. Of those that a mesh axis runs over, the one named last changes fastest.
Arguments:
- images: bfloat16 [32, 32, 32, 512], P('img', 'band'), may hold values from -18 to 18
- cotangent: bfloat16 [32, 32, 32, 512], P('img', 'band'), may hold values from -6 to 6
- sizes: int32 [32], P('img'), may hold values from 16 to 32, as said below
- matrix_weight: float32 [5767168], P(('img', 'band')), may hold values from -0.8838835 to 0.8838835
- matrix_momentum: float32 [5767168], P(('img', 'band')), may hold values from -512 to 512
- matrix_average: float32 [5767168], P(('img', 'band')), may hold values from -0.8838835 to 0.8838835
- vector_weight: float32 [11, 512], replicated, may hold values from -0.3 to 1.45
- vector_momentum: float32 [11, 512], replicated, may hold values from -512 to 512
- vector_average: float32 [11, 512], replicated, may hold values from -0.3 to 1.45
Outputs:
- block_out: bfloat16 [32, 32, 32, 512], P('img', 'band')
- input_grad: float32 [32, 32, 32, 512], P('img', 'band')
- matrix_grads: float32 [5767168], P(('img', 'band'))
- matrix_moments: float32 [5767168], P(('img', 'band'))
- matrix_means: float32 [5767168], P(('img', 'band'))
- matrix_masters: float32 [5767168], P(('img', 'band'))
- vector_grads: float32 [11, 512], replicated
- vector_moments: float32 [11, 512], replicated
- vector_means: float32 [11, 512], replicated
- vector_masters: float32 [11, 512], replicated
The draws below stay inside these ranges and needn't reach their ends.
Inputs may be any that keep to these rules, and one draw needn't show every extreme that they name: `sizes`: each value is 16, 24 or 32; among images 4 k to 4 k + 3 at least one has size 32.
All inputs are finite; a program needn't handle non-finite values.
Results may differ from the reference program's by a relative error of at most 0.013.
The reference program's roundings to bfloat16 on the way count: a program that leaves them out, or rounds other values in their place, can miss the bound.
Values may be sent and summed in bfloat16 or wider, within the bound.
No kernel may reach another device: no remote copies, remote signals or barrier semaphores. Data moves between devices by JAX's collectives and lax.ppermute only.
A program may use at most 192 MiB of HBM per device.

```python
import jax
import jax.numpy as jnp
from jax import lax

CHANNEL_COUNT = 512
GROUPS = 32
SIDE = 32
IMG_GRP = 4
IMAGES = 32


def matrix_scale():
    index = jnp.arange(22 * CHANNEL_COUNT * CHANNEL_COUNT)
    factor = jnp.where(index < 20 * CHANNEL_COUNT * CHANNEL_COUNT, 1.0, jnp.where(index < 21 * CHANNEL_COUNT * CHANNEL_COUNT, 4.0, 5.0))
    return factor * CHANNEL_COUNT ** (-0.5)


def draw_images(key, part):
    key = jax.random.fold_in(key, 1)
    shape = (IMAGES, SIDE, SIDE, CHANNEL_COUNT)
    height = jnp.arange(SIDE).astype(jnp.float32)[None, :, None, None] / (SIDE - 1)
    base = jnp.clip(jax.random.normal(key, shape, jnp.float32), -6.0, 6.0)
    slope = 2.0
    return (base * (1.0 + slope * height)).astype(jnp.bfloat16)


def draw_sizes(key, part):
    key = jax.random.fold_in(key, 11)
    pick_key, full_key = jax.random.split(key)
    pick = jax.random.randint(pick_key, (IMAGES,), 0, 3)
    chosen = SIDE // 2 + pick * (SIDE // 4)
    full_slot = jax.random.randint(full_key, (IMAGES // IMG_GRP,), 0, IMG_GRP)
    slots = jnp.arange(IMAGES)
    return jnp.where(slots % IMG_GRP == full_slot[slots // IMG_GRP], SIDE, chosen).astype(jnp.int32)


def draw_matrix_weight(key, part):
    key = jax.random.fold_in(key, 2)
    base = jnp.clip(jax.random.normal(key, (22 * CHANNEL_COUNT * CHANNEL_COUNT,), jnp.float32), -4.0, 4.0)
    return base * matrix_scale()


def draw_matrix_average(key, part):
    key = jax.random.fold_in(key, 3)
    base = jnp.clip(jax.random.normal(key, (22 * CHANNEL_COUNT * CHANNEL_COUNT,), jnp.float32), -4.0, 4.0)
    return base * matrix_scale()


def draw_vector_weight(key, part):
    key = jax.random.fold_in(key, 5)
    rows = jnp.arange(11)[:, None]
    gains = (rows == 0) | (rows == 3) | (rows == 6)
    base = jnp.clip(jax.random.normal(key, (11, CHANNEL_COUNT), jnp.float32), -3.0, 3.0)
    return jnp.where(gains, 1.0 + 0.15 * base, 0.1 * base)


def draw_vector_average(key, part):
    key = jax.random.fold_in(key, 6)
    rows = jnp.arange(11)[:, None]
    gains = (rows == 0) | (rows == 3) | (rows == 6)
    base = jnp.clip(jax.random.normal(key, (11, CHANNEL_COUNT), jnp.float32), -3.0, 3.0)
    return jnp.where(gains, 1.0 + 0.15 * base, 0.1 * base)


def levels(own_key, shape, cuts, least, high):
    loudness, own = 1.0, jax.random.fold_in(own_key, 6)
    for axis_at, blocks in cuts:
        draws = jnp.exp(jax.random.uniform(jax.random.fold_in(own, axis_at), (blocks,), jnp.float32, least / len(cuts), high / len(cuts)))
        loudness = loudness * jnp.repeat(draws, shape[axis_at] // blocks).reshape([-1 if axis == axis_at else 1 for axis in range(len(shape))])
    return loudness


def bell_draw(own_key, extent, width, reach, cuts=(), kind=jnp.bfloat16):
    entries = width * jax.random.normal(own_key, extent, jnp.float32)
    if cuts:
        entries = entries * levels(own_key, extent, cuts, -0.22, 0.18)
    return jnp.clip(entries, -reach, reach).astype(kind)


def setup_inputs(seed: int = 0) -> dict:
    streams_of = jax.random.split(jax.random.key(seed), 10)
    images = draw_images(jax.random.fold_in(streams_of[9], 71), 0)
    cotangent = bell_draw(streams_of[1], (IMAGES, SIDE, SIDE, CHANNEL_COUNT), 1.0, 6.0, ((0, 8), (1, 4)))
    sizes = draw_sizes(jax.random.fold_in(streams_of[9], 71), 0)
    matrix_weight = draw_matrix_weight(jax.random.fold_in(streams_of[9], 71), 0)
    matrix_momentum = bell_draw(streams_of[4], (22 * CHANNEL_COUNT * CHANNEL_COUNT,), ((IMAGES * SIDE * SIDE) ** 0.5 / 2), 512.0, ((0, 32),), jnp.float32)
    matrix_average = draw_matrix_average(jax.random.fold_in(streams_of[9], 71), 0)
    vector_weight = draw_vector_weight(jax.random.fold_in(streams_of[9], 71), 0)
    vector_momentum = bell_draw(streams_of[7], (11, CHANNEL_COUNT), ((IMAGES * SIDE * SIDE) ** 0.5 / 2), 512.0, (), jnp.float32)
    vector_average = draw_vector_average(jax.random.fold_in(streams_of[9], 71), 0)
    return dict(images=images, cotangent=cotangent, sizes=sizes, matrix_weight=matrix_weight, matrix_momentum=matrix_momentum, matrix_average=matrix_average, vector_weight=vector_weight, vector_momentum=vector_momentum, vector_average=vector_average)


@jax.custom_vjp
def low(v):
    return lax.optimization_barrier(v.astype(jnp.bfloat16)).astype(jnp.float32)

@jax.custom_vjp
def low_back(v):
    return v

def low_keep(v):
    return (low(v), None)

def low_pass(kept, grad):
    return (grad,)

def back_keep(v):
    return (v, None)

def back_low(kept, grad):
    return (low(grad),)
low.defvjp(low_keep, low_pass)
low_back.defvjp(back_keep, back_low)
EPS = 1e-06
MOMENTUM = 0.9
LR_MATRIX = 4e-05
LR_VECTOR = 0.0001
AVERAGE = 0.75

def group_norm(field, mask, gain, shift):
    shaped = field.reshape(field.shape[:3] + (GROUPS, CHANNEL_COUNT // GROUPS))
    weighted = shaped * mask[..., None]
    count = lax.optimization_barrier(jnp.sum(mask, axis=(1, 2, 3))) * (CHANNEL_COUNT // GROUPS)
    total = lax.optimization_barrier(jnp.sum(weighted, axis=(1, 2, 4)))
    squares = lax.optimization_barrier(jnp.sum(weighted * shaped, axis=(1, 2, 4)))
    center = total / count[:, None]
    spread = squares / count[:, None] - center * center
    scale = lax.rsqrt(spread + EPS)
    normed = (shaped - center[:, None, None, :, None]) * scale[:, None, None, :, None]
    return normed.reshape(field.shape) * gain + shift

def convolve(field, kernel):
    padded = jnp.pad(field, ((0, 0), (1, 1), (1, 1), (0, 0)))
    total = jnp.zeros(field.shape, jnp.float32)
    for tap in range(9):
        row, column = (tap // 3, tap % 3)
        total = total + jnp.einsum('bhwc,cd->bhwd', padded[:, row:row + SIDE, column:column + SIDE], kernel[tap], precision=lax.Precision.HIGHEST)
    return total

def forward(images, matrices, vector_params, mask):
    weights = low(matrices)
    square = CHANNEL_COUNT * CHANNEL_COUNT
    kernel_one = weights[:9 * square].reshape(9, CHANNEL_COUNT, CHANNEL_COUNT)
    kernel_two = weights[9 * square:18 * square].reshape(9, CHANNEL_COUNT, CHANNEL_COUNT)
    attn_in = weights[18 * square:21 * square].reshape(3, CHANNEL_COUNT, CHANNEL_COUNT)
    attention_output = weights[21 * square:].reshape(CHANNEL_COUNT, CHANNEL_COUNT)
    start = images * mask
    act_one = low(jax.nn.silu(group_norm(start, mask, vector_params[0], vector_params[1])) * mask)
    conv_one = low_back(convolve(act_one, kernel_one)) + vector_params[2]
    act_two = low(jax.nn.silu(group_norm(conv_one, mask, vector_params[3], vector_params[4])) * mask)
    conv_two = low_back(convolve(act_two, kernel_two)) + vector_params[5]
    resid = (start + conv_two) * mask
    normed = low(group_norm(resid, mask, vector_params[6], vector_params[7]) * mask)
    batch = images.shape[0]
    tokens = normed.reshape(batch, SIDE * SIDE, CHANNEL_COUNT)
    projected = jnp.einsum('bqc,jcd->jbqd', tokens, attn_in, precision=lax.Precision.HIGHEST)
    query_matrix = low(low_back(projected[0] + vector_params[8]))
    key = low(low_back(projected[1]))
    value_matrix = low(low_back(projected[2] + vector_params[9]))
    valid = mask.reshape(batch, 1, SIDE * SIDE) > 0
    score_matrix = low_back(jnp.einsum('ruh,rmh->rum', query_matrix, key, precision=lax.Precision.HIGHEST)) * CHANNEL_COUNT ** (-0.5)
    score_matrix = jnp.where(valid, score_matrix, -1e+30)
    top = lax.optimization_barrier(jnp.max(score_matrix, axis=2, keepdims=True))
    raised = jnp.exp(score_matrix - top)
    probability_rows = low(raised / lax.optimization_barrier(jnp.sum(raised, axis=2, keepdims=True)))
    mixed_values = low(low_back(jnp.einsum('fat,ftw->faw', probability_rows, value_matrix, precision=lax.Precision.HIGHEST)))
    output_rows = low_back(jnp.einsum('how,wi->hoi', mixed_values, attention_output, precision=lax.Precision.HIGHEST)) + vector_params[10]
    return (resid + output_rows.reshape(images.shape)) * mask

def reference(images, cotangent, sizes, matrix_weight, matrix_momentum, matrix_average, vector_weight, vector_momentum, vector_average):
    lines = jnp.arange(SIDE).astype(jnp.int32)
    inside = (lines[None, :, None] < sizes[:, None, None]) & (lines[None, None, :] < sizes[:, None, None])
    masks = jnp.where(inside, 1.0, 0.0).astype(jnp.float32)[..., None]
    blocks = IMAGES // IMG_GRP
    shaped = (blocks, IMG_GRP, SIDE, SIDE, CHANNEL_COUNT)
    inputs = (images.astype(jnp.float32).reshape(shaped), cotangent.astype(jnp.float32).reshape(shaped), masks.reshape((blocks, IMG_GRP, SIDE, SIDE, 1)))

    def block(carry, piece):
        matrix_sum, vector_sum = carry
        image_block, grad_block, mask_block = piece
        result, pull = jax.vjp(lambda field, mats, vecs: forward(field, mats, vecs, mask_block), image_block, matrix_weight, vector_weight)
        grad_image, grad_matrix, grad_vector = pull(grad_block)
        return ((matrix_sum + grad_matrix, vector_sum + grad_vector), (result, grad_image))
    begin = (jnp.zeros_like(matrix_weight), jnp.zeros_like(vector_weight))
    (matrix_grads, vector_grads), (results, input_grads) = lax.scan(block, begin, inputs)
    block_out = results.reshape(images.shape).astype(jnp.bfloat16)
    input_grad = input_grads.reshape(images.shape)
    matrix_moments = MOMENTUM * matrix_momentum + matrix_grads
    matrix_masters = matrix_weight - LR_MATRIX * (matrix_grads + MOMENTUM * matrix_moments)
    matrix_means = AVERAGE * matrix_average + (1.0 - AVERAGE) * matrix_masters
    vector_moments = MOMENTUM * vector_momentum + vector_grads
    vector_masters = vector_weight - LR_VECTOR * (vector_grads + MOMENTUM * vector_moments)
    vector_means = AVERAGE * vector_average + (1.0 - AVERAGE) * vector_masters
    return (block_out, input_grad, matrix_grads, matrix_moments, matrix_means, matrix_masters, vector_grads, vector_moments, vector_means, vector_masters)
```

```python
import jax
import jax.numpy as jnp
from jax import lax
from jax.experimental import pallas as pl
from jax.experimental.pallas import tpu as pltpu
from jax.sharding import PartitionSpec as P

GROUPS = 32


EPS = 1e-06
MOMENTUM = 0.9
LR_MATRIX = 4e-05
LR_VECTOR = 0.0001
AVERAGE = 0.75


def extended(array, sides, width):
    for axis, dim in sides:
        count, length = (lax.axis_size(axis), array.shape[dim])
        up = [(i, (i + 1) % count) for i in range(count - 1)]
        down = [(j, i) for i, j in up]
        last = lax.slice_in_dim(array, length - width, length, axis=dim)
        initial = lax.slice_in_dim(array, 0, width, axis=dim)
        before = lax.ppermute(last, axis, up)
        after = lax.ppermute(initial, axis, down)
        array = jnp.concatenate([before, array, after], axis=dim)
    return array


def split_groups(field):
    return field.reshape(field.shape[:3] + (GROUPS, field.shape[3] // GROUPS))


def group_sums(field, mask):
    shaped = split_groups(field)
    weighted = shaped * mask[..., None]
    return (jnp.sum(weighted, axis=(1, 2, 4)), jnp.sum(weighted * shaped, axis=(1, 2, 4)))


def group_apply(field, sums, count, gain, shift):
    center = sums[0] / count[:, None]
    spread = sums[1] / count[:, None] - center * center
    scale = lax.rsqrt(spread + EPS)
    shaped = split_groups(field)
    normed = (shaped - center[:, None, None, :, None]) * scale[:, None, None, :, None]
    return normed.reshape(field.shape) * gain + shift


def normalize(field, mask, count, gain, shift):
    sums = lax.psum(group_sums(field, mask), "band")
    return (group_apply(field, sums, count, gain, shift), sums)


def normalize_back(field, sums, mask, count, gain, shift, upstream):
    _, pull = jax.vjp(
        lambda field_in, sums_in, gain_in, shift_in: group_apply(
            field_in, sums_in, count, gain_in, shift_in
        ),
        field,
        sums,
        gain,
        shift,
    )
    direct, grad_sums, grad_gain, grad_shift = pull(upstream)
    grad_sums = lax.psum(grad_sums, "band")
    _, pull_sums = jax.vjp(lambda field_in: group_sums(field_in, mask), field)
    return (direct + pull_sums(grad_sums)[0], grad_gain, grad_shift)


def activate(field, mask):
    return jax.nn.silu(field) * mask


def activate_back(field, mask, upstream):
    _, pull = jax.vjp(lambda inner: activate(inner, mask), field)
    return pull(upstream)[0]


def widen(field):
    return jnp.pad(field, ((0, 0), (0, 0), (1, 1), (0, 0)))


def taps(padded, kernel, height, width):
    total = jnp.zeros(padded.shape[:1] + (height, width, kernel.shape[2]), jnp.float32)
    for tap in range(9):
        row, column = (tap // 3, tap % 3)
        total = total + jnp.einsum(
            "ghwc,cd->ghwd",
            padded[:, row : row + height, column : column + width],
            kernel[tap],
            preferred_element_type=jnp.float32,
        )
    return total


def conv_forward(low_field, kernel):
    padded = widen(extended(low_field, (("band", 1),), 1))
    return (taps(padded, kernel, low_field.shape[1], low_field.shape[2]), padded)


def conv_backward(low_grad, kernel, padded):
    height, width = (low_grad.shape[1], low_grad.shape[2])
    grad_pad = widen(extended(low_grad, (("band", 1),), 1))
    flipped = jnp.swapaxes(kernel[::-1], 1, 2)
    grad_in = taps(grad_pad, flipped, height, width)
    pieces = []
    for tap in range(9):
        row, column = (tap // 3, tap % 3)
        pieces.append(
            jnp.einsum(
                "ghwc,ghwd->cd",
                padded[:, row : row + height, column : column + width],
                low_grad,
                preferred_element_type=jnp.float32,
            )
        )
    return (grad_in, jnp.stack(pieces))


def attend(query_low, key_full, key_valid, factor):
    score_matrix = (
        jnp.einsum("gqc,gkc->gqk", query_low, key_full, preferred_element_type=jnp.float32) * factor
    )
    score_matrix = jnp.where(key_valid[:, None, :], score_matrix, -1e30)
    top = jnp.max(score_matrix, axis=2, keepdims=True)
    raised = jnp.exp(score_matrix - top)
    total = jnp.sum(raised, axis=2, keepdims=True)
    return (raised / total, top, total)


def banded(
    images,
    cotangent,
    sizes,
    matrix_weight,
    matrix_momentum,
    matrix_average,
    vector_weight,
    vector_momentum,
    vector_average,
):
    batch, height, width, channels = images.shape
    square = channels * channels
    queries = height * width
    positions = width * width
    factor = channels ** (-0.5)
    weights = lax.all_gather(
        matrix_weight.astype(jnp.bfloat16), ("img", "band"), axis=0, tiled=True
    )
    kernel_one = weights[: 9 * square].reshape(9, channels, channels)
    kernel_two = weights[9 * square : 18 * square].reshape(9, channels, channels)
    attn_in = weights[18 * square : 21 * square].reshape(3, channels, channels)
    attention_output = weights[21 * square :].reshape(channels, channels)
    lines = lax.axis_index("band") * height + jnp.arange(height)
    across = jnp.arange(width)
    limit = sizes[:, None, None]
    inside = (lines[None, :, None] < limit) & (across[None, None, :] < limit)
    mask = jnp.where(inside, 1.0, 0.0).astype(jnp.float32)[..., None]
    count = (sizes * sizes * (channels // GROUPS)).astype(jnp.float32)
    spots = jnp.arange(positions)
    key_valid = ((spots // width)[None, :] < sizes[:, None]) & (
        (spots % width)[None, :] < sizes[:, None]
    )
    start = images.astype(jnp.float32) * mask
    norm_one, sums_one = normalize(start, mask, count, vector_weight[0], vector_weight[1])
    act_one = activate(norm_one, mask).astype(jnp.bfloat16)
    conv_raw, padded_one = conv_forward(act_one, kernel_one)
    conv_out = conv_raw + vector_weight[2]
    norm_two, sums_two = normalize(conv_out, mask, count, vector_weight[3], vector_weight[4])
    act_two = activate(norm_two, mask).astype(jnp.bfloat16)
    conv_raw, padded_two = conv_forward(act_two, kernel_two)
    resid = (start + conv_raw + vector_weight[5]) * mask
    norm_three, sums_three = normalize(resid, mask, count, vector_weight[6], vector_weight[7])
    normed = (norm_three * mask).astype(jnp.bfloat16).reshape(batch, queries, channels)
    projected = jnp.einsum("gqc,jcd->jgqd", normed, attn_in, preferred_element_type=jnp.float32)
    query_low = (projected[0] + vector_weight[8]).astype(jnp.bfloat16)
    key_low = projected[1].astype(jnp.bfloat16)
    value_low = (projected[2] + vector_weight[9]).astype(jnp.bfloat16)
    key_full, value_full = (
        lax.all_gather(key_low, "band", axis=1, tiled=True),
        lax.all_gather(value_low, "band", axis=1, tiled=True),
    )
    probability_rows, row_top, row_total = attend(query_low, key_full, key_valid, factor)
    mixed_values = jnp.einsum(
        "gqk,gkc->gqc",
        probability_rows.astype(jnp.bfloat16),
        value_full,
        preferred_element_type=jnp.float32,
    ).astype(jnp.bfloat16)
    output_rows = (
        jnp.einsum(
            "gqc,cd->gqd", mixed_values, attention_output, preferred_element_type=jnp.float32
        )
        + vector_weight[10]
    )
    block_out = ((resid + output_rows.reshape(images.shape)) * mask).astype(jnp.bfloat16)
    grad_top = cotangent.astype(jnp.float32) * mask
    grad_proj = grad_top.reshape(batch, queries, channels)
    grad_proj_low = grad_proj.astype(jnp.bfloat16)
    grad_out_weight = jnp.einsum(
        "gqc,gqd->cd", mixed_values, grad_proj_low, preferred_element_type=jnp.float32
    )
    grad_mixed = jnp.einsum(
        "gqd,cd->gqc", grad_proj_low, attention_output, preferred_element_type=jnp.float32
    ).astype(jnp.bfloat16)
    back_keys, back_values = (
        lax.all_gather(key_low, "band", axis=1, tiled=True),
        lax.all_gather(value_low, "band", axis=1, tiled=True),
    )
    back_probs = attend(query_low, back_keys, key_valid, factor)[0]
    grad_probs = jnp.einsum(
        "gqc,gkc->gqk", grad_mixed, back_values, preferred_element_type=jnp.float32
    )
    weighted_sum = jnp.sum(back_probs * grad_probs, axis=2, keepdims=True)
    grad_scores = back_probs * (grad_probs - weighted_sum)
    grad_scores_low = (grad_scores * factor).astype(jnp.bfloat16)
    grad_query = jnp.einsum(
        "gqk,gkc->gqc", grad_scores_low, back_keys, preferred_element_type=jnp.float32
    ).astype(jnp.bfloat16)
    key_terms = jnp.einsum(
        "gqk,gqc->gkc", grad_scores_low, query_low, preferred_element_type=jnp.float32
    )
    value_terms = jnp.einsum(
        "gqk,gqc->gkc",
        back_probs.astype(jnp.bfloat16),
        grad_mixed,
        preferred_element_type=jnp.float32,
    )
    grad_key, grad_value = (
        lax.psum_scatter(
            key_terms.astype(jnp.bfloat16), "band", scatter_dimension=1, tiled=True
        ).astype(jnp.float32),
        lax.psum_scatter(
            value_terms.astype(jnp.bfloat16), "band", scatter_dimension=1, tiled=True
        ).astype(jnp.float32),
    )
    grad_value_low = grad_value.astype(jnp.bfloat16)
    grads_low = jnp.stack([grad_query, grad_key.astype(jnp.bfloat16), grad_value_low])
    grad_in_weights = jnp.einsum(
        "gqc,jgqd->jcd", normed, grads_low, preferred_element_type=jnp.float32
    )
    grad_normed = (
        jnp.einsum("jgqd,jcd->gqc", grads_low, attn_in, preferred_element_type=jnp.float32).reshape(
            images.shape
        )
        * mask
    )
    grad_resid_norm, grad_gain_three, grad_shift_three = normalize_back(
        resid, sums_three, mask, count, vector_weight[6], vector_weight[7], grad_normed
    )
    grad_resid = (grad_top + grad_resid_norm) * mask
    grad_act_two, grad_kernel_two = conv_backward(
        grad_resid.astype(jnp.bfloat16), kernel_two, padded_two
    )
    grad_norm_two = activate_back(norm_two, mask, grad_act_two)
    grad_conv_out, grad_gain_two, grad_shift_two = normalize_back(
        conv_out, sums_two, mask, count, vector_weight[3], vector_weight[4], grad_norm_two
    )
    grad_act_one, grad_kernel_one = conv_backward(
        grad_conv_out.astype(jnp.bfloat16), kernel_one, padded_one
    )
    grad_norm_one = activate_back(norm_one, mask, grad_act_one)
    grad_start, grad_gain_one, grad_shift_one = normalize_back(
        start, sums_one, mask, count, vector_weight[0], vector_weight[1], grad_norm_one
    )
    input_grad = (grad_resid + grad_start) * mask
    vector_terms = jnp.stack(
        [
            grad_gain_one,
            grad_shift_one,
            jnp.sum(grad_conv_out, axis=(0, 1, 2)),
            grad_gain_two,
            grad_shift_two,
            jnp.sum(grad_resid, axis=(0, 1, 2)),
            grad_gain_three,
            grad_shift_three,
            jnp.sum(grad_query, axis=(0, 1), dtype=jnp.float32),
            jnp.sum(grad_value_low, axis=(0, 1), dtype=jnp.float32),
            jnp.sum(grad_proj, axis=(0, 1)),
        ]
    )
    vector_grads = lax.psum(vector_terms, ("img", "band"))
    grad_flat = jnp.concatenate(
        [
            grad_kernel_one.reshape(-1),
            grad_kernel_two.reshape(-1),
            grad_in_weights.reshape(-1),
            grad_out_weight.reshape(-1),
        ]
    )
    matrix_grads = lax.psum_scatter(grad_flat, ("img", "band"), scatter_dimension=0, tiled=True)
    matrix_moments = MOMENTUM * matrix_momentum + matrix_grads
    matrix_masters = matrix_weight - LR_MATRIX * (matrix_grads + MOMENTUM * matrix_moments)
    matrix_means = AVERAGE * matrix_average + (1.0 - AVERAGE) * matrix_masters
    vector_moments = MOMENTUM * vector_momentum + vector_grads
    vector_masters = vector_weight - LR_VECTOR * (vector_grads + MOMENTUM * vector_moments)
    vector_means = AVERAGE * vector_average + (1.0 - AVERAGE) * vector_masters
    return (
        block_out,
        input_grad,
        matrix_grads,
        matrix_moments,
        matrix_means,
        matrix_masters,
        vector_grads,
        vector_moments,
        vector_means,
        vector_masters,
    )


F32 = jnp.float32
BF16 = jnp.bfloat16
SIDE = 32
VMEM_LIMIT = 58 * 1024 * 1024


def dot(a, b):
    return lax.dot_general(a, b, (((1,), (0,)), ((), ())), preferred_element_type=F32)


def dot_nt(a, b):
    return lax.dot_general(a, b, (((1,), (1,)), ((), ())), preferred_element_type=F32)


def dot_tn(a, b):
    return lax.dot_general(a, b, (((0,), (0,)), ((), ())), preferred_element_type=F32)


def call(body, outs, ins, scratch=(), flops=0, name=None):
    spaces = {"v": pl.BlockSpec(memory_space=pltpu.VMEM), "s": pl.BlockSpec(memory_space=pltpu.SMEM),
              "a": pl.BlockSpec(memory_space=pl.ANY)}
    moved = sum(a.size * a.dtype.itemsize for a, _ in ins) + sum(
        o.size * o.dtype.itemsize for o, _ in outs)
    return pl.pallas_call(
        body,
        out_shape=[o for o, _ in outs],
        in_specs=[spaces[s] for _, s in ins],
        out_specs=[spaces[s] for _, s in outs],
        scratch_shapes=list(scratch),
        compiler_params=pltpu.CompilerParams(vmem_limit_bytes=VMEM_LIMIT),
        cost_estimate=pl.CostEstimate(flops=flops, bytes_accessed=moved, transcendentals=0),
        name=name,
    )(*[a for a, _ in ins])


def shape(dims, dtype):
    return jax.ShapeDtypeStruct(dims, dtype)


def fold(x):
    return jnp.sum(x.reshape(x.shape[0] // 8, 8, x.shape[1]), axis=0)


def group_total(x):
    lane = lax.broadcasted_iota(jnp.int32, x.shape, 1)
    width = x.shape[1]
    for s in (1, 2, 4, 8):
        up = pltpu.roll(x, width - s, 1)
        down = pltpu.roll(x, s, 1)
        x = x + jnp.where((lane & s) == 0, up, down)
    return x


def total_of(*parts):
    rows = [jnp.sum(p, axis=0, keepdims=True) for p in parts]
    pad = jnp.zeros((8 - len(rows), rows[0].shape[1]), F32)
    return jnp.concatenate(rows + [pad], axis=0)


def moments(s1, s2, size):
    count = (size * size * 16).astype(F32)
    both = group_total(total_of(s1, s2)) / count
    mean = both[0:1]
    spread = both[1:2] - mean * mean
    return mean, lax.rsqrt(spread + EPS)


def row_mask(size, channels):
    across = lax.broadcasted_iota(jnp.int32, (SIDE, channels), 0)
    inside = across < size
    return lambda h: inside & (h < size)


def sigmoid(y):
    return 0.5 * jnp.tanh(0.5 * y) + 0.5


def rows(h):
    return pl.ds(pl.multiple_of(h * SIDE, SIDE), SIDE)


def put_shifted(ref, h, r, forward):
    channels = r.shape[1]
    w = lax.broadcasted_iota(jnp.int32, r.shape, 0)
    before = jnp.where(w == 0, 0.0, pltpu.roll(r, 1, 0)).astype(BF16)
    after = jnp.where(w == SIDE - 1, 0.0, pltpu.roll(r, SIDE - 1, 0)).astype(BF16)
    first, last = (before, after) if forward else (after, before)
    at = pl.ds(pl.multiple_of((h + 1) * SIDE, SIDE), SIDE)
    ref[at, 0:channels] = first
    ref[at, channels : 2 * channels] = r.astype(BF16)
    ref[at, 2 * channels :] = last


def clear_border(ref):
    zero = jnp.zeros((SIDE, ref.shape[1]), BF16)
    ref[0:SIDE, :] = zero
    ref[(SIDE + 1) * SIDE :, :] = zero


def put_transposed(ref, src_ref, row0, lane0):
    channels, count = ref.shape
    for j in range(count // 256):
        block = src_ref[row0 + j * 256 : row0 + (j + 1) * 256, lane0 : lane0 + channels]
        ref[:, j * 256 : (j + 1) * 256] = block.T


def act_one_body(size_ref, img_ref, vec_ref, a3_ref, at_ref, stat_ref):
    size = size_ref[0]
    channels = img_ref.shape[1]
    mask = row_mask(size, channels)

    def sums(h, carry):
        x = jnp.where(mask(h), img_ref[rows(h), :].astype(F32), 0.0)
        return carry[0] + fold(x), carry[1] + fold(x * x)

    zero = jnp.zeros((8, channels), F32)
    s1, s2 = lax.fori_loop(0, SIDE, sums, (zero, zero), unroll=2)
    mean, scale = moments(s1, s2, size)
    stat_ref[0:1, :] = mean
    stat_ref[1:2, :] = scale
    stat_ref[2:8, :] = jnp.zeros((6, channels), F32)
    apply_norm(img_ref, mean, scale * vec_ref[0:1, :], vec_ref[1:2, :], mask, a3_ref)
    put_transposed(at_ref, a3_ref, SIDE, channels)


def apply_norm(src_ref, mean, scale, shift, mask, a3_ref):
    clear_border(a3_ref)

    def apply(h, carry):
        y = (src_ref[rows(h), :].astype(F32) - mean) * scale + shift
        r = jnp.where(mask(h), y * sigmoid(y), 0.0).astype(BF16).astype(F32)
        put_shifted(a3_ref, h, r, True)
        return carry

    lax.fori_loop(0, SIDE, apply, 0, unroll=2)


def act_one(size, img, vec):
    n, c = img.shape
    return call(act_one_body,
        [(shape((n + 64, 3 * c), BF16), "v"), (shape((c, n), BF16), "v"), (shape((8, c), F32), "v")],
        [(size, "s"), (img, "v"), (vec, "v")], name="act_one")


MB = 512


def start_copies(src_ref, dst_ref, sems, parts, offset=0):
    length = dst_ref.shape[0] // parts
    copies = [
        pltpu.make_async_copy(src_ref.at[pl.ds(offset + p * length, length)], dst_ref.at[pl.ds(p * length, length)], sems.at[p])
        for p in range(parts)
    ]
    for copy in copies:
        copy.start()
    return copies


def conv(a3_ref, k_ref, copies, out_ref, finish):
    n, c = out_ref.shape
    depth = 3 * c
    for dy in range(3):
        copies[dy].wait()
        kernel = k_ref[dy * depth : (dy + 1) * depth, :]

        def block(m, carry):
            at = pl.multiple_of(m * MB, MB)
            value = dot(a3_ref[pl.ds(at + dy * SIDE, MB), :], kernel)
            if dy > 0:
                value = value + out_ref[pl.ds(at, MB), :]
            if dy == 2:
                value = finish(at, value)
            out_ref[pl.ds(at, MB), :] = value
            return carry

        lax.fori_loop(0, n // MB, block, 0, unroll=True)


def conv_one_body(size_ref, a3_ref, k_ref, vec_ref, conv_ref, a3_out, at_out, stat_ref, k_vmem, sems):
    copies = start_copies(k_ref, k_vmem, sems, 3)
    size = size_ref[0]
    channels = conv_ref.shape[1]
    mask = row_mask(size, channels)
    bias = vec_ref[2:3, :]
    conv(a3_ref, k_vmem, copies, conv_ref, lambda at, v: v + bias)

    def sums(h, carry):
        x = jnp.where(mask(h), conv_ref[rows(h), :], 0.0)
        return carry[0] + fold(x), carry[1] + fold(x * x)

    zero = jnp.zeros((8, channels), F32)
    s1, s2 = lax.fori_loop(0, SIDE, sums, (zero, zero), unroll=2)
    mean, scale = moments(s1, s2, size)
    stat_ref[0:1, :] = mean
    stat_ref[1:2, :] = scale
    stat_ref[2:8, :] = jnp.zeros((6, channels), F32)
    apply_norm(conv_ref, mean, scale * vec_ref[3:4, :], vec_ref[4:5, :], mask, a3_out)
    put_transposed(at_out, a3_out, SIDE, channels)


def conv_one(size, a3, weights, vec):
    n, c = a3.shape[0] - 64, a3.shape[1] // 3
    return call(conv_one_body,
        [(shape((n, c), F32), "v"), (shape((n + 64, 3 * c), BF16), "v"), (shape((c, n), BF16), "v"), (shape((8, c), F32), "v")],
        [(size, "s"), (a3, "v"), (weights, "a"), (vec, "v")],
        [pltpu.VMEM((9 * c, c), BF16), pltpu.SemaphoreType.DMA((3,))],
        flops=2 * n * 9 * c * c, name="conv_one")


def conv_two_body(size_ref, a3_ref, k_ref, vec_ref, img_ref, resid_ref, normed_ref, stat_ref, k_vmem, sems):
    channels = resid_ref.shape[1]
    copies = start_copies(k_ref, k_vmem, sems, 3, 9 * channels)
    size = size_ref[0]
    mask = row_mask(size, channels)
    bias = vec_ref[5:6, :]
    conv(a3_ref, k_vmem, copies, resid_ref, lambda at, v: v + bias + img_ref[pl.ds(at, MB), :].astype(F32))

    def sums(h, carry):
        x = jnp.where(mask(h), resid_ref[rows(h), :], 0.0)
        resid_ref[rows(h), :] = x
        return carry[0] + fold(x), carry[1] + fold(x * x)

    zero = jnp.zeros((8, channels), F32)
    s1, s2 = lax.fori_loop(0, SIDE, sums, (zero, zero), unroll=2)
    mean, scale = moments(s1, s2, size)
    stat_ref[0:1, :] = mean
    stat_ref[1:2, :] = scale
    stat_ref[2:8, :] = jnp.zeros((6, channels), F32)
    gain = scale * vec_ref[6:7, :]
    shift = vec_ref[7:8, :]

    def apply(h, carry):
        y = (resid_ref[rows(h), :] - mean) * gain + shift
        normed_ref[rows(h), :] = jnp.where(mask(h), y, 0.0).astype(BF16)
        return carry

    lax.fori_loop(0, SIDE, apply, 0, unroll=2)


def conv_two(size, a3, weights, vec, img):
    n, c = img.shape
    return call(conv_two_body,
        [(shape((n, c), F32), "v"), (shape((n, c), BF16), "v"), (shape((8, c), F32), "v")],
        [(size, "s"), (a3, "v"), (weights, "a"), (vec, "v"), (img, "v")],
        [pltpu.VMEM((9 * c, c), BF16), pltpu.SemaphoreType.DMA((3,))],
        flops=2 * n * 9 * c * c, name="conv_two")


QB = 256


def attention_body(size_ref, normed_ref, w_ref, vec_ref, resid_ref, cot_ref, stat_ref,
                   out_ref, gw_ref, grad_ref, e3_ref, vout_ref,
                   w_vmem, q_ref, k_ref, v_ref, p_ref, ds_ref, mixed_ref, top_ref, gm_ref, gq_ref, gk_ref, gv_ref, nt_ref, sems):
    n, c = normed_ref.shape
    copies = start_copies(w_ref, w_vmem, sems, 4, 18 * c)
    size = size_ref[0]
    mask = row_mask(size, c)
    factor = c ** (-0.5)

    def top_rows(h, carry):
        t = jnp.where(mask(h), cot_ref[rows(h), :].astype(F32), 0.0)
        top_ref[rows(h), :] = t.astype(BF16)
        return carry + fold(t)

    zero = jnp.zeros((8, c), F32)
    top_sum = lax.fori_loop(0, SIDE, top_rows, zero, unroll=2)
    put_transposed(nt_ref, normed_ref, 0, 0)
    for j in range(4):
        copies[j].wait()
    wq, wk, wv, wo = (w_vmem[j * c : (j + 1) * c, :] for j in range(4))
    qb, vb, ob = (vec_ref[j : j + 1, :] for j in (8, 9, 10))

    for m in range(n // MB):
        at = slice(m * MB, (m + 1) * MB)
        x = normed_ref[at, :]
        q_ref[at, :] = (dot(x, wq) + qb).astype(BF16)
        k_ref[at, :] = dot(x, wk).astype(BF16)
        v_ref[at, :] = (dot(x, wv) + vb).astype(BF16)
        gm_ref[at, :] = dot_nt(top_ref[at, :], wo).astype(BF16)

    spot = lax.broadcasted_iota(jnp.int32, (QB, n), 1)
    key_valid = ((spot >> 5) < size) & ((spot & 31) < size)

    def queries(m, carry):
        at = pl.ds(pl.multiple_of(m * QB, QB), QB)
        s = dot_nt(q_ref[at, :], k_ref[...]) * factor
        s = jnp.where(key_valid, s, -1e30)
        raised = jnp.exp(s - jnp.max(s, axis=1, keepdims=True))
        p = raised / jnp.sum(raised, axis=1, keepdims=True)
        low = p.astype(BF16)
        p_ref[at, :] = low
        mixed_ref[at, :] = dot(low, v_ref[...]).astype(BF16)
        gp = dot_nt(gm_ref[at, :], v_ref[...])
        weighted = jnp.sum(p * gp, axis=1, keepdims=True)
        ds = (p * (gp - weighted) * factor).astype(BF16)
        ds_ref[at, :] = ds
        gq_ref[at, :] = dot(ds, k_ref[...]).astype(BF16)
        return carry

    lax.fori_loop(0, n // QB, queries, 0)

    def keys(m, carry):
        at = pl.ds(pl.multiple_of(m * QB, QB), QB)
        gk_ref[at, :] = dot_tn(ds_ref[:, at], q_ref[...]).astype(BF16)
        gv_ref[at, :] = dot_tn(p_ref[:, at], gm_ref[...]).astype(BF16)
        return carry

    lax.fori_loop(0, n // QB, keys, 0)

    gw_ref[0:c, :] = dot(nt_ref[...], gq_ref[...]).astype(gw_ref.dtype)
    gw_ref[c : 2 * c, :] = dot(nt_ref[...], gk_ref[...]).astype(gw_ref.dtype)
    gw_ref[2 * c : 3 * c, :] = dot(nt_ref[...], gv_ref[...]).astype(gw_ref.dtype)
    gw_ref[3 * c : 4 * c, :] = dot_tn(mixed_ref[...], top_ref[...]).astype(gw_ref.dtype)

    for m in range(n // MB):
        at = slice(m * MB, (m + 1) * MB)
        grad_ref[at, :] = dot_nt(gq_ref[at, :], wq) + dot_nt(gk_ref[at, :], wk) + dot_nt(gv_ref[at, :], wv)

    mean, scale = stat_ref[0:1, :], stat_ref[1:2, :]

    def sums(h, carry):
        u = jnp.where(mask(h), grad_ref[rows(h), :], 0.0)
        xhat = (resid_ref[rows(h), :] - mean) * scale
        gq = fold(gq_ref[rows(h), :].astype(F32))
        gv = fold(gv_ref[rows(h), :].astype(F32))
        return carry[0] + fold(u), carry[1] + fold(u * xhat), carry[2] + gq, carry[3] + gv

    su, sux, sq, sv = lax.fori_loop(0, SIDE, sums, (zero, zero, zero, zero), unroll=2)
    count = (size * size * 16).astype(F32)
    gain = vec_ref[6:7, :]
    channel = total_of(su, sux)
    both = group_total(channel * gain) / count
    m1, m2 = both[0:1], both[1:2]
    clear_border(e3_ref)

    def apply(h, carry):
        xhat = (resid_ref[rows(h), :] - mean) * scale
        g = (grad_ref[rows(h), :] * gain - m1 - xhat * m2) * scale + top_ref[rows(h), :].astype(F32)
        g = jnp.where(mask(h), g, 0.0)
        grad_ref[rows(h), :] = g
        put_shifted(e3_ref, h, g.astype(BF16).astype(F32), False)
        return carry + fold(g)

    sg = lax.fori_loop(0, SIDE, apply, zero, unroll=2)
    vout_ref[...] = total_of(sg, su * 0.0 + sux, su, sq, sv, top_sum)

    for m in range(n // MB):
        at = slice(m * MB, (m + 1) * MB)
        out_rows = dot(mixed_ref[at, :], wo) + ob + resid_ref[at, :]
        place = lax.broadcasted_iota(jnp.int32, (MB, c), 0) + m * MB
        good = ((place >> 5) < size) & ((place & 31) < size)
        out_ref[at, :] = jnp.where(good, out_rows, 0.0).astype(BF16)


def attention(size, normed, weights, vec, resid, cot, stat):
    n, c = normed.shape
    full, wide = pltpu.VMEM((n, c), BF16), pltpu.VMEM((n, n), BF16)
    return call(attention_body,
        [(shape((n, c), BF16), "v"), (shape((4 * c, c), BF16), "v"), (shape((n, c), F32), "v"),
         (shape((n + 64, 3 * c), BF16), "v"), (shape((8, c), F32), "v")],
        [(size, "s"), (normed, "v"), (weights, "a"), (vec, "v"), (resid, "v"), (cot, "v"), (stat, "v")],
        [pltpu.VMEM((4 * c, c), BF16), full, full, full, wide, wide, full, full, full, full, full, full,
         pltpu.VMEM((c, n), BF16), pltpu.SemaphoreType.DMA((4,))],
        flops=2 * n * c * (12 * c + 7 * n), name="attention")


def grad_kernel_body(e3_ref, at_ref, gk_ref, stage, sems):
    c, n = at_ref.shape
    copies = []
    for dy in range(3):
        for dx in range(3):
            tap = 3 * dy + dx
            lo = (2 - dy) * SIDE
            value = dot(at_ref[...], e3_ref[lo : lo + n, dx * c : (dx + 1) * c])
            stage[tap * c : (tap + 1) * c, :] = value.astype(gk_ref.dtype)
            copy = pltpu.make_async_copy(stage.at[pl.ds(tap * c, c)], gk_ref.at[pl.ds(tap * c, c)], sems.at[tap])
            copy.start()
            copies.append(copy)
    for copy in copies:
        copy.wait()


def grad_kernel(e3, at, name):
    c, n = at.shape
    return call(grad_kernel_body, [(shape((9 * c, c), BF16), "a")], [(e3, "v"), (at, "v")],
        [pltpu.VMEM((9 * c, c), BF16), pltpu.SemaphoreType.DMA((9,))],
        flops=2 * n * 9 * c * c, name=name)[0]


def conv_back(e3_ref, k_ref, copies, out_ref):
    n, c = out_ref.shape
    for dy in range(3):
        copies[dy].wait()
        lo = (2 - dy) * SIDE
        for m in range(n // MB):
            value = None
            for dx in range(3):
                tap = 3 * dy + dx
                term = dot_nt(e3_ref[lo + m * MB : lo + (m + 1) * MB, dx * c : (dx + 1) * c], k_ref[tap * c : (tap + 1) * c, :])
                value = term if value is None else value + term
            if dy > 0:
                value = value + out_ref[m * MB : (m + 1) * MB, :]
            out_ref[m * MB : (m + 1) * MB, :] = value


def norm_back_sums(src_ref, g_ref, mean, scale, gain, shift, mask, size):
    c = g_ref.shape[1]

    def sums(h, carry):
        xhat = (src_ref[rows(h), :].astype(F32) - mean) * scale
        y = xhat * gain + shift
        s = sigmoid(y)
        u = jnp.where(mask(h), g_ref[rows(h), :] * (s * (1.0 + y * (1.0 - s))), 0.0)
        g_ref[rows(h), :] = u
        return carry[0] + fold(u), carry[1] + fold(u * xhat)

    zero = jnp.zeros((8, c), F32)
    su, sux = lax.fori_loop(0, SIDE, sums, (zero, zero), unroll=2)
    count = (size * size * 16).astype(F32)
    both = group_total(total_of(su, sux) * gain) / count
    return su, sux, both[0:1], both[1:2]


def back_two_body(size_ref, e3_ref, k_ref, vec_ref, conv_ref, stat_ref, e3_out, vout_ref, g_ref, k_vmem, sems):
    n, c = conv_ref.shape
    copies = start_copies(k_ref, k_vmem, sems, 3, 9 * c)
    size = size_ref[0]
    mask = row_mask(size, c)
    conv_back(e3_ref, k_vmem, copies, g_ref)
    mean, scale = stat_ref[0:1, :], stat_ref[1:2, :]
    gain, shift = vec_ref[3:4, :], vec_ref[4:5, :]
    su, sux, m1, m2 = norm_back_sums(conv_ref, g_ref, mean, scale, gain, shift, mask, size)
    clear_border(e3_out)

    def apply(h, carry):
        xhat = (conv_ref[rows(h), :] - mean) * scale
        g = jnp.where(mask(h), (g_ref[rows(h), :] * gain - m1 - xhat * m2) * scale, 0.0)
        put_shifted(e3_out, h, g.astype(BF16).astype(F32), False)
        return carry + fold(g)

    sg = lax.fori_loop(0, SIDE, apply, jnp.zeros((8, c), F32), unroll=2)
    vout_ref[...] = total_of(sg, sux, su)


def back_two(size, e3, weights, vec, conv_out, stat):
    n, c = conv_out.shape
    return call(back_two_body, [(shape((n + 64, 3 * c), BF16), "v"), (shape((8, c), F32), "v")],
        [(size, "s"), (e3, "v"), (weights, "a"), (vec, "v"), (conv_out, "v"), (stat, "v")],
        [pltpu.VMEM((n, c), F32), pltpu.VMEM((9 * c, c), BF16), pltpu.SemaphoreType.DMA((3,))],
        flops=2 * n * 9 * c * c, name="back_two")


def back_one_body(size_ref, e3_ref, k_ref, vec_ref, img_ref, stat_ref, resid_ref, out_ref, vout_ref, g_ref, k_vmem, sems):
    n, c = img_ref.shape
    copies = start_copies(k_ref, k_vmem, sems, 3)
    size = size_ref[0]
    mask = row_mask(size, c)
    conv_back(e3_ref, k_vmem, copies, g_ref)
    mean, scale = stat_ref[0:1, :], stat_ref[1:2, :]
    gain, shift = vec_ref[0:1, :], vec_ref[1:2, :]
    su, sux, m1, m2 = norm_back_sums(img_ref, g_ref, mean, scale, gain, shift, mask, size)

    def apply(h, carry):
        xhat = (img_ref[rows(h), :].astype(F32) - mean) * scale
        g = (g_ref[rows(h), :] * gain - m1 - xhat * m2) * scale + resid_ref[rows(h), :]
        out_ref[rows(h), :] = jnp.where(mask(h), g, 0.0).astype(out_ref.dtype)
        return carry

    lax.fori_loop(0, SIDE, apply, 0, unroll=2)
    vout_ref[...] = total_of(sux, su)


def back_one(size, e3, weights, vec, img, stat, grad_resid):
    n, c = img.shape
    return call(back_one_body, [(shape((n, c), BF16), "v"), (shape((8, c), F32), "v")],
        [(size, "s"), (e3, "v"), (weights, "a"), (vec, "v"), (img, "v"), (stat, "v"), (grad_resid, "v")],
        [pltpu.VMEM((n, c), F32), pltpu.VMEM((9 * c, c), BF16), pltpu.SemaphoreType.DMA((3,))],
        flops=2 * n * 9 * c * c, name="back_one")


ALL = ("img", "band")


def whole_image(
    images,
    cotangent,
    sizes,
    matrix_weight,
    matrix_momentum,
    matrix_average,
    vector_weight,
    vector_momentum,
    vector_average,
):
    batch, height, width, c = images.shape
    n = width * width
    mine = lax.axis_index("band")
    size = lax.dynamic_slice_in_dim(sizes, mine, 1)

    def to_image(field):
        parts = field.reshape(batch, height * width, c)
        return lax.all_to_all(parts, "band", 0, 0, tiled=True).reshape(n, c)

    def to_bands(field):
        parts = field.reshape(batch, height * width, c)
        return lax.all_to_all(parts, "band", 0, 0, tiled=True).reshape(batch, height, width, c)

    weights = lax.all_gather(matrix_weight.astype(BF16).reshape(-1, c), ALL, axis=0, tiled=True)
    img = to_image(images)
    cot = to_image(cotangent)
    a3_one, at_one, stat_one = act_one(size, img, vector_weight)
    conv_out, a3_two, at_two, stat_two = conv_one(size, a3_one, weights, vector_weight)
    resid, normed, stat_three = conv_two(size, a3_two, weights, vector_weight, img)
    out, gw, grad_resid, e3_two, v3 = attention(size, normed, weights, vector_weight, resid, cot, stat_three)
    gk2 = grad_kernel(e3_two, at_two, "grad_kernel_two")
    e3_one, v2 = back_two(size, e3_two, weights, vector_weight, conv_out, stat_two)
    gk1 = grad_kernel(e3_one, at_one, "grad_kernel_one")
    grad_in, v1 = back_one(size, e3_one, weights, vector_weight, img, stat_one, grad_resid)
    block_out = to_bands(out)
    input_grad = to_bands(grad_in).astype(F32)
    vecs = jnp.stack([v1[0], v1[1], v2[0], v2[1], v2[2], v3[0], v3[1], v3[2], v3[3], v3[4], v3[5]])
    vector_grads = lax.psum(vecs, ALL)
    low_grads = lax.psum_scatter(jnp.concatenate([gk1, gk2, gw]), ALL, scatter_dimension=0, tiled=True)
    matrix_grads = low_grads.astype(F32).reshape(-1)
    matrix_moments = MOMENTUM * matrix_momentum + matrix_grads
    matrix_masters = matrix_weight - LR_MATRIX * (matrix_grads + MOMENTUM * matrix_moments)
    matrix_means = AVERAGE * matrix_average + (1.0 - AVERAGE) * matrix_masters
    vector_moments = MOMENTUM * vector_momentum + vector_grads
    vector_masters = vector_weight - LR_VECTOR * (vector_grads + MOMENTUM * vector_moments)
    vector_means = AVERAGE * vector_average + (1.0 - AVERAGE) * vector_masters
    return (
        block_out,
        input_grad,
        matrix_grads,
        matrix_moments,
        matrix_means,
        matrix_masters,
        vector_grads,
        vector_moments,
        vector_means,
        vector_masters,
    )


def solution(mesh):
    whole = mesh.shape["band"]

    def per_device(images, *rest):
        step = whole_image if images.shape[0] == whole and SIDE == images.shape[2] else banded
        return step(images, *rest)

    return jax.shard_map(
            per_device,
        mesh=mesh,
        in_specs=(
            P("img", "band", None, None),
            P("img", "band", None, None),
            P("img"),
            P(("img", "band")),
            P(("img", "band")),
            P(("img", "band")),
            P(),
            P(),
            P(),
        ),
        out_specs=(
            P("img", "band", None, None),
            P("img", "band", None, None),
            P(("img", "band")),
            P(("img", "band")),
            P(("img", "band")),
            P(("img", "band")),
            P(),
            P(),
            P(),
            P(),
        ),
        check_vma=False,
    )
```

```python
import functools

import jax
import jax.numpy as jnp
from jax import lax
from jax.experimental import pallas as pl
from jax.experimental.pallas import tpu as pltpu
from jax.sharding import PartitionSpec as P

GROUPS = 32


EPS = 1e-06
MOMENTUM = 0.9
LR_MATRIX = 4e-05
LR_VECTOR = 0.0001
AVERAGE = 0.75


def extended(array, sides, width):
    for axis, dim in sides:
        count, length = (lax.axis_size(axis), array.shape[dim])
        up = [(i, (i + 1) % count) for i in range(count - 1)]
        down = [(j, i) for i, j in up]
        last = lax.slice_in_dim(array, length - width, length, axis=dim)
        initial = lax.slice_in_dim(array, 0, width, axis=dim)
        before = lax.ppermute(last, axis, up)
        after = lax.ppermute(initial, axis, down)
        array = jnp.concatenate([before, array, after], axis=dim)
    return array


def split_groups(field):
    return field.reshape(field.shape[:3] + (GROUPS, field.shape[3] // GROUPS))


def group_sums(field, mask):
    shaped = split_groups(field)
    weighted = shaped * mask[..., None]
    return (jnp.sum(weighted, axis=(1, 2, 4)), jnp.sum(weighted * shaped, axis=(1, 2, 4)))


def group_apply(field, sums, count, gain, shift):
    center = sums[0] / count[:, None]
    spread = sums[1] / count[:, None] - center * center
    scale = lax.rsqrt(spread + EPS)
    shaped = split_groups(field)
    normed = (shaped - center[:, None, None, :, None]) * scale[:, None, None, :, None]
    return normed.reshape(field.shape) * gain + shift


def normalize(field, mask, count, gain, shift):
    sums = lax.psum(group_sums(field, mask), "band")
    return (group_apply(field, sums, count, gain, shift), sums)


def normalize_back(field, sums, mask, count, gain, shift, upstream):
    _, pull = jax.vjp(
        lambda field_in, sums_in, gain_in, shift_in: group_apply(
            field_in, sums_in, count, gain_in, shift_in
        ),
        field,
        sums,
        gain,
        shift,
    )
    direct, grad_sums, grad_gain, grad_shift = pull(upstream)
    grad_sums = lax.psum(grad_sums, "band")
    _, pull_sums = jax.vjp(lambda field_in: group_sums(field_in, mask), field)
    return (direct + pull_sums(grad_sums)[0], grad_gain, grad_shift)


def activate(field, mask):
    return jax.nn.silu(field) * mask


def activate_back(field, mask, upstream):
    _, pull = jax.vjp(lambda inner: activate(inner, mask), field)
    return pull(upstream)[0]


def widen(field):
    return jnp.pad(field, ((0, 0), (0, 0), (1, 1), (0, 0)))


def taps(padded, kernel, height, width):
    total = jnp.zeros(padded.shape[:1] + (height, width, kernel.shape[2]), jnp.float32)
    for tap in range(9):
        row, column = (tap // 3, tap % 3)
        total = total + jnp.einsum(
            "ghwc,cd->ghwd",
            padded[:, row : row + height, column : column + width],
            kernel[tap],
            preferred_element_type=jnp.float32,
        )
    return total


def conv_forward(low_field, kernel):
    padded = widen(extended(low_field, (("band", 1),), 1))
    return (taps(padded, kernel, low_field.shape[1], low_field.shape[2]), padded)


def conv_backward(low_grad, kernel, padded):
    height, width = (low_grad.shape[1], low_grad.shape[2])
    grad_pad = widen(extended(low_grad, (("band", 1),), 1))
    flipped = jnp.swapaxes(kernel[::-1], 1, 2)
    grad_in = taps(grad_pad, flipped, height, width)
    pieces = []
    for tap in range(9):
        row, column = (tap // 3, tap % 3)
        pieces.append(
            jnp.einsum(
                "ghwc,ghwd->cd",
                padded[:, row : row + height, column : column + width],
                low_grad,
                preferred_element_type=jnp.float32,
            )
        )
    return (grad_in, jnp.stack(pieces))


def attend(query_low, key_full, key_valid, factor):
    score_matrix = (
        jnp.einsum("gqc,gkc->gqk", query_low, key_full, preferred_element_type=jnp.float32) * factor
    )
    score_matrix = jnp.where(key_valid[:, None, :], score_matrix, -1e30)
    top = jnp.max(score_matrix, axis=2, keepdims=True)
    raised = jnp.exp(score_matrix - top)
    total = jnp.sum(raised, axis=2, keepdims=True)
    return (raised / total, top, total)


def banded(
    images,
    cotangent,
    sizes,
    matrix_weight,
    matrix_momentum,
    matrix_average,
    vector_weight,
    vector_momentum,
    vector_average,
):
    batch, height, width, channels = images.shape
    square = channels * channels
    queries = height * width
    positions = width * width
    factor = channels ** (-0.5)
    weights = lax.all_gather(
        matrix_weight.astype(jnp.bfloat16), ("img", "band"), axis=0, tiled=True
    )
    kernel_one = weights[: 9 * square].reshape(9, channels, channels)
    kernel_two = weights[9 * square : 18 * square].reshape(9, channels, channels)
    attn_in = weights[18 * square : 21 * square].reshape(3, channels, channels)
    attention_output = weights[21 * square :].reshape(channels, channels)
    lines = lax.axis_index("band") * height + jnp.arange(height)
    across = jnp.arange(width)
    limit = sizes[:, None, None]
    inside = (lines[None, :, None] < limit) & (across[None, None, :] < limit)
    mask = jnp.where(inside, 1.0, 0.0).astype(jnp.float32)[..., None]
    count = (sizes * sizes * (channels // GROUPS)).astype(jnp.float32)
    spots = jnp.arange(positions)
    key_valid = ((spots // width)[None, :] < sizes[:, None]) & (
        (spots % width)[None, :] < sizes[:, None]
    )
    start = images.astype(jnp.float32) * mask
    norm_one, sums_one = normalize(start, mask, count, vector_weight[0], vector_weight[1])
    act_one = activate(norm_one, mask).astype(jnp.bfloat16)
    conv_raw, padded_one = conv_forward(act_one, kernel_one)
    conv_out = conv_raw + vector_weight[2]
    norm_two, sums_two = normalize(conv_out, mask, count, vector_weight[3], vector_weight[4])
    act_two = activate(norm_two, mask).astype(jnp.bfloat16)
    conv_raw, padded_two = conv_forward(act_two, kernel_two)
    resid = (start + conv_raw + vector_weight[5]) * mask
    norm_three, sums_three = normalize(resid, mask, count, vector_weight[6], vector_weight[7])
    normed = (norm_three * mask).astype(jnp.bfloat16).reshape(batch, queries, channels)
    projected = jnp.einsum("gqc,jcd->jgqd", normed, attn_in, preferred_element_type=jnp.float32)
    query_low = (projected[0] + vector_weight[8]).astype(jnp.bfloat16)
    key_low = projected[1].astype(jnp.bfloat16)
    value_low = (projected[2] + vector_weight[9]).astype(jnp.bfloat16)
    key_full, value_full = (
        lax.all_gather(key_low, "band", axis=1, tiled=True),
        lax.all_gather(value_low, "band", axis=1, tiled=True),
    )
    probability_rows, row_top, row_total = attend(query_low, key_full, key_valid, factor)
    mixed_values = jnp.einsum(
        "gqk,gkc->gqc",
        probability_rows.astype(jnp.bfloat16),
        value_full,
        preferred_element_type=jnp.float32,
    ).astype(jnp.bfloat16)
    output_rows = (
        jnp.einsum(
            "gqc,cd->gqd", mixed_values, attention_output, preferred_element_type=jnp.float32
        )
        + vector_weight[10]
    )
    block_out = ((resid + output_rows.reshape(images.shape)) * mask).astype(jnp.bfloat16)
    grad_top = cotangent.astype(jnp.float32) * mask
    grad_proj = grad_top.reshape(batch, queries, channels)
    grad_proj_low = grad_proj.astype(jnp.bfloat16)
    grad_out_weight = jnp.einsum(
        "gqc,gqd->cd", mixed_values, grad_proj_low, preferred_element_type=jnp.float32
    )
    grad_mixed = jnp.einsum(
        "gqd,cd->gqc", grad_proj_low, attention_output, preferred_element_type=jnp.float32
    ).astype(jnp.bfloat16)
    back_keys, back_values = (
        lax.all_gather(key_low, "band", axis=1, tiled=True),
        lax.all_gather(value_low, "band", axis=1, tiled=True),
    )
    back_probs = attend(query_low, back_keys, key_valid, factor)[0]
    grad_probs = jnp.einsum(
        "gqc,gkc->gqk", grad_mixed, back_values, preferred_element_type=jnp.float32
    )
    weighted_sum = jnp.sum(back_probs * grad_probs, axis=2, keepdims=True)
    grad_scores = back_probs * (grad_probs - weighted_sum)
    grad_scores_low = (grad_scores * factor).astype(jnp.bfloat16)
    grad_query = jnp.einsum(
        "gqk,gkc->gqc", grad_scores_low, back_keys, preferred_element_type=jnp.float32
    ).astype(jnp.bfloat16)
    key_terms = jnp.einsum(
        "gqk,gqc->gkc", grad_scores_low, query_low, preferred_element_type=jnp.float32
    )
    value_terms = jnp.einsum(
        "gqk,gqc->gkc",
        back_probs.astype(jnp.bfloat16),
        grad_mixed,
        preferred_element_type=jnp.float32,
    )
    grad_key, grad_value = (
        lax.psum_scatter(
            key_terms.astype(jnp.bfloat16), "band", scatter_dimension=1, tiled=True
        ).astype(jnp.float32),
        lax.psum_scatter(
            value_terms.astype(jnp.bfloat16), "band", scatter_dimension=1, tiled=True
        ).astype(jnp.float32),
    )
    grad_value_low = grad_value.astype(jnp.bfloat16)
    grads_low = jnp.stack([grad_query, grad_key.astype(jnp.bfloat16), grad_value_low])
    grad_in_weights = jnp.einsum(
        "gqc,jgqd->jcd", normed, grads_low, preferred_element_type=jnp.float32
    )
    grad_normed = (
        jnp.einsum("jgqd,jcd->gqc", grads_low, attn_in, preferred_element_type=jnp.float32).reshape(
            images.shape
        )
        * mask
    )
    grad_resid_norm, grad_gain_three, grad_shift_three = normalize_back(
        resid, sums_three, mask, count, vector_weight[6], vector_weight[7], grad_normed
    )
    grad_resid = (grad_top + grad_resid_norm) * mask
    grad_act_two, grad_kernel_two = conv_backward(
        grad_resid.astype(jnp.bfloat16), kernel_two, padded_two
    )
    grad_norm_two = activate_back(norm_two, mask, grad_act_two)
    grad_conv_out, grad_gain_two, grad_shift_two = normalize_back(
        conv_out, sums_two, mask, count, vector_weight[3], vector_weight[4], grad_norm_two
    )
    grad_act_one, grad_kernel_one = conv_backward(
        grad_conv_out.astype(jnp.bfloat16), kernel_one, padded_one
    )
    grad_norm_one = activate_back(norm_one, mask, grad_act_one)
    grad_start, grad_gain_one, grad_shift_one = normalize_back(
        start, sums_one, mask, count, vector_weight[0], vector_weight[1], grad_norm_one
    )
    input_grad = (grad_resid + grad_start) * mask
    vector_terms = jnp.stack(
        [
            grad_gain_one,
            grad_shift_one,
            jnp.sum(grad_conv_out, axis=(0, 1, 2)),
            grad_gain_two,
            grad_shift_two,
            jnp.sum(grad_resid, axis=(0, 1, 2)),
            grad_gain_three,
            grad_shift_three,
            jnp.sum(grad_query, axis=(0, 1), dtype=jnp.float32),
            jnp.sum(grad_value_low, axis=(0, 1), dtype=jnp.float32),
            jnp.sum(grad_proj, axis=(0, 1)),
        ]
    )
    vector_grads = lax.psum(vector_terms, ("img", "band"))
    grad_flat = jnp.concatenate(
        [
            grad_kernel_one.reshape(-1),
            grad_kernel_two.reshape(-1),
            grad_in_weights.reshape(-1),
            grad_out_weight.reshape(-1),
        ]
    )
    matrix_grads = lax.psum_scatter(grad_flat, ("img", "band"), scatter_dimension=0, tiled=True)
    matrix_moments = MOMENTUM * matrix_momentum + matrix_grads
    matrix_masters = matrix_weight - LR_MATRIX * (matrix_grads + MOMENTUM * matrix_moments)
    matrix_means = AVERAGE * matrix_average + (1.0 - AVERAGE) * matrix_masters
    vector_moments = MOMENTUM * vector_momentum + vector_grads
    vector_masters = vector_weight - LR_VECTOR * (vector_grads + MOMENTUM * vector_moments)
    vector_means = AVERAGE * vector_average + (1.0 - AVERAGE) * vector_masters
    return (
        block_out,
        input_grad,
        matrix_grads,
        matrix_moments,
        matrix_means,
        matrix_masters,
        vector_grads,
        vector_moments,
        vector_means,
        vector_masters,
    )


F32 = jnp.float32
BF16 = jnp.bfloat16
SIDE = 32
VMEM_LIMIT = 58 * 1024 * 1024


def dot(a, b):
    return lax.dot_general(a, b, (((1,), (0,)), ((), ())), preferred_element_type=F32)


def dot_nt(a, b):
    return lax.dot_general(a, b, (((1,), (1,)), ((), ())), preferred_element_type=F32)


def dot_tn(a, b):
    return lax.dot_general(a, b, (((0,), (0,)), ((), ())), preferred_element_type=F32)


def call(body, outs, ins, scratch=(), flops=0, name=None, aliases=None):
    spaces = {"v": pl.BlockSpec(memory_space=pltpu.VMEM), "s": pl.BlockSpec(memory_space=pltpu.SMEM),
              "a": pl.BlockSpec(memory_space=pl.ANY)}
    moved = sum(a.size * a.dtype.itemsize for a, _ in ins) + sum(
        o.size * o.dtype.itemsize for o, _ in outs)
    return pl.pallas_call(
        body,
        out_shape=[o for o, _ in outs],
        in_specs=[spaces[s] for _, s in ins],
        out_specs=[spaces[s] for _, s in outs],
        scratch_shapes=list(scratch),
        input_output_aliases=aliases or {},
        compiler_params=pltpu.CompilerParams(vmem_limit_bytes=VMEM_LIMIT),
        cost_estimate=pl.CostEstimate(flops=flops, bytes_accessed=moved, transcendentals=0),
        name=name,
    )(*[a for a, _ in ins])


def shape(dims, dtype):
    return jax.ShapeDtypeStruct(dims, dtype)


def fold(x):
    return jnp.sum(x.reshape(x.shape[0] // 8, 8, x.shape[1]), axis=0)


def group_total(x):
    lane = lax.broadcasted_iota(jnp.int32, x.shape, 1)
    width = x.shape[1]
    for s in (1, 2, 4, 8):
        up = pltpu.roll(x, width - s, 1)
        down = pltpu.roll(x, s, 1)
        x = x + jnp.where((lane & s) == 0, up, down)
    return x


def total_of(*parts):
    rows = [jnp.sum(p, axis=0, keepdims=True) for p in parts]
    pad = jnp.zeros((8 - len(rows), rows[0].shape[1]), F32)
    return jnp.concatenate(rows + [pad], axis=0)


def moments(s1, s2, size):
    count = (size * size * 16).astype(F32)
    both = group_total(total_of(s1, s2)) / count
    mean = both[0:1]
    spread = both[1:2] - mean * mean
    return mean, lax.rsqrt(spread + EPS)


def row_mask(size, channels):
    across = lax.broadcasted_iota(jnp.int32, (SIDE, channels), 0)
    inside = across < size
    return lambda h: inside & (h < size)


def sigmoid(y):
    return 0.5 * jnp.tanh(0.5 * y) + 0.5


def rows(h):
    return pl.ds(pl.multiple_of(h * SIDE, SIDE), SIDE)


def put_shifted(ref, h, r, forward):
    channels = r.shape[1]
    w = lax.broadcasted_iota(jnp.int32, r.shape, 0)
    before = jnp.where(w == 0, 0.0, pltpu.roll(r, 1, 0)).astype(BF16)
    after = jnp.where(w == SIDE - 1, 0.0, pltpu.roll(r, SIDE - 1, 0)).astype(BF16)
    first, last = (before, after) if forward else (after, before)
    at = pl.ds(pl.multiple_of((h + 1) * SIDE, SIDE), SIDE)
    ref[at, 0:channels] = first
    ref[at, channels : 2 * channels] = r.astype(BF16)
    ref[at, 2 * channels :] = last


def clear_border(ref):
    zero = jnp.zeros((SIDE, ref.shape[1]), BF16)
    ref[0:SIDE, :] = zero
    ref[(SIDE + 1) * SIDE :, :] = zero


def put_transposed(ref, src_ref, row0, lane0):
    channels, count = ref.shape
    for j in range(count // 256):
        block = src_ref[row0 + j * 256 : row0 + (j + 1) * 256, lane0 : lane0 + channels]
        ref[:, j * 256 : (j + 1) * 256] = block.T


def act_one_body(size_ref, img_ref, vec_ref, a3_ref, at_ref, stat_ref):
    size = size_ref[0]
    channels = img_ref.shape[1]
    mask = row_mask(size, channels)

    def sums(h, carry):
        x = jnp.where(mask(h), img_ref[rows(h), :].astype(F32), 0.0)
        return carry[0] + fold(x), carry[1] + fold(x * x)

    zero = jnp.zeros((8, channels), F32)
    s1, s2 = lax.fori_loop(0, SIDE, sums, (zero, zero), unroll=2)
    mean, scale = moments(s1, s2, size)
    stat_ref[0:1, :] = mean
    stat_ref[1:2, :] = scale
    stat_ref[2:8, :] = jnp.zeros((6, channels), F32)
    apply_norm(img_ref, mean, scale * vec_ref[0:1, :], vec_ref[1:2, :], mask, a3_ref)
    put_transposed(at_ref, a3_ref, SIDE, channels)


def apply_norm(src_ref, mean, scale, shift, mask, a3_ref):
    clear_border(a3_ref)

    def apply(h, carry):
        y = (src_ref[rows(h), :].astype(F32) - mean) * scale + shift
        r = jnp.where(mask(h), y * sigmoid(y), 0.0).astype(BF16).astype(F32)
        put_shifted(a3_ref, h, r, True)
        return carry

    lax.fori_loop(0, SIDE, apply, 0, unroll=2)


def act_one(size, img, vec):
    n, c = img.shape
    return call(act_one_body,
        [(shape((n + 64, 3 * c), BF16), "v"), (shape((c, n), BF16), "v"), (shape((8, c), F32), "v")],
        [(size, "s"), (img, "v"), (vec, "v")], name="act_one")


MB = 512


def start_copies(src_ref, dst_ref, sems, parts, offset=0):
    length = dst_ref.shape[0] // parts
    copies = [
        pltpu.make_async_copy(src_ref.at[pl.ds(offset + p * length, length)], dst_ref.at[pl.ds(p * length, length)], sems.at[p])
        for p in range(parts)
    ]
    for copy in copies:
        copy.start()
    return copies


def conv(a3_ref, k_ref, copies, out_ref, finish):
    n, c = out_ref.shape
    depth = 3 * c
    for dy in range(3):
        copies[dy].wait()
        kernel = k_ref[dy * depth : (dy + 1) * depth, :]

        def block(m, carry):
            at = pl.multiple_of(m * MB, MB)
            value = dot(a3_ref[pl.ds(at + dy * SIDE, MB), :], kernel)
            if dy > 0:
                value = value + out_ref[pl.ds(at, MB), :]
            if dy == 2:
                value = finish(at, value)
            out_ref[pl.ds(at, MB), :] = value
            return carry

        lax.fori_loop(0, n // MB, block, 0, unroll=True)


def conv_one_body(size_ref, a3_ref, k_ref, vec_ref, conv_ref, a3_out, at_out, stat_ref, k_vmem, sems):
    copies = start_copies(k_ref, k_vmem, sems, 3)
    size = size_ref[0]
    channels = conv_ref.shape[1]
    mask = row_mask(size, channels)
    bias = vec_ref[2:3, :]
    conv(a3_ref, k_vmem, copies, conv_ref, lambda at, v: v + bias)

    def sums(h, carry):
        x = jnp.where(mask(h), conv_ref[rows(h), :], 0.0)
        return carry[0] + fold(x), carry[1] + fold(x * x)

    zero = jnp.zeros((8, channels), F32)
    s1, s2 = lax.fori_loop(0, SIDE, sums, (zero, zero), unroll=2)
    mean, scale = moments(s1, s2, size)
    stat_ref[0:1, :] = mean
    stat_ref[1:2, :] = scale
    stat_ref[2:8, :] = jnp.zeros((6, channels), F32)
    apply_norm(conv_ref, mean, scale * vec_ref[3:4, :], vec_ref[4:5, :], mask, a3_out)
    put_transposed(at_out, a3_out, SIDE, channels)


def conv_one(size, a3, weights, vec):
    n, c = a3.shape[0] - 64, a3.shape[1] // 3
    return call(conv_one_body,
        [(shape((n, c), F32), "v"), (shape((n + 64, 3 * c), BF16), "v"), (shape((c, n), BF16), "v"), (shape((8, c), F32), "v")],
        [(size, "s"), (a3, "v"), (weights, "a"), (vec, "v")],
        [pltpu.VMEM((9 * c, c), BF16), pltpu.SemaphoreType.DMA((3,))],
        flops=2 * n * 9 * c * c, name="conv_one")


def conv_two_body(size_ref, a3_ref, k_ref, vec_ref, img_ref, resid_ref, normed_ref, stat_ref, k_vmem, sems):
    channels = resid_ref.shape[1]
    copies = start_copies(k_ref, k_vmem, sems, 3, 9 * channels)
    size = size_ref[0]
    mask = row_mask(size, channels)
    bias = vec_ref[5:6, :]
    conv(a3_ref, k_vmem, copies, resid_ref, lambda at, v: v + bias + img_ref[pl.ds(at, MB), :].astype(F32))

    def sums(h, carry):
        x = jnp.where(mask(h), resid_ref[rows(h), :], 0.0)
        resid_ref[rows(h), :] = x
        return carry[0] + fold(x), carry[1] + fold(x * x)

    zero = jnp.zeros((8, channels), F32)
    s1, s2 = lax.fori_loop(0, SIDE, sums, (zero, zero), unroll=2)
    mean, scale = moments(s1, s2, size)
    stat_ref[0:1, :] = mean
    stat_ref[1:2, :] = scale
    stat_ref[2:8, :] = jnp.zeros((6, channels), F32)
    gain = scale * vec_ref[6:7, :]
    shift = vec_ref[7:8, :]

    def apply(h, carry):
        y = (resid_ref[rows(h), :] - mean) * gain + shift
        normed_ref[rows(h), :] = jnp.where(mask(h), y, 0.0).astype(BF16)
        return carry

    lax.fori_loop(0, SIDE, apply, 0, unroll=2)


def conv_two(size, a3, weights, vec, img):
    n, c = img.shape
    return call(conv_two_body,
        [(shape((n, c), F32), "v"), (shape((n, c), BF16), "v"), (shape((8, c), F32), "v")],
        [(size, "s"), (a3, "v"), (weights, "a"), (vec, "v"), (img, "v")],
        [pltpu.VMEM((9 * c, c), BF16), pltpu.SemaphoreType.DMA((3,))],
        flops=2 * n * 9 * c * c, name="conv_two")


def pieces_of(row, count, block):
    found = []
    for owner in range(row // block, (row + count - 1) // block + 1):
        found.append((owner, max(row, owner * block), min(row + count, (owner + 1) * block)))
    return found


def send_rows(stage, base, row, count, at_ref, halves, sem, block):
    started = []
    for owner, lo, hi in pieces_of(row, count, block):
        half, spot = owner // 16, owner % 16
        z, x, y, c = spot // 8, (spot >> 2) & 1, (spot >> 1) & 1, spot & 1
        index = ((at_ref[1] ^ x) * 2 + (at_ref[2] ^ y)) * 2 + z
        source = stage.at[pl.ds(base + lo - row, hi - lo)]
        place = pl.ds(lo - owner * block, hi - lo)
        for kept, ref in enumerate(halves[half]):

            @pl.when(((at_ref[3] ^ c) == kept))
            def _(ref=ref, source=source, place=place):
                pltpu.make_async_copy(source, ref.at[index, place], sem).start()

    wait = pltpu.make_async_copy(stage.at[pl.ds(base, count)], stage.at[pl.ds(base, count)], sem)
    return wait


QB = 256


def attention_body(size_ref, normed_ref, w_ref, vec_ref, resid_ref, cot_ref, stat_ref,
                   out_ref, mine_ref, theirs_ref, grad_ref, e3_ref, vout_ref,
                   gw_ref, gw_sem, w_vmem, q_ref, k_ref, v_ref, p_ref, ds_ref, mixed_ref, top_ref, gm_ref, gq_ref, gk_ref, gv_ref, nt_ref, sems):
    n, c = normed_ref.shape
    copies = start_copies(w_ref, w_vmem, sems, 4, 18 * c)
    size = size_ref[0]
    mask = row_mask(size, c)
    factor = c ** (-0.5)

    def top_rows(h, carry):
        t = jnp.where(mask(h), cot_ref[rows(h), :].astype(F32), 0.0)
        top_ref[rows(h), :] = t.astype(BF16)
        return carry + fold(t)

    zero = jnp.zeros((8, c), F32)
    top_sum = lax.fori_loop(0, SIDE, top_rows, zero, unroll=2)
    put_transposed(nt_ref, normed_ref, 0, 0)
    for j in range(4):
        copies[j].wait()
    wq, wk, wv, wo = (w_vmem[j * c : (j + 1) * c, :] for j in range(4))
    qb, vb, ob = (vec_ref[j : j + 1, :] for j in (8, 9, 10))

    for m in range(n // MB):
        at = slice(m * MB, (m + 1) * MB)
        x = normed_ref[at, :]
        q_ref[at, :] = (dot(x, wq) + qb).astype(BF16)
        k_ref[at, :] = dot(x, wk).astype(BF16)
        v_ref[at, :] = (dot(x, wv) + vb).astype(BF16)
        gm_ref[at, :] = dot_nt(top_ref[at, :], wo).astype(BF16)

    spot = lax.broadcasted_iota(jnp.int32, (QB, n), 1)
    key_valid = ((spot >> 5) < size) & ((spot & 31) < size)

    def queries(m, carry):
        at = pl.ds(pl.multiple_of(m * QB, QB), QB)
        s = dot_nt(q_ref[at, :], k_ref[...]) * factor
        s = jnp.where(key_valid, s, -1e30)
        raised = jnp.exp(s - jnp.max(s, axis=1, keepdims=True))
        p = raised / jnp.sum(raised, axis=1, keepdims=True)
        low = p.astype(BF16)
        p_ref[at, :] = low
        mixed_ref[at, :] = dot(low, v_ref[...]).astype(BF16)
        gp = dot_nt(gm_ref[at, :], v_ref[...])
        weighted = jnp.sum(p * gp, axis=1, keepdims=True)
        ds = (p * (gp - weighted) * factor).astype(BF16)
        ds_ref[at, :] = ds
        gq_ref[at, :] = dot(ds, k_ref[...]).astype(BF16)
        return carry

    lax.fori_loop(0, n // QB, queries, 0)

    def keys(m, carry):
        at = pl.ds(pl.multiple_of(m * QB, QB), QB)
        gk_ref[at, :] = dot_tn(ds_ref[:, at], q_ref[...]).astype(BF16)
        gv_ref[at, :] = dot_tn(p_ref[:, at], gm_ref[...]).astype(BF16)
        return carry

    lax.fori_loop(0, n // QB, keys, 0)

    gw_ref[0:c, :] = dot(nt_ref[...], gq_ref[...]).astype(gw_ref.dtype)
    gw_ref[c : 2 * c, :] = dot(nt_ref[...], gk_ref[...]).astype(gw_ref.dtype)
    gw_ref[2 * c : 3 * c, :] = dot(nt_ref[...], gv_ref[...]).astype(gw_ref.dtype)
    gw_ref[3 * c : 4 * c, :] = dot_tn(mixed_ref[...], top_ref[...]).astype(gw_ref.dtype)

    halves = (None, (mine_ref, theirs_ref))
    block = mine_ref.shape[1]
    waits = [send_rows(gw_ref, 0, 18 * c, 4 * c, size_ref, halves, gw_sem, block)]

    for m in range(n // MB):
        at = slice(m * MB, (m + 1) * MB)
        grad_ref[at, :] = dot_nt(gq_ref[at, :], wq) + dot_nt(gk_ref[at, :], wk) + dot_nt(gv_ref[at, :], wv)

    mean, scale = stat_ref[0:1, :], stat_ref[1:2, :]

    def sums(h, carry):
        u = jnp.where(mask(h), grad_ref[rows(h), :], 0.0)
        xhat = (resid_ref[rows(h), :] - mean) * scale
        gq = fold(gq_ref[rows(h), :].astype(F32))
        gv = fold(gv_ref[rows(h), :].astype(F32))
        return carry[0] + fold(u), carry[1] + fold(u * xhat), carry[2] + gq, carry[3] + gv

    su, sux, sq, sv = lax.fori_loop(0, SIDE, sums, (zero, zero, zero, zero), unroll=2)
    count = (size * size * 16).astype(F32)
    gain = vec_ref[6:7, :]
    channel = total_of(su, sux)
    both = group_total(channel * gain) / count
    m1, m2 = both[0:1], both[1:2]
    clear_border(e3_ref)

    def apply(h, carry):
        xhat = (resid_ref[rows(h), :] - mean) * scale
        g = (grad_ref[rows(h), :] * gain - m1 - xhat * m2) * scale + top_ref[rows(h), :].astype(F32)
        g = jnp.where(mask(h), g, 0.0)
        grad_ref[rows(h), :] = g
        put_shifted(e3_ref, h, g.astype(BF16).astype(F32), False)
        return carry + fold(g)

    sg = lax.fori_loop(0, SIDE, apply, zero, unroll=2)
    vout_ref[...] = total_of(sg, su * 0.0 + sux, su, sq, sv, top_sum)

    for m in range(n // MB):
        at = slice(m * MB, (m + 1) * MB)
        out_rows = dot(mixed_ref[at, :], wo) + ob + resid_ref[at, :]
        place = lax.broadcasted_iota(jnp.int32, (MB, c), 0) + m * MB
        good = ((place >> 5) < size) & ((place & 31) < size)
        out_ref[at, :] = jnp.where(good, out_rows, 0.0).astype(BF16)
    for wait in waits:
        wait.wait()


def attention(size, normed, weights, vec, resid, cot, stat):
    n, c = normed.shape
    half = shape((8, weights.shape[0] // 32, c), BF16)
    full, wide = pltpu.VMEM((n, c), BF16), pltpu.VMEM((n, n), BF16)
    return call(attention_body,
        [(shape((n, c), BF16), "v"), (half, "a"), (half, "a"), (shape((n, c), F32), "v"),
         (shape((n + 64, 3 * c), BF16), "v"), (shape((8, c), F32), "v")],
        [(size, "s"), (normed, "v"), (weights, "a"), (vec, "v"), (resid, "v"), (cot, "v"), (stat, "v")],
        [pltpu.VMEM((4 * c, c), BF16), pltpu.SemaphoreType.DMA, pltpu.VMEM((4 * c, c), BF16), full, full, full, wide, wide, full, full, full, full, full, full,
         pltpu.VMEM((c, n), BF16), pltpu.SemaphoreType.DMA((4,))],
        flops=2 * n * c * (12 * c + 7 * n), name="attention")


def grad_kernel_body(at_ref, e3_ref, act_ref, *refs, row, kept):
    *outs, stage, sems = refs[kept:]
    halves = (outs[0:2], outs[2:4])
    c, n = act_ref.shape
    block = outs[0].shape[1]
    waits = []
    for dy in range(3):
        for dx in range(3):
            tap = 3 * dy + dx
            lo = (2 - dy) * SIDE
            value = dot(act_ref[...], e3_ref[lo : lo + n, dx * c : (dx + 1) * c])
            stage[tap * c : (tap + 1) * c, :] = value.astype(BF16)
            waits.append(send_rows(stage, tap * c, row + tap * c, c, at_ref, halves, sems.at[tap], block))
    for wait in waits:
        wait.wait()


def grad_kernel_two(at, e3, act, mine_high, theirs_high):
    c, n = act.shape
    half = shape(mine_high.shape, BF16)
    return call(functools.partial(grad_kernel_body, row=9 * c, kept=2),
        [(half, "a"), (half, "a"), (half, "a"), (half, "a")],
        [(at, "s"), (e3, "v"), (act, "v"), (mine_high, "a"), (theirs_high, "a")],
        [pltpu.VMEM((9 * c, c), BF16), pltpu.SemaphoreType.DMA((9,))],
        flops=2 * n * 9 * c * c, name="grad_kernel_two", aliases={3: 2, 4: 3})


def grad_kernel_one(at, e3, act, mine_low, theirs_low):
    c, n = act.shape
    half = shape(mine_low.shape, BF16)
    return call(functools.partial(grad_kernel_body, row=0, kept=2),
        [(half, "a"), (half, "a")],
        [(at, "s"), (e3, "v"), (act, "v"), (mine_low, "a"), (theirs_low, "a")],
        [pltpu.VMEM((9 * c, c), BF16), pltpu.SemaphoreType.DMA((9,))],
        flops=2 * n * 9 * c * c, name="grad_kernel_one", aliases={3: 0, 4: 1})


def conv_back(e3_ref, k_ref, copies, out_ref):
    n, c = out_ref.shape
    for dy in range(3):
        copies[dy].wait()
        lo = (2 - dy) * SIDE
        for m in range(n // MB):
            value = None
            for dx in range(3):
                tap = 3 * dy + dx
                term = dot_nt(e3_ref[lo + m * MB : lo + (m + 1) * MB, dx * c : (dx + 1) * c], k_ref[tap * c : (tap + 1) * c, :])
                value = term if value is None else value + term
            if dy > 0:
                value = value + out_ref[m * MB : (m + 1) * MB, :]
            out_ref[m * MB : (m + 1) * MB, :] = value


def norm_back_sums(src_ref, g_ref, mean, scale, gain, shift, mask, size):
    c = g_ref.shape[1]

    def sums(h, carry):
        xhat = (src_ref[rows(h), :].astype(F32) - mean) * scale
        y = xhat * gain + shift
        s = sigmoid(y)
        u = jnp.where(mask(h), g_ref[rows(h), :] * (s * (1.0 + y * (1.0 - s))), 0.0)
        g_ref[rows(h), :] = u
        return carry[0] + fold(u), carry[1] + fold(u * xhat)

    zero = jnp.zeros((8, c), F32)
    su, sux = lax.fori_loop(0, SIDE, sums, (zero, zero), unroll=2)
    count = (size * size * 16).astype(F32)
    both = group_total(total_of(su, sux) * gain) / count
    return su, sux, both[0:1], both[1:2]


def back_two_body(size_ref, e3_ref, k_ref, vec_ref, conv_ref, stat_ref, e3_out, vout_ref, g_ref, k_vmem, sems):
    n, c = conv_ref.shape
    copies = start_copies(k_ref, k_vmem, sems, 3, 9 * c)
    size = size_ref[0]
    mask = row_mask(size, c)
    conv_back(e3_ref, k_vmem, copies, g_ref)
    mean, scale = stat_ref[0:1, :], stat_ref[1:2, :]
    gain, shift = vec_ref[3:4, :], vec_ref[4:5, :]
    su, sux, m1, m2 = norm_back_sums(conv_ref, g_ref, mean, scale, gain, shift, mask, size)
    clear_border(e3_out)

    def apply(h, carry):
        xhat = (conv_ref[rows(h), :] - mean) * scale
        g = jnp.where(mask(h), (g_ref[rows(h), :] * gain - m1 - xhat * m2) * scale, 0.0)
        put_shifted(e3_out, h, g.astype(BF16).astype(F32), False)
        return carry + fold(g)

    sg = lax.fori_loop(0, SIDE, apply, jnp.zeros((8, c), F32), unroll=2)
    vout_ref[...] = total_of(sg, sux, su)


def back_two(size, e3, weights, vec, conv_out, stat):
    n, c = conv_out.shape
    return call(back_two_body, [(shape((n + 64, 3 * c), BF16), "v"), (shape((8, c), F32), "v")],
        [(size, "s"), (e3, "v"), (weights, "a"), (vec, "v"), (conv_out, "v"), (stat, "v")],
        [pltpu.VMEM((n, c), F32), pltpu.VMEM((9 * c, c), BF16), pltpu.SemaphoreType.DMA((3,))],
        flops=2 * n * 9 * c * c, name="back_two")


def back_one_body(size_ref, e3_ref, k_ref, vec_ref, img_ref, stat_ref, resid_ref, out_ref, vout_ref, g_ref, k_vmem, sems):
    n, c = img_ref.shape
    copies = start_copies(k_ref, k_vmem, sems, 3)
    size = size_ref[0]
    mask = row_mask(size, c)
    conv_back(e3_ref, k_vmem, copies, g_ref)
    mean, scale = stat_ref[0:1, :], stat_ref[1:2, :]
    gain, shift = vec_ref[0:1, :], vec_ref[1:2, :]
    su, sux, m1, m2 = norm_back_sums(img_ref, g_ref, mean, scale, gain, shift, mask, size)

    def apply(h, carry):
        xhat = (img_ref[rows(h), :].astype(F32) - mean) * scale
        g = (g_ref[rows(h), :] * gain - m1 - xhat * m2) * scale + resid_ref[rows(h), :]
        out_ref[rows(h), :] = jnp.where(mask(h), g, 0.0).astype(out_ref.dtype)
        return carry

    lax.fori_loop(0, SIDE, apply, 0, unroll=2)
    vout_ref[...] = total_of(sux, su)


def back_one(size, e3, weights, vec, img, stat, grad_resid):
    n, c = img.shape
    return call(back_one_body, [(shape((n, c), BF16), "v"), (shape((8, c), F32), "v")],
        [(size, "s"), (e3, "v"), (weights, "a"), (vec, "v"), (img, "v"), (stat, "v"), (grad_resid, "v")],
        [pltpu.VMEM((n, c), F32), pltpu.VMEM((9 * c, c), BF16), pltpu.SemaphoreType.DMA((3,))],
        flops=2 * n * 9 * c * c, name="back_one")


ALL = ("img", "band")
CORE = [(b, b ^ 1) for b in range(4)]
ACROSS_Y = [(b, b ^ 2) for b in range(4)]
ACROSS_X = [(i, i ^ 1) for i in range(8)]
PLANES = {
    2: (((3, 2), (2, 3)), ((1, 2), (0, 3)), ((0, 2), (1, 3))),
    0: (((0, 1), (1, 0)), ((2, 1), (3, 0)), ((3, 1), (2, 0))),
}


def wide(*parts):
    total = parts[0].astype(F32)
    for part in parts[1:]:
        total = total + part.astype(F32)
    return total


def reduce_half(mine, theirs, first):
    block, c = mine.shape[1:]
    cut = block // 2
    dims = (2, 2, 2, block, c)
    other = lax.ppermute(theirs, "band", CORE).reshape(dims)
    mine = mine.reshape(dims)

    def chip(*index):
        return (mine[index], other[index])

    head, tail = slice(0, cut), slice(cut, block)
    every = slice(None)
    send_a = wide(*chip(1, every, every, head)).astype(BF16)
    send_b = wide(*chip(every, 1, every, tail)).astype(BF16)
    got_a = lax.ppermute(send_a, "img", ACROSS_X)
    got_b = lax.ppermute(send_b, "band", ACROSS_Y)
    next_a = wide(*chip(0, 1, every, head), got_a[1]).astype(BF16)
    next_b = wide(*chip(1, 0, every, tail), got_b[1]).astype(BF16)
    last_a = lax.ppermute(next_a, "band", ACROSS_Y)
    last_b = lax.ppermute(next_b, "img", ACROSS_X)
    sum_a = wide(*chip(0, 0, every, head), got_a[0], last_a)
    sum_b = wide(*chip(0, 0, every, tail), got_b[0], last_b)
    plane = jnp.concatenate([sum_a, sum_b], axis=1)
    low = plane.astype(BF16)
    z = lax.axis_index("img") // 2
    parts = [lax.dynamic_index_in_dim(plane, jnp.clip(z - first, 0, 1), 0, False)]
    for moves in PLANES[first]:
        table = [0] * 4
        for source, target in moves:
            table[source] = target - first
        sent = lax.dynamic_index_in_dim(low, jnp.array(table, jnp.int32)[z], 0, False)
        pairs = [(2 * a + x, 2 * b + x) for a, b in moves for x in range(2)]
        parts.append(lax.ppermute(sent, "img", pairs))
    return parts


def sum_everywhere(v):
    for axis, pairs in (("band", CORE), ("band", ACROSS_Y), ("img", ACROSS_X)):
        v = v + lax.ppermute(v, axis, pairs)
    for bit in (2, 4):
        v = v + lax.ppermute(v, "img", [(i, i ^ bit) for i in range(8)])
    return v


def whole_image(
    images,
    cotangent,
    sizes,
    matrix_weight,
    matrix_momentum,
    matrix_average,
    vector_weight,
    vector_momentum,
    vector_average,
):
    batch, height, width, c = images.shape
    n = width * width
    mine = lax.axis_index("band")
    place = lax.axis_index("img")
    at = jnp.stack([lax.dynamic_index_in_dim(sizes, mine, 0, False), place % 2, mine // 2, mine % 2])

    def to_image(field):
        parts = field.reshape(batch, height * width, c)
        return lax.all_to_all(parts, "band", 0, 0, tiled=True).reshape(n, c)

    def to_bands(field):
        parts = field.reshape(batch, height * width, c)
        return lax.all_to_all(parts, "band", 0, 0, tiled=True).reshape(batch, height, width, c)

    weights = lax.all_gather(matrix_weight.astype(BF16).reshape(-1, c), ALL, axis=0, tiled=True)
    img = to_image(images)
    cot = to_image(cotangent)
    a3_one, at_one, stat_one = act_one(at, img, vector_weight)
    conv_out, a3_two, at_two, stat_two = conv_one(at, a3_one, weights, vector_weight)
    resid, normed, stat_three = conv_two(at, a3_two, weights, vector_weight, img)
    out, mine_high, theirs_high, grad_resid, e3_two, v3 = attention(
        at, normed, weights, vector_weight, resid, cot, stat_three
    )
    mine_low, theirs_low, mine_high, theirs_high = grad_kernel_two(at, e3_two, at_two, mine_high, theirs_high)
    high = reduce_half(mine_high, theirs_high, 2)
    e3_one, v2 = back_two(at, e3_two, weights, vector_weight, conv_out, stat_two)
    mine_low, theirs_low = grad_kernel_one(at, e3_one, at_one, mine_low, theirs_low)
    low = reduce_half(mine_low, theirs_low, 0)
    grad_in, v1 = back_one(at, e3_one, weights, vector_weight, img, stat_one, grad_resid)
    block_out = to_bands(out)
    input_grad = to_bands(grad_in).astype(F32)
    vecs = jnp.stack([v1[0], v1[1], v2[0], v2[1], v2[2], v3[0], v3[1], v3[2], v3[3], v3[4], v3[5]])
    vector_grads = sum_everywhere(vecs)
    matrix_grads = jnp.where(place < 4, wide(*low), wide(*high)).reshape(-1)
    matrix_moments = MOMENTUM * matrix_momentum + matrix_grads
    matrix_masters = matrix_weight - LR_MATRIX * (matrix_grads + MOMENTUM * matrix_moments)
    matrix_means = AVERAGE * matrix_average + (1.0 - AVERAGE) * matrix_masters
    vector_moments = MOMENTUM * vector_momentum + vector_grads
    vector_masters = vector_weight - LR_VECTOR * (vector_grads + MOMENTUM * vector_moments)
    vector_means = AVERAGE * vector_average + (1.0 - AVERAGE) * vector_masters
    return (
        block_out,
        input_grad,
        matrix_grads,
        matrix_moments,
        matrix_means,
        matrix_masters,
        vector_grads,
        vector_moments,
        vector_means,
        vector_masters,
    )


def solution(mesh):
    fits = mesh.shape["img"] == 8 and mesh.shape["band"] == 4

    def per_device(images, *rest):
        step = whole_image if fits and images.shape[:3] == (4, 8, SIDE) else banded
        return step(images, *rest)

    return jax.shard_map(
            per_device,
        mesh=mesh,
        in_specs=(
            P("img", "band", None, None),
            P("img", "band", None, None),
            P("img"),
            P(("img", "band")),
            P(("img", "band")),
            P(("img", "band")),
            P(),
            P(),
            P(),
        ),
        out_specs=(
            P("img", "band", None, None),
            P("img", "band", None, None),
            P(("img", "band")),
            P(("img", "band")),
            P(("img", "band")),
            P(("img", "band")),
            P(),
            P(),
            P(),
            P(),
        ),
        check_vma=False,
    )
```

```python
import functools

import jax
import jax.numpy as jnp
from jax import lax
from jax.experimental import pallas as pl
from jax.experimental.pallas import tpu as pltpu
from jax.sharding import PartitionSpec as P

GROUPS = 32


EPS = 1e-06
MOMENTUM = 0.9
LR_MATRIX = 4e-05
LR_VECTOR = 0.0001
AVERAGE = 0.75


def extended(array, sides, width):
    for axis, dim in sides:
        count, length = (lax.axis_size(axis), array.shape[dim])
        up = [(i, (i + 1) % count) for i in range(count - 1)]
        down = [(j, i) for i, j in up]
        last = lax.slice_in_dim(array, length - width, length, axis=dim)
        initial = lax.slice_in_dim(array, 0, width, axis=dim)
        before = lax.ppermute(last, axis, up)
        after = lax.ppermute(initial, axis, down)
        array = jnp.concatenate([before, array, after], axis=dim)
    return array


def split_groups(field):
    return field.reshape(field.shape[:3] + (GROUPS, field.shape[3] // GROUPS))


def group_sums(field, mask):
    shaped = split_groups(field)
    weighted = shaped * mask[..., None]
    return (jnp.sum(weighted, axis=(1, 2, 4)), jnp.sum(weighted * shaped, axis=(1, 2, 4)))


def group_apply(field, sums, count, gain, shift):
    center = sums[0] / count[:, None]
    spread = sums[1] / count[:, None] - center * center
    scale = lax.rsqrt(spread + EPS)
    shaped = split_groups(field)
    normed = (shaped - center[:, None, None, :, None]) * scale[:, None, None, :, None]
    return normed.reshape(field.shape) * gain + shift


def normalize(field, mask, count, gain, shift):
    sums = lax.psum(group_sums(field, mask), "band")
    return (group_apply(field, sums, count, gain, shift), sums)


def normalize_back(field, sums, mask, count, gain, shift, upstream):
    _, pull = jax.vjp(
        lambda field_in, sums_in, gain_in, shift_in: group_apply(
            field_in, sums_in, count, gain_in, shift_in
        ),
        field,
        sums,
        gain,
        shift,
    )
    direct, grad_sums, grad_gain, grad_shift = pull(upstream)
    grad_sums = lax.psum(grad_sums, "band")
    _, pull_sums = jax.vjp(lambda field_in: group_sums(field_in, mask), field)
    return (direct + pull_sums(grad_sums)[0], grad_gain, grad_shift)


def activate(field, mask):
    return jax.nn.silu(field) * mask


def activate_back(field, mask, upstream):
    _, pull = jax.vjp(lambda inner: activate(inner, mask), field)
    return pull(upstream)[0]


def widen(field):
    return jnp.pad(field, ((0, 0), (0, 0), (1, 1), (0, 0)))


def taps(padded, kernel, height, width):
    total = jnp.zeros(padded.shape[:1] + (height, width, kernel.shape[2]), jnp.float32)
    for tap in range(9):
        row, column = (tap // 3, tap % 3)
        total = total + jnp.einsum(
            "ghwc,cd->ghwd",
            padded[:, row : row + height, column : column + width],
            kernel[tap],
            preferred_element_type=jnp.float32,
        )
    return total


def conv_forward(low_field, kernel):
    padded = widen(extended(low_field, (("band", 1),), 1))
    return (taps(padded, kernel, low_field.shape[1], low_field.shape[2]), padded)


def conv_backward(low_grad, kernel, padded):
    height, width = (low_grad.shape[1], low_grad.shape[2])
    grad_pad = widen(extended(low_grad, (("band", 1),), 1))
    flipped = jnp.swapaxes(kernel[::-1], 1, 2)
    grad_in = taps(grad_pad, flipped, height, width)
    pieces = []
    for tap in range(9):
        row, column = (tap // 3, tap % 3)
        pieces.append(
            jnp.einsum(
                "ghwc,ghwd->cd",
                padded[:, row : row + height, column : column + width],
                low_grad,
                preferred_element_type=jnp.float32,
            )
        )
    return (grad_in, jnp.stack(pieces))


def attend(query_low, key_full, key_valid, factor):
    score_matrix = (
        jnp.einsum("gqc,gkc->gqk", query_low, key_full, preferred_element_type=jnp.float32) * factor
    )
    score_matrix = jnp.where(key_valid[:, None, :], score_matrix, -1e30)
    top = jnp.max(score_matrix, axis=2, keepdims=True)
    raised = jnp.exp(score_matrix - top)
    total = jnp.sum(raised, axis=2, keepdims=True)
    return (raised / total, top, total)


def banded(
    images,
    cotangent,
    sizes,
    matrix_weight,
    matrix_momentum,
    matrix_average,
    vector_weight,
    vector_momentum,
    vector_average,
):
    batch, height, width, channels = images.shape
    square = channels * channels
    queries = height * width
    positions = width * width
    factor = channels ** (-0.5)
    weights = lax.all_gather(
        matrix_weight.astype(jnp.bfloat16), ("img", "band"), axis=0, tiled=True
    )
    kernel_one = weights[: 9 * square].reshape(9, channels, channels)
    kernel_two = weights[9 * square : 18 * square].reshape(9, channels, channels)
    attn_in = weights[18 * square : 21 * square].reshape(3, channels, channels)
    attention_output = weights[21 * square :].reshape(channels, channels)
    lines = lax.axis_index("band") * height + jnp.arange(height)
    across = jnp.arange(width)
    limit = sizes[:, None, None]
    inside = (lines[None, :, None] < limit) & (across[None, None, :] < limit)
    mask = jnp.where(inside, 1.0, 0.0).astype(jnp.float32)[..., None]
    count = (sizes * sizes * (channels // GROUPS)).astype(jnp.float32)
    spots = jnp.arange(positions)
    key_valid = ((spots // width)[None, :] < sizes[:, None]) & (
        (spots % width)[None, :] < sizes[:, None]
    )
    start = images.astype(jnp.float32) * mask
    norm_one, sums_one = normalize(start, mask, count, vector_weight[0], vector_weight[1])
    act_one = activate(norm_one, mask).astype(jnp.bfloat16)
    conv_raw, padded_one = conv_forward(act_one, kernel_one)
    conv_out = conv_raw + vector_weight[2]
    norm_two, sums_two = normalize(conv_out, mask, count, vector_weight[3], vector_weight[4])
    act_two = activate(norm_two, mask).astype(jnp.bfloat16)
    conv_raw, padded_two = conv_forward(act_two, kernel_two)
    resid = (start + conv_raw + vector_weight[5]) * mask
    norm_three, sums_three = normalize(resid, mask, count, vector_weight[6], vector_weight[7])
    normed = (norm_three * mask).astype(jnp.bfloat16).reshape(batch, queries, channels)
    projected = jnp.einsum("gqc,jcd->jgqd", normed, attn_in, preferred_element_type=jnp.float32)
    query_low = (projected[0] + vector_weight[8]).astype(jnp.bfloat16)
    key_low = projected[1].astype(jnp.bfloat16)
    value_low = (projected[2] + vector_weight[9]).astype(jnp.bfloat16)
    key_full, value_full = (
        lax.all_gather(key_low, "band", axis=1, tiled=True),
        lax.all_gather(value_low, "band", axis=1, tiled=True),
    )
    probability_rows, row_top, row_total = attend(query_low, key_full, key_valid, factor)
    mixed_values = jnp.einsum(
        "gqk,gkc->gqc",
        probability_rows.astype(jnp.bfloat16),
        value_full,
        preferred_element_type=jnp.float32,
    ).astype(jnp.bfloat16)
    output_rows = (
        jnp.einsum(
            "gqc,cd->gqd", mixed_values, attention_output, preferred_element_type=jnp.float32
        )
        + vector_weight[10]
    )
    block_out = ((resid + output_rows.reshape(images.shape)) * mask).astype(jnp.bfloat16)
    grad_top = cotangent.astype(jnp.float32) * mask
    grad_proj = grad_top.reshape(batch, queries, channels)
    grad_proj_low = grad_proj.astype(jnp.bfloat16)
    grad_out_weight = jnp.einsum(
        "gqc,gqd->cd", mixed_values, grad_proj_low, preferred_element_type=jnp.float32
    )
    grad_mixed = jnp.einsum(
        "gqd,cd->gqc", grad_proj_low, attention_output, preferred_element_type=jnp.float32
    ).astype(jnp.bfloat16)
    back_keys, back_values = (
        lax.all_gather(key_low, "band", axis=1, tiled=True),
        lax.all_gather(value_low, "band", axis=1, tiled=True),
    )
    back_probs = attend(query_low, back_keys, key_valid, factor)[0]
    grad_probs = jnp.einsum(
        "gqc,gkc->gqk", grad_mixed, back_values, preferred_element_type=jnp.float32
    )
    weighted_sum = jnp.sum(back_probs * grad_probs, axis=2, keepdims=True)
    grad_scores = back_probs * (grad_probs - weighted_sum)
    grad_scores_low = (grad_scores * factor).astype(jnp.bfloat16)
    grad_query = jnp.einsum(
        "gqk,gkc->gqc", grad_scores_low, back_keys, preferred_element_type=jnp.float32
    ).astype(jnp.bfloat16)
    key_terms = jnp.einsum(
        "gqk,gqc->gkc", grad_scores_low, query_low, preferred_element_type=jnp.float32
    )
    value_terms = jnp.einsum(
        "gqk,gqc->gkc",
        back_probs.astype(jnp.bfloat16),
        grad_mixed,
        preferred_element_type=jnp.float32,
    )
    grad_key, grad_value = (
        lax.psum_scatter(
            key_terms.astype(jnp.bfloat16), "band", scatter_dimension=1, tiled=True
        ).astype(jnp.float32),
        lax.psum_scatter(
            value_terms.astype(jnp.bfloat16), "band", scatter_dimension=1, tiled=True
        ).astype(jnp.float32),
    )
    grad_value_low = grad_value.astype(jnp.bfloat16)
    grads_low = jnp.stack([grad_query, grad_key.astype(jnp.bfloat16), grad_value_low])
    grad_in_weights = jnp.einsum(
        "gqc,jgqd->jcd", normed, grads_low, preferred_element_type=jnp.float32
    )
    grad_normed = (
        jnp.einsum("jgqd,jcd->gqc", grads_low, attn_in, preferred_element_type=jnp.float32).reshape(
            images.shape
        )
        * mask
    )
    grad_resid_norm, grad_gain_three, grad_shift_three = normalize_back(
        resid, sums_three, mask, count, vector_weight[6], vector_weight[7], grad_normed
    )
    grad_resid = (grad_top + grad_resid_norm) * mask
    grad_act_two, grad_kernel_two = conv_backward(
        grad_resid.astype(jnp.bfloat16), kernel_two, padded_two
    )
    grad_norm_two = activate_back(norm_two, mask, grad_act_two)
    grad_conv_out, grad_gain_two, grad_shift_two = normalize_back(
        conv_out, sums_two, mask, count, vector_weight[3], vector_weight[4], grad_norm_two
    )
    grad_act_one, grad_kernel_one = conv_backward(
        grad_conv_out.astype(jnp.bfloat16), kernel_one, padded_one
    )
    grad_norm_one = activate_back(norm_one, mask, grad_act_one)
    grad_start, grad_gain_one, grad_shift_one = normalize_back(
        start, sums_one, mask, count, vector_weight[0], vector_weight[1], grad_norm_one
    )
    input_grad = (grad_resid + grad_start) * mask
    vector_terms = jnp.stack(
        [
            grad_gain_one,
            grad_shift_one,
            jnp.sum(grad_conv_out, axis=(0, 1, 2)),
            grad_gain_two,
            grad_shift_two,
            jnp.sum(grad_resid, axis=(0, 1, 2)),
            grad_gain_three,
            grad_shift_three,
            jnp.sum(grad_query, axis=(0, 1), dtype=jnp.float32),
            jnp.sum(grad_value_low, axis=(0, 1), dtype=jnp.float32),
            jnp.sum(grad_proj, axis=(0, 1)),
        ]
    )
    vector_grads = lax.psum(vector_terms, ("img", "band"))
    grad_flat = jnp.concatenate(
        [
            grad_kernel_one.reshape(-1),
            grad_kernel_two.reshape(-1),
            grad_in_weights.reshape(-1),
            grad_out_weight.reshape(-1),
        ]
    )
    matrix_grads = lax.psum_scatter(grad_flat, ("img", "band"), scatter_dimension=0, tiled=True)
    matrix_moments = MOMENTUM * matrix_momentum + matrix_grads
    matrix_masters = matrix_weight - LR_MATRIX * (matrix_grads + MOMENTUM * matrix_moments)
    matrix_means = AVERAGE * matrix_average + (1.0 - AVERAGE) * matrix_masters
    vector_moments = MOMENTUM * vector_momentum + vector_grads
    vector_masters = vector_weight - LR_VECTOR * (vector_grads + MOMENTUM * vector_moments)
    vector_means = AVERAGE * vector_average + (1.0 - AVERAGE) * vector_masters
    return (
        block_out,
        input_grad,
        matrix_grads,
        matrix_moments,
        matrix_means,
        matrix_masters,
        vector_grads,
        vector_moments,
        vector_means,
        vector_masters,
    )


F32 = jnp.float32
BF16 = jnp.bfloat16
SIDE = 32
VMEM_LIMIT = 58 * 1024 * 1024


def dot(a, b):
    return lax.dot_general(a, b, (((1,), (0,)), ((), ())), preferred_element_type=F32)


def dot_nt(a, b):
    return lax.dot_general(a, b, (((1,), (1,)), ((), ())), preferred_element_type=F32)


def dot_tn(a, b):
    return lax.dot_general(a, b, (((0,), (0,)), ((), ())), preferred_element_type=F32)


def call(body, outs, ins, scratch=(), flops=0, name=None, aliases=None):
    spaces = {"v": pl.BlockSpec(memory_space=pltpu.VMEM), "s": pl.BlockSpec(memory_space=pltpu.SMEM),
              "a": pl.BlockSpec(memory_space=pl.ANY)}
    return pl.pallas_call(
        body,
        out_shape=[o for o, _ in outs],
        in_specs=[spaces[s] for _, s in ins],
        out_specs=[spaces[s] for _, s in outs],
        scratch_shapes=list(scratch),
        input_output_aliases=aliases or {},
        compiler_params=pltpu.CompilerParams(vmem_limit_bytes=VMEM_LIMIT),
        cost_estimate=pl.CostEstimate(flops=flops, bytes_accessed=0, transcendentals=0),
        name=name,
    )(*[a for a, _ in ins])


def shape(dims, dtype):
    return jax.ShapeDtypeStruct(dims, dtype)


def fold(x):
    return jnp.sum(x.reshape(x.shape[0] // 8, 8, x.shape[1]), axis=0)


def group_total(x):
    lane = lax.broadcasted_iota(jnp.int32, x.shape, 1)
    width = x.shape[1]
    for s in (1, 2, 4, 8):
        up = pltpu.roll(x, width - s, 1)
        down = pltpu.roll(x, s, 1)
        x = x + jnp.where((lane & s) == 0, up, down)
    return x


def total_of(*parts):
    rows = [jnp.sum(p, axis=0, keepdims=True) for p in parts]
    pad = jnp.zeros((8 - len(rows), rows[0].shape[1]), F32)
    return jnp.concatenate(rows + [pad], axis=0)


def moments(s1, s2, size):
    count = (size * size * 16).astype(F32)
    both = group_total(total_of(s1, s2)) / count
    mean = both[0:1]
    spread = both[1:2] - mean * mean
    return mean, lax.rsqrt(spread + EPS)


def row_mask(size, channels):
    across = lax.broadcasted_iota(jnp.int32, (SIDE, channels), 0)
    inside = across < size
    return lambda h: inside & (h < size)


def sigmoid(y):
    return 0.5 * jnp.tanh(0.5 * y) + 0.5


def rows(h):
    return pl.ds(pl.multiple_of(h * SIDE, SIDE), SIDE)


def put_shifted(ref, h, r, forward):
    channels = r.shape[1]
    w = lax.broadcasted_iota(jnp.int32, r.shape, 0)
    before = jnp.where(w == 0, 0.0, pltpu.roll(r, 1, 0)).astype(BF16)
    after = jnp.where(w == SIDE - 1, 0.0, pltpu.roll(r, SIDE - 1, 0)).astype(BF16)
    first, last = (before, after) if forward else (after, before)
    at = pl.ds(pl.multiple_of((h + 1) * SIDE, SIDE), SIDE)
    ref[at, 0:channels] = first
    ref[at, channels : 2 * channels] = r.astype(BF16)
    ref[at, 2 * channels :] = last


def clear_border(ref):
    zero = jnp.zeros((SIDE, ref.shape[1]), BF16)
    ref[0:SIDE, :] = zero
    ref[(SIDE + 1) * SIDE :, :] = zero


def put_transposed(ref, src_ref, row0, lane0):
    channels, count = ref.shape
    for j in range(count // 256):
        block = src_ref[row0 + j * 256 : row0 + (j + 1) * 256, lane0 : lane0 + channels]
        ref[:, j * 256 : (j + 1) * 256] = block.T


def act_one_body(size_ref, img_ref, vec_ref, pad_ref, at_ref, stat_ref):
    size = size_ref[0]
    channels = img_ref.shape[1]
    mask = row_mask(size, channels)

    def sums(h, carry):
        x = jnp.where(mask(h), img_ref[rows(h), :].astype(F32), 0.0)
        return carry[0] + fold(x), carry[1] + fold(x * x)

    zero = jnp.zeros((8, channels), F32)
    s1, s2 = lax.fori_loop(0, SIDE, sums, (zero, zero), unroll=2)
    mean, scale = moments(s1, s2, size)
    stat_ref[0:1, :] = mean
    stat_ref[1:2, :] = scale
    stat_ref[2:8, :] = jnp.zeros((6, channels), F32)
    apply_norm(img_ref, mean, scale * vec_ref[0:1, :], vec_ref[1:2, :], mask, pad_ref)
    put_transposed(at_ref, pad_ref, SIDE, 0)


def apply_norm(src_ref, mean, scale, shift, mask, pad_ref):
    clear_border(pad_ref)

    def apply(h, carry):
        y = (src_ref[rows(h), :].astype(F32) - mean) * scale + shift
        at = pl.ds(pl.multiple_of((h + 1) * SIDE, SIDE), SIDE)
        pad_ref[at, :] = jnp.where(mask(h), y * sigmoid(y), 0.0).astype(BF16)
        return carry

    lax.fori_loop(0, SIDE, apply, 0, unroll=4)


def act_one(size, img, vec):
    n, c = img.shape
    return call(act_one_body,
        [(shape((n + 64, c), BF16), "v"), (shape((c, n), BF16), "v"), (shape((8, c), F32), "v")],
        [(size, "s"), (img, "v"), (vec, "v")], name="act_one")


MB = 256


def start_copies(src_ref, dst_ref, sems, parts, offset=0):
    length = dst_ref.shape[0] // parts
    copies = [
        pltpu.make_async_copy(src_ref.at[pl.ds(offset + p * length, length)], dst_ref.at[pl.ds(p * length, length)], sems.at[p])
        for p in range(parts)
    ]
    for copy in copies:
        copy.start()
    return copies


COLUMNS = (1, 0, 2)


def start_kernel(src_ref, dst_ref, sems, offset):
    c = dst_ref.shape[1]
    copies = {}
    for dx in COLUMNS:
        for dy in range(3):
            tap = 3 * dy + dx
            copies[tap] = pltpu.make_async_copy(
                src_ref.at[pl.ds(offset + tap * c, c)], dst_ref.at[pl.ds(tap * c, c)], sems.at[tap]
            )
            copies[tap].start()
    return copies


def conv(pad_ref, k_ref, copies, out_ref, mb, finish):
    n, c = out_ref.shape
    zero = jnp.zeros((8, c), F32)
    carry = (zero, zero)
    across = lax.broadcasted_iota(jnp.int32, (mb, c), 0) & (SIDE - 1)
    for dx in COLUMNS:
        for dy in range(3):
            copies[3 * dy + dx].wait()
        for m in range(n // mb):
            at = slice(m * mb, (m + 1) * mb)
            value = None
            for dy in range(3):
                tap = 3 * dy + dx
                term = dot(pad_ref[m * mb + dy * SIDE : (m + 1) * mb + dy * SIDE, :], k_ref[tap * c : (tap + 1) * c, :])
                value = term if value is None else value + term
            if dx == 0:
                value = jnp.where(across == 0, 0.0, pltpu.roll(value, 1, 0))
            if dx == 2:
                value = jnp.where(across == SIDE - 1, 0.0, pltpu.roll(value, mb - 1, 0))
            if dx != COLUMNS[0]:
                value = value + out_ref[at, :]
            if dx == COLUMNS[-1]:
                value, carry = finish(m * mb, value, carry)
            out_ref[at, :] = value
    return carry


def pixel_mask(size, first, count, c):
    place = lax.broadcasted_iota(jnp.int32, (count, c), 0) + first
    return ((place >> 5) < size) & ((place & (SIDE - 1)) < size)


def put_stats(stat_ref, mean, scale):
    stat_ref[...] = jnp.concatenate([mean, scale, jnp.zeros((6, mean.shape[1]), F32)], axis=0)


def pieces_of(row, count, half):
    found = []
    for spot in range(row // half, (row + count - 1) // half + 1):
        found.append((spot, max(row, spot * half), min(row + count, (spot + 1) * half)))
    return found


def send_rows(stage, base, row, count, at_ref, rounds, sem):
    half = rounds[-1][0].shape[1]
    for spot, lo, hi in pieces_of(row, count, half):
        owner, tail = spot // 2, spot % 2
        refs, inner = rounds[owner // 16], owner % 16
        z, x, y, c = inner // 8, (inner >> 2) & 1, (inner >> 1) & 1, inner & 1
        index = ((at_ref[1] ^ x) * 2 + (at_ref[2] ^ y)) * 2 + z
        source = stage.at[pl.ds(base + lo - row, hi - lo)]
        place = pl.ds(lo - spot * half, hi - lo)
        for other in range(2):

            @pl.when((at_ref[3] ^ c) == other)
            def _(ref=refs[2 * other + tail], source=source, place=place):
                pltpu.make_async_copy(source, ref.at[index, place], sem).start()

    return pltpu.make_async_copy(stage.at[pl.ds(base, count)], stage.at[pl.ds(base, count)], sem)


QB = 256


def forward_body(
    at_ref, pad_one_ref, vec_ref, w_any, img_any, cot_any,
    conv_any, stat_two_ref, mixed_any, resid_any, grad_any, e3_any, vout_ref, *refs,
):
    high, low = refs[0:4], refs[4:8]
    (k_one, k_two, w_ref, img_ref, cot_ref, conv_ref, pad_ref, act_t, resid_ref, normed_ref, normed_t,
     q_ref, k_ref, v_ref, p_ref, ds_ref, mixed_ref, top_ref, gm_ref, gq_ref, gk_ref, gv_ref, grad_ref, e3_ref, gw_ref,
     one_sems, two_sems, w_sems, in_sems, out_sems, gw_sem, gk_sems) = refs[8:]
    n, c = normed_ref.shape
    size = at_ref[0]
    one_copies = start_kernel(w_any, k_one, one_sems, 0)
    two_copies = start_kernel(w_any, k_two, two_sems, 9 * c)
    img_copy = pltpu.make_async_copy(img_any, img_ref, in_sems.at[0])
    cot_copy = pltpu.make_async_copy(cot_any, cot_ref, in_sems.at[1])
    img_copy.start()
    w_copies = start_copies(w_any, w_ref, w_sems, 4, 18 * c)
    cot_copy.start()
    leaving = []

    def leave(src, dst):
        copy = pltpu.make_async_copy(src, dst, out_sems.at[len(leaving)])
        copy.start()
        leaving.append(copy)

    mask = row_mask(size, c)
    zero = jnp.zeros((8, c), F32)

    bias_one = vec_ref[2:3, :]

    def finish_one(first, v, carry):
        v = v + bias_one
        x = jnp.where(pixel_mask(size, first, MB, c), v, 0.0)
        return v, (carry[0] + fold(x), carry[1] + fold(x * x))

    s1, s2 = conv(pad_one_ref, k_one, one_copies, conv_ref, MB, finish_one)
    leave(conv_ref, conv_any)
    mean, scale = moments(s1, s2, size)
    put_stats(stat_two_ref, mean, scale)
    apply_norm(conv_ref, mean, scale * vec_ref[3:4, :], vec_ref[4:5, :], mask, pad_ref)
    put_transposed(act_t, pad_ref, SIDE, 0)

    bias_two = vec_ref[5:6, :]
    img_copy.wait()

    def finish_two(first, v, carry):
        v = v + bias_two + img_ref[first : first + MB, :].astype(F32)
        x = jnp.where(pixel_mask(size, first, MB, c), v, 0.0)
        return x, (carry[0] + fold(x), carry[1] + fold(x * x))

    s1, s2 = conv(pad_ref, k_two, two_copies, resid_ref, MB, finish_two)
    leave(resid_ref, resid_any)
    mean, scale = moments(s1, s2, size)
    gain = vec_ref[6:7, :]
    full_gain, shift = scale * gain, vec_ref[7:8, :]
    cot_copy.wait()

    def apply(h, carry):
        y = (resid_ref[rows(h), :] - mean) * full_gain + shift
        normed_ref[rows(h), :] = jnp.where(mask(h), y, 0.0).astype(BF16)
        t = jnp.where(mask(h), cot_ref[rows(h), :].astype(F32), 0.0)
        top_ref[rows(h), :] = t.astype(BF16)
        return carry + fold(t)

    top_sum = lax.fori_loop(0, SIDE, apply, zero, unroll=4)
    put_transposed(normed_t, normed_ref, 0, 0)

    for copy in w_copies:
        copy.wait()
    factor = c ** (-0.5)
    wq, wk, wv, wo = (w_ref[j * c : (j + 1) * c, :] for j in range(4))
    qb, vb = vec_ref[8:9, :], vec_ref[9:10, :]
    for m in range(n // MB):
        at = slice(m * MB, (m + 1) * MB)
        x = normed_ref[at, :]
        q_ref[at, :] = (dot(x, wq) + qb).astype(BF16)
        k_ref[at, :] = dot(x, wk).astype(BF16)
        v_ref[at, :] = (dot(x, wv) + vb).astype(BF16)
        gm_ref[at, :] = dot_nt(top_ref[at, :], wo).astype(BF16)

    spot = lax.broadcasted_iota(jnp.int32, (1, n), 1)
    key_bias = jnp.where(((spot >> 5) < size) & ((spot & (SIDE - 1)) < size), 0.0, -1e30)

    def queries(m, carry):
        at = pl.ds(pl.multiple_of(m * QB, QB), QB)
        s = dot_nt(q_ref[at, :], k_ref[...]) * factor + key_bias
        raised = jnp.exp(s - jnp.max(s, axis=1, keepdims=True))
        p = raised * (1.0 / jnp.sum(raised, axis=1, keepdims=True))
        low_p = p.astype(BF16)
        p_ref[at, :] = low_p
        mixed_ref[at, :] = dot(low_p, v_ref[...]).astype(BF16)
        gp = dot_nt(gm_ref[at, :], v_ref[...])
        weighted = jnp.sum(p * gp, axis=1, keepdims=True)
        ds = (p * ((gp - weighted) * factor)).astype(BF16)
        ds_ref[at, :] = ds
        gq_ref[at, :] = dot(ds, k_ref[...]).astype(BF16)
        return carry

    lax.fori_loop(0, n // QB, queries, 0)
    leave(mixed_ref, mixed_any)

    def keys(m, carry):
        at = pl.ds(pl.multiple_of(m * QB, QB), QB)
        gk_ref[at, :] = dot_tn(ds_ref[:, at], q_ref[...]).astype(BF16)
        gv_ref[at, :] = dot_tn(p_ref[:, at], gm_ref[...]).astype(BF16)
        return carry

    lax.fori_loop(0, n // QB, keys, 0)
    gw_ref[0:c, :] = dot(normed_t[...], gq_ref[...]).astype(BF16)
    gw_ref[c : 2 * c, :] = dot(normed_t[...], gk_ref[...]).astype(BF16)
    gw_ref[2 * c : 3 * c, :] = dot(normed_t[...], gv_ref[...]).astype(BF16)
    gw_ref[3 * c : 4 * c, :] = dot_tn(mixed_ref[...], top_ref[...]).astype(BF16)
    waits = [send_rows(gw_ref, 0, 18 * c, 4 * c, at_ref, (None, high), gw_sem)]

    su = sux = sq = sv = zero
    for m in range(n // MB):
        at = slice(m * MB, (m + 1) * MB)
        gq, gk, gv = gq_ref[at, :], gk_ref[at, :], gv_ref[at, :]
        u = dot_nt(gq, wq) + dot_nt(gk, wk) + dot_nt(gv, wv)
        u = jnp.where(pixel_mask(size, m * MB, MB, c), u, 0.0)
        grad_ref[at, :] = u
        xhat = (resid_ref[at, :] - mean) * scale
        su, sux = su + fold(u), sux + fold(u * xhat)
        sq, sv = sq + fold(gq.astype(F32)), sv + fold(gv.astype(F32))
    count = (size * size * 16).astype(F32)
    both = group_total(total_of(su, sux) * gain) / count
    m1, m2 = both[0:1], both[1:2]
    clear_border(e3_ref)

    def back(h, carry):
        xhat = (resid_ref[rows(h), :] - mean) * scale
        g = (grad_ref[rows(h), :] * gain - m1 - xhat * m2) * scale + top_ref[rows(h), :].astype(F32)
        g = jnp.where(mask(h), g, 0.0)
        grad_ref[rows(h), :] = g
        put_shifted(e3_ref, h, g.astype(BF16).astype(F32), False)
        return carry + fold(g)

    sg = lax.fori_loop(0, SIDE, back, zero, unroll=2)
    leave(e3_ref, e3_any)
    leave(grad_ref, grad_any)
    vout_ref[...] = total_of(sg, sux, su, sq, sv, top_sum)
    waits += kernel_gradient(act_t, e3_ref, k_one, 9 * c, at_ref, (low, high), gk_sems)
    for wait in waits + leaving:
        wait.wait()


def forward(at, pad_one, vec, weights, img, cot):
    n, c = img.shape
    half = (shape((8, weights.shape[0] // 64, c), BF16), "a")

    def low(*dims):
        return pltpu.VMEM(dims, BF16)

    full = low(n, c)
    found = call(forward_body,
        [(shape((n, c), F32), "a"), (shape((8, c), F32), "v"), (shape((n, c), BF16), "a"), (shape((n, c), F32), "a"),
         (shape((n, c), F32), "a"), (shape((n + 2 * SIDE, 3 * c), BF16), "a"), (shape((8, c), F32), "v")] + [half] * 8,
        [(at, "s"), (pad_one, "v"), (vec, "v"), (weights, "a"), (img, "a"), (cot, "a")],
        [low(9 * c, c), low(9 * c, c), low(4 * c, c), full, full, pltpu.VMEM((n, c), F32), low(n + 2 * SIDE, c), low(c, n),
         pltpu.VMEM((n, c), F32), full, low(c, n), full, full, full, low(n, n), low(n, n), full, full, full, full, full, full,
         pltpu.VMEM((n, c), F32), low(n + 2 * SIDE, 3 * c), low(4 * c, c),
         pltpu.SemaphoreType.DMA((9,)), pltpu.SemaphoreType.DMA((9,)), pltpu.SemaphoreType.DMA((4,)),
         pltpu.SemaphoreType.DMA((2,)), pltpu.SemaphoreType.DMA((5,)), pltpu.SemaphoreType.DMA, pltpu.SemaphoreType.DMA((9,))],
        name="forward")
    return found[:7], found[7:11], found[11:15]


def out_body(at_ref, mixed_ref, resid_ref, vec_ref, w_any, out_ref, wo_ref, sem):
    n, c = mixed_ref.shape
    copy = pltpu.make_async_copy(w_any.at[pl.ds(21 * c, c)], wo_ref, sem)
    copy.start()
    copy.wait()
    for m in range(n // MB):
        at = slice(m * MB, (m + 1) * MB)
        value = dot(mixed_ref[at, :], wo_ref[...]) + vec_ref[10:11, :] + resid_ref[at, :]
        out_ref[at, :] = jnp.where(pixel_mask(at_ref[0], m * MB, MB, c), value, 0.0).astype(BF16)


def block_rows(at, mixed, resid, vec, weights):
    n, c = mixed.shape
    return call(out_body, [(shape((n, c), BF16), "v")],
        [(at, "s"), (mixed, "v"), (resid, "v"), (vec, "v"), (weights, "a")],
        [pltpu.VMEM((c, c), BF16), pltpu.SemaphoreType.DMA], name="block_rows")[0]


def kernel_gradient(act_t, e3_ref, stage, row, at_ref, rounds, sems):
    c, n = act_t.shape
    waits = []
    for dy in range(3):
        for dx in range(3):
            tap = 3 * dy + dx
            lo = (2 - dy) * SIDE
            value = dot(act_t[...], e3_ref[lo : lo + n, dx * c : (dx + 1) * c])
            stage[tap * c : (tap + 1) * c, :] = value.astype(BF16)
            waits.append(send_rows(stage, tap * c, row + tap * c, c, at_ref, rounds, sems.at[tap]))
    return waits


def conv_back(e3_ref, k_ref, copies, out_ref):
    n, c = out_ref.shape
    for dy in range(3):
        copies[dy].wait()
        lo = (2 - dy) * SIDE
        for m in range(n // MB):
            value = None
            for dx in range(3):
                tap = 3 * dy + dx
                term = dot_nt(e3_ref[lo + m * MB : lo + (m + 1) * MB, dx * c : (dx + 1) * c], k_ref[tap * c : (tap + 1) * c, :])
                value = term if value is None else value + term
            if dy > 0:
                value = value + out_ref[m * MB : (m + 1) * MB, :]
            out_ref[m * MB : (m + 1) * MB, :] = value


def norm_back_sums(src_ref, g_ref, mean, scale, gain, shift, mask, size):
    c = g_ref.shape[1]

    def sums(h, carry):
        xhat = (src_ref[rows(h), :].astype(F32) - mean) * scale
        y = xhat * gain + shift
        s = sigmoid(y)
        u = jnp.where(mask(h), g_ref[rows(h), :] * (s * (1.0 + y * (1.0 - s))), 0.0)
        g_ref[rows(h), :] = u
        return carry[0] + fold(u), carry[1] + fold(u * xhat)

    zero = jnp.zeros((8, c), F32)
    su, sux = lax.fori_loop(0, SIDE, sums, (zero, zero), unroll=2)
    count = (size * size * 16).astype(F32)
    both = group_total(total_of(su, sux) * gain) / count
    return su, sux, both[0:1], both[1:2]


def back_two_body(
    at_ref, e3_ref, vec_ref, stat_ref, k_any, conv_any, act_any, i0, i1, i2, i3,
    e3_any, vout_ref, o0, o1, o2, o3, g_ref, conv_ref, act_t, e3_out, k_vmem, sems, in_sems, out_sem, gk_sems,
):
    n, c = conv_ref.shape
    copies = start_copies(k_any, k_vmem, sems, 3, 9 * c)
    conv_copy = pltpu.make_async_copy(conv_any, conv_ref, in_sems.at[0])
    act_copy = pltpu.make_async_copy(act_any, act_t, in_sems.at[1])
    conv_copy.start()
    act_copy.start()
    size = at_ref[0]
    mask = row_mask(size, c)
    conv_back(e3_ref, k_vmem, copies, g_ref)
    conv_copy.wait()
    mean, scale = stat_ref[0:1, :], stat_ref[1:2, :]
    gain, shift = vec_ref[3:4, :], vec_ref[4:5, :]
    su, sux, m1, m2 = norm_back_sums(conv_ref, g_ref, mean, scale, gain, shift, mask, size)
    clear_border(e3_out)

    def apply(h, carry):
        xhat = (conv_ref[rows(h), :] - mean) * scale
        g = jnp.where(mask(h), (g_ref[rows(h), :] * gain - m1 - xhat * m2) * scale, 0.0)
        put_shifted(e3_out, h, g.astype(BF16).astype(F32), False)
        return carry + fold(g)

    sg = lax.fori_loop(0, SIDE, apply, jnp.zeros((8, c), F32), unroll=2)
    leaving = pltpu.make_async_copy(e3_out, e3_any, out_sem)
    leaving.start()
    vout_ref[...] = total_of(sg, sux, su)
    act_copy.wait()
    for wait in kernel_gradient(act_t, e3_out, k_vmem, 0, at_ref, ((o0, o1, o2, o3),), gk_sems):
        wait.wait()
    leaving.wait()


def back_two(at, e3, weights, vec, conv_out, stat, act, low):
    n, c = conv_out.shape
    half = shape(low[0].shape, BF16)
    e3_out, vout, *low = call(back_two_body,
        [(shape((n + 64, 3 * c), BF16), "a"), (shape((8, c), F32), "v")] + [(half, "a")] * 4,
        [(at, "s"), (e3, "v"), (vec, "v"), (stat, "v"), (weights, "a"), (conv_out, "a"), (act, "a")] + [(v, "a") for v in low],
        [pltpu.VMEM((n, c), F32), pltpu.VMEM((n, c), F32), pltpu.VMEM((c, n), BF16), pltpu.VMEM((n + 64, 3 * c), BF16),
         pltpu.VMEM((9 * c, c), BF16), pltpu.SemaphoreType.DMA((3,)), pltpu.SemaphoreType.DMA((2,)), pltpu.SemaphoreType.DMA,
         pltpu.SemaphoreType.DMA((9,))],
        name="back_two", aliases={7 + i: 2 + i for i in range(4)})
    return e3_out, vout, low


def back_one_body(size_ref, e3_ref, k_ref, vec_ref, img_ref, stat_ref, resid_ref, out_ref, vout_ref, g_ref, k_vmem, sems):
    n, c = img_ref.shape
    copies = start_copies(k_ref, k_vmem, sems, 3)
    size = size_ref[0]
    mask = row_mask(size, c)
    conv_back(e3_ref, k_vmem, copies, g_ref)
    mean, scale = stat_ref[0:1, :], stat_ref[1:2, :]
    gain, shift = vec_ref[0:1, :], vec_ref[1:2, :]
    su, sux, m1, m2 = norm_back_sums(img_ref, g_ref, mean, scale, gain, shift, mask, size)

    def apply(h, carry):
        xhat = (img_ref[rows(h), :].astype(F32) - mean) * scale
        g = (g_ref[rows(h), :] * gain - m1 - xhat * m2) * scale + resid_ref[rows(h), :]
        out_ref[rows(h), :] = jnp.where(mask(h), g, 0.0).astype(out_ref.dtype)
        return carry

    lax.fori_loop(0, SIDE, apply, 0, unroll=2)
    vout_ref[...] = total_of(sux, su)


def back_one(size, e3, weights, vec, img, stat, grad_resid):
    n, c = img.shape
    return call(back_one_body, [(shape((n, c), BF16), "v"), (shape((8, c), F32), "v")],
        [(size, "s"), (e3, "v"), (weights, "a"), (vec, "v"), (img, "v"), (stat, "v"), (grad_resid, "v")],
        [pltpu.VMEM((n, c), F32), pltpu.VMEM((9 * c, c), BF16), pltpu.SemaphoreType.DMA((3,))],
        flops=2 * n * 9 * c * c, name="back_one")


ALL = ("img", "band")
CORE = [(b, b ^ 1) for b in range(4)]
ACROSS_Y = [(b, b ^ 2) for b in range(4)]
ACROSS_X = [(i, i ^ 1) for i in range(8)]
PLANES = {
    2: (((3, 2), (2, 3)), ((1, 2), (0, 3)), ((0, 2), (1, 3))),
    0: (((0, 1), (1, 0)), ((2, 1), (3, 0)), ((3, 1), (2, 0))),
}


def after(value, *earlier, flops=0):
    def body(*refs):
        pass

    anywhere = pl.BlockSpec(memory_space=pl.ANY)
    return pl.pallas_call(
        body,
        out_shape=shape(value.shape, value.dtype),
        in_specs=[anywhere] * (1 + len(earlier)),
        out_specs=anywhere,
        input_output_aliases={0: 0},
        cost_estimate=pl.CostEstimate(flops=flops, bytes_accessed=0, transcendentals=0),
        name="after",
    )(value, *earlier)


def wide(*parts):
    total = parts[0].astype(F32)
    for part in parts[1:]:
        total = total + part.astype(F32)
    return total


def chip_sends(arrays, *earlier):
    mine_a, mine_b, theirs_a, theirs_b = arrays
    half, c = mine_a.shape[1:]
    dims = (2, 2, 2, half, c)
    if earlier:
        theirs_a, theirs_b = after(theirs_a, *earlier), after(theirs_b, *earlier)
    got = [lax.ppermute(v, "band", CORE) for v in (theirs_a, theirs_b)]
    pair_a = (mine_a.reshape(dims), got[0].reshape(dims))
    pair_b = (mine_b.reshape(dims), got[1].reshape(dims))
    send_a = wide(*(v[1] for v in pair_a)).astype(BF16)
    send_b = wide(*(v[:, 1] for v in pair_b)).astype(BF16)
    return pair_a, pair_b, send_a, send_b


def plane_swap(send_a, send_b):
    return lax.ppermute(send_a, "img", ACROSS_X), lax.ppermute(send_b, "band", ACROSS_Y)


def plane_sends(pair_a, pair_b, got_a, got_b):
    next_a = wide(*(v[0, 1] for v in pair_a), got_a[1]).astype(BF16)
    next_b = wide(*(v[1, 0] for v in pair_b), got_b[1]).astype(BF16)
    kept_a = (*(v[0, 0] for v in pair_a), got_a[0])
    kept_b = (*(v[0, 0] for v in pair_b), got_b[0])
    return kept_a, kept_b, next_a, next_b


def owner_parts(kept_a, kept_b, next_a, next_b, first, *earlier):
    last_a = lax.ppermute(next_a, "band", ACROSS_Y)
    last_b = lax.ppermute(next_b, "img", ACROSS_X)
    if earlier:
        last_a, last_b = after(last_a, *earlier), after(last_b, *earlier)
    plane = jnp.concatenate([wide(*kept_a, last_a), wide(*kept_b, last_b)], axis=1)
    low = plane.astype(BF16)
    z = lax.axis_index("img") // 2
    parts = [lax.dynamic_index_in_dim(plane, jnp.clip(z - first, 0, 1), 0, False)]
    for moves in PLANES[first]:
        sent = low[0]
        for source, target in moves:
            if target != first:
                sent = jnp.where(z == source, low[1], sent)
        pairs = [(2 * a + x, 2 * b + x) for a, b in moves for x in range(2)]
        parts.append(lax.ppermute(sent, "img", pairs))
    return parts, sent


def sum_chip_planes(v):
    for axis, pairs in (("band", CORE), ("band", ACROSS_Y), ("img", ACROSS_X)):
        v = v + lax.ppermute(v, axis, pairs)
    return v


def sum_planes(v):
    for bit in (2, 4):
        v = v + lax.ppermute(v, "img", [(i, i ^ bit) for i in range(8)])
    return v


def whole_image(
    images,
    cotangent,
    sizes,
    matrix_weight,
    matrix_momentum,
    matrix_average,
    vector_weight,
    vector_momentum,
    vector_average,
):
    batch, height, width, c = images.shape
    n = width * width
    mine = lax.axis_index("band")
    place = lax.axis_index("img")
    at = jnp.stack([lax.dynamic_index_in_dim(sizes, mine, 0, False), place % 2, mine // 2, mine % 2])

    def to_image(field):
        parts = field.reshape(batch, height * width, c)
        return lax.all_to_all(parts, "band", 0, 0, tiled=True).reshape(n, c)

    def to_bands(field):
        parts = field.reshape(batch, height * width, c)
        return lax.all_to_all(parts, "band", 0, 0, tiled=True).reshape(batch, height, width, c)

    weights = lax.all_gather(matrix_weight.astype(BF16).reshape(-1, c), ALL, axis=0, tiled=True)
    img = to_image(images)
    cot = to_image(cotangent)
    pad_one, act_t, stat_one = act_one(at, img, vector_weight)
    (conv_out, stat_two, mixed, resid, grad_resid, e3_two, v3), high, low = forward(
        at, pad_one, vector_weight, weights, img, cot
    )
    high = chip_sends(high)
    out = block_rows(at, mixed, resid, vector_weight, weights)
    block_out = to_bands(out)
    e3_two = after(e3_two, high[2], high[3], out)
    swapped = plane_swap(high[2], high[3])
    e3_one, v2, low = back_two(at, e3_two, weights, vector_weight, conv_out, stat_two, act_t, low)
    low = chip_sends(low, *swapped)
    high = plane_sends(*high[:2], *swapped)
    e3_one = after(e3_one, low[2], low[3], block_out)
    swapped = plane_swap(low[2], low[3])
    grad_in, v1 = back_one(at, e3_one, weights, vector_weight, img, stat_one, grad_resid)
    vecs = jnp.stack([v1[0], v1[1], v2[0], v2[1], v2[2], v3[0], v3[1], v3[2], v3[3], v3[4], v3[5]])
    high, _ = owner_parts(*high, 2)
    low = plane_sends(*low[:2], *(after(v, v1) for v in swapped))
    given = to_bands(after(grad_in, low[2], low[3]))
    input_grad = given.astype(F32)
    low, shown = owner_parts(*low, 0)
    vector_grads = sum_planes(after(sum_chip_planes(after(vecs, shown, *high[1:])), given))
    matrix_grads = jnp.where(place < 4, wide(*low), wide(*high)).reshape(-1)
    matrix_moments = MOMENTUM * matrix_momentum + matrix_grads
    matrix_masters = matrix_weight - LR_MATRIX * (matrix_grads + MOMENTUM * matrix_moments)
    matrix_means = AVERAGE * matrix_average + (1.0 - AVERAGE) * matrix_masters
    vector_moments = MOMENTUM * vector_momentum + vector_grads
    vector_masters = vector_weight - LR_VECTOR * (vector_grads + MOMENTUM * vector_moments)
    vector_means = AVERAGE * vector_average + (1.0 - AVERAGE) * vector_masters
    return (
        block_out,
        input_grad,
        matrix_grads,
        matrix_moments,
        matrix_means,
        matrix_masters,
        vector_grads,
        vector_moments,
        vector_means,
        vector_masters,
    )


def solution(mesh):
    fits = mesh.shape["img"] == 8 and mesh.shape["band"] == 4

    def per_device(images, *rest):
        step = whole_image if fits and images.shape[:3] == (4, 8, SIDE) else banded
        return step(images, *rest)

    return jax.shard_map(
            per_device,
        mesh=mesh,
        in_specs=(
            P("img", "band", None, None),
            P("img", "band", None, None),
            P("img"),
            P(("img", "band")),
            P(("img", "band")),
            P(("img", "band")),
            P(),
            P(),
            P(),
        ),
        out_specs=(
            P("img", "band", None, None),
            P("img", "band", None, None),
            P(("img", "band")),
            P(("img", "band")),
            P(("img", "band")),
            P(("img", "band")),
            P(),
            P(),
            P(),
            P(),
        ),
        check_vma=False,
    )
```

```python
import functools

import jax
import jax.numpy as jnp
from jax import lax
from jax.experimental import pallas as pl
from jax.experimental.pallas import tpu as pltpu
from jax.sharding import PartitionSpec as P

GROUPS = 32


EPS = 1e-06
MOMENTUM = 0.9
LR_MATRIX = 4e-05
LR_VECTOR = 0.0001
AVERAGE = 0.75


def extended(array, sides, width):
    for axis, dim in sides:
        count, length = (lax.axis_size(axis), array.shape[dim])
        up = [(i, (i + 1) % count) for i in range(count - 1)]
        down = [(j, i) for i, j in up]
        last = lax.slice_in_dim(array, length - width, length, axis=dim)
        initial = lax.slice_in_dim(array, 0, width, axis=dim)
        before = lax.ppermute(last, axis, up)
        after = lax.ppermute(initial, axis, down)
        array = jnp.concatenate([before, array, after], axis=dim)
    return array


def split_groups(field):
    return field.reshape(field.shape[:3] + (GROUPS, field.shape[3] // GROUPS))


def group_sums(field, mask):
    shaped = split_groups(field)
    weighted = shaped * mask[..., None]
    return (jnp.sum(weighted, axis=(1, 2, 4)), jnp.sum(weighted * shaped, axis=(1, 2, 4)))


def group_apply(field, sums, count, gain, shift):
    center = sums[0] / count[:, None]
    spread = sums[1] / count[:, None] - center * center
    scale = lax.rsqrt(spread + EPS)
    shaped = split_groups(field)
    normed = (shaped - center[:, None, None, :, None]) * scale[:, None, None, :, None]
    return normed.reshape(field.shape) * gain + shift


def normalize(field, mask, count, gain, shift):
    sums = lax.psum(group_sums(field, mask), "band")
    return (group_apply(field, sums, count, gain, shift), sums)


def normalize_back(field, sums, mask, count, gain, shift, upstream):
    _, pull = jax.vjp(
        lambda field_in, sums_in, gain_in, shift_in: group_apply(
            field_in, sums_in, count, gain_in, shift_in
        ),
        field,
        sums,
        gain,
        shift,
    )
    direct, grad_sums, grad_gain, grad_shift = pull(upstream)
    grad_sums = lax.psum(grad_sums, "band")
    _, pull_sums = jax.vjp(lambda field_in: group_sums(field_in, mask), field)
    return (direct + pull_sums(grad_sums)[0], grad_gain, grad_shift)


def activate(field, mask):
    return jax.nn.silu(field) * mask


def activate_back(field, mask, upstream):
    _, pull = jax.vjp(lambda inner: activate(inner, mask), field)
    return pull(upstream)[0]


def widen(field):
    return jnp.pad(field, ((0, 0), (0, 0), (1, 1), (0, 0)))


def taps(padded, kernel, height, width):
    total = jnp.zeros(padded.shape[:1] + (height, width, kernel.shape[2]), jnp.float32)
    for tap in range(9):
        row, column = (tap // 3, tap % 3)
        total = total + jnp.einsum(
            "ghwc,cd->ghwd",
            padded[:, row : row + height, column : column + width],
            kernel[tap],
            preferred_element_type=jnp.float32,
        )
    return total


def conv_forward(low_field, kernel):
    padded = widen(extended(low_field, (("band", 1),), 1))
    return (taps(padded, kernel, low_field.shape[1], low_field.shape[2]), padded)


def conv_backward(low_grad, kernel, padded):
    height, width = (low_grad.shape[1], low_grad.shape[2])
    grad_pad = widen(extended(low_grad, (("band", 1),), 1))
    flipped = jnp.swapaxes(kernel[::-1], 1, 2)
    grad_in = taps(grad_pad, flipped, height, width)
    pieces = []
    for tap in range(9):
        row, column = (tap // 3, tap % 3)
        pieces.append(
            jnp.einsum(
                "ghwc,ghwd->cd",
                padded[:, row : row + height, column : column + width],
                low_grad,
                preferred_element_type=jnp.float32,
            )
        )
    return (grad_in, jnp.stack(pieces))


def attend(query_low, key_full, key_valid, factor):
    score_matrix = (
        jnp.einsum("gqc,gkc->gqk", query_low, key_full, preferred_element_type=jnp.float32) * factor
    )
    score_matrix = jnp.where(key_valid[:, None, :], score_matrix, -1e30)
    top = jnp.max(score_matrix, axis=2, keepdims=True)
    raised = jnp.exp(score_matrix - top)
    total = jnp.sum(raised, axis=2, keepdims=True)
    return (raised / total, top, total)


def banded(
    images,
    cotangent,
    sizes,
    matrix_weight,
    matrix_momentum,
    matrix_average,
    vector_weight,
    vector_momentum,
    vector_average,
):
    batch, height, width, channels = images.shape
    square = channels * channels
    queries = height * width
    positions = width * width
    factor = channels ** (-0.5)
    weights = lax.all_gather(
        matrix_weight.astype(jnp.bfloat16), ("img", "band"), axis=0, tiled=True
    )
    kernel_one = weights[: 9 * square].reshape(9, channels, channels)
    kernel_two = weights[9 * square : 18 * square].reshape(9, channels, channels)
    attn_in = weights[18 * square : 21 * square].reshape(3, channels, channels)
    attention_output = weights[21 * square :].reshape(channels, channels)
    lines = lax.axis_index("band") * height + jnp.arange(height)
    across = jnp.arange(width)
    limit = sizes[:, None, None]
    inside = (lines[None, :, None] < limit) & (across[None, None, :] < limit)
    mask = jnp.where(inside, 1.0, 0.0).astype(jnp.float32)[..., None]
    count = (sizes * sizes * (channels // GROUPS)).astype(jnp.float32)
    spots = jnp.arange(positions)
    key_valid = ((spots // width)[None, :] < sizes[:, None]) & (
        (spots % width)[None, :] < sizes[:, None]
    )
    start = images.astype(jnp.float32) * mask
    norm_one, sums_one = normalize(start, mask, count, vector_weight[0], vector_weight[1])
    act_one = activate(norm_one, mask).astype(jnp.bfloat16)
    conv_raw, padded_one = conv_forward(act_one, kernel_one)
    conv_out = conv_raw + vector_weight[2]
    norm_two, sums_two = normalize(conv_out, mask, count, vector_weight[3], vector_weight[4])
    act_two = activate(norm_two, mask).astype(jnp.bfloat16)
    conv_raw, padded_two = conv_forward(act_two, kernel_two)
    resid = (start + conv_raw + vector_weight[5]) * mask
    norm_three, sums_three = normalize(resid, mask, count, vector_weight[6], vector_weight[7])
    normed = (norm_three * mask).astype(jnp.bfloat16).reshape(batch, queries, channels)
    projected = jnp.einsum("gqc,jcd->jgqd", normed, attn_in, preferred_element_type=jnp.float32)
    query_low = (projected[0] + vector_weight[8]).astype(jnp.bfloat16)
    key_low = projected[1].astype(jnp.bfloat16)
    value_low = (projected[2] + vector_weight[9]).astype(jnp.bfloat16)
    key_full, value_full = (
        lax.all_gather(key_low, "band", axis=1, tiled=True),
        lax.all_gather(value_low, "band", axis=1, tiled=True),
    )
    probability_rows, row_top, row_total = attend(query_low, key_full, key_valid, factor)
    mixed_values = jnp.einsum(
        "gqk,gkc->gqc",
        probability_rows.astype(jnp.bfloat16),
        value_full,
        preferred_element_type=jnp.float32,
    ).astype(jnp.bfloat16)
    output_rows = (
        jnp.einsum(
            "gqc,cd->gqd", mixed_values, attention_output, preferred_element_type=jnp.float32
        )
        + vector_weight[10]
    )
    block_out = ((resid + output_rows.reshape(images.shape)) * mask).astype(jnp.bfloat16)
    grad_top = cotangent.astype(jnp.float32) * mask
    grad_proj = grad_top.reshape(batch, queries, channels)
    grad_proj_low = grad_proj.astype(jnp.bfloat16)
    grad_out_weight = jnp.einsum(
        "gqc,gqd->cd", mixed_values, grad_proj_low, preferred_element_type=jnp.float32
    )
    grad_mixed = jnp.einsum(
        "gqd,cd->gqc", grad_proj_low, attention_output, preferred_element_type=jnp.float32
    ).astype(jnp.bfloat16)
    back_keys, back_values = (
        lax.all_gather(key_low, "band", axis=1, tiled=True),
        lax.all_gather(value_low, "band", axis=1, tiled=True),
    )
    back_probs = attend(query_low, back_keys, key_valid, factor)[0]
    grad_probs = jnp.einsum(
        "gqc,gkc->gqk", grad_mixed, back_values, preferred_element_type=jnp.float32
    )
    weighted_sum = jnp.sum(back_probs * grad_probs, axis=2, keepdims=True)
    grad_scores = back_probs * (grad_probs - weighted_sum)
    grad_scores_low = (grad_scores * factor).astype(jnp.bfloat16)
    grad_query = jnp.einsum(
        "gqk,gkc->gqc", grad_scores_low, back_keys, preferred_element_type=jnp.float32
    ).astype(jnp.bfloat16)
    key_terms = jnp.einsum(
        "gqk,gqc->gkc", grad_scores_low, query_low, preferred_element_type=jnp.float32
    )
    value_terms = jnp.einsum(
        "gqk,gqc->gkc",
        back_probs.astype(jnp.bfloat16),
        grad_mixed,
        preferred_element_type=jnp.float32,
    )
    grad_key, grad_value = (
        lax.psum_scatter(
            key_terms.astype(jnp.bfloat16), "band", scatter_dimension=1, tiled=True
        ).astype(jnp.float32),
        lax.psum_scatter(
            value_terms.astype(jnp.bfloat16), "band", scatter_dimension=1, tiled=True
        ).astype(jnp.float32),
    )
    grad_value_low = grad_value.astype(jnp.bfloat16)
    grads_low = jnp.stack([grad_query, grad_key.astype(jnp.bfloat16), grad_value_low])
    grad_in_weights = jnp.einsum(
        "gqc,jgqd->jcd", normed, grads_low, preferred_element_type=jnp.float32
    )
    grad_normed = (
        jnp.einsum("jgqd,jcd->gqc", grads_low, attn_in, preferred_element_type=jnp.float32).reshape(
            images.shape
        )
        * mask
    )
    grad_resid_norm, grad_gain_three, grad_shift_three = normalize_back(
        resid, sums_three, mask, count, vector_weight[6], vector_weight[7], grad_normed
    )
    grad_resid = (grad_top + grad_resid_norm) * mask
    grad_act_two, grad_kernel_two = conv_backward(
        grad_resid.astype(jnp.bfloat16), kernel_two, padded_two
    )
    grad_norm_two = activate_back(norm_two, mask, grad_act_two)
    grad_conv_out, grad_gain_two, grad_shift_two = normalize_back(
        conv_out, sums_two, mask, count, vector_weight[3], vector_weight[4], grad_norm_two
    )
    grad_act_one, grad_kernel_one = conv_backward(
        grad_conv_out.astype(jnp.bfloat16), kernel_one, padded_one
    )
    grad_norm_one = activate_back(norm_one, mask, grad_act_one)
    grad_start, grad_gain_one, grad_shift_one = normalize_back(
        start, sums_one, mask, count, vector_weight[0], vector_weight[1], grad_norm_one
    )
    input_grad = (grad_resid + grad_start) * mask
    vector_terms = jnp.stack(
        [
            grad_gain_one,
            grad_shift_one,
            jnp.sum(grad_conv_out, axis=(0, 1, 2)),
            grad_gain_two,
            grad_shift_two,
            jnp.sum(grad_resid, axis=(0, 1, 2)),
            grad_gain_three,
            grad_shift_three,
            jnp.sum(grad_query, axis=(0, 1), dtype=jnp.float32),
            jnp.sum(grad_value_low, axis=(0, 1), dtype=jnp.float32),
            jnp.sum(grad_proj, axis=(0, 1)),
        ]
    )
    vector_grads = lax.psum(vector_terms, ("img", "band"))
    grad_flat = jnp.concatenate(
        [
            grad_kernel_one.reshape(-1),
            grad_kernel_two.reshape(-1),
            grad_in_weights.reshape(-1),
            grad_out_weight.reshape(-1),
        ]
    )
    matrix_grads = lax.psum_scatter(grad_flat, ("img", "band"), scatter_dimension=0, tiled=True)
    matrix_moments = MOMENTUM * matrix_momentum + matrix_grads
    matrix_masters = matrix_weight - LR_MATRIX * (matrix_grads + MOMENTUM * matrix_moments)
    matrix_means = AVERAGE * matrix_average + (1.0 - AVERAGE) * matrix_masters
    vector_moments = MOMENTUM * vector_momentum + vector_grads
    vector_masters = vector_weight - LR_VECTOR * (vector_grads + MOMENTUM * vector_moments)
    vector_means = AVERAGE * vector_average + (1.0 - AVERAGE) * vector_masters
    return (
        block_out,
        input_grad,
        matrix_grads,
        matrix_moments,
        matrix_means,
        matrix_masters,
        vector_grads,
        vector_moments,
        vector_means,
        vector_masters,
    )


F32 = jnp.float32
BF16 = jnp.bfloat16
SIDE = 32
VMEM_LIMIT = 58 * 1024 * 1024


def dot(a, b):
    return lax.dot_general(a, b, (((1,), (0,)), ((), ())), preferred_element_type=F32)


def dot_nt(a, b):
    return lax.dot_general(a, b, (((1,), (1,)), ((), ())), preferred_element_type=F32)


def dot_tn(a, b):
    return lax.dot_general(a, b, (((0,), (0,)), ((), ())), preferred_element_type=F32)


def call(body, outs, ins, scratch=(), flops=0, name=None, aliases=None):
    spaces = {"v": pl.BlockSpec(memory_space=pltpu.VMEM), "s": pl.BlockSpec(memory_space=pltpu.SMEM),
              "a": pl.BlockSpec(memory_space=pl.ANY)}
    return pl.pallas_call(
        body,
        out_shape=[o for o, _ in outs],
        in_specs=[spaces[s] for _, s in ins],
        out_specs=[spaces[s] for _, s in outs],
        scratch_shapes=list(scratch),
        input_output_aliases=aliases or {},
        compiler_params=pltpu.CompilerParams(vmem_limit_bytes=VMEM_LIMIT),
        cost_estimate=pl.CostEstimate(flops=flops, bytes_accessed=0, transcendentals=0),
        name=name,
    )(*[a for a, _ in ins])


def shape(dims, dtype):
    return jax.ShapeDtypeStruct(dims, dtype)


def fold(x):
    return jnp.sum(x.reshape(x.shape[0] // 8, 8, x.shape[1]), axis=0)


def group_total(x):
    lane = lax.broadcasted_iota(jnp.int32, x.shape, 1)
    width = x.shape[1]
    for s in (1, 2, 4, 8):
        up = pltpu.roll(x, width - s, 1)
        down = pltpu.roll(x, s, 1)
        x = x + jnp.where((lane & s) == 0, up, down)
    return x


def total_of(*parts):
    rows = [jnp.sum(p, axis=0, keepdims=True) for p in parts]
    pad = jnp.zeros((8 - len(rows), rows[0].shape[1]), F32)
    return jnp.concatenate(rows + [pad], axis=0)


def moments(s1, s2, size):
    count = (size * size * 16).astype(F32)
    both = group_total(total_of(s1, s2)) / count
    mean = both[0:1]
    spread = both[1:2] - mean * mean
    return mean, lax.rsqrt(spread + EPS)


def row_mask(size, channels):
    across = lax.broadcasted_iota(jnp.int32, (SIDE, channels), 0)
    inside = across < size
    return lambda h: inside & (h < size)


def sigmoid(y):
    return 0.5 * jnp.tanh(0.5 * y) + 0.5


def rows(h):
    return pl.ds(pl.multiple_of(h * SIDE, SIDE), SIDE)


def put_shifted(ref, h, r, forward):
    channels = r.shape[1]
    w = lax.broadcasted_iota(jnp.int32, r.shape, 0)
    before = jnp.where(w == 0, 0.0, pltpu.roll(r, 1, 0)).astype(BF16)
    after = jnp.where(w == SIDE - 1, 0.0, pltpu.roll(r, SIDE - 1, 0)).astype(BF16)
    first, last = (before, after) if forward else (after, before)
    at = pl.ds(pl.multiple_of((h + 1) * SIDE, SIDE), SIDE)
    ref[at, 0:channels] = first
    ref[at, channels : 2 * channels] = r.astype(BF16)
    ref[at, 2 * channels :] = last


def clear_border(ref):
    zero = jnp.zeros((SIDE, ref.shape[1]), BF16)
    ref[0:SIDE, :] = zero
    ref[(SIDE + 1) * SIDE :, :] = zero


def put_transposed(ref, src_ref, row0, lane0):
    channels, count = ref.shape
    for j in range(count // 256):
        block = src_ref[row0 + j * 256 : row0 + (j + 1) * 256, lane0 : lane0 + channels]
        ref[:, j * 256 : (j + 1) * 256] = block.T


def act_one_body(size_ref, img_ref, vec_ref, pad_ref, at_ref, stat_ref):
    size = size_ref[0]
    channels = img_ref.shape[1]
    mask = row_mask(size, channels)

    def sums(h, carry):
        x = jnp.where(mask(h), img_ref[rows(h), :].astype(F32), 0.0)
        return carry[0] + fold(x), carry[1] + fold(x * x)

    zero = jnp.zeros((8, channels), F32)
    s1, s2 = lax.fori_loop(0, SIDE, sums, (zero, zero), unroll=2)
    mean, scale = moments(s1, s2, size)
    stat_ref[0:1, :] = mean
    stat_ref[1:2, :] = scale
    stat_ref[2:8, :] = jnp.zeros((6, channels), F32)
    apply_norm(img_ref, mean, scale * vec_ref[0:1, :], vec_ref[1:2, :], mask, pad_ref)
    put_transposed(at_ref, pad_ref, SIDE, 0)


def apply_norm(src_ref, mean, scale, shift, mask, pad_ref):
    clear_border(pad_ref)

    def apply(h, carry):
        y = (src_ref[rows(h), :].astype(F32) - mean) * scale + shift
        at = pl.ds(pl.multiple_of((h + 1) * SIDE, SIDE), SIDE)
        pad_ref[at, :] = jnp.where(mask(h), y * sigmoid(y), 0.0).astype(BF16)
        return carry

    lax.fori_loop(0, SIDE, apply, 0, unroll=4)


def act_one(size, img, vec):
    n, c = img.shape
    return call(act_one_body,
        [(shape((n + 64, c), BF16), "v"), (shape((c, n), BF16), "v"), (shape((8, c), F32), "v")],
        [(size, "s"), (img, "v"), (vec, "v")], name="act_one")


MB = 256


def start_copies(src_ref, dst_ref, sems, parts, offset=0):
    length = dst_ref.shape[0] // parts
    copies = [
        pltpu.make_async_copy(src_ref.at[pl.ds(offset + p * length, length)], dst_ref.at[pl.ds(p * length, length)], sems.at[p])
        for p in range(parts)
    ]
    for copy in copies:
        copy.start()
    return copies


COLUMNS = (1, 0, 2)


def start_kernel(src_ref, dst_ref, sems, offset):
    c = dst_ref.shape[1]
    copies = {}
    for dx in COLUMNS:
        for dy in range(3):
            tap = 3 * dy + dx
            copies[tap] = pltpu.make_async_copy(
                src_ref.at[pl.ds(offset + tap * c, c)], dst_ref.at[pl.ds(tap * c, c)], sems.at[tap]
            )
            copies[tap].start()
    return copies


def conv(pad_ref, k_ref, copies, out_ref, mb, finish):
    n, c = out_ref.shape
    zero = jnp.zeros((8, c), F32)
    carry = (zero, zero)
    across = lax.broadcasted_iota(jnp.int32, (mb, c), 0) & (SIDE - 1)
    for dx in COLUMNS:
        for dy in range(3):
            copies[3 * dy + dx].wait()

        def block(m, carry, dx=dx):
            first = pl.multiple_of(m * mb, mb)
            at = pl.ds(first, mb)
            value = None
            for dy in range(3):
                tap = 3 * dy + dx
                term = dot(pad_ref[pl.ds(first + dy * SIDE, mb), :], k_ref[tap * c : (tap + 1) * c, :])
                value = term if value is None else value + term
            if dx == 0:
                value = jnp.where(across == 0, 0.0, pltpu.roll(value, 1, 0))
            if dx == 2:
                value = jnp.where(across == SIDE - 1, 0.0, pltpu.roll(value, mb - 1, 0))
            if dx != COLUMNS[0]:
                value = value + out_ref[at, :]
            if dx == COLUMNS[-1]:
                value, carry = finish(first, value, carry)
            out_ref[at, :] = value
            return carry

        carry = lax.fori_loop(0, n // mb, block, carry, unroll=4)
    return carry


def pixel_mask(size, first, count, c):
    place = lax.broadcasted_iota(jnp.int32, (count, c), 0) + first
    return ((place >> 5) < size) & ((place & (SIDE - 1)) < size)


def put_stats(stat_ref, mean, scale):
    stat_ref[...] = jnp.concatenate([mean, scale, jnp.zeros((6, mean.shape[1]), F32)], axis=0)


def pieces_of(row, count, half):
    found = []
    for spot in range(row // half, (row + count - 1) // half + 1):
        found.append((spot, max(row, spot * half), min(row + count, (spot + 1) * half)))
    return found


def send_rows(stage, base, row, count, at_ref, rounds, sem):
    half = rounds[-1][0].shape[1]
    for spot, lo, hi in pieces_of(row, count, half):
        owner, tail = spot // 2, spot % 2
        refs, inner = rounds[owner // 16], owner % 16
        z, x, y, c = inner // 8, (inner >> 2) & 1, (inner >> 1) & 1, inner & 1
        index = ((at_ref[1] ^ x) * 2 + (at_ref[2] ^ y)) * 2 + z
        source = stage.at[pl.ds(base + lo - row, hi - lo)]
        place = pl.ds(lo - spot * half, hi - lo)
        for other in range(2):

            @pl.when((at_ref[3] ^ c) == other)
            def _(ref=refs[2 * other + tail], source=source, place=place):
                pltpu.make_async_copy(source, ref.at[index, place], sem).start()

    return pltpu.make_async_copy(stage.at[pl.ds(base, count)], stage.at[pl.ds(base, count)], sem)


QB = 256
PB = 256


def forward_body(
    at_ref, pad_one_ref, vec_ref, w_any, img_any, cot_any,
    conv_any, stat_two_ref, mixed_any, resid_any, grad_any, e3_any, vout_ref, *refs,
):
    high, low = refs[0:4], refs[4:8]
    (k_one, k_two, w_ref, img_ref, cot_ref, conv_ref, pad_ref, act_t, resid_ref, normed_ref, normed_t,
     q_ref, k_ref, v_ref, p_ref, ds_ref, mixed_ref, top_ref, gm_ref, gq_ref, gk_ref, gv_ref, grad_ref, e3_ref, gw_ref,
     one_sems, two_sems, w_sems, in_sems, out_sems, gw_sem, gk_sems) = refs[8:]
    n, c = normed_ref.shape
    size = at_ref[0]
    one_copies = start_kernel(w_any, k_one, one_sems, 0)
    two_copies = start_kernel(w_any, k_two, two_sems, 9 * c)
    img_copy = pltpu.make_async_copy(img_any, img_ref, in_sems.at[0])
    cot_copy = pltpu.make_async_copy(cot_any, cot_ref, in_sems.at[1])
    img_copy.start()
    w_copies = start_copies(w_any, w_ref, w_sems, 4, 18 * c)
    cot_copy.start()
    leaving = []

    def leave(src, dst):
        copy = pltpu.make_async_copy(src, dst, out_sems.at[len(leaving)])
        copy.start()
        leaving.append(copy)

    mask = row_mask(size, c)
    zero = jnp.zeros((8, c), F32)

    bias_one = vec_ref[2:3, :]

    def finish_one(first, v, carry):
        v = v + bias_one
        x = jnp.where(pixel_mask(size, first, MB, c), v, 0.0)
        return v, (carry[0] + fold(x), carry[1] + fold(x * x))

    s1, s2 = conv(pad_one_ref, k_one, one_copies, conv_ref, MB, finish_one)
    leave(conv_ref, conv_any)
    mean, scale = moments(s1, s2, size)
    put_stats(stat_two_ref, mean, scale)
    apply_norm(conv_ref, mean, scale * vec_ref[3:4, :], vec_ref[4:5, :], mask, pad_ref)
    put_transposed(act_t, pad_ref, SIDE, 0)

    bias_two = vec_ref[5:6, :]
    img_copy.wait()

    def finish_two(first, v, carry):
        v = v + bias_two + img_ref[pl.ds(first, MB), :].astype(F32)
        x = jnp.where(pixel_mask(size, first, MB, c), v, 0.0)
        return x, (carry[0] + fold(x), carry[1] + fold(x * x))

    s1, s2 = conv(pad_ref, k_two, two_copies, resid_ref, MB, finish_two)
    leave(resid_ref, resid_any)
    mean, scale = moments(s1, s2, size)
    gain = vec_ref[6:7, :]
    full_gain, shift = scale * gain, vec_ref[7:8, :]
    cot_copy.wait()

    def apply(h, carry):
        y = (resid_ref[rows(h), :] - mean) * full_gain + shift
        normed_ref[rows(h), :] = jnp.where(mask(h), y, 0.0).astype(BF16)
        t = jnp.where(mask(h), cot_ref[rows(h), :].astype(F32), 0.0)
        top_ref[rows(h), :] = t.astype(BF16)
        return carry + fold(t)

    top_sum = lax.fori_loop(0, SIDE, apply, zero, unroll=4)
    put_transposed(normed_t, normed_ref, 0, 0)

    for copy in w_copies:
        copy.wait()
    factor = c ** (-0.5)
    wq, wk, wv, wo = (functools.partial(lambda j: w_ref[j * c : (j + 1) * c, :], j) for j in range(4))
    qb, vb = vec_ref[8:9, :], vec_ref[9:10, :]
    def project(m, carry):
        at = pl.ds(pl.multiple_of(m * PB, PB), PB)
        x = normed_ref[at, :]
        q_ref[at, :] = (dot(x, wq()) + qb).astype(BF16)
        k_ref[at, :] = dot(x, wk()).astype(BF16)
        v_ref[at, :] = (dot(x, wv()) + vb).astype(BF16)
        gm_ref[at, :] = dot_nt(top_ref[at, :], wo()).astype(BF16)
        return carry

    lax.fori_loop(0, n // PB, project, 0, unroll=2)

    spot = lax.broadcasted_iota(jnp.int32, (1, n), 1)
    key_bias = jnp.where(((spot >> 5) < size) & ((spot & (SIDE - 1)) < size), 0.0, -1e30)

    def queries(m, carry):
        at = pl.ds(pl.multiple_of(m * QB, QB), QB)
        s = dot_nt(q_ref[at, :], k_ref[...]) * factor + key_bias
        raised = jnp.exp(s - jnp.max(s, axis=1, keepdims=True))
        p = raised * (1.0 / jnp.sum(raised, axis=1, keepdims=True))
        low_p = p.astype(BF16)
        p_ref[at, :] = low_p
        mixed_ref[at, :] = dot(low_p, v_ref[...]).astype(BF16)
        gp = dot_nt(gm_ref[at, :], v_ref[...])
        weighted = jnp.sum(p * gp, axis=1, keepdims=True)
        ds = (p * ((gp - weighted) * factor)).astype(BF16)
        ds_ref[at, :] = ds
        gq_ref[at, :] = dot(ds, k_ref[...]).astype(BF16)
        return carry

    lax.fori_loop(0, n // QB, queries, 0)
    leave(mixed_ref, mixed_any)

    def keys(m, carry):
        at = pl.ds(pl.multiple_of(m * QB, QB), QB)
        gk_ref[at, :] = dot_tn(ds_ref[:, at], q_ref[...]).astype(BF16)
        gv_ref[at, :] = dot_tn(p_ref[:, at], gm_ref[...]).astype(BF16)
        return carry

    lax.fori_loop(0, n // QB, keys, 0)
    gw_ref[0:c, :] = dot(normed_t[...], gq_ref[...]).astype(BF16)
    gw_ref[c : 2 * c, :] = dot(normed_t[...], gk_ref[...]).astype(BF16)
    gw_ref[2 * c : 3 * c, :] = dot(normed_t[...], gv_ref[...]).astype(BF16)
    gw_ref[3 * c : 4 * c, :] = dot_tn(mixed_ref[...], top_ref[...]).astype(BF16)
    waits = [send_rows(gw_ref, 0, 18 * c, 4 * c, at_ref, (None, high), gw_sem)]

    def normed_grad(m, carry):
        su, sux, sq, sv = carry
        first = pl.multiple_of(m * PB, PB)
        at = pl.ds(first, PB)
        gq, gk, gv = gq_ref[at, :], gk_ref[at, :], gv_ref[at, :]
        u = dot_nt(gq, wq()) + dot_nt(gk, wk()) + dot_nt(gv, wv())
        u = jnp.where(pixel_mask(size, first, PB, c), u, 0.0)
        grad_ref[at, :] = u
        xhat = (resid_ref[at, :] - mean) * scale
        return su + fold(u), sux + fold(u * xhat), sq + fold(gq.astype(F32)), sv + fold(gv.astype(F32))

    su, sux, sq, sv = lax.fori_loop(0, n // PB, normed_grad, (zero, zero, zero, zero), unroll=2)
    count = (size * size * 16).astype(F32)
    both = group_total(total_of(su, sux) * gain) / count
    m1, m2 = both[0:1], both[1:2]
    clear_border(e3_ref)

    def back(h, carry):
        xhat = (resid_ref[rows(h), :] - mean) * scale
        g = (grad_ref[rows(h), :] * gain - m1 - xhat * m2) * scale + top_ref[rows(h), :].astype(F32)
        g = jnp.where(mask(h), g, 0.0)
        grad_ref[rows(h), :] = g
        put_shifted(e3_ref, h, g.astype(BF16).astype(F32), False)
        return carry + fold(g)

    sg = lax.fori_loop(0, SIDE, back, zero, unroll=2)
    leave(e3_ref, e3_any)
    leave(grad_ref, grad_any)
    vout_ref[...] = total_of(sg, sux, su, sq, sv, top_sum)
    waits += kernel_gradient(act_t, e3_ref, k_one, 9 * c, at_ref, (low, high), gk_sems)
    for wait in waits + leaving:
        wait.wait()


def forward(at, pad_one, vec, weights, img, cot):
    n, c = img.shape
    half = (shape((8, weights.shape[0] // 64, c), BF16), "a")

    def low(*dims):
        return pltpu.VMEM(dims, BF16)

    full = low(n, c)
    found = call(forward_body,
        [(shape((n, c), F32), "a"), (shape((8, c), F32), "v"), (shape((n, c), BF16), "a"), (shape((n, c), F32), "a"),
         (shape((n, c), F32), "a"), (shape((n + 2 * SIDE, 3 * c), BF16), "a"), (shape((8, c), F32), "v")] + [half] * 8,
        [(at, "s"), (pad_one, "v"), (vec, "v"), (weights, "a"), (img, "a"), (cot, "a")],
        [low(9 * c, c), low(9 * c, c), low(4 * c, c), full, full, pltpu.VMEM((n, c), F32), low(n + 2 * SIDE, c), low(c, n),
         pltpu.VMEM((n, c), F32), full, low(c, n), full, full, full, low(n, n), low(n, n), full, full, full, full, full, full,
         pltpu.VMEM((n, c), F32), low(n + 2 * SIDE, 3 * c), low(4 * c, c),
         pltpu.SemaphoreType.DMA((9,)), pltpu.SemaphoreType.DMA((9,)), pltpu.SemaphoreType.DMA((4,)),
         pltpu.SemaphoreType.DMA((2,)), pltpu.SemaphoreType.DMA((5,)), pltpu.SemaphoreType.DMA, pltpu.SemaphoreType.DMA((9,))],
        name="forward")
    return found[:7], found[7:11], found[11:15]


def out_body(at_ref, mixed_ref, resid_ref, vec_ref, w_any, out_ref, wo_ref, sem):
    n, c = mixed_ref.shape
    copy = pltpu.make_async_copy(w_any.at[pl.ds(21 * c, c)], wo_ref, sem)
    copy.start()
    copy.wait()
    for m in range(n // MB):
        at = slice(m * MB, (m + 1) * MB)
        value = dot(mixed_ref[at, :], wo_ref[...]) + vec_ref[10:11, :] + resid_ref[at, :]
        out_ref[at, :] = jnp.where(pixel_mask(at_ref[0], m * MB, MB, c), value, 0.0).astype(BF16)


def block_rows(at, mixed, resid, vec, weights):
    n, c = mixed.shape
    return call(out_body, [(shape((n, c), BF16), "v")],
        [(at, "s"), (mixed, "v"), (resid, "v"), (vec, "v"), (weights, "a")],
        [pltpu.VMEM((c, c), BF16), pltpu.SemaphoreType.DMA], name="block_rows")[0]


def kernel_gradient(act_t, e3_ref, stage, row, at_ref, rounds, sems):
    c, n = act_t.shape

    def one_row(dy, carry):
        lo = pl.multiple_of((2 - dy) * SIDE, SIDE)
        for dx in range(3):
            value = dot(act_t[...], e3_ref[pl.ds(lo, n), dx * c : (dx + 1) * c])
            stage[pl.ds(pl.multiple_of((3 * dy + dx) * c, c), c), :] = value.astype(BF16)
        for now in range(3):

            @pl.when(dy == now)
            def _(now=now):
                send_rows(stage, 3 * now * c, row + 3 * now * c, 3 * c, at_ref, rounds, sems.at[now])

        return carry

    lax.fori_loop(0, 3, one_row, 0, unroll=1)
    places = [stage.at[pl.ds(3 * dy * c, 3 * c)] for dy in range(3)]
    return [pltpu.make_async_copy(place, place, sems.at[dy]) for dy, place in enumerate(places)]


def conv_back(e3_ref, k_ref, copies, out_ref):
    n, c = out_ref.shape
    for dy in range(3):
        copies[dy].wait()
        lo = (2 - dy) * SIDE

        def block(m, carry, dy=dy, lo=lo):
            first = pl.multiple_of(m * MB, MB)
            value = None
            for dx in range(3):
                tap = 3 * dy + dx
                term = dot_nt(e3_ref[pl.ds(first + lo, MB), dx * c : (dx + 1) * c], k_ref[tap * c : (tap + 1) * c, :])
                value = term if value is None else value + term
            if dy > 0:
                value = value + out_ref[pl.ds(first, MB), :]
            out_ref[pl.ds(first, MB), :] = value
            return carry

        lax.fori_loop(0, n // MB, block, 0, unroll=4)


def norm_back_sums(src_ref, g_ref, mean, scale, gain, shift, mask, size):
    c = g_ref.shape[1]

    def sums(h, carry):
        xhat = (src_ref[rows(h), :].astype(F32) - mean) * scale
        y = xhat * gain + shift
        s = sigmoid(y)
        u = jnp.where(mask(h), g_ref[rows(h), :] * (s * (1.0 + y * (1.0 - s))), 0.0)
        g_ref[rows(h), :] = u
        return carry[0] + fold(u), carry[1] + fold(u * xhat)

    zero = jnp.zeros((8, c), F32)
    su, sux = lax.fori_loop(0, SIDE, sums, (zero, zero), unroll=2)
    count = (size * size * 16).astype(F32)
    both = group_total(total_of(su, sux) * gain) / count
    return su, sux, both[0:1], both[1:2]


def back_two_body(
    at_ref, e3_ref, vec_ref, stat_ref, k_any, conv_any, act_any, i0, i1, i2, i3,
    e3_any, vout_ref, o0, o1, o2, o3, g_ref, conv_ref, act_t, e3_out, k_vmem, sems, in_sems, out_sem, gk_sems,
):
    n, c = conv_ref.shape
    copies = start_copies(k_any, k_vmem, sems, 3, 9 * c)
    conv_copy = pltpu.make_async_copy(conv_any, conv_ref, in_sems.at[0])
    act_copy = pltpu.make_async_copy(act_any, act_t, in_sems.at[1])
    conv_copy.start()
    act_copy.start()
    size = at_ref[0]
    mask = row_mask(size, c)
    conv_back(e3_ref, k_vmem, copies, g_ref)
    conv_copy.wait()
    mean, scale = stat_ref[0:1, :], stat_ref[1:2, :]
    gain, shift = vec_ref[3:4, :], vec_ref[4:5, :]
    su, sux, m1, m2 = norm_back_sums(conv_ref, g_ref, mean, scale, gain, shift, mask, size)
    clear_border(e3_out)

    def apply(h, carry):
        xhat = (conv_ref[rows(h), :] - mean) * scale
        g = jnp.where(mask(h), (g_ref[rows(h), :] * gain - m1 - xhat * m2) * scale, 0.0)
        put_shifted(e3_out, h, g.astype(BF16).astype(F32), False)
        return carry + fold(g)

    sg = lax.fori_loop(0, SIDE, apply, jnp.zeros((8, c), F32), unroll=2)
    leaving = pltpu.make_async_copy(e3_out, e3_any, out_sem)
    leaving.start()
    vout_ref[...] = total_of(sg, sux, su)
    act_copy.wait()
    for wait in kernel_gradient(act_t, e3_out, k_vmem, 0, at_ref, ((o0, o1, o2, o3),), gk_sems):
        wait.wait()
    leaving.wait()


def back_two(at, e3, weights, vec, conv_out, stat, act, low):
    n, c = conv_out.shape
    half = shape(low[0].shape, BF16)
    e3_out, vout, *low = call(back_two_body,
        [(shape((n + 64, 3 * c), BF16), "a"), (shape((8, c), F32), "v")] + [(half, "a")] * 4,
        [(at, "s"), (e3, "v"), (vec, "v"), (stat, "v"), (weights, "a"), (conv_out, "a"), (act, "a")] + [(v, "a") for v in low],
        [pltpu.VMEM((n, c), F32), pltpu.VMEM((n, c), F32), pltpu.VMEM((c, n), BF16), pltpu.VMEM((n + 64, 3 * c), BF16),
         pltpu.VMEM((9 * c, c), BF16), pltpu.SemaphoreType.DMA((3,)), pltpu.SemaphoreType.DMA((2,)), pltpu.SemaphoreType.DMA,
         pltpu.SemaphoreType.DMA((9,))],
        name="back_two", aliases={7 + i: 2 + i for i in range(4)})
    return e3_out, vout, low


def back_one_body(
    size_ref, e3_ref, k_ref, vec_ref, img_ref, stat_ref, resid_ref, rows_ref, both_any, vout_ref,
    g_ref, out_ref, k_vmem, sems, rows_sem, out_sem,
):
    n, c = img_ref.shape
    copies = start_copies(k_ref, k_vmem, sems, 3)
    bands, quarter = both_any.shape[0], both_any.shape[2]
    kept = [pltpu.make_async_copy(rows_ref.at[pl.ds(j * quarter, quarter)], both_any.at[j, 0], rows_sem.at[j]) for j in range(bands)]
    for copy in kept:
        copy.start()
    size = size_ref[0]
    mask = row_mask(size, c)
    conv_back(e3_ref, k_vmem, copies, g_ref)
    mean, scale = stat_ref[0:1, :], stat_ref[1:2, :]
    gain, shift = vec_ref[0:1, :], vec_ref[1:2, :]
    su, sux, m1, m2 = norm_back_sums(img_ref, g_ref, mean, scale, gain, shift, mask, size)

    def apply(h, carry):
        xhat = (img_ref[rows(h), :].astype(F32) - mean) * scale
        g = (g_ref[rows(h), :] * gain - m1 - xhat * m2) * scale + resid_ref[rows(h), :]
        out_ref[rows(h), :] = jnp.where(mask(h), g, 0.0).astype(out_ref.dtype)
        return carry

    lax.fori_loop(0, SIDE, apply, 0, unroll=2)
    for j in range(bands):
        copy = pltpu.make_async_copy(out_ref.at[pl.ds(j * quarter, quarter)], both_any.at[j, 1], out_sem.at[j])
        copy.start()
        kept.append(copy)
    vout_ref[...] = total_of(sux, su)
    for copy in kept:
        copy.wait()


def back_one(at, e3, weights, vec, img, stat, grad_resid, out, bands):
    n, c = img.shape
    return call(back_one_body, [(shape((bands, 2, n // bands, c), BF16), "a"), (shape((8, c), F32), "v")],
        [(at, "s"), (e3, "v"), (weights, "a"), (vec, "v"), (img, "v"), (stat, "v"), (grad_resid, "v"), (out, "v")],
        [pltpu.VMEM((n, c), F32), pltpu.VMEM((n, c), BF16), pltpu.VMEM((9 * c, c), BF16), pltpu.SemaphoreType.DMA((3,)),
         pltpu.SemaphoreType.DMA((bands,)), pltpu.SemaphoreType.DMA((bands,))],
        name="back_one")


ALL = ("img", "band")
CORE = [(b, b ^ 1) for b in range(4)]
ACROSS_Y = [(b, b ^ 2) for b in range(4)]
ACROSS_X = [(i, i ^ 1) for i in range(8)]

def after(value, *earlier, flops=0):
    def body(*refs):
        pass

    anywhere = pl.BlockSpec(memory_space=pl.ANY)
    return pl.pallas_call(
        body,
        out_shape=shape(value.shape, value.dtype),
        in_specs=[anywhere] * (1 + len(earlier)),
        out_specs=anywhere,
        input_output_aliases={0: 0},
        cost_estimate=pl.CostEstimate(flops=flops, bytes_accessed=0, transcendentals=0),
        name="after",
    )(value, *earlier)


def wide(*parts):
    total = parts[0].astype(F32)
    for part in parts[1:]:
        total = total + part.astype(F32)
    return total


def chip_sends(arrays, *earlier):
    mine_a, mine_b, theirs_a, theirs_b = arrays
    half, c = mine_a.shape[1:]
    dims = (2, 2, 2, half, c)
    if earlier:
        theirs_a, theirs_b = after(theirs_a, *earlier), after(theirs_b, *earlier)
    got = [lax.ppermute(v, "band", CORE) for v in (theirs_a, theirs_b)]
    pair_a = (mine_a.reshape(dims), got[0].reshape(dims))
    pair_b = (mine_b.reshape(dims), got[1].reshape(dims))
    send_a = wide(*(v[1] for v in pair_a)).astype(BF16)
    send_b = wide(*(v[:, 1] for v in pair_b)).astype(BF16)
    return pair_a, pair_b, send_a, send_b


def plane_swap(send_a, send_b):
    return lax.ppermute(send_a, "img", ACROSS_X), lax.ppermute(send_b, "band", ACROSS_Y)


def plane_sends(pair_a, pair_b, got_a, got_b):
    next_a = wide(*(v[0, 1] for v in pair_a), got_a[1]).astype(BF16)
    next_b = wide(*(v[1, 0] for v in pair_b), got_b[1]).astype(BF16)
    kept_a = (*(v[0, 0] for v in pair_a), got_a[0])
    kept_b = (*(v[0, 0] for v in pair_b), got_b[0])
    return kept_a, kept_b, next_a, next_b


def plane_sums(kept_a, kept_b, next_a, next_b, *earlier):
    last_a = lax.ppermute(next_a, "band", ACROSS_Y)
    last_b = lax.ppermute(next_b, "img", ACROSS_X)
    if earlier:
        last_a, last_b = after(last_a, *earlier), after(last_b, *earlier)
    return jnp.concatenate([wide(*kept_a, last_a), wide(*kept_b, last_b)], axis=1)


def owner_parts(low, high):
    z = lax.axis_index("img") // 2

    def block_of(plane):
        found = high[1]
        for at, block in ((2, high[0]), (1, low[1]), (0, low[0])):
            found = jnp.where(plane == at, block, found)
        return found

    sent = [block_of(z ^ step).astype(BF16) for step in (1, 2, 3)]
    got = [lax.ppermute(v, "img", [(i, i ^ (2 * step)) for i in range(8)]) for v, step in zip(sent, (1, 2, 3))]
    return [block_of(z)] + got, sent


def four_sum(v, axis, steps):
    a, b, c = (lax.ppermute(v, axis, [(i, i ^ step) for i in range(lax.axis_size(axis))]) for step in steps)
    return (v + a) + (b + c)


def whole_image(
    images,
    cotangent,
    sizes,
    matrix_weight,
    matrix_momentum,
    matrix_average,
    vector_weight,
    vector_momentum,
    vector_average,
):
    batch, height, width, c = images.shape
    n = width * width
    mine = lax.axis_index("band")
    place = lax.axis_index("img")
    at = jnp.stack([lax.dynamic_index_in_dim(sizes, mine, 0, False), place % 2, mine // 2, mine % 2])

    def to_image(field):
        parts = field.reshape(batch, height * width, c)
        return lax.all_to_all(parts, "band", 0, 0, tiled=True).reshape(n, c)

    weights = lax.all_gather(matrix_weight.astype(BF16).reshape(-1, c), ALL, axis=0, tiled=True)
    img = to_image(images)
    cot = to_image(cotangent)
    pad_one, act_t, stat_one = act_one(at, img, vector_weight)
    (conv_out, stat_two, mixed, resid, grad_resid, e3_two, v3), high, low = forward(
        at, pad_one, vector_weight, weights, img, cot
    )
    high = chip_sends(high)
    out = block_rows(at, mixed, resid, vector_weight, weights)
    e3_two = after(e3_two, high[2], high[3], out)
    swapped = plane_swap(high[2], high[3])
    e3_one, v2, low = back_two(at, e3_two, weights, vector_weight, conv_out, stat_two, act_t, low)
    low = chip_sends(low, *swapped)
    high = plane_sends(*high[:2], *swapped)
    low_sends = low[2:4]
    e3_one = after(e3_one, *low_sends)
    swapped = plane_swap(low[2], low[3])
    both, v1 = back_one(at, e3_one, weights, vector_weight, img, stat_one, grad_resid, out, batch)
    vecs = jnp.stack([v1[0], v1[1], v2[0], v2[1], v2[2], v3[0], v3[1], v3[2], v3[3], v3[4], v3[5]])
    low = plane_sends(*low[:2], *(after(v, v1) for v in swapped))
    vecs = four_sum(after(vecs, low[2], low[3]), "img", (2, 4, 6))
    high = plane_sums(*high, low[2], low[3])
    low = plane_sums(*low, vecs)
    parts, sent = owner_parts(low, high)
    given = lax.all_to_all(after(both, *sent), "band", 0, 0, tiled=True)
    block_out = given[:, 0].reshape(images.shape)
    input_grad = given[:, 1].reshape(images.shape).astype(F32)
    vecs = after(vecs, parts[1])
    vecs = vecs + lax.ppermute(vecs, "img", ACROSS_X)
    vector_grads = four_sum(vecs, "band", (1, 2, 3))
    vector_moments = MOMENTUM * vector_momentum + vector_grads
    vector_masters = vector_weight - LR_VECTOR * (vector_grads + MOMENTUM * vector_moments)
    vector_means = AVERAGE * vector_average + (1.0 - AVERAGE) * vector_masters
    matrix_grads = wide(*parts).reshape(-1)
    matrix_moments = MOMENTUM * matrix_momentum + matrix_grads
    matrix_masters = matrix_weight - LR_MATRIX * (matrix_grads + MOMENTUM * matrix_moments)
    matrix_means = AVERAGE * matrix_average + (1.0 - AVERAGE) * matrix_masters
    return (
        block_out,
        input_grad,
        matrix_grads,
        matrix_moments,
        matrix_means,
        matrix_masters,
        vector_grads,
        vector_moments,
        vector_means,
        vector_masters,
    )


def solution(mesh):
    fits = mesh.shape["img"] == 8 and mesh.shape["band"] == 4

    def per_device(images, *rest):
        step = whole_image if fits and images.shape[:3] == (4, 8, SIDE) else banded
        return step(images, *rest)

    return jax.shard_map(
            per_device,
        mesh=mesh,
        in_specs=(
            P("img", "band", None, None),
            P("img", "band", None, None),
            P("img"),
            P(("img", "band")),
            P(("img", "band")),
            P(("img", "band")),
            P(),
            P(),
            P(),
        ),
        out_specs=(
            P("img", "band", None, None),
            P("img", "band", None, None),
            P(("img", "band")),
            P(("img", "band")),
            P(("img", "band")),
            P(("img", "band")),
            P(),
            P(),
            P(),
            P(),
        ),
        check_vma=False,
    )
```

```python
import functools

import jax
import jax.numpy as jnp
from jax import lax
from jax.experimental import pallas as pl
from jax.experimental.pallas import tpu as pltpu
from jax.sharding import PartitionSpec as P

GROUPS = 32


EPS = 1e-06
MOMENTUM = 0.9
LR_MATRIX = 4e-05
LR_VECTOR = 0.0001
AVERAGE = 0.75


def extended(array, sides, width):
    for axis, dim in sides:
        count, length = (lax.axis_size(axis), array.shape[dim])
        up = [(i, (i + 1) % count) for i in range(count - 1)]
        down = [(j, i) for i, j in up]
        last = lax.slice_in_dim(array, length - width, length, axis=dim)
        initial = lax.slice_in_dim(array, 0, width, axis=dim)
        before = lax.ppermute(last, axis, up)
        after = lax.ppermute(initial, axis, down)
        array = jnp.concatenate([before, array, after], axis=dim)
    return array


def split_groups(field):
    return field.reshape(field.shape[:3] + (GROUPS, field.shape[3] // GROUPS))


def group_sums(field, mask):
    shaped = split_groups(field)
    weighted = shaped * mask[..., None]
    return (jnp.sum(weighted, axis=(1, 2, 4)), jnp.sum(weighted * shaped, axis=(1, 2, 4)))


def group_apply(field, sums, count, gain, shift):
    center = sums[0] / count[:, None]
    spread = sums[1] / count[:, None] - center * center
    scale = lax.rsqrt(spread + EPS)
    shaped = split_groups(field)
    normed = (shaped - center[:, None, None, :, None]) * scale[:, None, None, :, None]
    return normed.reshape(field.shape) * gain + shift


def normalize(field, mask, count, gain, shift):
    sums = lax.psum(group_sums(field, mask), "band")
    return (group_apply(field, sums, count, gain, shift), sums)


def normalize_back(field, sums, mask, count, gain, shift, upstream):
    _, pull = jax.vjp(
        lambda field_in, sums_in, gain_in, shift_in: group_apply(
            field_in, sums_in, count, gain_in, shift_in
        ),
        field,
        sums,
        gain,
        shift,
    )
    direct, grad_sums, grad_gain, grad_shift = pull(upstream)
    grad_sums = lax.psum(grad_sums, "band")
    _, pull_sums = jax.vjp(lambda field_in: group_sums(field_in, mask), field)
    return (direct + pull_sums(grad_sums)[0], grad_gain, grad_shift)


def activate(field, mask):
    return jax.nn.silu(field) * mask


def activate_back(field, mask, upstream):
    _, pull = jax.vjp(lambda inner: activate(inner, mask), field)
    return pull(upstream)[0]


def widen(field):
    return jnp.pad(field, ((0, 0), (0, 0), (1, 1), (0, 0)))


def taps(padded, kernel, height, width):
    total = jnp.zeros(padded.shape[:1] + (height, width, kernel.shape[2]), jnp.float32)
    for tap in range(9):
        row, column = (tap // 3, tap % 3)
        total = total + jnp.einsum(
            "ghwc,cd->ghwd",
            padded[:, row : row + height, column : column + width],
            kernel[tap],
            preferred_element_type=jnp.float32,
        )
    return total


def conv_forward(low_field, kernel):
    padded = widen(extended(low_field, (("band", 1),), 1))
    return (taps(padded, kernel, low_field.shape[1], low_field.shape[2]), padded)


def conv_backward(low_grad, kernel, padded):
    height, width = (low_grad.shape[1], low_grad.shape[2])
    grad_pad = widen(extended(low_grad, (("band", 1),), 1))
    flipped = jnp.swapaxes(kernel[::-1], 1, 2)
    grad_in = taps(grad_pad, flipped, height, width)
    pieces = []
    for tap in range(9):
        row, column = (tap // 3, tap % 3)
        pieces.append(
            jnp.einsum(
                "ghwc,ghwd->cd",
                padded[:, row : row + height, column : column + width],
                low_grad,
                preferred_element_type=jnp.float32,
            )
        )
    return (grad_in, jnp.stack(pieces))


def attend(query_low, key_full, key_valid, factor):
    score_matrix = (
        jnp.einsum("gqc,gkc->gqk", query_low, key_full, preferred_element_type=jnp.float32) * factor
    )
    score_matrix = jnp.where(key_valid[:, None, :], score_matrix, -1e30)
    top = jnp.max(score_matrix, axis=2, keepdims=True)
    raised = jnp.exp(score_matrix - top)
    total = jnp.sum(raised, axis=2, keepdims=True)
    return (raised / total, top, total)


def banded(
    images,
    cotangent,
    sizes,
    matrix_weight,
    matrix_momentum,
    matrix_average,
    vector_weight,
    vector_momentum,
    vector_average,
):
    batch, height, width, channels = images.shape
    square = channels * channels
    queries = height * width
    positions = width * width
    factor = channels ** (-0.5)
    weights = lax.all_gather(
        matrix_weight.astype(jnp.bfloat16), ("img", "band"), axis=0, tiled=True
    )
    kernel_one = weights[: 9 * square].reshape(9, channels, channels)
    kernel_two = weights[9 * square : 18 * square].reshape(9, channels, channels)
    attn_in = weights[18 * square : 21 * square].reshape(3, channels, channels)
    attention_output = weights[21 * square :].reshape(channels, channels)
    lines = lax.axis_index("band") * height + jnp.arange(height)
    across = jnp.arange(width)
    limit = sizes[:, None, None]
    inside = (lines[None, :, None] < limit) & (across[None, None, :] < limit)
    mask = jnp.where(inside, 1.0, 0.0).astype(jnp.float32)[..., None]
    count = (sizes * sizes * (channels // GROUPS)).astype(jnp.float32)
    spots = jnp.arange(positions)
    key_valid = ((spots // width)[None, :] < sizes[:, None]) & (
        (spots % width)[None, :] < sizes[:, None]
    )
    start = images.astype(jnp.float32) * mask
    norm_one, sums_one = normalize(start, mask, count, vector_weight[0], vector_weight[1])
    act_one = activate(norm_one, mask).astype(jnp.bfloat16)
    conv_raw, padded_one = conv_forward(act_one, kernel_one)
    conv_out = conv_raw + vector_weight[2]
    norm_two, sums_two = normalize(conv_out, mask, count, vector_weight[3], vector_weight[4])
    act_two = activate(norm_two, mask).astype(jnp.bfloat16)
    conv_raw, padded_two = conv_forward(act_two, kernel_two)
    resid = (start + conv_raw + vector_weight[5]) * mask
    norm_three, sums_three = normalize(resid, mask, count, vector_weight[6], vector_weight[7])
    normed = (norm_three * mask).astype(jnp.bfloat16).reshape(batch, queries, channels)
    projected = jnp.einsum("gqc,jcd->jgqd", normed, attn_in, preferred_element_type=jnp.float32)
    query_low = (projected[0] + vector_weight[8]).astype(jnp.bfloat16)
    key_low = projected[1].astype(jnp.bfloat16)
    value_low = (projected[2] + vector_weight[9]).astype(jnp.bfloat16)
    key_full, value_full = (
        lax.all_gather(key_low, "band", axis=1, tiled=True),
        lax.all_gather(value_low, "band", axis=1, tiled=True),
    )
    probability_rows, row_top, row_total = attend(query_low, key_full, key_valid, factor)
    mixed_values = jnp.einsum(
        "gqk,gkc->gqc",
        probability_rows.astype(jnp.bfloat16),
        value_full,
        preferred_element_type=jnp.float32,
    ).astype(jnp.bfloat16)
    output_rows = (
        jnp.einsum(
            "gqc,cd->gqd", mixed_values, attention_output, preferred_element_type=jnp.float32
        )
        + vector_weight[10]
    )
    block_out = ((resid + output_rows.reshape(images.shape)) * mask).astype(jnp.bfloat16)
    grad_top = cotangent.astype(jnp.float32) * mask
    grad_proj = grad_top.reshape(batch, queries, channels)
    grad_proj_low = grad_proj.astype(jnp.bfloat16)
    grad_out_weight = jnp.einsum(
        "gqc,gqd->cd", mixed_values, grad_proj_low, preferred_element_type=jnp.float32
    )
    grad_mixed = jnp.einsum(
        "gqd,cd->gqc", grad_proj_low, attention_output, preferred_element_type=jnp.float32
    ).astype(jnp.bfloat16)
    back_keys, back_values = (
        lax.all_gather(key_low, "band", axis=1, tiled=True),
        lax.all_gather(value_low, "band", axis=1, tiled=True),
    )
    back_probs = attend(query_low, back_keys, key_valid, factor)[0]
    grad_probs = jnp.einsum(
        "gqc,gkc->gqk", grad_mixed, back_values, preferred_element_type=jnp.float32
    )
    weighted_sum = jnp.sum(back_probs * grad_probs, axis=2, keepdims=True)
    grad_scores = back_probs * (grad_probs - weighted_sum)
    grad_scores_low = (grad_scores * factor).astype(jnp.bfloat16)
    grad_query = jnp.einsum(
        "gqk,gkc->gqc", grad_scores_low, back_keys, preferred_element_type=jnp.float32
    ).astype(jnp.bfloat16)
    key_terms = jnp.einsum(
        "gqk,gqc->gkc", grad_scores_low, query_low, preferred_element_type=jnp.float32
    )
    value_terms = jnp.einsum(
        "gqk,gqc->gkc",
        back_probs.astype(jnp.bfloat16),
        grad_mixed,
        preferred_element_type=jnp.float32,
    )
    grad_key, grad_value = (
        lax.psum_scatter(
            key_terms.astype(jnp.bfloat16), "band", scatter_dimension=1, tiled=True
        ).astype(jnp.float32),
        lax.psum_scatter(
            value_terms.astype(jnp.bfloat16), "band", scatter_dimension=1, tiled=True
        ).astype(jnp.float32),
    )
    grad_value_low = grad_value.astype(jnp.bfloat16)
    grads_low = jnp.stack([grad_query, grad_key.astype(jnp.bfloat16), grad_value_low])
    grad_in_weights = jnp.einsum(
        "gqc,jgqd->jcd", normed, grads_low, preferred_element_type=jnp.float32
    )
    grad_normed = (
        jnp.einsum("jgqd,jcd->gqc", grads_low, attn_in, preferred_element_type=jnp.float32).reshape(
            images.shape
        )
        * mask
    )
    grad_resid_norm, grad_gain_three, grad_shift_three = normalize_back(
        resid, sums_three, mask, count, vector_weight[6], vector_weight[7], grad_normed
    )
    grad_resid = (grad_top + grad_resid_norm) * mask
    grad_act_two, grad_kernel_two = conv_backward(
        grad_resid.astype(jnp.bfloat16), kernel_two, padded_two
    )
    grad_norm_two = activate_back(norm_two, mask, grad_act_two)
    grad_conv_out, grad_gain_two, grad_shift_two = normalize_back(
        conv_out, sums_two, mask, count, vector_weight[3], vector_weight[4], grad_norm_two
    )
    grad_act_one, grad_kernel_one = conv_backward(
        grad_conv_out.astype(jnp.bfloat16), kernel_one, padded_one
    )
    grad_norm_one = activate_back(norm_one, mask, grad_act_one)
    grad_start, grad_gain_one, grad_shift_one = normalize_back(
        start, sums_one, mask, count, vector_weight[0], vector_weight[1], grad_norm_one
    )
    input_grad = (grad_resid + grad_start) * mask
    vector_terms = jnp.stack(
        [
            grad_gain_one,
            grad_shift_one,
            jnp.sum(grad_conv_out, axis=(0, 1, 2)),
            grad_gain_two,
            grad_shift_two,
            jnp.sum(grad_resid, axis=(0, 1, 2)),
            grad_gain_three,
            grad_shift_three,
            jnp.sum(grad_query, axis=(0, 1), dtype=jnp.float32),
            jnp.sum(grad_value_low, axis=(0, 1), dtype=jnp.float32),
            jnp.sum(grad_proj, axis=(0, 1)),
        ]
    )
    vector_grads = lax.psum(vector_terms, ("img", "band"))
    grad_flat = jnp.concatenate(
        [
            grad_kernel_one.reshape(-1),
            grad_kernel_two.reshape(-1),
            grad_in_weights.reshape(-1),
            grad_out_weight.reshape(-1),
        ]
    )
    matrix_grads = lax.psum_scatter(grad_flat, ("img", "band"), scatter_dimension=0, tiled=True)
    matrix_moments = MOMENTUM * matrix_momentum + matrix_grads
    matrix_masters = matrix_weight - LR_MATRIX * (matrix_grads + MOMENTUM * matrix_moments)
    matrix_means = AVERAGE * matrix_average + (1.0 - AVERAGE) * matrix_masters
    vector_moments = MOMENTUM * vector_momentum + vector_grads
    vector_masters = vector_weight - LR_VECTOR * (vector_grads + MOMENTUM * vector_moments)
    vector_means = AVERAGE * vector_average + (1.0 - AVERAGE) * vector_masters
    return (
        block_out,
        input_grad,
        matrix_grads,
        matrix_moments,
        matrix_means,
        matrix_masters,
        vector_grads,
        vector_moments,
        vector_means,
        vector_masters,
    )


F32 = jnp.float32
BF16 = jnp.bfloat16
SIDE = 32
VMEM_LIMIT = 58 * 1024 * 1024


def dot(a, b):
    return lax.dot_general(a, b, (((1,), (0,)), ((), ())), preferred_element_type=F32)


def dot_nt(a, b):
    return lax.dot_general(a, b, (((1,), (1,)), ((), ())), preferred_element_type=F32)


def dot_tn(a, b):
    return lax.dot_general(a, b, (((0,), (0,)), ((), ())), preferred_element_type=F32)


def call(body, outs, ins, scratch=(), flops=0, name=None, aliases=None):
    spaces = {"v": pl.BlockSpec(memory_space=pltpu.VMEM), "s": pl.BlockSpec(memory_space=pltpu.SMEM),
              "a": pl.BlockSpec(memory_space=pl.ANY)}
    return pl.pallas_call(
        body,
        out_shape=[o for o, _ in outs],
        in_specs=[spaces[s] for _, s in ins],
        out_specs=[spaces[s] for _, s in outs],
        scratch_shapes=list(scratch),
        input_output_aliases=aliases or {},
        compiler_params=pltpu.CompilerParams(vmem_limit_bytes=VMEM_LIMIT),
        cost_estimate=pl.CostEstimate(flops=flops, bytes_accessed=0, transcendentals=0),
        name=name,
    )(*[a for a, _ in ins])


def shape(dims, dtype):
    return jax.ShapeDtypeStruct(dims, dtype)


def fold(x):
    return jnp.sum(x.reshape(x.shape[0] // 8, 8, x.shape[1]), axis=0)


def group_total(x):
    lane = lax.broadcasted_iota(jnp.int32, x.shape, 1)
    width = x.shape[1]
    for s in (1, 2, 4, 8):
        up = pltpu.roll(x, width - s, 1)
        down = pltpu.roll(x, s, 1)
        x = x + jnp.where((lane & s) == 0, up, down)
    return x


def total_of(*parts):
    rows = [jnp.sum(p, axis=0, keepdims=True) for p in parts]
    pad = jnp.zeros((8 - len(rows), rows[0].shape[1]), F32)
    return jnp.concatenate(rows + [pad], axis=0)


def moments(s1, s2, size):
    count = (size * size * 16).astype(F32)
    both = group_total(total_of(s1, s2)) / count
    mean = both[0:1]
    spread = both[1:2] - mean * mean
    return mean, lax.rsqrt(spread + EPS)


def row_mask(size, channels):
    across = lax.broadcasted_iota(jnp.int32, (SIDE, channels), 0)
    inside = across < size
    return lambda h: inside & (h < size)


def sigmoid(y):
    return 0.5 * jnp.tanh(0.5 * y) + 0.5


def rows(h):
    return pl.ds(pl.multiple_of(h * SIDE, SIDE), SIDE)


def put_shifted(ref, h, r, forward):
    channels = r.shape[1]
    w = lax.broadcasted_iota(jnp.int32, r.shape, 0)
    before = jnp.where(w == 0, 0.0, pltpu.roll(r, 1, 0)).astype(BF16)
    after = jnp.where(w == SIDE - 1, 0.0, pltpu.roll(r, SIDE - 1, 0)).astype(BF16)
    first, last = (before, after) if forward else (after, before)
    at = pl.ds(pl.multiple_of((h + 1) * SIDE, SIDE), SIDE)
    ref[at, 0:channels] = first
    ref[at, channels : 2 * channels] = r.astype(BF16)
    ref[at, 2 * channels :] = last


def clear_border(ref):
    zero = jnp.zeros((SIDE, ref.shape[1]), BF16)
    ref[0:SIDE, :] = zero
    ref[(SIDE + 1) * SIDE :, :] = zero


def put_transposed(ref, src_ref, row0, lane0):
    channels, count = ref.shape
    for j in range(count // 256):
        block = src_ref[row0 + j * 256 : row0 + (j + 1) * 256, lane0 : lane0 + channels]
        ref[:, j * 256 : (j + 1) * 256] = block.T


def act_one_body(size_ref, img_ref, vec_ref, pad_ref, at_ref, stat_ref):
    size = size_ref[0]
    channels = img_ref.shape[1]
    mask = row_mask(size, channels)

    def sums(h, carry):
        x = jnp.where(mask(h), img_ref[rows(h), :].astype(F32), 0.0)
        return carry[0] + fold(x), carry[1] + fold(x * x)

    zero = jnp.zeros((8, channels), F32)
    s1, s2 = lax.fori_loop(0, SIDE, sums, (zero, zero), unroll=2)
    mean, scale = moments(s1, s2, size)
    stat_ref[0:1, :] = mean
    stat_ref[1:2, :] = scale
    stat_ref[2:8, :] = jnp.zeros((6, channels), F32)
    apply_norm(img_ref, mean, scale * vec_ref[0:1, :], vec_ref[1:2, :], mask, pad_ref)
    put_transposed(at_ref, pad_ref, SIDE, 0)


def apply_norm(src_ref, mean, scale, shift, mask, pad_ref):
    clear_border(pad_ref)

    def apply(h, carry):
        y = (src_ref[rows(h), :].astype(F32) - mean) * scale + shift
        at = pl.ds(pl.multiple_of((h + 1) * SIDE, SIDE), SIDE)
        pad_ref[at, :] = jnp.where(mask(h), y * sigmoid(y), 0.0).astype(BF16)
        return carry

    lax.fori_loop(0, SIDE, apply, 0, unroll=4)


def act_one(size, img, vec):
    n, c = img.shape
    return call(act_one_body,
        [(shape((n + 64, c), BF16), "v"), (shape((c, n), BF16), "v"), (shape((8, c), F32), "v")],
        [(size, "s"), (img, "v"), (vec, "v")], name="act_one")


MB = 256


def start_copies(src_ref, dst_ref, sems, parts, offset=0):
    length = dst_ref.shape[0] // parts
    copies = [
        pltpu.make_async_copy(src_ref.at[pl.ds(offset + p * length, length)], dst_ref.at[pl.ds(p * length, length)], sems.at[p])
        for p in range(parts)
    ]
    for copy in copies:
        copy.start()
    return copies


COLUMNS = (1, 0, 2)


def fetch_rows(at_ref, gathered, dst_ref, base, row, count, sem):
    heads, mine, other = gathered
    tail = mine.shape[1]
    head = heads.shape[0] // 32
    block = head + tail
    for owner in range(row // block, (row + count - 1) // block + 1):
        first = owner * block
        lo, hi = max(row, first), min(row + count, first + head)
        if lo < hi:
            inside = pl.ds(base + lo - row, hi - lo)
            pltpu.make_async_copy(heads.at[pl.ds(owner * head + lo - first, hi - lo)], dst_ref.at[inside], sem).start()
        lo, hi = max(row, first + head), min(row + count, first + block)
        if lo >= hi:
            continue
        inside = pl.ds(base + lo - row, hi - lo)
        z, x, y, c = at_ref[4] ^ (owner >> 3), at_ref[1] ^ ((owner >> 2) & 1), at_ref[2] ^ ((owner >> 1) & 1), owner & 1
        slot = jnp.where(z < 2, x * 4 + y * 2 + z, 6 + y * 4 + x * 2 + z)
        place = pl.ds(lo - first - head, hi - lo)
        for far, ref in enumerate((mine, other)):

            @pl.when((at_ref[3] ^ c) == far)
            def _(ref=ref, place=place, inside=inside, slot=slot):
                pltpu.make_async_copy(ref.at[slot, place], dst_ref.at[inside], sem).start()

    whole = dst_ref.at[pl.ds(base, count)]
    return pltpu.make_async_copy(whole, whole, sem)


def start_kernel(at_ref, gathered, dst_ref, sems, row):
    c = dst_ref.shape[1]
    copies = {}
    for dx in COLUMNS:
        for dy in range(3):
            tap = 3 * dy + dx
            copies[tap] = fetch_rows(at_ref, gathered, dst_ref, tap * c, row + tap * c, c, sems.at[tap])
    return copies


def conv(pad_ref, k_ref, copies, out_ref, mb, finish):
    n, c = out_ref.shape
    zero = jnp.zeros((8, c), F32)
    carry = (zero, zero)
    across = lax.broadcasted_iota(jnp.int32, (mb, c), 0) & (SIDE - 1)
    for dx in COLUMNS:
        for dy in range(3):
            copies[3 * dy + dx].wait()

        def block(m, carry, dx=dx):
            first = pl.multiple_of(m * mb, mb)
            at = pl.ds(first, mb)
            value = None
            for dy in range(3):
                tap = 3 * dy + dx
                term = dot(pad_ref[pl.ds(first + dy * SIDE, mb), :], k_ref[tap * c : (tap + 1) * c, :])
                value = term if value is None else value + term
            if dx == 0:
                value = jnp.where(across == 0, 0.0, pltpu.roll(value, 1, 0))
            if dx == 2:
                value = jnp.where(across == SIDE - 1, 0.0, pltpu.roll(value, mb - 1, 0))
            if dx != COLUMNS[0]:
                value = value + out_ref[at, :]
            if dx == COLUMNS[-1]:
                value, carry = finish(first, value, carry)
            out_ref[at, :] = value
            return carry

        carry = lax.fori_loop(0, n // mb, block, carry, unroll=4)
    return carry


def pixel_mask(size, first, count, c):
    place = lax.broadcasted_iota(jnp.int32, (count, c), 0) + first
    return ((place >> 5) < size) & ((place & (SIDE - 1)) < size)


def put_stats(stat_ref, mean, scale):
    stat_ref[...] = jnp.concatenate([mean, scale, jnp.zeros((6, mean.shape[1]), F32)], axis=0)


def pieces_of(row, count, half):
    found = []
    for spot in range(row // half, (row + count - 1) // half + 1):
        found.append((spot, max(row, spot * half), min(row + count, (spot + 1) * half)))
    return found


def send_rows(stage, base, row, count, at_ref, rounds, sem):
    half = rounds[-1][0].shape[1]
    for spot, lo, hi in pieces_of(row, count, half):
        owner, tail = spot // 2, spot % 2
        refs, inner = rounds[owner // 16], owner % 16
        z, x, y, c = inner // 8, (inner >> 2) & 1, (inner >> 1) & 1, inner & 1
        index = ((at_ref[1] ^ x) * 2 + (at_ref[2] ^ y)) * 2 + z
        source = stage.at[pl.ds(base + lo - row, hi - lo)]
        place = pl.ds(lo - spot * half, hi - lo)
        for other in range(2):

            @pl.when((at_ref[3] ^ c) == other)
            def _(ref=refs[2 * other + tail], source=source, place=place):
                pltpu.make_async_copy(source, ref.at[index, place], sem).start()

    return pltpu.make_async_copy(stage.at[pl.ds(base, count)], stage.at[pl.ds(base, count)], sem)


QB = 256
PB = 256


def forward_body(
    at_ref, pad_one_ref, vec_ref, heads_any, mine_any, other_any, img_any, cot_any,
    weights_any, conv_any, stat_two_ref, mixed_any, resid_any, grad_any, e3_any, vout_ref, *refs,
):
    high, low = refs[0:4], refs[4:8]
    (k_one, k_two, w_ref, img_ref, cot_ref, conv_ref, pad_ref, act_t, resid_ref, normed_ref, normed_t,
     q_ref, k_ref, v_ref, p_ref, ds_ref, mixed_ref, top_ref, gm_ref, gq_ref, gk_ref, gv_ref, grad_ref, e3_ref, gw_ref,
     one_sems, two_sems, w_sems, in_sems, out_sems, gw_sem, gk_sems) = refs[8:]
    n, c = normed_ref.shape
    size = at_ref[0]
    gathered = (heads_any, mine_any, other_any)
    one_copies = start_kernel(at_ref, gathered, k_one, one_sems, 0)
    img_copy = pltpu.make_async_copy(img_any, img_ref, in_sems.at[0])
    cot_copy = pltpu.make_async_copy(cot_any, cot_ref, in_sems.at[1])
    img_copy.start()
    two_copies = start_kernel(at_ref, gathered, k_two, two_sems, 9 * c)
    w_copies = [fetch_rows(at_ref, gathered, w_ref, j * c, (18 + j) * c, c, w_sems.at[j]) for j in range(4)]
    cot_copy.start()
    leaving = []

    def leave(src, dst):
        copy = pltpu.make_async_copy(src, dst, out_sems.at[len(leaving)])
        copy.start()
        leaving.append(copy)

    mask = row_mask(size, c)
    zero = jnp.zeros((8, c), F32)

    bias_one = vec_ref[2:3, :]

    def finish_one(first, v, carry):
        v = v + bias_one
        x = jnp.where(pixel_mask(size, first, MB, c), v, 0.0)
        return v, (carry[0] + fold(x), carry[1] + fold(x * x))

    s1, s2 = conv(pad_one_ref, k_one, one_copies, conv_ref, MB, finish_one)
    leave(conv_ref, conv_any)
    leave(k_one, weights_any.at[pl.ds(0, 9 * c)])
    kept_one = leaving[-1]
    mean, scale = moments(s1, s2, size)
    put_stats(stat_two_ref, mean, scale)
    apply_norm(conv_ref, mean, scale * vec_ref[3:4, :], vec_ref[4:5, :], mask, pad_ref)
    put_transposed(act_t, pad_ref, SIDE, 0)

    bias_two = vec_ref[5:6, :]
    img_copy.wait()

    def finish_two(first, v, carry):
        v = v + bias_two + img_ref[pl.ds(first, MB), :].astype(F32)
        x = jnp.where(pixel_mask(size, first, MB, c), v, 0.0)
        return x, (carry[0] + fold(x), carry[1] + fold(x * x))

    s1, s2 = conv(pad_ref, k_two, two_copies, resid_ref, MB, finish_two)
    leave(resid_ref, resid_any)
    leave(k_two, weights_any.at[pl.ds(9 * c, 9 * c)])
    mean, scale = moments(s1, s2, size)
    gain = vec_ref[6:7, :]
    full_gain, shift = scale * gain, vec_ref[7:8, :]
    cot_copy.wait()

    def apply(h, carry):
        y = (resid_ref[rows(h), :] - mean) * full_gain + shift
        normed_ref[rows(h), :] = jnp.where(mask(h), y, 0.0).astype(BF16)
        t = jnp.where(mask(h), cot_ref[rows(h), :].astype(F32), 0.0)
        top_ref[rows(h), :] = t.astype(BF16)
        return carry + fold(t)

    top_sum = lax.fori_loop(0, SIDE, apply, zero, unroll=4)
    put_transposed(normed_t, normed_ref, 0, 0)

    for copy in w_copies:
        copy.wait()
    leave(w_ref, weights_any.at[pl.ds(18 * c, 4 * c)])
    factor = c ** (-0.5)
    wq, wk, wv, wo = (functools.partial(lambda j: w_ref[j * c : (j + 1) * c, :], j) for j in range(4))
    qb, vb = vec_ref[8:9, :], vec_ref[9:10, :]
    def project(m, carry):
        at = pl.ds(pl.multiple_of(m * PB, PB), PB)
        x = normed_ref[at, :]
        q_ref[at, :] = (dot(x, wq()) + qb).astype(BF16)
        k_ref[at, :] = dot(x, wk()).astype(BF16)
        v_ref[at, :] = (dot(x, wv()) + vb).astype(BF16)
        gm_ref[at, :] = dot_nt(top_ref[at, :], wo()).astype(BF16)
        return carry

    lax.fori_loop(0, n // PB, project, 0, unroll=2)

    spot = lax.broadcasted_iota(jnp.int32, (1, n), 1)
    key_bias = jnp.where(((spot >> 5) < size) & ((spot & (SIDE - 1)) < size), 0.0, -1e30)

    def queries(m, carry):
        at = pl.ds(pl.multiple_of(m * QB, QB), QB)
        s = dot_nt(q_ref[at, :], k_ref[...]) * factor + key_bias
        raised = jnp.exp(s - jnp.max(s, axis=1, keepdims=True))
        p = raised * (1.0 / jnp.sum(raised, axis=1, keepdims=True))
        low_p = p.astype(BF16)
        p_ref[at, :] = low_p
        mixed_ref[at, :] = dot(low_p, v_ref[...]).astype(BF16)
        gp = dot_nt(gm_ref[at, :], v_ref[...])
        weighted = jnp.sum(p * gp, axis=1, keepdims=True)
        ds = (p * ((gp - weighted) * factor)).astype(BF16)
        ds_ref[at, :] = ds
        gq_ref[at, :] = dot(ds, k_ref[...]).astype(BF16)
        return carry

    lax.fori_loop(0, n // QB, queries, 0)
    leave(mixed_ref, mixed_any)

    def keys(m, carry):
        at = pl.ds(pl.multiple_of(m * QB, QB), QB)
        gk_ref[at, :] = dot_tn(ds_ref[:, at], q_ref[...]).astype(BF16)
        gv_ref[at, :] = dot_tn(p_ref[:, at], gm_ref[...]).astype(BF16)
        return carry

    lax.fori_loop(0, n // QB, keys, 0)
    gw_ref[0:c, :] = dot(normed_t[...], gq_ref[...]).astype(BF16)
    gw_ref[c : 2 * c, :] = dot(normed_t[...], gk_ref[...]).astype(BF16)
    gw_ref[2 * c : 3 * c, :] = dot(normed_t[...], gv_ref[...]).astype(BF16)
    gw_ref[3 * c : 4 * c, :] = dot_tn(mixed_ref[...], top_ref[...]).astype(BF16)
    waits = [send_rows(gw_ref, 0, 18 * c, 4 * c, at_ref, (None, high), gw_sem)]

    def normed_grad(m, carry):
        su, sux, sq, sv = carry
        first = pl.multiple_of(m * PB, PB)
        at = pl.ds(first, PB)
        gq, gk, gv = gq_ref[at, :], gk_ref[at, :], gv_ref[at, :]
        u = dot_nt(gq, wq()) + dot_nt(gk, wk()) + dot_nt(gv, wv())
        u = jnp.where(pixel_mask(size, first, PB, c), u, 0.0)
        grad_ref[at, :] = u
        xhat = (resid_ref[at, :] - mean) * scale
        return su + fold(u), sux + fold(u * xhat), sq + fold(gq.astype(F32)), sv + fold(gv.astype(F32))

    su, sux, sq, sv = lax.fori_loop(0, n // PB, normed_grad, (zero, zero, zero, zero), unroll=2)
    count = (size * size * 16).astype(F32)
    both = group_total(total_of(su, sux) * gain) / count
    m1, m2 = both[0:1], both[1:2]
    clear_border(e3_ref)

    def back(h, carry):
        xhat = (resid_ref[rows(h), :] - mean) * scale
        g = (grad_ref[rows(h), :] * gain - m1 - xhat * m2) * scale + top_ref[rows(h), :].astype(F32)
        g = jnp.where(mask(h), g, 0.0)
        grad_ref[rows(h), :] = g
        put_shifted(e3_ref, h, g.astype(BF16).astype(F32), False)
        return carry + fold(g)

    sg = lax.fori_loop(0, SIDE, back, zero, unroll=2)
    leave(e3_ref, e3_any)
    leave(grad_ref, grad_any)
    vout_ref[...] = total_of(sg, sux, su, sq, sv, top_sum)
    still = [v for v in leaving if v is not kept_one]
    kept_one.wait()
    waits += kernel_gradient(act_t, e3_ref, k_one, 9 * c, at_ref, (low, high), gk_sems)
    for wait in waits + still:
        wait.wait()


def forward(at, pad_one, vec, gathered, img, cot):
    n, c = img.shape
    heads, mine, other = gathered
    half = (shape((8, 22 * c // 64, c), BF16), "a")

    def low(*dims):
        return pltpu.VMEM(dims, BF16)

    full = low(n, c)
    found = call(forward_body,
        [(shape((22 * c, c), BF16), "a"), (shape((n, c), F32), "a"), (shape((8, c), F32), "v"), (shape((n, c), BF16), "a"), (shape((n, c), F32), "a"),
         (shape((n, c), F32), "a"), (shape((n + 2 * SIDE, 3 * c), BF16), "a"), (shape((8, c), F32), "v")] + [half] * 8,
        [(at, "s"), (pad_one, "v"), (vec, "v"), (heads, "a"), (mine, "a"), (other, "a"), (img, "a"), (cot, "a")],
        [low(9 * c, c), low(9 * c, c), low(4 * c, c), full, full, pltpu.VMEM((n, c), F32), low(n + 2 * SIDE, c), low(c, n),
         pltpu.VMEM((n, c), F32), full, low(c, n), full, full, full, low(n, n), low(n, n), full, full, full, full, full, full,
         pltpu.VMEM((n, c), F32), low(n + 2 * SIDE, 3 * c), low(4 * c, c),
         pltpu.SemaphoreType.DMA((9,)), pltpu.SemaphoreType.DMA((9,)), pltpu.SemaphoreType.DMA((4,)),
         pltpu.SemaphoreType.DMA((2,)), pltpu.SemaphoreType.DMA((8,)), pltpu.SemaphoreType.DMA, pltpu.SemaphoreType.DMA((9,))],
        name="forward")
    return found[:8], found[8:12], found[12:16]


def kernel_gradient(act_t, e3_ref, stage, row, at_ref, rounds, sems):
    c, n = act_t.shape

    def one_row(dy, carry):
        lo = pl.multiple_of((2 - dy) * SIDE, SIDE)
        for dx in range(3):
            value = dot(act_t[...], e3_ref[pl.ds(lo, n), dx * c : (dx + 1) * c])
            stage[pl.ds(pl.multiple_of((3 * dy + dx) * c, c), c), :] = value.astype(BF16)
        for now in range(3):

            @pl.when(dy == now)
            def _(now=now):
                send_rows(stage, 3 * now * c, row + 3 * now * c, 3 * c, at_ref, rounds, sems.at[now])

        return carry

    lax.fori_loop(0, 3, one_row, 0, unroll=1)
    places = [stage.at[pl.ds(3 * dy * c, 3 * c)] for dy in range(3)]
    return [pltpu.make_async_copy(place, place, sems.at[dy]) for dy, place in enumerate(places)]


def conv_back(e3_ref, k_ref, copies, out_ref):
    n, c = out_ref.shape
    for dy in range(3):
        copies[dy].wait()
        lo = (2 - dy) * SIDE

        def block(m, carry, dy=dy, lo=lo):
            first = pl.multiple_of(m * MB, MB)
            value = None
            for dx in range(3):
                tap = 3 * dy + dx
                term = dot_nt(e3_ref[pl.ds(first + lo, MB), dx * c : (dx + 1) * c], k_ref[tap * c : (tap + 1) * c, :])
                value = term if value is None else value + term
            if dy > 0:
                value = value + out_ref[pl.ds(first, MB), :]
            out_ref[pl.ds(first, MB), :] = value
            return carry

        lax.fori_loop(0, n // MB, block, 0, unroll=4)


def norm_back_sums(src_ref, g_ref, mean, scale, gain, shift, mask, size):
    c = g_ref.shape[1]

    def sums(h, carry):
        xhat = (src_ref[rows(h), :].astype(F32) - mean) * scale
        y = xhat * gain + shift
        s = sigmoid(y)
        u = jnp.where(mask(h), g_ref[rows(h), :] * (s * (1.0 + y * (1.0 - s))), 0.0)
        g_ref[rows(h), :] = u
        return carry[0] + fold(u), carry[1] + fold(u * xhat)

    zero = jnp.zeros((8, c), F32)
    su, sux = lax.fori_loop(0, SIDE, sums, (zero, zero), unroll=2)
    count = (size * size * 16).astype(F32)
    both = group_total(total_of(su, sux) * gain) / count
    return su, sux, both[0:1], both[1:2]


def back_two_body(
    at_ref, e3_ref, vec_ref, stat_ref, k_any, conv_any, act_any, i0, i1, i2, i3,
    e3_any, vout_ref, o0, o1, o2, o3, g_ref, conv_ref, act_t, e3_out, k_vmem, sems, in_sems, out_sem, gk_sems,
):
    n, c = conv_ref.shape
    copies = start_copies(k_any, k_vmem, sems, 3, 9 * c)
    conv_copy = pltpu.make_async_copy(conv_any, conv_ref, in_sems.at[0])
    act_copy = pltpu.make_async_copy(act_any, act_t, in_sems.at[1])
    conv_copy.start()
    act_copy.start()
    size = at_ref[0]
    mask = row_mask(size, c)
    conv_back(e3_ref, k_vmem, copies, g_ref)
    conv_copy.wait()
    mean, scale = stat_ref[0:1, :], stat_ref[1:2, :]
    gain, shift = vec_ref[3:4, :], vec_ref[4:5, :]
    su, sux, m1, m2 = norm_back_sums(conv_ref, g_ref, mean, scale, gain, shift, mask, size)
    clear_border(e3_out)

    def apply(h, carry):
        xhat = (conv_ref[rows(h), :] - mean) * scale
        g = jnp.where(mask(h), (g_ref[rows(h), :] * gain - m1 - xhat * m2) * scale, 0.0)
        put_shifted(e3_out, h, g.astype(BF16).astype(F32), False)
        return carry + fold(g)

    sg = lax.fori_loop(0, SIDE, apply, jnp.zeros((8, c), F32), unroll=2)
    leaving = pltpu.make_async_copy(e3_out, e3_any, out_sem)
    leaving.start()
    vout_ref[...] = total_of(sg, sux, su)
    act_copy.wait()
    for wait in kernel_gradient(act_t, e3_out, k_vmem, 0, at_ref, ((o0, o1, o2, o3),), gk_sems):
        wait.wait()
    leaving.wait()


def back_two(at, e3, weights, vec, conv_out, stat, act, low):
    n, c = conv_out.shape
    half = shape(low[0].shape, BF16)
    e3_out, vout, *low = call(back_two_body,
        [(shape((n + 64, 3 * c), BF16), "a"), (shape((8, c), F32), "v")] + [(half, "a")] * 4,
        [(at, "s"), (e3, "v"), (vec, "v"), (stat, "v"), (weights, "a"), (conv_out, "a"), (act, "a")] + [(v, "a") for v in low],
        [pltpu.VMEM((n, c), F32), pltpu.VMEM((n, c), F32), pltpu.VMEM((c, n), BF16), pltpu.VMEM((n + 64, 3 * c), BF16),
         pltpu.VMEM((9 * c, c), BF16), pltpu.SemaphoreType.DMA((3,)), pltpu.SemaphoreType.DMA((2,)), pltpu.SemaphoreType.DMA,
         pltpu.SemaphoreType.DMA((9,))],
        name="back_two", aliases={7 + i: 2 + i for i in range(4)})
    return e3_out, vout, low


def back_one_body(
    size_ref, e3_ref, k_ref, vec_ref, img_ref, stat_ref, grad_ref, mixed_any, resid_any, both_any, vout_ref,
    g_ref, out_ref, rows_ref, mixed_ref, resid_ref, wo_ref, k_vmem, sems, in_sems, out_sems,
):
    n, c = img_ref.shape
    copies = start_copies(k_ref, k_vmem, sems, 3)
    bands, quarter = both_any.shape[0], both_any.shape[2]
    later = [
        pltpu.make_async_copy(src, dst, in_sems.at[i])
        for i, (src, dst) in enumerate(((mixed_any, mixed_ref), (resid_any, resid_ref), (k_ref.at[pl.ds(21 * c, c)], wo_ref)))
    ]
    for copy in later:
        copy.start()
    leaving = []

    def leave(src_ref, which):
        for j in range(bands):
            copy = pltpu.make_async_copy(src_ref.at[pl.ds(j * quarter, quarter)], both_any.at[j, which], out_sems.at[len(leaving)])
            copy.start()
            leaving.append(copy)

    size = size_ref[0]
    mask = row_mask(size, c)
    conv_back(e3_ref, k_vmem, copies, g_ref)
    for copy in later:
        copy.wait()

    def block_rows(m, carry):
        first = pl.multiple_of(m * MB, MB)
        at = pl.ds(first, MB)
        value = dot(mixed_ref[at, :], wo_ref[...]) + vec_ref[10:11, :] + resid_ref[at, :]
        rows_ref[at, :] = jnp.where(pixel_mask(size, first, MB, c), value, 0.0).astype(BF16)
        return carry

    lax.fori_loop(0, n // MB, block_rows, 0)
    leave(rows_ref, 0)
    mean, scale = stat_ref[0:1, :], stat_ref[1:2, :]
    gain, shift = vec_ref[0:1, :], vec_ref[1:2, :]
    su, sux, m1, m2 = norm_back_sums(img_ref, g_ref, mean, scale, gain, shift, mask, size)

    def apply(h, carry):
        xhat = (img_ref[rows(h), :].astype(F32) - mean) * scale
        g = (g_ref[rows(h), :] * gain - m1 - xhat * m2) * scale + grad_ref[rows(h), :]
        out_ref[rows(h), :] = jnp.where(mask(h), g, 0.0).astype(out_ref.dtype)
        return carry

    lax.fori_loop(0, SIDE, apply, 0, unroll=2)
    leave(out_ref, 1)
    vout_ref[...] = total_of(sux, su)
    for copy in leaving:
        copy.wait()


def back_one(at, e3, weights, vec, img, stat, grad_resid, mixed, resid, bands):
    n, c = img.shape
    low, full = pltpu.VMEM((n, c), BF16), pltpu.VMEM((n, c), F32)
    return call(back_one_body, [(shape((bands, 2, n // bands, c), BF16), "a"), (shape((8, c), F32), "v")],
        [(at, "s"), (e3, "v"), (weights, "a"), (vec, "v"), (img, "v"), (stat, "v"), (grad_resid, "v"), (mixed, "a"), (resid, "a")],
        [full, low, low, low, full, pltpu.VMEM((c, c), BF16), pltpu.VMEM((9 * c, c), BF16), pltpu.SemaphoreType.DMA((3,)),
         pltpu.SemaphoreType.DMA((3,)), pltpu.SemaphoreType.DMA((2 * bands,))],
        name="back_one")


ALL = ("img", "band")
CORE = [(b, b ^ 1) for b in range(4)]
ACROSS_Y = [(b, b ^ 2) for b in range(4)]
ACROSS_X = [(i, i ^ 1) for i in range(8)]

def after(value, *earlier, flops=0):
    def body(*refs):
        pass

    anywhere = pl.BlockSpec(memory_space=pl.ANY)
    return pl.pallas_call(
        body,
        out_shape=shape(value.shape, value.dtype),
        in_specs=[anywhere] * (1 + len(earlier)),
        out_specs=anywhere,
        input_output_aliases={0: 0},
        cost_estimate=pl.CostEstimate(flops=flops, bytes_accessed=0, transcendentals=0),
        name="after",
    )(value, *earlier)


def wide(*parts):
    total = parts[0].astype(F32)
    for part in parts[1:]:
        total = total + part.astype(F32)
    return total


def chip_sends(arrays, *earlier):
    mine_a, mine_b, theirs_a, theirs_b = arrays
    half, c = mine_a.shape[1:]
    dims = (2, 2, 2, half, c)
    if earlier:
        theirs_a, theirs_b = after(theirs_a, *earlier), after(theirs_b, *earlier)
    got = [lax.ppermute(v, "band", CORE) for v in (theirs_a, theirs_b)]
    pair_a = (mine_a.reshape(dims), got[0].reshape(dims))
    pair_b = (mine_b.reshape(dims), got[1].reshape(dims))
    send_a = wide(*(v[1] for v in pair_a)).astype(BF16)
    send_b = wide(*(v[:, 1] for v in pair_b)).astype(BF16)
    return pair_a, pair_b, send_a, send_b


def plane_swap(send_a, send_b):
    return lax.ppermute(send_a, "img", ACROSS_X), lax.ppermute(send_b, "band", ACROSS_Y)


def plane_sends(pair_a, pair_b, got_a, got_b):
    next_a = wide(*(v[0, 1] for v in pair_a), got_a[1]).astype(BF16)
    next_b = wide(*(v[1, 0] for v in pair_b), got_b[1]).astype(BF16)
    kept_a = (*(v[0, 0] for v in pair_a), got_a[0])
    kept_b = (*(v[0, 0] for v in pair_b), got_b[0])
    return kept_a, kept_b, next_a, next_b


def plane_gather(own):
    z = [lax.ppermute(own, "img", [(i, i ^ (2 * step)) for i in range(8)]) for step in (1, 2, 3)]
    first, last = jnp.stack([own, z[0]]), jnp.stack([z[1], z[2]])
    first = jnp.concatenate([first, lax.ppermute(first, "band", ACROSS_Y)])
    last = jnp.concatenate([last, lax.ppermute(last, "img", ACROSS_X)])
    mine = jnp.concatenate([first, lax.ppermute(first, "img", ACROSS_X), last, lax.ppermute(last, "band", ACROSS_Y)])
    return mine, lax.ppermute(mine, "band", CORE)


def plane_sums(kept_a, kept_b, next_a, next_b, *earlier):
    last_a = lax.ppermute(next_a, "band", ACROSS_Y)
    last_b = lax.ppermute(next_b, "img", ACROSS_X)
    if earlier:
        last_a, last_b = after(last_a, *earlier), after(last_b, *earlier)
    return jnp.concatenate([wide(*kept_a, last_a), wide(*kept_b, last_b)], axis=1)


def owner_parts(low, high):
    z = lax.axis_index("img") // 2

    def block_of(plane):
        found = high[1]
        for at, block in ((2, high[0]), (1, low[1]), (0, low[0])):
            found = jnp.where(plane == at, block, found)
        return found

    sent = [block_of(z ^ step).astype(BF16) for step in (1, 2, 3)]
    got = [lax.ppermute(v, "img", [(i, i ^ (2 * step)) for i in range(8)]) for v, step in zip(sent, (1, 2, 3))]
    return [block_of(z)] + got, sent


def four_sum(v, axis, steps):
    a, b, c = (lax.ppermute(v, axis, [(i, i ^ step) for i in range(lax.axis_size(axis))]) for step in steps)
    return (v + a) + (b + c)


def whole_image(
    images,
    cotangent,
    sizes,
    matrix_weight,
    matrix_momentum,
    matrix_average,
    vector_weight,
    vector_momentum,
    vector_average,
):
    batch, height, width, c = images.shape
    n = width * width
    mine = lax.axis_index("band")
    place = lax.axis_index("img")
    at = jnp.stack([lax.dynamic_index_in_dim(sizes, mine, 0, False), place % 2, mine // 2, mine % 2, place // 2])

    def to_image(field):
        parts = field.reshape(batch, height * width, c)
        return lax.all_to_all(parts, "band", 0, 0, tiled=True).reshape(n, c)

    own = matrix_weight.astype(BF16).reshape(-1, c)
    head = 288
    gathered = (lax.all_gather(own[:head], ALL, axis=0, tiled=True), *plane_gather(own[head:]))
    img = to_image(images)
    cot = to_image(cotangent)
    pad_one, act_t, stat_one = act_one(at, img, vector_weight)
    (weights, conv_out, stat_two, mixed, resid, grad_resid, e3_two, v3), high, low = forward(
        at, pad_one, vector_weight, gathered, img, cot
    )
    high = chip_sends(high)
    e3_two = after(e3_two, high[2], high[3])
    swapped = plane_swap(high[2], high[3])
    e3_one, v2, low = back_two(at, e3_two, weights, vector_weight, conv_out, stat_two, act_t, low)
    low = chip_sends(low, *swapped)
    high = plane_sends(*high[:2], *swapped)
    low_sends = low[2:4]
    e3_one = after(e3_one, *low_sends)
    swapped = plane_swap(low[2], low[3])
    both, v1 = back_one(at, e3_one, weights, vector_weight, img, stat_one, grad_resid, mixed, resid, batch)
    vecs = jnp.stack([v1[0], v1[1], v2[0], v2[1], v2[2], v3[0], v3[1], v3[2], v3[3], v3[4], v3[5]])
    low = plane_sends(*low[:2], *(after(v, v1) for v in swapped))
    vecs = four_sum(after(vecs, low[2], low[3]), "img", (2, 4, 6))
    high = plane_sums(*high, low[2], low[3])
    low = plane_sums(*low, vecs)
    parts, sent = owner_parts(low, high)
    given = lax.all_to_all(after(both, *sent), "band", 0, 0, tiled=True)
    block_out = given[:, 0].reshape(images.shape)
    input_grad = given[:, 1].reshape(images.shape).astype(F32)
    vecs = after(vecs, parts[1])
    vecs = vecs + lax.ppermute(vecs, "img", ACROSS_X)
    vector_grads = four_sum(vecs, "band", (1, 2, 3))
    vector_moments = MOMENTUM * vector_momentum + vector_grads
    vector_masters = vector_weight - LR_VECTOR * (vector_grads + MOMENTUM * vector_moments)
    vector_means = AVERAGE * vector_average + (1.0 - AVERAGE) * vector_masters
    matrix_grads = wide(*parts).reshape(-1)
    matrix_moments = MOMENTUM * matrix_momentum + matrix_grads
    matrix_masters = matrix_weight - LR_MATRIX * (matrix_grads + MOMENTUM * matrix_moments)
    matrix_means = AVERAGE * matrix_average + (1.0 - AVERAGE) * matrix_masters
    return (
        block_out,
        input_grad,
        matrix_grads,
        matrix_moments,
        matrix_means,
        matrix_masters,
        vector_grads,
        vector_moments,
        vector_means,
        vector_masters,
    )


def solution(mesh):
    fits = mesh.shape["img"] == 8 and mesh.shape["band"] == 4

    def per_device(images, *rest):
        step = whole_image if fits and images.shape[:3] == (4, 8, SIDE) else banded
        return step(images, *rest)

    return jax.shard_map(
            per_device,
        mesh=mesh,
        in_specs=(
            P("img", "band", None, None),
            P("img", "band", None, None),
            P("img"),
            P(("img", "band")),
            P(("img", "band")),
            P(("img", "band")),
            P(),
            P(),
            P(),
        ),
        out_specs=(
            P("img", "band", None, None),
            P("img", "band", None, None),
            P(("img", "band")),
            P(("img", "band")),
            P(("img", "band")),
            P(("img", "band")),
            P(),
            P(),
            P(),
            P(),
        ),
        check_vma=False,
    )
```

```python
import functools

import jax
import jax.numpy as jnp
from jax import lax
from jax.experimental import pallas as pl
from jax.experimental.pallas import tpu as pltpu
from jax.sharding import PartitionSpec as P

GROUPS = 32


EPS = 1e-06
MOMENTUM = 0.9
LR_MATRIX = 4e-05
LR_VECTOR = 0.0001
AVERAGE = 0.75


def extended(array, sides, width):
    for axis, dim in sides:
        count, length = (lax.axis_size(axis), array.shape[dim])
        up = [(i, (i + 1) % count) for i in range(count - 1)]
        down = [(j, i) for i, j in up]
        last = lax.slice_in_dim(array, length - width, length, axis=dim)
        initial = lax.slice_in_dim(array, 0, width, axis=dim)
        before = lax.ppermute(last, axis, up)
        after = lax.ppermute(initial, axis, down)
        array = jnp.concatenate([before, array, after], axis=dim)
    return array


def split_groups(field):
    return field.reshape(field.shape[:3] + (GROUPS, field.shape[3] // GROUPS))


def group_sums(field, mask):
    shaped = split_groups(field)
    weighted = shaped * mask[..., None]
    return (jnp.sum(weighted, axis=(1, 2, 4)), jnp.sum(weighted * shaped, axis=(1, 2, 4)))


def group_apply(field, sums, count, gain, shift):
    center = sums[0] / count[:, None]
    spread = sums[1] / count[:, None] - center * center
    scale = lax.rsqrt(spread + EPS)
    shaped = split_groups(field)
    normed = (shaped - center[:, None, None, :, None]) * scale[:, None, None, :, None]
    return normed.reshape(field.shape) * gain + shift


def normalize(field, mask, count, gain, shift):
    sums = lax.psum(group_sums(field, mask), "band")
    return (group_apply(field, sums, count, gain, shift), sums)


def normalize_back(field, sums, mask, count, gain, shift, upstream):
    _, pull = jax.vjp(
        lambda field_in, sums_in, gain_in, shift_in: group_apply(
            field_in, sums_in, count, gain_in, shift_in
        ),
        field,
        sums,
        gain,
        shift,
    )
    direct, grad_sums, grad_gain, grad_shift = pull(upstream)
    grad_sums = lax.psum(grad_sums, "band")
    _, pull_sums = jax.vjp(lambda field_in: group_sums(field_in, mask), field)
    return (direct + pull_sums(grad_sums)[0], grad_gain, grad_shift)


def activate(field, mask):
    return jax.nn.silu(field) * mask


def activate_back(field, mask, upstream):
    _, pull = jax.vjp(lambda inner: activate(inner, mask), field)
    return pull(upstream)[0]


def widen(field):
    return jnp.pad(field, ((0, 0), (0, 0), (1, 1), (0, 0)))


def taps(padded, kernel, height, width):
    total = jnp.zeros(padded.shape[:1] + (height, width, kernel.shape[2]), jnp.float32)
    for tap in range(9):
        row, column = (tap // 3, tap % 3)
        total = total + jnp.einsum(
            "ghwc,cd->ghwd",
            padded[:, row : row + height, column : column + width],
            kernel[tap],
            preferred_element_type=jnp.float32,
        )
    return total


def conv_forward(low_field, kernel):
    padded = widen(extended(low_field, (("band", 1),), 1))
    return (taps(padded, kernel, low_field.shape[1], low_field.shape[2]), padded)


def conv_backward(low_grad, kernel, padded):
    height, width = (low_grad.shape[1], low_grad.shape[2])
    grad_pad = widen(extended(low_grad, (("band", 1),), 1))
    flipped = jnp.swapaxes(kernel[::-1], 1, 2)
    grad_in = taps(grad_pad, flipped, height, width)
    pieces = []
    for tap in range(9):
        row, column = (tap // 3, tap % 3)
        pieces.append(
            jnp.einsum(
                "ghwc,ghwd->cd",
                padded[:, row : row + height, column : column + width],
                low_grad,
                preferred_element_type=jnp.float32,
            )
        )
    return (grad_in, jnp.stack(pieces))


def attend(query_low, key_full, key_valid, factor):
    score_matrix = (
        jnp.einsum("gqc,gkc->gqk", query_low, key_full, preferred_element_type=jnp.float32) * factor
    )
    score_matrix = jnp.where(key_valid[:, None, :], score_matrix, -1e30)
    top = jnp.max(score_matrix, axis=2, keepdims=True)
    raised = jnp.exp(score_matrix - top)
    total = jnp.sum(raised, axis=2, keepdims=True)
    return (raised / total, top, total)


def banded(
    images,
    cotangent,
    sizes,
    matrix_weight,
    matrix_momentum,
    matrix_average,
    vector_weight,
    vector_momentum,
    vector_average,
):
    batch, height, width, channels = images.shape
    square = channels * channels
    queries = height * width
    positions = width * width
    factor = channels ** (-0.5)
    weights = lax.all_gather(
        matrix_weight.astype(jnp.bfloat16), ("img", "band"), axis=0, tiled=True
    )
    kernel_one = weights[: 9 * square].reshape(9, channels, channels)
    kernel_two = weights[9 * square : 18 * square].reshape(9, channels, channels)
    attn_in = weights[18 * square : 21 * square].reshape(3, channels, channels)
    attention_output = weights[21 * square :].reshape(channels, channels)
    lines = lax.axis_index("band") * height + jnp.arange(height)
    across = jnp.arange(width)
    limit = sizes[:, None, None]
    inside = (lines[None, :, None] < limit) & (across[None, None, :] < limit)
    mask = jnp.where(inside, 1.0, 0.0).astype(jnp.float32)[..., None]
    count = (sizes * sizes * (channels // GROUPS)).astype(jnp.float32)
    spots = jnp.arange(positions)
    key_valid = ((spots // width)[None, :] < sizes[:, None]) & (
        (spots % width)[None, :] < sizes[:, None]
    )
    start = images.astype(jnp.float32) * mask
    norm_one, sums_one = normalize(start, mask, count, vector_weight[0], vector_weight[1])
    act_one = activate(norm_one, mask).astype(jnp.bfloat16)
    conv_raw, padded_one = conv_forward(act_one, kernel_one)
    conv_out = conv_raw + vector_weight[2]
    norm_two, sums_two = normalize(conv_out, mask, count, vector_weight[3], vector_weight[4])
    act_two = activate(norm_two, mask).astype(jnp.bfloat16)
    conv_raw, padded_two = conv_forward(act_two, kernel_two)
    resid = (start + conv_raw + vector_weight[5]) * mask
    norm_three, sums_three = normalize(resid, mask, count, vector_weight[6], vector_weight[7])
    normed = (norm_three * mask).astype(jnp.bfloat16).reshape(batch, queries, channels)
    projected = jnp.einsum("gqc,jcd->jgqd", normed, attn_in, preferred_element_type=jnp.float32)
    query_low = (projected[0] + vector_weight[8]).astype(jnp.bfloat16)
    key_low = projected[1].astype(jnp.bfloat16)
    value_low = (projected[2] + vector_weight[9]).astype(jnp.bfloat16)
    key_full, value_full = (
        lax.all_gather(key_low, "band", axis=1, tiled=True),
        lax.all_gather(value_low, "band", axis=1, tiled=True),
    )
    probability_rows, row_top, row_total = attend(query_low, key_full, key_valid, factor)
    mixed_values = jnp.einsum(
        "gqk,gkc->gqc",
        probability_rows.astype(jnp.bfloat16),
        value_full,
        preferred_element_type=jnp.float32,
    ).astype(jnp.bfloat16)
    output_rows = (
        jnp.einsum(
            "gqc,cd->gqd", mixed_values, attention_output, preferred_element_type=jnp.float32
        )
        + vector_weight[10]
    )
    block_out = ((resid + output_rows.reshape(images.shape)) * mask).astype(jnp.bfloat16)
    grad_top = cotangent.astype(jnp.float32) * mask
    grad_proj = grad_top.reshape(batch, queries, channels)
    grad_proj_low = grad_proj.astype(jnp.bfloat16)
    grad_out_weight = jnp.einsum(
        "gqc,gqd->cd", mixed_values, grad_proj_low, preferred_element_type=jnp.float32
    )
    grad_mixed = jnp.einsum(
        "gqd,cd->gqc", grad_proj_low, attention_output, preferred_element_type=jnp.float32
    ).astype(jnp.bfloat16)
    back_keys, back_values = (
        lax.all_gather(key_low, "band", axis=1, tiled=True),
        lax.all_gather(value_low, "band", axis=1, tiled=True),
    )
    back_probs = attend(query_low, back_keys, key_valid, factor)[0]
    grad_probs = jnp.einsum(
        "gqc,gkc->gqk", grad_mixed, back_values, preferred_element_type=jnp.float32
    )
    weighted_sum = jnp.sum(back_probs * grad_probs, axis=2, keepdims=True)
    grad_scores = back_probs * (grad_probs - weighted_sum)
    grad_scores_low = (grad_scores * factor).astype(jnp.bfloat16)
    grad_query = jnp.einsum(
        "gqk,gkc->gqc", grad_scores_low, back_keys, preferred_element_type=jnp.float32
    ).astype(jnp.bfloat16)
    key_terms = jnp.einsum(
        "gqk,gqc->gkc", grad_scores_low, query_low, preferred_element_type=jnp.float32
    )
    value_terms = jnp.einsum(
        "gqk,gqc->gkc",
        back_probs.astype(jnp.bfloat16),
        grad_mixed,
        preferred_element_type=jnp.float32,
    )
    grad_key, grad_value = (
        lax.psum_scatter(
            key_terms.astype(jnp.bfloat16), "band", scatter_dimension=1, tiled=True
        ).astype(jnp.float32),
        lax.psum_scatter(
            value_terms.astype(jnp.bfloat16), "band", scatter_dimension=1, tiled=True
        ).astype(jnp.float32),
    )
    grad_value_low = grad_value.astype(jnp.bfloat16)
    grads_low = jnp.stack([grad_query, grad_key.astype(jnp.bfloat16), grad_value_low])
    grad_in_weights = jnp.einsum(
        "gqc,jgqd->jcd", normed, grads_low, preferred_element_type=jnp.float32
    )
    grad_normed = (
        jnp.einsum("jgqd,jcd->gqc", grads_low, attn_in, preferred_element_type=jnp.float32).reshape(
            images.shape
        )
        * mask
    )
    grad_resid_norm, grad_gain_three, grad_shift_three = normalize_back(
        resid, sums_three, mask, count, vector_weight[6], vector_weight[7], grad_normed
    )
    grad_resid = (grad_top + grad_resid_norm) * mask
    grad_act_two, grad_kernel_two = conv_backward(
        grad_resid.astype(jnp.bfloat16), kernel_two, padded_two
    )
    grad_norm_two = activate_back(norm_two, mask, grad_act_two)
    grad_conv_out, grad_gain_two, grad_shift_two = normalize_back(
        conv_out, sums_two, mask, count, vector_weight[3], vector_weight[4], grad_norm_two
    )
    grad_act_one, grad_kernel_one = conv_backward(
        grad_conv_out.astype(jnp.bfloat16), kernel_one, padded_one
    )
    grad_norm_one = activate_back(norm_one, mask, grad_act_one)
    grad_start, grad_gain_one, grad_shift_one = normalize_back(
        start, sums_one, mask, count, vector_weight[0], vector_weight[1], grad_norm_one
    )
    input_grad = (grad_resid + grad_start) * mask
    vector_terms = jnp.stack(
        [
            grad_gain_one,
            grad_shift_one,
            jnp.sum(grad_conv_out, axis=(0, 1, 2)),
            grad_gain_two,
            grad_shift_two,
            jnp.sum(grad_resid, axis=(0, 1, 2)),
            grad_gain_three,
            grad_shift_three,
            jnp.sum(grad_query, axis=(0, 1), dtype=jnp.float32),
            jnp.sum(grad_value_low, axis=(0, 1), dtype=jnp.float32),
            jnp.sum(grad_proj, axis=(0, 1)),
        ]
    )
    vector_grads = lax.psum(vector_terms, ("img", "band"))
    grad_flat = jnp.concatenate(
        [
            grad_kernel_one.reshape(-1),
            grad_kernel_two.reshape(-1),
            grad_in_weights.reshape(-1),
            grad_out_weight.reshape(-1),
        ]
    )
    matrix_grads = lax.psum_scatter(grad_flat, ("img", "band"), scatter_dimension=0, tiled=True)
    matrix_moments = MOMENTUM * matrix_momentum + matrix_grads
    matrix_masters = matrix_weight - LR_MATRIX * (matrix_grads + MOMENTUM * matrix_moments)
    matrix_means = AVERAGE * matrix_average + (1.0 - AVERAGE) * matrix_masters
    vector_moments = MOMENTUM * vector_momentum + vector_grads
    vector_masters = vector_weight - LR_VECTOR * (vector_grads + MOMENTUM * vector_moments)
    vector_means = AVERAGE * vector_average + (1.0 - AVERAGE) * vector_masters
    return (
        block_out,
        input_grad,
        matrix_grads,
        matrix_moments,
        matrix_means,
        matrix_masters,
        vector_grads,
        vector_moments,
        vector_means,
        vector_masters,
    )


F32 = jnp.float32
BF16 = jnp.bfloat16
SIDE = 32
VMEM_LIMIT = 58 * 1024 * 1024


def dot(a, b):
    return lax.dot_general(a, b, (((1,), (0,)), ((), ())), preferred_element_type=F32)


def dot_nt(a, b):
    return lax.dot_general(a, b, (((1,), (1,)), ((), ())), preferred_element_type=F32)


def dot_tn(a, b):
    return lax.dot_general(a, b, (((0,), (0,)), ((), ())), preferred_element_type=F32)


def call(body, outs, ins, scratch=(), flops=0, name=None, aliases=None, vmem=VMEM_LIMIT):
    spaces = {"v": pl.BlockSpec(memory_space=pltpu.VMEM), "s": pl.BlockSpec(memory_space=pltpu.SMEM),
              "a": pl.BlockSpec(memory_space=pl.ANY)}
    return pl.pallas_call(
        body,
        out_shape=[o for o, _ in outs],
        in_specs=[spaces[s] for _, s in ins],
        out_specs=[spaces[s] for _, s in outs],
        scratch_shapes=list(scratch),
        input_output_aliases=aliases or {},
        compiler_params=pltpu.CompilerParams(vmem_limit_bytes=vmem),
        cost_estimate=pl.CostEstimate(flops=flops, bytes_accessed=0, transcendentals=0),
        name=name,
    )(*[a for a, _ in ins])


def shape(dims, dtype):
    return jax.ShapeDtypeStruct(dims, dtype)


def fold(x):
    return jnp.sum(x.reshape(x.shape[0] // 8, 8, x.shape[1]), axis=0)


def group_total(x):
    lane = lax.broadcasted_iota(jnp.int32, x.shape, 1)
    width = x.shape[1]
    for s in (1, 2, 4, 8):
        up = pltpu.roll(x, width - s, 1)
        down = pltpu.roll(x, s, 1)
        x = x + jnp.where((lane & s) == 0, up, down)
    return x


def total_of(*parts):
    rows = [jnp.sum(p, axis=0, keepdims=True) for p in parts]
    pad = jnp.zeros((8 - len(rows), rows[0].shape[1]), F32)
    return jnp.concatenate(rows + [pad], axis=0)


def moments(s1, s2, size):
    count = (size * size * 16).astype(F32)
    both = group_total(total_of(s1, s2)) / count
    mean = both[0:1]
    spread = both[1:2] - mean * mean
    return mean, lax.rsqrt(spread + EPS)


def row_mask(size, channels):
    across = lax.broadcasted_iota(jnp.int32, (SIDE, channels), 0)
    inside = across < size
    return lambda h: inside & (h < size)


def sigmoid(y):
    return 0.5 * jnp.tanh(0.5 * y) + 0.5


def rows(h):
    return pl.ds(pl.multiple_of(h * SIDE, SIDE), SIDE)


def put_shifted(ref, h, r, forward):
    channels = r.shape[1]
    w = lax.broadcasted_iota(jnp.int32, r.shape, 0)
    before = jnp.where(w == 0, 0.0, pltpu.roll(r, 1, 0)).astype(BF16)
    after = jnp.where(w == SIDE - 1, 0.0, pltpu.roll(r, SIDE - 1, 0)).astype(BF16)
    first, last = (before, after) if forward else (after, before)
    at = pl.ds(pl.multiple_of((h + 1) * SIDE, SIDE), SIDE)
    ref[at, 0:channels] = first
    ref[at, channels : 2 * channels] = r.astype(BF16)
    ref[at, 2 * channels :] = last


def clear_border(ref):
    zero = jnp.zeros((SIDE, ref.shape[1]), BF16)
    ref[0:SIDE, :] = zero
    ref[(SIDE + 1) * SIDE :, :] = zero


def put_transposed(ref, src_ref, row0, lane0):
    channels, count = ref.shape
    for j in range(count // 256):
        block = src_ref[row0 + j * 256 : row0 + (j + 1) * 256, lane0 : lane0 + channels]
        ref[:, j * 256 : (j + 1) * 256] = block.T


def act_one_body(size_ref, img_ref, vec_ref, pad_ref, at_ref, stat_ref):
    size = size_ref[0]
    channels = img_ref.shape[1]
    mask = row_mask(size, channels)

    def sums(h, carry):
        x = jnp.where(mask(h), img_ref[rows(h), :].astype(F32), 0.0)
        return carry[0] + fold(x), carry[1] + fold(x * x)

    zero = jnp.zeros((8, channels), F32)
    s1, s2 = lax.fori_loop(0, SIDE, sums, (zero, zero), unroll=2)
    mean, scale = moments(s1, s2, size)
    stat_ref[0:1, :] = mean
    stat_ref[1:2, :] = scale
    stat_ref[2:8, :] = jnp.zeros((6, channels), F32)
    apply_norm(img_ref, mean, scale * vec_ref[0:1, :], vec_ref[1:2, :], mask, pad_ref)
    put_transposed(at_ref, pad_ref, SIDE, 0)


def apply_norm(src_ref, mean, scale, shift, mask, pad_ref):
    clear_border(pad_ref)

    def apply(h, carry):
        y = (src_ref[rows(h), :].astype(F32) - mean) * scale + shift
        at = pl.ds(pl.multiple_of((h + 1) * SIDE, SIDE), SIDE)
        pad_ref[at, :] = jnp.where(mask(h), y * sigmoid(y), 0.0).astype(BF16)
        return carry

    lax.fori_loop(0, SIDE, apply, 0, unroll=4)


def act_one(size, img, vec):
    n, c = img.shape
    return call(act_one_body,
        [(shape((n + 64, c), BF16), "v"), (shape((c, n), BF16), "v"), (shape((8, c), F32), "v")],
        [(size, "s"), (img, "v"), (vec, "v")], name="act_one")


MB = 256


def start_copies(src_ref, dst_ref, sems, parts, offset=0):
    length = dst_ref.shape[0] // parts
    copies = [
        pltpu.make_async_copy(src_ref.at[pl.ds(offset + p * length, length)], dst_ref.at[pl.ds(p * length, length)], sems.at[p])
        for p in range(parts)
    ]
    for copy in copies:
        copy.start()
    return copies


COLUMNS = (1, 0, 2)


def fetch_rows(at_ref, gathered, dst_ref, base, row, count, sem):
    heads, mine, other = gathered
    tail = mine.shape[1]
    head = heads.shape[0] // 32
    block = head + tail
    for owner in range(row // block, (row + count - 1) // block + 1):
        first = owner * block
        lo, hi = max(row, first), min(row + count, first + head)
        if lo < hi:
            inside = pl.ds(base + lo - row, hi - lo)
            pltpu.make_async_copy(heads.at[pl.ds(owner * head + lo - first, hi - lo)], dst_ref.at[inside], sem).start()
        lo, hi = max(row, first + head), min(row + count, first + block)
        if lo >= hi:
            continue
        inside = pl.ds(base + lo - row, hi - lo)
        z, x, y, c = at_ref[4] ^ (owner >> 3), at_ref[1] ^ ((owner >> 2) & 1), at_ref[2] ^ ((owner >> 1) & 1), owner & 1
        slot = jnp.where(z < 2, x * 4 + y * 2 + z, 6 + y * 4 + x * 2 + z)
        place = pl.ds(lo - first - head, hi - lo)
        for far, ref in enumerate((mine, other)):

            @pl.when((at_ref[3] ^ c) == far)
            def _(ref=ref, place=place, inside=inside, slot=slot):
                pltpu.make_async_copy(ref.at[slot, place], dst_ref.at[inside], sem).start()

    whole = dst_ref.at[pl.ds(base, count)]
    return pltpu.make_async_copy(whole, whole, sem)


def start_kernel(at_ref, gathered, dst_ref, sems, row):
    c = dst_ref.shape[1]
    copies = {}
    for dx in COLUMNS:
        for dy in range(3):
            tap = 3 * dy + dx
            copies[tap] = fetch_rows(at_ref, gathered, dst_ref, tap * c, row + tap * c, c, sems.at[tap])
    return copies


def conv(pad_ref, k_ref, copies, out_ref, mb, finish):
    n, c = out_ref.shape
    zero = jnp.zeros((8, c), F32)
    carry = (zero, zero)
    across = lax.broadcasted_iota(jnp.int32, (mb, c), 0) & (SIDE - 1)
    for dx in COLUMNS:
        for dy in range(3):
            copies[3 * dy + dx].wait()

        def block(m, carry, dx=dx):
            first = pl.multiple_of(m * mb, mb)
            at = pl.ds(first, mb)
            value = None
            for dy in range(3):
                tap = 3 * dy + dx
                term = dot(pad_ref[pl.ds(first + dy * SIDE, mb), :], k_ref[tap * c : (tap + 1) * c, :])
                value = term if value is None else value + term
            if dx == 0:
                value = jnp.where(across == 0, 0.0, pltpu.roll(value, 1, 0))
            if dx == 2:
                value = jnp.where(across == SIDE - 1, 0.0, pltpu.roll(value, mb - 1, 0))
            if dx != COLUMNS[0]:
                value = value + out_ref[at, :]
            if dx == COLUMNS[-1]:
                value, carry = finish(first, value, carry)
            out_ref[at, :] = value
            return carry

        carry = lax.fori_loop(0, n // mb, block, carry, unroll=4)
    return carry


def pixel_mask(size, first, count, c):
    place = lax.broadcasted_iota(jnp.int32, (count, c), 0) + first
    return ((place >> 5) < size) & ((place & (SIDE - 1)) < size)


def put_stats(stat_ref, mean, scale):
    stat_ref[...] = jnp.concatenate([mean, scale, jnp.zeros((6, mean.shape[1]), F32)], axis=0)


def pieces_of(row, count, half):
    found = []
    for spot in range(row // half, (row + count - 1) // half + 1):
        found.append((spot, max(row, spot * half), min(row + count, (spot + 1) * half)))
    return found


def send_rows(stage, base, row, count, at_ref, rounds, sem):
    half = rounds[-1][0].shape[1]
    for spot, lo, hi in pieces_of(row, count, half):
        owner, tail = spot // 2, spot % 2
        refs, inner = rounds[owner // 16], owner % 16
        z, x, y, c = inner // 8, (inner >> 2) & 1, (inner >> 1) & 1, inner & 1
        index = ((at_ref[1] ^ x) * 2 + (at_ref[2] ^ y)) * 2 + z
        source = stage.at[pl.ds(base + lo - row, hi - lo)]
        place = pl.ds(lo - spot * half, hi - lo)
        for other in range(2):

            @pl.when((at_ref[3] ^ c) == other)
            def _(ref=refs[2 * other + tail], source=source, place=place):
                pltpu.make_async_copy(source, ref.at[index, place], sem).start()

    return pltpu.make_async_copy(stage.at[pl.ds(base, count)], stage.at[pl.ds(base, count)], sem)


QB = 1024
PB = 512


def forward_body(
    at_ref, pad_one_ref, vec_ref, heads_any, mine_any, other_any, img_any, cot_any,
    weights_any, conv_any, stat_two_ref, mixed_any, resid_any, grad_any, e3_any, vout_ref, *refs,
):
    high, low = refs[0:4], refs[4:8]
    (k_one, k_two, w_ref, img_ref, cot_ref, conv_ref, pad_ref, act_t, resid_ref, normed_ref, normed_t,
     q_ref, k_ref, v_ref, p_ref, ds_ref, mixed_ref, top_ref, gm_ref, gq_ref, gk_ref, gv_ref, grad_ref, e3_ref, gw_ref,
     one_sems, two_sems, w_sems, in_sems, out_sems, gw_sem, gk_sems) = refs[8:]
    n, c = normed_ref.shape
    size = at_ref[0]
    gathered = (heads_any, mine_any, other_any)
    one_copies = start_kernel(at_ref, gathered, k_one, one_sems, 0)
    img_copy = pltpu.make_async_copy(img_any, img_ref, in_sems.at[0])
    cot_copy = pltpu.make_async_copy(cot_any, cot_ref, in_sems.at[1])
    img_copy.start()
    two_copies = start_kernel(at_ref, gathered, k_two, two_sems, 9 * c)
    w_copies = [fetch_rows(at_ref, gathered, w_ref, j * c, (18 + j) * c, c, w_sems.at[j]) for j in range(4)]
    cot_copy.start()
    leaving = []

    def leave(src, dst):
        copy = pltpu.make_async_copy(src, dst, out_sems.at[len(leaving)])
        copy.start()
        leaving.append(copy)

    mask = row_mask(size, c)
    zero = jnp.zeros((8, c), F32)

    bias_one = vec_ref[2:3, :]

    def finish_one(first, v, carry):
        v = v + bias_one
        x = jnp.where(pixel_mask(size, first, MB, c), v, 0.0)
        return v, (carry[0] + fold(x), carry[1] + fold(x * x))

    s1, s2 = conv(pad_one_ref, k_one, one_copies, conv_ref, MB, finish_one)
    leave(conv_ref, conv_any)
    leave(k_one, weights_any.at[pl.ds(0, 9 * c)])
    kept_one = leaving[-1]
    mean, scale = moments(s1, s2, size)
    put_stats(stat_two_ref, mean, scale)
    apply_norm(conv_ref, mean, scale * vec_ref[3:4, :], vec_ref[4:5, :], mask, pad_ref)
    put_transposed(act_t, pad_ref, SIDE, 0)

    bias_two = vec_ref[5:6, :]
    img_copy.wait()

    def finish_two(first, v, carry):
        v = v + bias_two + img_ref[pl.ds(first, MB), :].astype(F32)
        x = jnp.where(pixel_mask(size, first, MB, c), v, 0.0)
        return x, (carry[0] + fold(x), carry[1] + fold(x * x))

    s1, s2 = conv(pad_ref, k_two, two_copies, resid_ref, MB, finish_two)
    leave(resid_ref, resid_any)
    leave(k_two, weights_any.at[pl.ds(9 * c, 9 * c)])
    mean, scale = moments(s1, s2, size)
    gain = vec_ref[6:7, :]
    full_gain, shift = scale * gain, vec_ref[7:8, :]
    cot_copy.wait()

    def apply(h, carry):
        y = (resid_ref[rows(h), :] - mean) * full_gain + shift
        normed_ref[rows(h), :] = jnp.where(mask(h), y, 0.0).astype(BF16)
        t = jnp.where(mask(h), cot_ref[rows(h), :].astype(F32), 0.0)
        top_ref[rows(h), :] = t.astype(BF16)
        return carry + fold(t)

    top_sum = lax.fori_loop(0, SIDE, apply, zero, unroll=4)
    put_transposed(normed_t, normed_ref, 0, 0)

    for copy in w_copies:
        copy.wait()
    leave(w_ref, weights_any.at[pl.ds(18 * c, 4 * c)])
    factor = c ** (-0.5)
    wq, wk, wv, wo = (functools.partial(lambda j: w_ref[j * c : (j + 1) * c, :], j) for j in range(4))
    qb, vb = vec_ref[8:9, :], vec_ref[9:10, :]
    def project(m, carry):
        at = pl.ds(pl.multiple_of(m * PB, PB), PB)
        x = normed_ref[at, :]
        q_ref[at, :] = (dot(x, wq()) + qb).astype(BF16)
        k_ref[at, :] = dot(x, wk()).astype(BF16)
        v_ref[at, :] = (dot(x, wv()) + vb).astype(BF16)
        gm_ref[at, :] = dot_nt(top_ref[at, :], wo()).astype(BF16)
        return carry

    lax.fori_loop(0, n // PB, project, 0, unroll=2)

    spot = lax.broadcasted_iota(jnp.int32, (1, n), 1)
    key_bias = jnp.where(((spot >> 5) < size) & ((spot & (SIDE - 1)) < size), 0.0, -1e30)

    def queries(m, carry):
        at = pl.ds(pl.multiple_of(m * QB, QB), QB)
        s = dot_nt(q_ref[at, :], k_ref[...]) * factor + key_bias
        raised = jnp.exp(s - jnp.max(s, axis=1, keepdims=True))
        p = raised * (1.0 / jnp.sum(raised, axis=1, keepdims=True))
        low_p = p.astype(BF16)
        p_ref[at, :] = low_p
        mixed_ref[at, :] = dot(low_p, v_ref[...]).astype(BF16)
        gp = dot_nt(gm_ref[at, :], v_ref[...])
        weighted = jnp.sum(p * gp, axis=1, keepdims=True)
        ds = (p * ((gp - weighted) * factor)).astype(BF16)
        ds_ref[at, :] = ds
        gq_ref[at, :] = dot(ds, k_ref[...]).astype(BF16)
        return carry

    lax.fori_loop(0, n // QB, queries, 0)
    leave(mixed_ref, mixed_any)

    def keys(m, carry):
        at = pl.ds(pl.multiple_of(m * QB, QB), QB)
        gk_ref[at, :] = dot_tn(ds_ref[:, at], q_ref[...]).astype(BF16)
        gv_ref[at, :] = dot_tn(p_ref[:, at], gm_ref[...]).astype(BF16)
        return carry

    lax.fori_loop(0, n // QB, keys, 0)
    gw_ref[0:c, :] = dot(normed_t[...], gq_ref[...]).astype(BF16)
    gw_ref[c : 2 * c, :] = dot(normed_t[...], gk_ref[...]).astype(BF16)
    gw_ref[2 * c : 3 * c, :] = dot(normed_t[...], gv_ref[...]).astype(BF16)
    gw_ref[3 * c : 4 * c, :] = dot_tn(mixed_ref[...], top_ref[...]).astype(BF16)
    waits = [send_rows(gw_ref, 0, 18 * c, 4 * c, at_ref, (None, high), gw_sem)]

    def normed_grad(m, carry):
        su, sux, sq, sv = carry
        first = pl.multiple_of(m * PB, PB)
        at = pl.ds(first, PB)
        gq, gk, gv = gq_ref[at, :], gk_ref[at, :], gv_ref[at, :]
        u = dot_nt(gq, wq()) + dot_nt(gk, wk()) + dot_nt(gv, wv())
        u = jnp.where(pixel_mask(size, first, PB, c), u, 0.0)
        grad_ref[at, :] = u
        xhat = (resid_ref[at, :] - mean) * scale
        return su + fold(u), sux + fold(u * xhat), sq + fold(gq.astype(F32)), sv + fold(gv.astype(F32))

    su, sux, sq, sv = lax.fori_loop(0, n // PB, normed_grad, (zero, zero, zero, zero), unroll=2)
    count = (size * size * 16).astype(F32)
    both = group_total(total_of(su, sux) * gain) / count
    m1, m2 = both[0:1], both[1:2]
    clear_border(e3_ref)

    def back(h, carry):
        xhat = (resid_ref[rows(h), :] - mean) * scale
        g = (grad_ref[rows(h), :] * gain - m1 - xhat * m2) * scale + top_ref[rows(h), :].astype(F32)
        g = jnp.where(mask(h), g, 0.0)
        grad_ref[rows(h), :] = g
        put_shifted(e3_ref, h, g.astype(BF16).astype(F32), False)
        return carry + fold(g)

    sg = lax.fori_loop(0, SIDE, back, zero, unroll=2)
    leave(e3_ref, e3_any)
    leave(grad_ref, grad_any)
    vout_ref[...] = total_of(sg, sux, su, sq, sv, top_sum)
    still = [v for v in leaving if v is not kept_one]
    kept_one.wait()
    waits += kernel_gradient(act_t, e3_ref, k_one, 9 * c, at_ref, (low, high), gk_sems)
    for wait in waits + still:
        wait.wait()


def forward(at, pad_one, vec, gathered, img, cot):
    n, c = img.shape
    heads, mine, other = gathered
    half = (shape((8, 22 * c // 64, c), BF16), "a")

    def low(*dims):
        return pltpu.VMEM(dims, BF16)

    full = low(n, c)
    found = call(forward_body,
        [(shape((22 * c, c), BF16), "a"), (shape((n, c), F32), "a"), (shape((8, c), F32), "v"), (shape((n, c), BF16), "a"), (shape((n, c), F32), "a"),
         (shape((n, c), F32), "a"), (shape((n + 2 * SIDE, 3 * c), BF16), "a"), (shape((8, c), F32), "v")] + [half] * 8,
        [(at, "s"), (pad_one, "v"), (vec, "v"), (heads, "a"), (mine, "a"), (other, "a"), (img, "a"), (cot, "a")],
        [low(9 * c, c), low(9 * c, c), low(4 * c, c), full, full, pltpu.VMEM((n, c), F32), low(n + 2 * SIDE, c), low(c, n),
         pltpu.VMEM((n, c), F32), full, low(c, n), full, full, full, low(n, n), low(n, n), full, full, full, full, full, full,
         pltpu.VMEM((n, c), F32), low(n + 2 * SIDE, 3 * c), low(4 * c, c),
         pltpu.SemaphoreType.DMA((9,)), pltpu.SemaphoreType.DMA((9,)), pltpu.SemaphoreType.DMA((4,)),
         pltpu.SemaphoreType.DMA((2,)), pltpu.SemaphoreType.DMA((8,)), pltpu.SemaphoreType.DMA, pltpu.SemaphoreType.DMA((9,))],
        name="forward")
    return found[:8], found[8:12], found[12:16]


def kernel_gradient(act_t, e3_ref, stage, row, at_ref, rounds, sems):
    c, n = act_t.shape

    def one_row(dy, carry):
        lo = pl.multiple_of((2 - dy) * SIDE, SIDE)
        for dx in range(3):
            value = dot(act_t[...], e3_ref[pl.ds(lo, n), dx * c : (dx + 1) * c])
            stage[pl.ds(pl.multiple_of((3 * dy + dx) * c, c), c), :] = value.astype(BF16)
        for now in range(3):

            @pl.when(dy == now)
            def _(now=now):
                send_rows(stage, 3 * now * c, row + 3 * now * c, 3 * c, at_ref, rounds, sems.at[now])

        return carry

    lax.fori_loop(0, 3, one_row, 0, unroll=1)
    places = [stage.at[pl.ds(3 * dy * c, 3 * c)] for dy in range(3)]
    return [pltpu.make_async_copy(place, place, sems.at[dy]) for dy, place in enumerate(places)]


def conv_back(e3_ref, k_ref, copies, out_ref):
    n, c = out_ref.shape
    for dy in range(3):
        copies[dy].wait()
        lo = (2 - dy) * SIDE

        def block(m, carry, dy=dy, lo=lo):
            first = pl.multiple_of(m * MB, MB)
            value = None
            for dx in range(3):
                tap = 3 * dy + dx
                term = dot_nt(e3_ref[pl.ds(first + lo, MB), dx * c : (dx + 1) * c], k_ref[tap * c : (tap + 1) * c, :])
                value = term if value is None else value + term
            if dy > 0:
                value = value + out_ref[pl.ds(first, MB), :]
            out_ref[pl.ds(first, MB), :] = value
            return carry

        lax.fori_loop(0, n // MB, block, 0, unroll=4)


def norm_back_sums(src_ref, g_ref, mean, scale, gain, shift, mask, size):
    c = g_ref.shape[1]

    def sums(h, carry):
        xhat = (src_ref[rows(h), :].astype(F32) - mean) * scale
        y = xhat * gain + shift
        s = sigmoid(y)
        u = jnp.where(mask(h), g_ref[rows(h), :] * (s * (1.0 + y * (1.0 - s))), 0.0)
        g_ref[rows(h), :] = u
        return carry[0] + fold(u), carry[1] + fold(u * xhat)

    zero = jnp.zeros((8, c), F32)
    su, sux = lax.fori_loop(0, SIDE, sums, (zero, zero), unroll=2)
    count = (size * size * 16).astype(F32)
    both = group_total(total_of(su, sux) * gain) / count
    return su, sux, both[0:1], both[1:2]


def back_two_body(
    at_ref, e3_ref, vec_ref, stat_ref, k_any, conv_any, act_any, i0, i1, i2, i3,
    e3_any, vout_ref, o0, o1, o2, o3, g_ref, conv_ref, act_t, e3_out, k_vmem, sems, in_sems, out_sem, gk_sems,
):
    n, c = conv_ref.shape
    copies = start_copies(k_any, k_vmem, sems, 3, 9 * c)
    conv_copy = pltpu.make_async_copy(conv_any, conv_ref, in_sems.at[0])
    act_copy = pltpu.make_async_copy(act_any, act_t, in_sems.at[1])
    conv_copy.start()
    act_copy.start()
    size = at_ref[0]
    mask = row_mask(size, c)
    conv_back(e3_ref, k_vmem, copies, g_ref)
    conv_copy.wait()
    mean, scale = stat_ref[0:1, :], stat_ref[1:2, :]
    gain, shift = vec_ref[3:4, :], vec_ref[4:5, :]
    su, sux, m1, m2 = norm_back_sums(conv_ref, g_ref, mean, scale, gain, shift, mask, size)
    clear_border(e3_out)

    def apply(h, carry):
        xhat = (conv_ref[rows(h), :] - mean) * scale
        g = jnp.where(mask(h), (g_ref[rows(h), :] * gain - m1 - xhat * m2) * scale, 0.0)
        put_shifted(e3_out, h, g.astype(BF16).astype(F32), False)
        return carry + fold(g)

    sg = lax.fori_loop(0, SIDE, apply, jnp.zeros((8, c), F32), unroll=2)
    leaving = pltpu.make_async_copy(e3_out, e3_any, out_sem)
    leaving.start()
    vout_ref[...] = total_of(sg, sux, su)
    act_copy.wait()
    for wait in kernel_gradient(act_t, e3_out, k_vmem, 0, at_ref, ((o0, o1, o2, o3),), gk_sems):
        wait.wait()
    leaving.wait()


def back_two(at, e3, weights, vec, conv_out, stat, act, low):
    n, c = conv_out.shape
    half = shape(low[0].shape, BF16)
    e3_out, vout, *low = call(back_two_body,
        [(shape((n + 64, 3 * c), BF16), "a"), (shape((8, c), F32), "v")] + [(half, "a")] * 4,
        [(at, "s"), (e3, "v"), (vec, "v"), (stat, "v"), (weights, "a"), (conv_out, "a"), (act, "a")] + [(v, "a") for v in low],
        [pltpu.VMEM((n, c), F32), pltpu.VMEM((n, c), F32), pltpu.VMEM((c, n), BF16), pltpu.VMEM((n + 64, 3 * c), BF16),
         pltpu.VMEM((9 * c, c), BF16), pltpu.SemaphoreType.DMA((3,)), pltpu.SemaphoreType.DMA((2,)), pltpu.SemaphoreType.DMA,
         pltpu.SemaphoreType.DMA((9,))],
        name="back_two", aliases={7 + i: 2 + i for i in range(4)})
    return e3_out, vout, low


def back_one_body(
    size_ref, e3_ref, k_ref, vec_ref, img_ref, stat_ref, grad_ref, mixed_any, resid_any, both_any, vout_ref,
    g_ref, out_ref, rows_ref, mixed_ref, resid_ref, wo_ref, k_vmem, sems, in_sems, out_sems,
):
    n, c = img_ref.shape
    copies = start_copies(k_ref, k_vmem, sems, 3)
    bands, quarter = both_any.shape[0], both_any.shape[2]
    later = [
        pltpu.make_async_copy(src, dst, in_sems.at[i])
        for i, (src, dst) in enumerate(((mixed_any, mixed_ref), (resid_any, resid_ref), (k_ref.at[pl.ds(21 * c, c)], wo_ref)))
    ]
    for copy in later:
        copy.start()
    leaving = []

    def leave(src_ref, which):
        for j in range(bands):
            copy = pltpu.make_async_copy(src_ref.at[pl.ds(j * quarter, quarter)], both_any.at[j, which], out_sems.at[len(leaving)])
            copy.start()
            leaving.append(copy)

    size = size_ref[0]
    mask = row_mask(size, c)
    conv_back(e3_ref, k_vmem, copies, g_ref)
    for copy in later:
        copy.wait()

    def block_rows(m, carry):
        first = pl.multiple_of(m * MB, MB)
        at = pl.ds(first, MB)
        value = dot(mixed_ref[at, :], wo_ref[...]) + vec_ref[10:11, :] + resid_ref[at, :]
        rows_ref[at, :] = jnp.where(pixel_mask(size, first, MB, c), value, 0.0).astype(BF16)
        return carry

    lax.fori_loop(0, n // MB, block_rows, 0)
    leave(rows_ref, 0)
    mean, scale = stat_ref[0:1, :], stat_ref[1:2, :]
    gain, shift = vec_ref[0:1, :], vec_ref[1:2, :]
    su, sux, m1, m2 = norm_back_sums(img_ref, g_ref, mean, scale, gain, shift, mask, size)

    def apply(h, carry):
        xhat = (img_ref[rows(h), :].astype(F32) - mean) * scale
        g = (g_ref[rows(h), :] * gain - m1 - xhat * m2) * scale + grad_ref[rows(h), :]
        out_ref[rows(h), :] = jnp.where(mask(h), g, 0.0).astype(out_ref.dtype)
        return carry

    lax.fori_loop(0, SIDE, apply, 0, unroll=2)
    leave(out_ref, 1)
    vout_ref[...] = total_of(sux, su)
    for copy in leaving:
        copy.wait()


def back_one(at, e3, weights, vec, img, stat, grad_resid, mixed, resid, bands):
    n, c = img.shape
    low, full = pltpu.VMEM((n, c), BF16), pltpu.VMEM((n, c), F32)
    return call(back_one_body, [(shape((bands, 2, n // bands, c), BF16), "a"), (shape((8, c), F32), "v")],
        [(at, "s"), (e3, "v"), (weights, "a"), (vec, "v"), (img, "v"), (stat, "v"), (grad_resid, "v"), (mixed, "a"), (resid, "a")],
        [full, low, low, low, full, pltpu.VMEM((c, c), BF16), pltpu.VMEM((9 * c, c), BF16), pltpu.SemaphoreType.DMA((3,)),
         pltpu.SemaphoreType.DMA((3,)), pltpu.SemaphoreType.DMA((2 * bands,))],
        name="back_one")


ALL = ("img", "band")
CORE = [(b, b ^ 1) for b in range(4)]
ACROSS_Y = [(b, b ^ 2) for b in range(4)]
ACROSS_X = [(i, i ^ 1) for i in range(8)]

def after(value, *earlier, flops=0):
    def body(*refs):
        pass

    anywhere = pl.BlockSpec(memory_space=pl.ANY)
    return pl.pallas_call(
        body,
        out_shape=shape(value.shape, value.dtype),
        in_specs=[anywhere] * (1 + len(earlier)),
        out_specs=anywhere,
        input_output_aliases={0: 0},
        cost_estimate=pl.CostEstimate(flops=flops, bytes_accessed=0, transcendentals=0),
        name="after",
    )(value, *earlier)


def wide(*parts):
    total = parts[0].astype(F32)
    for part in parts[1:]:
        total = total + part.astype(F32)
    return total


SUMS_VMEM = VMEM_LIMIT


def add_parts(held, ready, terms):
    lead = ready.shape[:-2]

    def one(k, carry):
        spot = (k,) if len(lead) == 1 else (k // lead[1], k % lead[1])
        total = held[(0, *spot)].astype(F32)
        for t in range(1, terms):
            total = total + held[(t, *spot)].astype(F32)
        ready[spot] = total.astype(ready.dtype)
        return carry

    count = lead[0] if len(lead) == 1 else lead[0] * lead[1]
    lax.fori_loop(0, count, one, 0)


def start_terms(ins, terms, held, sems):
    copies = [pltpu.make_async_copy(ins[at].at[index], held.at[t], sems.at[t]) for t, (at, index) in enumerate(terms)]
    for copy in copies:
        copy.start()
    return copies


def sums_body(*refs, arrays, groups):
    count = len(groups)
    ins, outs, rest = refs[:arrays], refs[arrays : arrays + count], refs[arrays + count :]
    held, ready, in_sems, out_sems = rest[:count], rest[count : 2 * count], rest[2 * count : 3 * count], rest[-1]
    copies = [start_terms(ins, terms, held[g], in_sems[g]) for g, terms in enumerate(groups)]
    leaving = []
    for g, terms in enumerate(groups):
        for copy in copies[g]:
            copy.wait()
        add_parts(held[g], ready[g], len(terms))
        leaving.append(pltpu.make_async_copy(ready[g], outs[g], out_sems.at[g]))
        leaving[-1].start()
    for copy in leaving:
        copy.wait()


def indexed(groups):
    arrays, places = [], {}
    for terms in groups:
        for array, _ in terms:
            if id(array) not in places:
                places[id(array)] = len(arrays)
                arrays.append(array)
    return arrays, [[(places[id(array)], index) for array, index in terms] for terms in groups]


def sum_shape(array, index):
    return tuple(array.shape[i] for i in range(array.ndim) if i >= len(index) or index[i] == slice(None))


def block_sums(groups, dtype, name):
    arrays, places = indexed(groups)
    dims = [sum_shape(*terms[0]) for terms in groups]
    return call(functools.partial(sums_body, arrays=len(arrays), groups=places),
        [(shape(d, dtype), "a") for d in dims],
        [(v, "a") for v in arrays],
        [pltpu.VMEM((len(terms), *d), BF16) for terms, d in zip(groups, dims)] + [pltpu.VMEM(d, dtype) for d in dims]
        + [pltpu.SemaphoreType.DMA((len(terms),)) for terms in groups] + [pltpu.SemaphoreType.DMA((len(groups),))],
        name=name, vmem=SUMS_VMEM)


def chip_sends(arrays, *earlier):
    mine_a, mine_b, theirs_a, theirs_b = arrays
    half, c = mine_a.shape[1:]
    dims = (2, 2, 2, half, c)
    if earlier:
        theirs_a, theirs_b = after(theirs_a, *earlier), after(theirs_b, *earlier)
    got = [lax.ppermute(v, "band", CORE) for v in (theirs_a, theirs_b)]
    pair_a = (mine_a.reshape(dims), got[0].reshape(dims))
    pair_b = (mine_b.reshape(dims), got[1].reshape(dims))
    every = slice(None)
    sends = block_sums([[(v, (1,)) for v in pair_a], [(v, (every, 1)) for v in pair_b]], BF16, "chip_sums")
    return pair_a, pair_b, *sends


def plane_swap(send_a, send_b):
    return lax.ppermute(send_a, "img", ACROSS_X), lax.ppermute(send_b, "band", ACROSS_Y)


def plane_sends(pair_a, pair_b, got_a, got_b):
    kept_a = [(v, (0, 0)) for v in pair_a] + [(got_a, (0,))]
    kept_b = [(v, (0, 0)) for v in pair_b] + [(got_b, (0,))]
    sends = block_sums(
        [[(v, (0, 1)) for v in pair_a] + [(got_a, (1,))], [(v, (1, 0)) for v in pair_b] + [(got_b, (1,))]], BF16, "row_sums"
    )
    return kept_a, kept_b, *sends


def plane_parts(kept_a, kept_b, next_a, next_b, *earlier):
    last_a = lax.ppermute(next_a, "band", ACROSS_Y)
    last_b = lax.ppermute(next_b, "img", ACROSS_X)
    if earlier:
        last_a, last_b = after(last_a, *earlier), after(last_b, *earlier)
    return [kept_a + [(last_a, ())], kept_b + [(last_b, ())]]


def owner_body(at_ref, *refs, arrays, groups):
    ins, (own, *sent), rest = refs[:arrays], refs[arrays : arrays + 4], refs[arrays + 4 :]
    high_a, high_b, held_a, held_b, total_a, total_b, sems_a, sems_b, high_sems = rest
    copies = [start_terms(ins, groups[0], held_a, sems_a), start_terms(ins, groups[1], held_b, sems_b)]
    highs = [pltpu.make_async_copy(ins[groups[2 + i][0][0]], ref, high_sems.at[i]) for i, ref in enumerate((high_a, high_b))]
    for copy in highs:
        copy.start()
    for i, (held, total) in enumerate(((held_a, total_a), (held_b, total_b))):
        for copy in copies[i]:
            copy.wait()
        add_parts(held, total, len(groups[i]))
    for copy in highs:
        copy.wait()
    half = total_a.shape[1]
    for step, ref in enumerate((own, *sent)):
        plane = at_ref[4] ^ step
        for upper, pair in enumerate(((total_a, total_b), (high_a, high_b))):

            @pl.when((plane >> 1) == upper)
            def _(ref=ref, pair=pair, plane=plane):
                for tail, part in enumerate(pair):
                    ref[tail * half : (tail + 1) * half, :] = part[plane & 1].astype(ref.dtype)


def owner_parts(at, low, high):
    groups = low + [[(v, ())] for v in high]
    arrays, places = indexed(groups)
    half, c = high[0].shape[1:]
    sums = pltpu.VMEM((2, half, c), F32)
    held = pltpu.VMEM((len(low[0]), 2, half, c), BF16)
    sems = pltpu.SemaphoreType.DMA((len(low[0]),))
    own, *sent = call(functools.partial(owner_body, arrays=len(arrays), groups=places),
        [(shape((2 * half, c), F32), "v")] + [(shape((2 * half, c), BF16), "v")] * 3,
        [(at, "s")] + [(v, "a") for v in arrays],
        [sums, sums, held, held, sums, sums, sems, sems, pltpu.SemaphoreType.DMA((2,))],
        name="owner_sums", vmem=SUMS_VMEM)
    got = [lax.ppermute(v, "img", [(i, i ^ (2 * step)) for i in range(8)]) for v, step in zip(sent, (1, 2, 3))]
    return [own] + got, sent


def plane_gather(own):
    z = [lax.ppermute(own, "img", [(i, i ^ (2 * step)) for i in range(8)]) for step in (1, 2, 3)]
    first, last = jnp.stack([own, z[0]]), jnp.stack([z[1], z[2]])
    first = jnp.concatenate([first, lax.ppermute(first, "band", ACROSS_Y)])
    last = jnp.concatenate([last, lax.ppermute(last, "img", ACROSS_X)])
    mine = jnp.concatenate([first, lax.ppermute(first, "img", ACROSS_X), last, lax.ppermute(last, "band", ACROSS_Y)])
    return mine, lax.ppermute(mine, "band", CORE)


def four_sum(v, axis, steps):
    a, b, c = (lax.ppermute(v, axis, [(i, i ^ step) for i in range(lax.axis_size(axis))]) for step in steps)
    return (v + a) + (b + c)


def whole_image(
    images,
    cotangent,
    sizes,
    matrix_weight,
    matrix_momentum,
    matrix_average,
    vector_weight,
    vector_momentum,
    vector_average,
):
    batch, height, width, c = images.shape
    n = width * width
    mine = lax.axis_index("band")
    place = lax.axis_index("img")
    at = jnp.stack([lax.dynamic_index_in_dim(sizes, mine, 0, False), place % 2, mine // 2, mine % 2, place // 2])

    def to_image(field):
        parts = field.reshape(batch, height * width, c)
        return lax.all_to_all(parts, "band", 0, 0, tiled=True).reshape(n, c)

    own = matrix_weight.astype(BF16).reshape(-1, c)
    head = 288
    gathered = (lax.all_gather(own[:head], ALL, axis=0, tiled=True), *plane_gather(own[head:]))
    img = to_image(images)
    cot = to_image(cotangent)
    pad_one, act_t, stat_one = act_one(at, img, vector_weight)
    (weights, conv_out, stat_two, mixed, resid, grad_resid, e3_two, v3), high, low = forward(
        at, pad_one, vector_weight, gathered, img, cot
    )
    high = chip_sends(high)
    e3_two = after(e3_two, high[2], high[3])
    swapped = plane_swap(high[2], high[3])
    e3_one, v2, low = back_two(at, e3_two, weights, vector_weight, conv_out, stat_two, act_t, low)
    low = chip_sends(low, *swapped)
    high = plane_sends(*high[:2], *swapped)
    low_sends = low[2:4]
    e3_one = after(e3_one, *low_sends)
    swapped = plane_swap(low[2], low[3])
    both, v1 = back_one(at, e3_one, weights, vector_weight, img, stat_one, grad_resid, mixed, resid, batch)
    vecs = jnp.stack([v1[0], v1[1], v2[0], v2[1], v2[2], v3[0], v3[1], v3[2], v3[3], v3[4], v3[5]])
    low = plane_sends(*low[:2], *(after(v, v1) for v in swapped))
    vecs = four_sum(after(vecs, low[2], low[3]), "img", (2, 4, 6))
    high = block_sums(plane_parts(*high, low[2], low[3]), F32, "plane_sums")
    parts, sent = owner_parts(at, plane_parts(*low, vecs), high)
    given = lax.all_to_all(after(both, *sent), "band", 0, 0, tiled=True)
    block_out = given[:, 0].reshape(images.shape)
    input_grad = given[:, 1].reshape(images.shape).astype(F32)
    vecs = after(vecs, parts[1])
    vecs = vecs + lax.ppermute(vecs, "img", ACROSS_X)
    vector_grads = four_sum(vecs, "band", (1, 2, 3))
    vector_moments = MOMENTUM * vector_momentum + vector_grads
    vector_masters = vector_weight - LR_VECTOR * (vector_grads + MOMENTUM * vector_moments)
    vector_means = AVERAGE * vector_average + (1.0 - AVERAGE) * vector_masters
    matrix_grads = wide(*parts).reshape(-1)
    matrix_moments = MOMENTUM * matrix_momentum + matrix_grads
    matrix_masters = matrix_weight - LR_MATRIX * (matrix_grads + MOMENTUM * matrix_moments)
    matrix_means = AVERAGE * matrix_average + (1.0 - AVERAGE) * matrix_masters
    return (
        block_out,
        input_grad,
        matrix_grads,
        matrix_moments,
        matrix_means,
        matrix_masters,
        vector_grads,
        vector_moments,
        vector_means,
        vector_masters,
    )


def solution(mesh):
    fits = mesh.shape["img"] == 8 and mesh.shape["band"] == 4

    def per_device(images, *rest):
        step = whole_image if fits and images.shape[:3] == (4, 8, SIDE) else banded
        return step(images, *rest)

    return jax.shard_map(
            per_device,
        mesh=mesh,
        in_specs=(
            P("img", "band", None, None),
            P("img", "band", None, None),
            P("img"),
            P(("img", "band")),
            P(("img", "band")),
            P(("img", "band")),
            P(),
            P(),
            P(),
        ),
        out_specs=(
            P("img", "band", None, None),
            P("img", "band", None, None),
            P(("img", "band")),
            P(("img", "band")),
            P(("img", "band")),
            P(("img", "band")),
            P(),
            P(),
            P(),
            P(),
        ),
        check_vma=False,
    )
```

```python
import functools

import jax
import jax.numpy as jnp
from jax import lax
from jax.experimental import pallas as pl
from jax.experimental.pallas import tpu as pltpu
from jax.sharding import PartitionSpec as P

GROUPS = 32


EPS = 1e-06
MOMENTUM = 0.9
LR_MATRIX = 4e-05
LR_VECTOR = 0.0001
AVERAGE = 0.75


def extended(array, sides, width):
    for axis, dim in sides:
        count, length = (lax.axis_size(axis), array.shape[dim])
        up = [(i, (i + 1) % count) for i in range(count - 1)]
        down = [(j, i) for i, j in up]
        last = lax.slice_in_dim(array, length - width, length, axis=dim)
        initial = lax.slice_in_dim(array, 0, width, axis=dim)
        before = lax.ppermute(last, axis, up)
        after = lax.ppermute(initial, axis, down)
        array = jnp.concatenate([before, array, after], axis=dim)
    return array


def split_groups(field):
    return field.reshape(field.shape[:3] + (GROUPS, field.shape[3] // GROUPS))


def group_sums(field, mask):
    shaped = split_groups(field)
    weighted = shaped * mask[..., None]
    return (jnp.sum(weighted, axis=(1, 2, 4)), jnp.sum(weighted * shaped, axis=(1, 2, 4)))


def group_apply(field, sums, count, gain, shift):
    center = sums[0] / count[:, None]
    spread = sums[1] / count[:, None] - center * center
    scale = lax.rsqrt(spread + EPS)
    shaped = split_groups(field)
    normed = (shaped - center[:, None, None, :, None]) * scale[:, None, None, :, None]
    return normed.reshape(field.shape) * gain + shift


def normalize(field, mask, count, gain, shift):
    sums = lax.psum(group_sums(field, mask), "band")
    return (group_apply(field, sums, count, gain, shift), sums)


def normalize_back(field, sums, mask, count, gain, shift, upstream):
    _, pull = jax.vjp(
        lambda field_in, sums_in, gain_in, shift_in: group_apply(
            field_in, sums_in, count, gain_in, shift_in
        ),
        field,
        sums,
        gain,
        shift,
    )
    direct, grad_sums, grad_gain, grad_shift = pull(upstream)
    grad_sums = lax.psum(grad_sums, "band")
    _, pull_sums = jax.vjp(lambda field_in: group_sums(field_in, mask), field)
    return (direct + pull_sums(grad_sums)[0], grad_gain, grad_shift)


def activate(field, mask):
    return jax.nn.silu(field) * mask


def activate_back(field, mask, upstream):
    _, pull = jax.vjp(lambda inner: activate(inner, mask), field)
    return pull(upstream)[0]


def widen(field):
    return jnp.pad(field, ((0, 0), (0, 0), (1, 1), (0, 0)))


def taps(padded, kernel, height, width):
    total = jnp.zeros(padded.shape[:1] + (height, width, kernel.shape[2]), jnp.float32)
    for tap in range(9):
        row, column = (tap // 3, tap % 3)
        total = total + jnp.einsum(
            "ghwc,cd->ghwd",
            padded[:, row : row + height, column : column + width],
            kernel[tap],
            preferred_element_type=jnp.float32,
        )
    return total


def conv_forward(low_field, kernel):
    padded = widen(extended(low_field, (("band", 1),), 1))
    return (taps(padded, kernel, low_field.shape[1], low_field.shape[2]), padded)


def conv_backward(low_grad, kernel, padded):
    height, width = (low_grad.shape[1], low_grad.shape[2])
    grad_pad = widen(extended(low_grad, (("band", 1),), 1))
    flipped = jnp.swapaxes(kernel[::-1], 1, 2)
    grad_in = taps(grad_pad, flipped, height, width)
    pieces = []
    for tap in range(9):
        row, column = (tap // 3, tap % 3)
        pieces.append(
            jnp.einsum(
                "ghwc,ghwd->cd",
                padded[:, row : row + height, column : column + width],
                low_grad,
                preferred_element_type=jnp.float32,
            )
        )
    return (grad_in, jnp.stack(pieces))


def attend(query_low, key_full, key_valid, factor):
    score_matrix = (
        jnp.einsum("gqc,gkc->gqk", query_low, key_full, preferred_element_type=jnp.float32) * factor
    )
    score_matrix = jnp.where(key_valid[:, None, :], score_matrix, -1e30)
    top = jnp.max(score_matrix, axis=2, keepdims=True)
    raised = jnp.exp(score_matrix - top)
    total = jnp.sum(raised, axis=2, keepdims=True)
    return (raised / total, top, total)


def banded(
    images,
    cotangent,
    sizes,
    matrix_weight,
    matrix_momentum,
    matrix_average,
    vector_weight,
    vector_momentum,
    vector_average,
):
    batch, height, width, channels = images.shape
    square = channels * channels
    queries = height * width
    positions = width * width
    factor = channels ** (-0.5)
    weights = lax.all_gather(
        matrix_weight.astype(jnp.bfloat16), ("img", "band"), axis=0, tiled=True
    )
    kernel_one = weights[: 9 * square].reshape(9, channels, channels)
    kernel_two = weights[9 * square : 18 * square].reshape(9, channels, channels)
    attn_in = weights[18 * square : 21 * square].reshape(3, channels, channels)
    attention_output = weights[21 * square :].reshape(channels, channels)
    lines = lax.axis_index("band") * height + jnp.arange(height)
    across = jnp.arange(width)
    limit = sizes[:, None, None]
    inside = (lines[None, :, None] < limit) & (across[None, None, :] < limit)
    mask = jnp.where(inside, 1.0, 0.0).astype(jnp.float32)[..., None]
    count = (sizes * sizes * (channels // GROUPS)).astype(jnp.float32)
    spots = jnp.arange(positions)
    key_valid = ((spots // width)[None, :] < sizes[:, None]) & (
        (spots % width)[None, :] < sizes[:, None]
    )
    start = images.astype(jnp.float32) * mask
    norm_one, sums_one = normalize(start, mask, count, vector_weight[0], vector_weight[1])
    act_one = activate(norm_one, mask).astype(jnp.bfloat16)
    conv_raw, padded_one = conv_forward(act_one, kernel_one)
    conv_out = conv_raw + vector_weight[2]
    norm_two, sums_two = normalize(conv_out, mask, count, vector_weight[3], vector_weight[4])
    act_two = activate(norm_two, mask).astype(jnp.bfloat16)
    conv_raw, padded_two = conv_forward(act_two, kernel_two)
    resid = (start + conv_raw + vector_weight[5]) * mask
    norm_three, sums_three = normalize(resid, mask, count, vector_weight[6], vector_weight[7])
    normed = (norm_three * mask).astype(jnp.bfloat16).reshape(batch, queries, channels)
    projected = jnp.einsum("gqc,jcd->jgqd", normed, attn_in, preferred_element_type=jnp.float32)
    query_low = (projected[0] + vector_weight[8]).astype(jnp.bfloat16)
    key_low = projected[1].astype(jnp.bfloat16)
    value_low = (projected[2] + vector_weight[9]).astype(jnp.bfloat16)
    key_full, value_full = (
        lax.all_gather(key_low, "band", axis=1, tiled=True),
        lax.all_gather(value_low, "band", axis=1, tiled=True),
    )
    probability_rows, row_top, row_total = attend(query_low, key_full, key_valid, factor)
    mixed_values = jnp.einsum(
        "gqk,gkc->gqc",
        probability_rows.astype(jnp.bfloat16),
        value_full,
        preferred_element_type=jnp.float32,
    ).astype(jnp.bfloat16)
    output_rows = (
        jnp.einsum(
            "gqc,cd->gqd", mixed_values, attention_output, preferred_element_type=jnp.float32
        )
        + vector_weight[10]
    )
    block_out = ((resid + output_rows.reshape(images.shape)) * mask).astype(jnp.bfloat16)
    grad_top = cotangent.astype(jnp.float32) * mask
    grad_proj = grad_top.reshape(batch, queries, channels)
    grad_proj_low = grad_proj.astype(jnp.bfloat16)
    grad_out_weight = jnp.einsum(
        "gqc,gqd->cd", mixed_values, grad_proj_low, preferred_element_type=jnp.float32
    )
    grad_mixed = jnp.einsum(
        "gqd,cd->gqc", grad_proj_low, attention_output, preferred_element_type=jnp.float32
    ).astype(jnp.bfloat16)
    back_keys, back_values = (
        lax.all_gather(key_low, "band", axis=1, tiled=True),
        lax.all_gather(value_low, "band", axis=1, tiled=True),
    )
    back_probs = attend(query_low, back_keys, key_valid, factor)[0]
    grad_probs = jnp.einsum(
        "gqc,gkc->gqk", grad_mixed, back_values, preferred_element_type=jnp.float32
    )
    weighted_sum = jnp.sum(back_probs * grad_probs, axis=2, keepdims=True)
    grad_scores = back_probs * (grad_probs - weighted_sum)
    grad_scores_low = (grad_scores * factor).astype(jnp.bfloat16)
    grad_query = jnp.einsum(
        "gqk,gkc->gqc", grad_scores_low, back_keys, preferred_element_type=jnp.float32
    ).astype(jnp.bfloat16)
    key_terms = jnp.einsum(
        "gqk,gqc->gkc", grad_scores_low, query_low, preferred_element_type=jnp.float32
    )
    value_terms = jnp.einsum(
        "gqk,gqc->gkc",
        back_probs.astype(jnp.bfloat16),
        grad_mixed,
        preferred_element_type=jnp.float32,
    )
    grad_key, grad_value = (
        lax.psum_scatter(
            key_terms.astype(jnp.bfloat16), "band", scatter_dimension=1, tiled=True
        ).astype(jnp.float32),
        lax.psum_scatter(
            value_terms.astype(jnp.bfloat16), "band", scatter_dimension=1, tiled=True
        ).astype(jnp.float32),
    )
    grad_value_low = grad_value.astype(jnp.bfloat16)
    grads_low = jnp.stack([grad_query, grad_key.astype(jnp.bfloat16), grad_value_low])
    grad_in_weights = jnp.einsum(
        "gqc,jgqd->jcd", normed, grads_low, preferred_element_type=jnp.float32
    )
    grad_normed = (
        jnp.einsum("jgqd,jcd->gqc", grads_low, attn_in, preferred_element_type=jnp.float32).reshape(
            images.shape
        )
        * mask
    )
    grad_resid_norm, grad_gain_three, grad_shift_three = normalize_back(
        resid, sums_three, mask, count, vector_weight[6], vector_weight[7], grad_normed
    )
    grad_resid = (grad_top + grad_resid_norm) * mask
    grad_act_two, grad_kernel_two = conv_backward(
        grad_resid.astype(jnp.bfloat16), kernel_two, padded_two
    )
    grad_norm_two = activate_back(norm_two, mask, grad_act_two)
    grad_conv_out, grad_gain_two, grad_shift_two = normalize_back(
        conv_out, sums_two, mask, count, vector_weight[3], vector_weight[4], grad_norm_two
    )
    grad_act_one, grad_kernel_one = conv_backward(
        grad_conv_out.astype(jnp.bfloat16), kernel_one, padded_one
    )
    grad_norm_one = activate_back(norm_one, mask, grad_act_one)
    grad_start, grad_gain_one, grad_shift_one = normalize_back(
        start, sums_one, mask, count, vector_weight[0], vector_weight[1], grad_norm_one
    )
    input_grad = (grad_resid + grad_start) * mask
    vector_terms = jnp.stack(
        [
            grad_gain_one,
            grad_shift_one,
            jnp.sum(grad_conv_out, axis=(0, 1, 2)),
            grad_gain_two,
            grad_shift_two,
            jnp.sum(grad_resid, axis=(0, 1, 2)),
            grad_gain_three,
            grad_shift_three,
            jnp.sum(grad_query, axis=(0, 1), dtype=jnp.float32),
            jnp.sum(grad_value_low, axis=(0, 1), dtype=jnp.float32),
            jnp.sum(grad_proj, axis=(0, 1)),
        ]
    )
    vector_grads = lax.psum(vector_terms, ("img", "band"))
    grad_flat = jnp.concatenate(
        [
            grad_kernel_one.reshape(-1),
            grad_kernel_two.reshape(-1),
            grad_in_weights.reshape(-1),
            grad_out_weight.reshape(-1),
        ]
    )
    matrix_grads = lax.psum_scatter(grad_flat, ("img", "band"), scatter_dimension=0, tiled=True)
    matrix_moments = MOMENTUM * matrix_momentum + matrix_grads
    matrix_masters = matrix_weight - LR_MATRIX * (matrix_grads + MOMENTUM * matrix_moments)
    matrix_means = AVERAGE * matrix_average + (1.0 - AVERAGE) * matrix_masters
    vector_moments = MOMENTUM * vector_momentum + vector_grads
    vector_masters = vector_weight - LR_VECTOR * (vector_grads + MOMENTUM * vector_moments)
    vector_means = AVERAGE * vector_average + (1.0 - AVERAGE) * vector_masters
    return (
        block_out,
        input_grad,
        matrix_grads,
        matrix_moments,
        matrix_means,
        matrix_masters,
        vector_grads,
        vector_moments,
        vector_means,
        vector_masters,
    )


F32 = jnp.float32
BF16 = jnp.bfloat16
SIDE = 32
VMEM_LIMIT = 58 * 1024 * 1024


def dot(a, b):
    return lax.dot_general(a, b, (((1,), (0,)), ((), ())), preferred_element_type=F32)


def dot_nt(a, b):
    return lax.dot_general(a, b, (((1,), (1,)), ((), ())), preferred_element_type=F32)


def dot_tn(a, b):
    return lax.dot_general(a, b, (((0,), (0,)), ((), ())), preferred_element_type=F32)


def call(body, outs, ins, scratch=(), flops=0, name=None, aliases=None, vmem=VMEM_LIMIT):
    spaces = {"v": pl.BlockSpec(memory_space=pltpu.VMEM), "s": pl.BlockSpec(memory_space=pltpu.SMEM),
              "a": pl.BlockSpec(memory_space=pl.ANY)}
    return pl.pallas_call(
        body,
        out_shape=[o for o, _ in outs],
        in_specs=[spaces[s] for _, s in ins],
        out_specs=[spaces[s] for _, s in outs],
        scratch_shapes=list(scratch),
        input_output_aliases=aliases or {},
        compiler_params=pltpu.CompilerParams(vmem_limit_bytes=vmem),
        cost_estimate=pl.CostEstimate(flops=flops, bytes_accessed=0, transcendentals=0),
        name=name,
    )(*[a for a, _ in ins])


def shape(dims, dtype):
    return jax.ShapeDtypeStruct(dims, dtype)


def fold(x):
    return jnp.sum(x.reshape(x.shape[0] // 8, 8, x.shape[1]), axis=0)


def group_total(x):
    lane = lax.broadcasted_iota(jnp.int32, x.shape, 1)
    width = x.shape[1]
    for s in (1, 2, 4, 8):
        up = pltpu.roll(x, width - s, 1)
        down = pltpu.roll(x, s, 1)
        x = x + jnp.where((lane & s) == 0, up, down)
    return x


def total_of(*parts):
    rows = [jnp.sum(p, axis=0, keepdims=True) for p in parts]
    pad = jnp.zeros((8 - len(rows), rows[0].shape[1]), F32)
    return jnp.concatenate(rows + [pad], axis=0)


def moments(s1, s2, size):
    count = (size * size * 16).astype(F32)
    both = group_total(total_of(s1, s2)) / count
    mean = both[0:1]
    spread = both[1:2] - mean * mean
    return mean, lax.rsqrt(spread + EPS)


def row_mask(size, channels):
    across = lax.broadcasted_iota(jnp.int32, (SIDE, channels), 0)
    inside = across < size
    return lambda h: inside & (h < size)


def sigmoid(y):
    return 0.5 * jnp.tanh(0.5 * y) + 0.5


def rows(h):
    return pl.ds(pl.multiple_of(h * SIDE, SIDE), SIDE)


def put_shifted(ref, h, r, forward):
    channels = r.shape[1]
    w = lax.broadcasted_iota(jnp.int32, r.shape, 0)
    before = jnp.where(w == 0, 0.0, pltpu.roll(r, 1, 0)).astype(BF16)
    after = jnp.where(w == SIDE - 1, 0.0, pltpu.roll(r, SIDE - 1, 0)).astype(BF16)
    first, last = (before, after) if forward else (after, before)
    at = pl.ds(pl.multiple_of((h + 1) * SIDE, SIDE), SIDE)
    ref[at, 0:channels] = first
    ref[at, channels : 2 * channels] = r.astype(BF16)
    ref[at, 2 * channels :] = last


def clear_border(ref):
    zero = jnp.zeros((SIDE, ref.shape[1]), BF16)
    ref[0:SIDE, :] = zero
    ref[(SIDE + 1) * SIDE :, :] = zero


def put_transposed(ref, src_ref, row0, lane0):
    channels, count = ref.shape
    for j in range(count // 256):
        block = src_ref[row0 + j * 256 : row0 + (j + 1) * 256, lane0 : lane0 + channels]
        ref[:, j * 256 : (j + 1) * 256] = block.T


def act_one_body(size_ref, img_ref, vec_ref, pad_ref, at_ref, stat_ref):
    size = size_ref[0]
    channels = img_ref.shape[1]
    mask = row_mask(size, channels)

    def sums(h, carry):
        x = jnp.where(mask(h), img_ref[rows(h), :].astype(F32), 0.0)
        return carry[0] + fold(x), carry[1] + fold(x * x)

    zero = jnp.zeros((8, channels), F32)
    s1, s2 = lax.fori_loop(0, SIDE, sums, (zero, zero), unroll=2)
    mean, scale = moments(s1, s2, size)
    stat_ref[0:1, :] = mean
    stat_ref[1:2, :] = scale
    stat_ref[2:8, :] = jnp.zeros((6, channels), F32)
    apply_norm(img_ref, mean, scale * vec_ref[0:1, :], vec_ref[1:2, :], mask, pad_ref)
    put_transposed(at_ref, pad_ref, SIDE, 0)


def apply_norm(src_ref, mean, scale, shift, mask, pad_ref):
    clear_border(pad_ref)

    def apply(h, carry):
        y = (src_ref[rows(h), :].astype(F32) - mean) * scale + shift
        at = pl.ds(pl.multiple_of((h + 1) * SIDE, SIDE), SIDE)
        pad_ref[at, :] = jnp.where(mask(h), y * sigmoid(y), 0.0).astype(BF16)
        return carry

    lax.fori_loop(0, SIDE, apply, 0, unroll=4)


def act_one(size, img, vec):
    n, c = img.shape
    return call(act_one_body,
        [(shape((n + 64, c), BF16), "v"), (shape((c, n), BF16), "v"), (shape((8, c), F32), "v")],
        [(size, "s"), (img, "v"), (vec, "v")], name="act_one")


MB = 256


def start_copies(src_ref, dst_ref, sems, parts, offset=0):
    length = dst_ref.shape[0] // parts
    copies = [
        pltpu.make_async_copy(src_ref.at[pl.ds(offset + p * length, length)], dst_ref.at[pl.ds(p * length, length)], sems.at[p])
        for p in range(parts)
    ]
    for copy in copies:
        copy.start()
    return copies


COLUMNS = (1, 0, 2)


def fetch_rows(at_ref, gathered, dst_ref, base, row, count, sem):
    heads, mine, other = gathered
    tail = mine.shape[1]
    head = heads.shape[0] // 32
    block = head + tail
    for owner in range(row // block, (row + count - 1) // block + 1):
        first = owner * block
        lo, hi = max(row, first), min(row + count, first + head)
        if lo < hi:
            inside = pl.ds(base + lo - row, hi - lo)
            pltpu.make_async_copy(heads.at[pl.ds(owner * head + lo - first, hi - lo)], dst_ref.at[inside], sem).start()
        lo, hi = max(row, first + head), min(row + count, first + block)
        if lo >= hi:
            continue
        inside = pl.ds(base + lo - row, hi - lo)
        z, x, y, c = at_ref[4] ^ (owner >> 3), at_ref[1] ^ ((owner >> 2) & 1), at_ref[2] ^ ((owner >> 1) & 1), owner & 1
        slot = jnp.where(z < 2, x * 4 + y * 2 + z, 6 + y * 4 + x * 2 + z)
        place = pl.ds(lo - first - head, hi - lo)
        for far, ref in enumerate((mine, other)):

            @pl.when((at_ref[3] ^ c) == far)
            def _(ref=ref, place=place, inside=inside, slot=slot):
                pltpu.make_async_copy(ref.at[slot, place], dst_ref.at[inside], sem).start()

    whole = dst_ref.at[pl.ds(base, count)]
    return pltpu.make_async_copy(whole, whole, sem)


def start_kernel(at_ref, gathered, dst_ref, sems, row):
    c = dst_ref.shape[1]
    copies = {}
    for dx in COLUMNS:
        for dy in range(3):
            tap = 3 * dy + dx
            copies[tap] = fetch_rows(at_ref, gathered, dst_ref, tap * c, row + tap * c, c, sems.at[tap])
    return copies


def conv(pad_ref, k_ref, copies, out_ref, mb, finish):
    n, c = out_ref.shape
    zero = jnp.zeros((8, c), F32)
    carry = (zero, zero)
    across = lax.broadcasted_iota(jnp.int32, (mb, c), 0) & (SIDE - 1)
    for dx in COLUMNS:
        for dy in range(3):
            copies[3 * dy + dx].wait()

        def block(m, carry, dx=dx):
            first = pl.multiple_of(m * mb, mb)
            at = pl.ds(first, mb)
            value = None
            for dy in range(3):
                tap = 3 * dy + dx
                term = dot(pad_ref[pl.ds(first + dy * SIDE, mb), :], k_ref[tap * c : (tap + 1) * c, :])
                value = term if value is None else value + term
            if dx == 0:
                value = jnp.where(across == 0, 0.0, pltpu.roll(value, 1, 0))
            if dx == 2:
                value = jnp.where(across == SIDE - 1, 0.0, pltpu.roll(value, mb - 1, 0))
            if dx != COLUMNS[0]:
                value = value + out_ref[at, :]
            if dx == COLUMNS[-1]:
                value, carry = finish(first, value, carry)
            out_ref[at, :] = value
            return carry

        carry = lax.fori_loop(0, n // mb, block, carry, unroll=2)
    return carry


def pixel_mask(size, first, count, c):
    place = lax.broadcasted_iota(jnp.int32, (count, c), 0) + first
    return ((place >> 5) < size) & ((place & (SIDE - 1)) < size)


def put_stats(stat_ref, mean, scale):
    stat_ref[...] = jnp.concatenate([mean, scale, jnp.zeros((6, mean.shape[1]), F32)], axis=0)


def pieces_of(row, count, half):
    found = []
    for spot in range(row // half, (row + count - 1) // half + 1):
        found.append((spot, max(row, spot * half), min(row + count, (spot + 1) * half)))
    return found


def send_rows(stage, base, row, count, at_ref, rounds, sem):
    half = rounds[-1][0].shape[1]
    for spot, lo, hi in pieces_of(row, count, half):
        owner, tail = spot // 2, spot % 2
        refs, inner = rounds[owner // 16], owner % 16
        z, x, y, c = inner // 8, (inner >> 2) & 1, (inner >> 1) & 1, inner & 1
        index = ((at_ref[1] ^ x) * 2 + (at_ref[2] ^ y)) * 2 + z
        source = stage.at[pl.ds(base + lo - row, hi - lo)]
        place = pl.ds(lo - spot * half, hi - lo)
        for other in range(2):

            @pl.when((at_ref[3] ^ c) == other)
            def _(ref=refs[2 * other + tail], source=source, place=place):
                pltpu.make_async_copy(source, ref.at[index, place], sem).start()

    return pltpu.make_async_copy(stage.at[pl.ds(base, count)], stage.at[pl.ds(base, count)], sem)


QB = 1024
PB = 512


def forward_body(
    at_ref, pad_one_ref, vec_ref, heads_any, mine_any, other_any, img_any, cot_any,
    weights_any, conv_any, stat_two_ref, mixed_any, resid_any, grad_any, e3_any, vout_ref, *refs,
):
    high, low = refs[0:4], refs[4:8]
    (k_one, k_two, w_ref, img_ref, cot_ref, conv_ref, pad_ref, act_t, resid_ref, normed_ref, normed_t,
     q_ref, k_ref, v_ref, p_ref, ds_ref, mixed_ref, top_ref, gm_ref, gq_ref, gk_ref, gv_ref, grad_ref, e3_ref, gw_ref,
     one_sems, two_sems, w_sems, in_sems, out_sems, gw_sem, gk_sems) = refs[8:]
    n, c = normed_ref.shape
    size = at_ref[0]
    gathered = (heads_any, mine_any, other_any)
    one_copies = start_kernel(at_ref, gathered, k_one, one_sems, 0)
    img_copy = pltpu.make_async_copy(img_any, img_ref, in_sems.at[0])
    cot_copy = pltpu.make_async_copy(cot_any, cot_ref, in_sems.at[1])
    img_copy.start()
    two_copies = start_kernel(at_ref, gathered, k_two, two_sems, 9 * c)
    w_copies = [fetch_rows(at_ref, gathered, w_ref, j * c, (18 + j) * c, c, w_sems.at[j]) for j in range(4)]
    cot_copy.start()
    leaving = []

    def leave(src, dst):
        copy = pltpu.make_async_copy(src, dst, out_sems.at[len(leaving)])
        copy.start()
        leaving.append(copy)

    mask = row_mask(size, c)
    zero = jnp.zeros((8, c), F32)

    bias_one = vec_ref[2:3, :]

    def finish_one(first, v, carry):
        v = v + bias_one
        x = jnp.where(pixel_mask(size, first, MB, c), v, 0.0)
        return v, (carry[0] + fold(x), carry[1] + fold(x * x))

    s1, s2 = conv(pad_one_ref, k_one, one_copies, conv_ref, MB, finish_one)
    leave(conv_ref, conv_any)
    leave(k_one, weights_any.at[pl.ds(0, 9 * c)])
    kept_one = leaving[-1]
    mean, scale = moments(s1, s2, size)
    put_stats(stat_two_ref, mean, scale)
    apply_norm(conv_ref, mean, scale * vec_ref[3:4, :], vec_ref[4:5, :], mask, pad_ref)
    put_transposed(act_t, pad_ref, SIDE, 0)

    bias_two = vec_ref[5:6, :]
    img_copy.wait()

    def finish_two(first, v, carry):
        v = v + bias_two + img_ref[pl.ds(first, MB), :].astype(F32)
        x = jnp.where(pixel_mask(size, first, MB, c), v, 0.0)
        return x, (carry[0] + fold(x), carry[1] + fold(x * x))

    s1, s2 = conv(pad_ref, k_two, two_copies, resid_ref, MB, finish_two)
    leave(resid_ref, resid_any)
    leave(k_two, weights_any.at[pl.ds(9 * c, 9 * c)])
    mean, scale = moments(s1, s2, size)
    gain = vec_ref[6:7, :]
    full_gain, shift = scale * gain, vec_ref[7:8, :]
    cot_copy.wait()

    def apply(h, carry):
        y = (resid_ref[rows(h), :] - mean) * full_gain + shift
        normed_ref[rows(h), :] = jnp.where(mask(h), y, 0.0).astype(BF16)
        t = jnp.where(mask(h), cot_ref[rows(h), :].astype(F32), 0.0)
        top_ref[rows(h), :] = t.astype(BF16)
        return carry + fold(t)

    top_sum = lax.fori_loop(0, SIDE, apply, zero, unroll=4)
    put_transposed(normed_t, normed_ref, 0, 0)

    for copy in w_copies:
        copy.wait()
    leave(w_ref, weights_any.at[pl.ds(18 * c, 4 * c)])
    factor = c ** (-0.5)
    wq, wk, wv, wo = (functools.partial(lambda j: w_ref[j * c : (j + 1) * c, :], j) for j in range(4))
    qb, vb = vec_ref[8:9, :], vec_ref[9:10, :]
    def project(m, carry):
        at = pl.ds(pl.multiple_of(m * PB, PB), PB)
        x = normed_ref[at, :]
        q_ref[at, :] = (dot(x, wq()) + qb).astype(BF16)
        k_ref[at, :] = dot(x, wk()).astype(BF16)
        v_ref[at, :] = (dot(x, wv()) + vb).astype(BF16)
        gm_ref[at, :] = dot_nt(top_ref[at, :], wo()).astype(BF16)
        return carry

    lax.fori_loop(0, n // PB, project, 0, unroll=1)

    spot = lax.broadcasted_iota(jnp.int32, (1, n), 1)
    key_bias = jnp.where(((spot >> 5) < size) & ((spot & (SIDE - 1)) < size), 0.0, -1e30)

    def queries(m, carry):
        at = pl.ds(pl.multiple_of(m * QB, QB), QB)
        s = dot_nt(q_ref[at, :], k_ref[...]) * factor + key_bias
        raised = jnp.exp(s - jnp.max(s, axis=1, keepdims=True))
        p = raised * (1.0 / jnp.sum(raised, axis=1, keepdims=True))
        low_p = p.astype(BF16)
        p_ref[at, :] = low_p
        mixed_ref[at, :] = dot(low_p, v_ref[...]).astype(BF16)
        gp = dot_nt(gm_ref[at, :], v_ref[...])
        weighted = jnp.sum(p * gp, axis=1, keepdims=True)
        ds = (p * ((gp - weighted) * factor)).astype(BF16)
        ds_ref[at, :] = ds
        gq_ref[at, :] = dot(ds, k_ref[...]).astype(BF16)
        return carry

    lax.fori_loop(0, n // QB, queries, 0)
    leave(mixed_ref, mixed_any)

    def keys(m, carry):
        at = pl.ds(pl.multiple_of(m * QB, QB), QB)
        gk_ref[at, :] = dot_tn(ds_ref[:, at], q_ref[...]).astype(BF16)
        gv_ref[at, :] = dot_tn(p_ref[:, at], gm_ref[...]).astype(BF16)
        return carry

    lax.fori_loop(0, n // QB, keys, 0)
    gw_ref[0:c, :] = dot(normed_t[...], gq_ref[...]).astype(BF16)
    gw_ref[c : 2 * c, :] = dot(normed_t[...], gk_ref[...]).astype(BF16)
    gw_ref[2 * c : 3 * c, :] = dot(normed_t[...], gv_ref[...]).astype(BF16)
    gw_ref[3 * c : 4 * c, :] = dot_tn(mixed_ref[...], top_ref[...]).astype(BF16)
    waits = [send_rows(gw_ref, 0, 18 * c, 4 * c, at_ref, (None, high), gw_sem)]

    def normed_grad(m, carry):
        su, sux, sq, sv = carry
        first = pl.multiple_of(m * PB, PB)
        at = pl.ds(first, PB)
        gq, gk, gv = gq_ref[at, :], gk_ref[at, :], gv_ref[at, :]
        u = dot_nt(gq, wq()) + dot_nt(gk, wk()) + dot_nt(gv, wv())
        u = jnp.where(pixel_mask(size, first, PB, c), u, 0.0)
        grad_ref[at, :] = u
        xhat = (resid_ref[at, :] - mean) * scale
        return su + fold(u), sux + fold(u * xhat), sq + fold(gq.astype(F32)), sv + fold(gv.astype(F32))

    su, sux, sq, sv = lax.fori_loop(0, n // PB, normed_grad, (zero, zero, zero, zero), unroll=1)
    count = (size * size * 16).astype(F32)
    both = group_total(total_of(su, sux) * gain) / count
    m1, m2 = both[0:1], both[1:2]
    clear_border(e3_ref)

    def back(h, carry):
        xhat = (resid_ref[rows(h), :] - mean) * scale
        g = (grad_ref[rows(h), :] * gain - m1 - xhat * m2) * scale + top_ref[rows(h), :].astype(F32)
        g = jnp.where(mask(h), g, 0.0)
        grad_ref[rows(h), :] = g
        put_shifted(e3_ref, h, g.astype(BF16).astype(F32), False)
        return carry + fold(g)

    sg = lax.fori_loop(0, SIDE, back, zero, unroll=2)
    leave(e3_ref, e3_any)
    leave(grad_ref, grad_any)
    vout_ref[...] = total_of(sg, sux, su, sq, sv, top_sum)
    still = [v for v in leaving if v is not kept_one]
    kept_one.wait()
    waits += kernel_gradient(act_t, e3_ref, k_one, 9 * c, at_ref, (low, high), gk_sems)
    for wait in waits + still:
        wait.wait()


def forward(at, pad_one, vec, gathered, img, cot):
    n, c = img.shape
    heads, mine, other = gathered
    half = (shape((8, 22 * c // 64, c), BF16), "a")

    def low(*dims):
        return pltpu.VMEM(dims, BF16)

    full = low(n, c)
    found = call(forward_body,
        [(shape((22 * c, c), BF16), "a"), (shape((n, c), F32), "a"), (shape((8, c), F32), "v"), (shape((n, c), BF16), "a"), (shape((n, c), F32), "a"),
         (shape((n, c), F32), "a"), (shape((n + 2 * SIDE, 3 * c), BF16), "a"), (shape((8, c), F32), "v")] + [half] * 8,
        [(at, "s"), (pad_one, "v"), (vec, "v"), (heads, "a"), (mine, "a"), (other, "a"), (img, "a"), (cot, "a")],
        [low(9 * c, c), low(9 * c, c), low(4 * c, c), full, full, pltpu.VMEM((n, c), F32), low(n + 2 * SIDE, c), low(c, n),
         pltpu.VMEM((n, c), F32), full, low(c, n), full, full, full, low(n, n), low(n, n), full, full, full, full, full, full,
         pltpu.VMEM((n, c), F32), low(n + 2 * SIDE, 3 * c), low(4 * c, c),
         pltpu.SemaphoreType.DMA((9,)), pltpu.SemaphoreType.DMA((9,)), pltpu.SemaphoreType.DMA((4,)),
         pltpu.SemaphoreType.DMA((2,)), pltpu.SemaphoreType.DMA((8,)), pltpu.SemaphoreType.DMA, pltpu.SemaphoreType.DMA((9,))],
        name="forward")
    return found[:8], found[8:12], found[12:16]


def kernel_gradient(act_t, e3_ref, stage, row, at_ref, rounds, sems):
    c, n = act_t.shape

    def one_row(dy, carry):
        lo = pl.multiple_of((2 - dy) * SIDE, SIDE)
        for dx in range(3):
            value = dot(act_t[...], e3_ref[pl.ds(lo, n), dx * c : (dx + 1) * c])
            stage[pl.ds(pl.multiple_of((3 * dy + dx) * c, c), c), :] = value.astype(BF16)
        for now in range(3):

            @pl.when(dy == now)
            def _(now=now):
                send_rows(stage, 3 * now * c, row + 3 * now * c, 3 * c, at_ref, rounds, sems.at[now])

        return carry

    lax.fori_loop(0, 3, one_row, 0, unroll=1)
    places = [stage.at[pl.ds(3 * dy * c, 3 * c)] for dy in range(3)]
    return [pltpu.make_async_copy(place, place, sems.at[dy]) for dy, place in enumerate(places)]


def conv_back(e3_ref, k_ref, copies, out_ref):
    n, c = out_ref.shape
    for dy in range(3):
        copies[dy].wait()
        lo = (2 - dy) * SIDE

        def block(m, carry, dy=dy, lo=lo):
            first = pl.multiple_of(m * MB, MB)
            value = None
            for dx in range(3):
                tap = 3 * dy + dx
                term = dot_nt(e3_ref[pl.ds(first + lo, MB), dx * c : (dx + 1) * c], k_ref[tap * c : (tap + 1) * c, :])
                value = term if value is None else value + term
            if dy > 0:
                value = value + out_ref[pl.ds(first, MB), :]
            out_ref[pl.ds(first, MB), :] = value
            return carry

        lax.fori_loop(0, n // MB, block, 0, unroll=4)


def norm_back_sums(src_ref, g_ref, mean, scale, gain, shift, mask, size):
    c = g_ref.shape[1]

    def sums(h, carry):
        xhat = (src_ref[rows(h), :].astype(F32) - mean) * scale
        y = xhat * gain + shift
        s = sigmoid(y)
        u = jnp.where(mask(h), g_ref[rows(h), :] * (s * (1.0 + y * (1.0 - s))), 0.0)
        g_ref[rows(h), :] = u
        return carry[0] + fold(u), carry[1] + fold(u * xhat)

    zero = jnp.zeros((8, c), F32)
    su, sux = lax.fori_loop(0, SIDE, sums, (zero, zero), unroll=2)
    count = (size * size * 16).astype(F32)
    both = group_total(total_of(su, sux) * gain) / count
    return su, sux, both[0:1], both[1:2]


def back_two_body(
    at_ref, e3_ref, vec_ref, stat_ref, k_any, conv_any, act_any, i0, i1, i2, i3,
    e3_any, vout_ref, o0, o1, o2, o3, g_ref, conv_ref, act_t, e3_out, k_vmem, sems, in_sems, out_sem, gk_sems,
):
    n, c = conv_ref.shape
    copies = start_copies(k_any, k_vmem, sems, 3, 9 * c)
    conv_copy = pltpu.make_async_copy(conv_any, conv_ref, in_sems.at[0])
    act_copy = pltpu.make_async_copy(act_any, act_t, in_sems.at[1])
    conv_copy.start()
    act_copy.start()
    size = at_ref[0]
    mask = row_mask(size, c)
    conv_back(e3_ref, k_vmem, copies, g_ref)
    conv_copy.wait()
    mean, scale = stat_ref[0:1, :], stat_ref[1:2, :]
    gain, shift = vec_ref[3:4, :], vec_ref[4:5, :]
    su, sux, m1, m2 = norm_back_sums(conv_ref, g_ref, mean, scale, gain, shift, mask, size)
    clear_border(e3_out)

    def apply(h, carry):
        xhat = (conv_ref[rows(h), :] - mean) * scale
        g = jnp.where(mask(h), (g_ref[rows(h), :] * gain - m1 - xhat * m2) * scale, 0.0)
        put_shifted(e3_out, h, g.astype(BF16).astype(F32), False)
        return carry + fold(g)

    sg = lax.fori_loop(0, SIDE, apply, jnp.zeros((8, c), F32), unroll=2)
    leaving = pltpu.make_async_copy(e3_out, e3_any, out_sem)
    leaving.start()
    vout_ref[...] = total_of(sg, sux, su)
    act_copy.wait()
    for wait in kernel_gradient(act_t, e3_out, k_vmem, 0, at_ref, ((o0, o1, o2, o3),), gk_sems):
        wait.wait()
    leaving.wait()


def back_two(at, e3, weights, vec, conv_out, stat, act, low):
    n, c = conv_out.shape
    half = shape(low[0].shape, BF16)
    e3_out, vout, *low = call(back_two_body,
        [(shape((n + 64, 3 * c), BF16), "a"), (shape((8, c), F32), "v")] + [(half, "a")] * 4,
        [(at, "s"), (e3, "v"), (vec, "v"), (stat, "v"), (weights, "a"), (conv_out, "a"), (act, "a")] + [(v, "a") for v in low],
        [pltpu.VMEM((n, c), F32), pltpu.VMEM((n, c), F32), pltpu.VMEM((c, n), BF16), pltpu.VMEM((n + 64, 3 * c), BF16),
         pltpu.VMEM((9 * c, c), BF16), pltpu.SemaphoreType.DMA((3,)), pltpu.SemaphoreType.DMA((2,)), pltpu.SemaphoreType.DMA,
         pltpu.SemaphoreType.DMA((9,))],
        name="back_two", aliases={7 + i: 2 + i for i in range(4)})
    return e3_out, vout, low


def back_one_body(
    size_ref, e3_ref, k_ref, vec_ref, img_ref, stat_ref, grad_ref, mixed_any, resid_any, both_any, vout_ref,
    g_ref, out_ref, rows_ref, mixed_ref, resid_ref, wo_ref, k_vmem, sems, in_sems, out_sems,
):
    n, c = img_ref.shape
    copies = start_copies(k_ref, k_vmem, sems, 3)
    bands, quarter = both_any.shape[0], both_any.shape[2]
    later = [
        pltpu.make_async_copy(src, dst, in_sems.at[i])
        for i, (src, dst) in enumerate(((mixed_any, mixed_ref), (resid_any, resid_ref), (k_ref.at[pl.ds(21 * c, c)], wo_ref)))
    ]
    for copy in later:
        copy.start()
    leaving = []

    def leave(src_ref, which):
        for j in range(bands):
            copy = pltpu.make_async_copy(src_ref.at[pl.ds(j * quarter, quarter)], both_any.at[j, which], out_sems.at[len(leaving)])
            copy.start()
            leaving.append(copy)

    size = size_ref[0]
    mask = row_mask(size, c)
    conv_back(e3_ref, k_vmem, copies, g_ref)
    for copy in later:
        copy.wait()

    def block_rows(m, carry):
        first = pl.multiple_of(m * MB, MB)
        at = pl.ds(first, MB)
        value = dot(mixed_ref[at, :], wo_ref[...]) + vec_ref[10:11, :] + resid_ref[at, :]
        rows_ref[at, :] = jnp.where(pixel_mask(size, first, MB, c), value, 0.0).astype(BF16)
        return carry

    lax.fori_loop(0, n // MB, block_rows, 0)
    leave(rows_ref, 0)
    mean, scale = stat_ref[0:1, :], stat_ref[1:2, :]
    gain, shift = vec_ref[0:1, :], vec_ref[1:2, :]
    su, sux, m1, m2 = norm_back_sums(img_ref, g_ref, mean, scale, gain, shift, mask, size)

    def apply(h, carry):
        xhat = (img_ref[rows(h), :].astype(F32) - mean) * scale
        g = (g_ref[rows(h), :] * gain - m1 - xhat * m2) * scale + grad_ref[rows(h), :]
        out_ref[rows(h), :] = jnp.where(mask(h), g, 0.0).astype(out_ref.dtype)
        return carry

    lax.fori_loop(0, SIDE, apply, 0, unroll=2)
    leave(out_ref, 1)
    vout_ref[...] = total_of(sux, su)
    for copy in leaving:
        copy.wait()


def back_one(at, e3, weights, vec, img, stat, grad_resid, mixed, resid, bands):
    n, c = img.shape
    low, full = pltpu.VMEM((n, c), BF16), pltpu.VMEM((n, c), F32)
    return call(back_one_body, [(shape((bands, 2, n // bands, c), BF16), "a"), (shape((8, c), F32), "v")],
        [(at, "s"), (e3, "v"), (weights, "a"), (vec, "v"), (img, "v"), (stat, "v"), (grad_resid, "v"), (mixed, "a"), (resid, "a")],
        [full, low, low, low, full, pltpu.VMEM((c, c), BF16), pltpu.VMEM((9 * c, c), BF16), pltpu.SemaphoreType.DMA((3,)),
         pltpu.SemaphoreType.DMA((3,)), pltpu.SemaphoreType.DMA((2 * bands,))],
        name="back_one")


ALL = ("img", "band")
CORE = [(b, b ^ 1) for b in range(4)]
ACROSS_Y = [(b, b ^ 2) for b in range(4)]
ACROSS_X = [(i, i ^ 1) for i in range(8)]

def after(value, *earlier, flops=0):
    def body(*refs):
        pass

    anywhere = pl.BlockSpec(memory_space=pl.ANY)
    return pl.pallas_call(
        body,
        out_shape=shape(value.shape, value.dtype),
        in_specs=[anywhere] * (1 + len(earlier)),
        out_specs=anywhere,
        input_output_aliases={0: 0},
        cost_estimate=pl.CostEstimate(flops=flops, bytes_accessed=0, transcendentals=0),
        name="after",
    )(value, *earlier)


def wide(*parts):
    total = parts[0].astype(F32)
    for part in parts[1:]:
        total = total + part.astype(F32)
    return total


SUMS_VMEM = VMEM_LIMIT


def add_parts(held, ready, terms):
    lead = ready.shape[:-2]

    def one(k, carry):
        spot = (k,) if len(lead) == 1 else (k // lead[1], k % lead[1])
        total = held[(0, *spot)].astype(F32)
        for t in range(1, terms):
            total = total + held[(t, *spot)].astype(F32)
        ready[spot] = total.astype(ready.dtype)
        return carry

    count = lead[0] if len(lead) == 1 else lead[0] * lead[1]
    lax.fori_loop(0, count, one, 0)


def start_terms(ins, terms, held, sems):
    copies = [pltpu.make_async_copy(ins[at].at[index], held.at[t], sems.at[t]) for t, (at, index) in enumerate(terms)]
    for copy in copies:
        copy.start()
    return copies


def sums_body(*refs, arrays, groups):
    count = len(groups)
    ins, outs, rest = refs[:arrays], refs[arrays : arrays + count], refs[arrays + count :]
    held, ready, in_sems, out_sems = rest[:count], rest[count : 2 * count], rest[2 * count : 3 * count], rest[-1]
    copies = [start_terms(ins, terms, held[g], in_sems[g]) for g, terms in enumerate(groups)]
    leaving = []
    for g, terms in enumerate(groups):
        for copy in copies[g]:
            copy.wait()
        add_parts(held[g], ready[g], len(terms))
        leaving.append(pltpu.make_async_copy(ready[g], outs[g], out_sems.at[g]))
        leaving[-1].start()
    for copy in leaving:
        copy.wait()


def indexed(groups):
    arrays, places = [], {}
    for terms in groups:
        for array, _ in terms:
            if id(array) not in places:
                places[id(array)] = len(arrays)
                arrays.append(array)
    return arrays, [[(places[id(array)], index) for array, index in terms] for terms in groups]


def sum_shape(array, index):
    return tuple(array.shape[i] for i in range(array.ndim) if i >= len(index) or index[i] == slice(None))


def block_sums(groups, dtype, name):
    arrays, places = indexed(groups)
    dims = [sum_shape(*terms[0]) for terms in groups]
    return call(functools.partial(sums_body, arrays=len(arrays), groups=places),
        [(shape(d, dtype), "a") for d in dims],
        [(v, "a") for v in arrays],
        [pltpu.VMEM((len(terms), *d), BF16) for terms, d in zip(groups, dims)] + [pltpu.VMEM(d, dtype) for d in dims]
        + [pltpu.SemaphoreType.DMA((len(terms),)) for terms in groups] + [pltpu.SemaphoreType.DMA((len(groups),))],
        name=name, vmem=SUMS_VMEM)


def chip_sends(arrays, *earlier):
    mine_a, mine_b, theirs_a, theirs_b = arrays
    half, c = mine_a.shape[1:]
    dims = (2, 2, 2, half, c)
    if earlier:
        theirs_a, theirs_b = after(theirs_a, *earlier), after(theirs_b, *earlier)
    got = [lax.ppermute(v, "band", CORE) for v in (theirs_a, theirs_b)]
    pair_a = (mine_a.reshape(dims), got[0].reshape(dims))
    pair_b = (mine_b.reshape(dims), got[1].reshape(dims))
    every = slice(None)
    sends = block_sums([[(v, (1,)) for v in pair_a], [(v, (every, 1)) for v in pair_b]], BF16, "chip_sums")
    return pair_a, pair_b, *sends


def plane_swap(send_a, send_b):
    return lax.ppermute(send_a, "img", ACROSS_X), lax.ppermute(send_b, "band", ACROSS_Y)


def plane_sends(pair_a, pair_b, got_a, got_b):
    kept_a = [(v, (0, 0)) for v in pair_a] + [(got_a, (0,))]
    kept_b = [(v, (0, 0)) for v in pair_b] + [(got_b, (0,))]
    sends = block_sums(
        [[(v, (0, 1)) for v in pair_a] + [(got_a, (1,))], [(v, (1, 0)) for v in pair_b] + [(got_b, (1,))]], BF16, "row_sums"
    )
    return kept_a, kept_b, *sends


def plane_parts(kept_a, kept_b, next_a, next_b, *earlier):
    last_a = lax.ppermute(next_a, "band", ACROSS_Y)
    last_b = lax.ppermute(next_b, "img", ACROSS_X)
    if earlier:
        last_a, last_b = after(last_a, *earlier), after(last_b, *earlier)
    return [kept_a + [(last_a, ())], kept_b + [(last_b, ())]]


def owner_body(at_ref, *refs, arrays, groups):
    ins, (own, *sent), rest = refs[:arrays], refs[arrays : arrays + 4], refs[arrays + 4 :]
    high_a, high_b, held_a, held_b, total_a, total_b, sems_a, sems_b, high_sems = rest
    copies = [start_terms(ins, groups[0], held_a, sems_a), start_terms(ins, groups[1], held_b, sems_b)]
    highs = [pltpu.make_async_copy(ins[groups[2 + i][0][0]], ref, high_sems.at[i]) for i, ref in enumerate((high_a, high_b))]
    for copy in highs:
        copy.start()
    for i, (held, total) in enumerate(((held_a, total_a), (held_b, total_b))):
        for copy in copies[i]:
            copy.wait()
        add_parts(held, total, len(groups[i]))
    for copy in highs:
        copy.wait()
    half = total_a.shape[1]
    for step, ref in enumerate((own, *sent)):
        plane = at_ref[4] ^ step
        for upper, pair in enumerate(((total_a, total_b), (high_a, high_b))):

            @pl.when((plane >> 1) == upper)
            def _(ref=ref, pair=pair, plane=plane):
                for tail, part in enumerate(pair):
                    ref[tail * half : (tail + 1) * half, :] = part[plane & 1].astype(ref.dtype)


def owner_parts(at, low, high):
    groups = low + [[(v, ())] for v in high]
    arrays, places = indexed(groups)
    half, c = high[0].shape[1:]
    sums = pltpu.VMEM((2, half, c), F32)
    held = pltpu.VMEM((len(low[0]), 2, half, c), BF16)
    sems = pltpu.SemaphoreType.DMA((len(low[0]),))
    own, *sent = call(functools.partial(owner_body, arrays=len(arrays), groups=places),
        [(shape((2 * half, c), F32), "v")] + [(shape((2 * half, c), BF16), "v")] * 3,
        [(at, "s")] + [(v, "a") for v in arrays],
        [sums, sums, held, held, sums, sums, sems, sems, pltpu.SemaphoreType.DMA((2,))],
        name="owner_sums", vmem=SUMS_VMEM)
    got = [lax.ppermute(v, "img", [(i, i ^ (2 * step)) for i in range(8)]) for v, step in zip(sent, (1, 2, 3))]
    return [own] + got, sent


def plane_gather(own):
    z = [lax.ppermute(own, "img", [(i, i ^ (2 * step)) for i in range(8)]) for step in (1, 2, 3)]
    first, last = jnp.stack([own, z[0]]), jnp.stack([z[1], z[2]])
    first = jnp.concatenate([first, lax.ppermute(first, "band", ACROSS_Y)])
    last = jnp.concatenate([last, lax.ppermute(last, "img", ACROSS_X)])
    mine = jnp.concatenate([first, lax.ppermute(first, "img", ACROSS_X), last, lax.ppermute(last, "band", ACROSS_Y)])
    return mine, lax.ppermute(mine, "band", CORE)


def four_sum(v, axis, steps):
    a, b, c = (lax.ppermute(v, axis, [(i, i ^ step) for i in range(lax.axis_size(axis))]) for step in steps)
    return (v + a) + (b + c)


def whole_image(
    images,
    cotangent,
    sizes,
    matrix_weight,
    matrix_momentum,
    matrix_average,
    vector_weight,
    vector_momentum,
    vector_average,
):
    batch, height, width, c = images.shape
    n = width * width
    mine = lax.axis_index("band")
    place = lax.axis_index("img")
    at = jnp.stack([lax.dynamic_index_in_dim(sizes, mine, 0, False), place % 2, mine // 2, mine % 2, place // 2])

    def to_image(field):
        parts = field.reshape(batch, height * width, c)
        return lax.all_to_all(parts, "band", 0, 0, tiled=True).reshape(n, c)

    own = matrix_weight.astype(BF16).reshape(-1, c)
    head = 288
    gathered = (lax.all_gather(own[:head], ALL, axis=0, tiled=True), *plane_gather(own[head:]))
    img = to_image(images)
    cot = to_image(cotangent)
    pad_one, act_t, stat_one = act_one(at, img, vector_weight)
    (weights, conv_out, stat_two, mixed, resid, grad_resid, e3_two, v3), high, low = forward(
        at, pad_one, vector_weight, gathered, img, cot
    )
    high = chip_sends(high)
    e3_two = after(e3_two, high[2], high[3])
    swapped = plane_swap(high[2], high[3])
    e3_one, v2, low = back_two(at, e3_two, weights, vector_weight, conv_out, stat_two, act_t, low)
    low = chip_sends(low, *swapped)
    high = plane_sends(*high[:2], *swapped)
    low_sends = low[2:4]
    e3_one = after(e3_one, *low_sends)
    swapped = plane_swap(low[2], low[3])
    both, v1 = back_one(at, e3_one, weights, vector_weight, img, stat_one, grad_resid, mixed, resid, batch)
    vecs = jnp.stack([v1[0], v1[1], v2[0], v2[1], v2[2], v3[0], v3[1], v3[2], v3[3], v3[4], v3[5]])
    low = plane_sends(*low[:2], *(after(v, v1) for v in swapped))
    vecs = four_sum(after(vecs, low[2], low[3]), "img", (2, 4, 6))
    high = block_sums(plane_parts(*high, low[2], low[3]), F32, "plane_sums")
    parts, sent = owner_parts(at, plane_parts(*low, vecs), high)
    given = lax.all_to_all(after(both, *sent), "band", 0, 0, tiled=True)
    block_out = given[:, 0].reshape(images.shape)
    input_grad = given[:, 1].reshape(images.shape).astype(F32)
    vecs = after(vecs, parts[1])
    vecs = vecs + lax.ppermute(vecs, "img", ACROSS_X)
    vector_grads = four_sum(vecs, "band", (1, 2, 3))
    vector_moments = MOMENTUM * vector_momentum + vector_grads
    vector_masters = vector_weight - LR_VECTOR * (vector_grads + MOMENTUM * vector_moments)
    vector_means = AVERAGE * vector_average + (1.0 - AVERAGE) * vector_masters
    matrix_grads = wide(*parts).reshape(-1)
    matrix_moments = MOMENTUM * matrix_momentum + matrix_grads
    matrix_masters = matrix_weight - LR_MATRIX * (matrix_grads + MOMENTUM * matrix_moments)
    matrix_means = AVERAGE * matrix_average + (1.0 - AVERAGE) * matrix_masters
    return (
        block_out,
        input_grad,
        matrix_grads,
        matrix_moments,
        matrix_means,
        matrix_masters,
        vector_grads,
        vector_moments,
        vector_means,
        vector_masters,
    )


def solution(mesh):
    fits = mesh.shape["img"] == 8 and mesh.shape["band"] == 4

    def per_device(images, *rest):
        step = whole_image if fits and images.shape[:3] == (4, 8, SIDE) else banded
        return step(images, *rest)

    return jax.shard_map(
            per_device,
        mesh=mesh,
        in_specs=(
            P("img", "band", None, None),
            P("img", "band", None, None),
            P("img"),
            P(("img", "band")),
            P(("img", "band")),
            P(("img", "band")),
            P(),
            P(),
            P(),
        ),
        out_specs=(
            P("img", "band", None, None),
            P("img", "band", None, None),
            P(("img", "band")),
            P(("img", "band")),
            P(("img", "band")),
            P(("img", "band")),
            P(),
            P(),
            P(),
            P(),
        ),
        check_vma=False,
    )
```

```python
import functools

import jax
import jax.numpy as jnp
from jax import lax
from jax.experimental import pallas as pl
from jax.experimental.pallas import tpu as pltpu
from jax.sharding import PartitionSpec as P

GROUPS = 32


EPS = 1e-06
MOMENTUM = 0.9
LR_MATRIX = 4e-05
LR_VECTOR = 0.0001
AVERAGE = 0.75


def extended(array, sides, width):
    for axis, dim in sides:
        count, length = (lax.axis_size(axis), array.shape[dim])
        up = [(i, (i + 1) % count) for i in range(count - 1)]
        down = [(j, i) for i, j in up]
        last = lax.slice_in_dim(array, length - width, length, axis=dim)
        initial = lax.slice_in_dim(array, 0, width, axis=dim)
        before = lax.ppermute(last, axis, up)
        after = lax.ppermute(initial, axis, down)
        array = jnp.concatenate([before, array, after], axis=dim)
    return array


def split_groups(field):
    return field.reshape(field.shape[:3] + (GROUPS, field.shape[3] // GROUPS))


def group_sums(field, mask):
    shaped = split_groups(field)
    weighted = shaped * mask[..., None]
    return (jnp.sum(weighted, axis=(1, 2, 4)), jnp.sum(weighted * shaped, axis=(1, 2, 4)))


def group_apply(field, sums, count, gain, shift):
    center = sums[0] / count[:, None]
    spread = sums[1] / count[:, None] - center * center
    scale = lax.rsqrt(spread + EPS)
    shaped = split_groups(field)
    normed = (shaped - center[:, None, None, :, None]) * scale[:, None, None, :, None]
    return normed.reshape(field.shape) * gain + shift


def normalize(field, mask, count, gain, shift):
    sums = lax.psum(group_sums(field, mask), "band")
    return (group_apply(field, sums, count, gain, shift), sums)


def normalize_back(field, sums, mask, count, gain, shift, upstream):
    _, pull = jax.vjp(
        lambda field_in, sums_in, gain_in, shift_in: group_apply(
            field_in, sums_in, count, gain_in, shift_in
        ),
        field,
        sums,
        gain,
        shift,
    )
    direct, grad_sums, grad_gain, grad_shift = pull(upstream)
    grad_sums = lax.psum(grad_sums, "band")
    _, pull_sums = jax.vjp(lambda field_in: group_sums(field_in, mask), field)
    return (direct + pull_sums(grad_sums)[0], grad_gain, grad_shift)


def activate(field, mask):
    return jax.nn.silu(field) * mask


def activate_back(field, mask, upstream):
    _, pull = jax.vjp(lambda inner: activate(inner, mask), field)
    return pull(upstream)[0]


def widen(field):
    return jnp.pad(field, ((0, 0), (0, 0), (1, 1), (0, 0)))


def taps(padded, kernel, height, width):
    total = jnp.zeros(padded.shape[:1] + (height, width, kernel.shape[2]), jnp.float32)
    for tap in range(9):
        row, column = (tap // 3, tap % 3)
        total = total + jnp.einsum(
            "ghwc,cd->ghwd",
            padded[:, row : row + height, column : column + width],
            kernel[tap],
            preferred_element_type=jnp.float32,
        )
    return total


def conv_forward(low_field, kernel):
    padded = widen(extended(low_field, (("band", 1),), 1))
    return (taps(padded, kernel, low_field.shape[1], low_field.shape[2]), padded)


def conv_backward(low_grad, kernel, padded):
    height, width = (low_grad.shape[1], low_grad.shape[2])
    grad_pad = widen(extended(low_grad, (("band", 1),), 1))
    flipped = jnp.swapaxes(kernel[::-1], 1, 2)
    grad_in = taps(grad_pad, flipped, height, width)
    pieces = []
    for tap in range(9):
        row, column = (tap // 3, tap % 3)
        pieces.append(
            jnp.einsum(
                "ghwc,ghwd->cd",
                padded[:, row : row + height, column : column + width],
                low_grad,
                preferred_element_type=jnp.float32,
            )
        )
    return (grad_in, jnp.stack(pieces))


def attend(query_low, key_full, key_valid, factor):
    score_matrix = (
        jnp.einsum("gqc,gkc->gqk", query_low, key_full, preferred_element_type=jnp.float32) * factor
    )
    score_matrix = jnp.where(key_valid[:, None, :], score_matrix, -1e30)
    top = jnp.max(score_matrix, axis=2, keepdims=True)
    raised = jnp.exp(score_matrix - top)
    total = jnp.sum(raised, axis=2, keepdims=True)
    return (raised / total, top, total)


def banded(
    images,
    cotangent,
    sizes,
    matrix_weight,
    matrix_momentum,
    matrix_average,
    vector_weight,
    vector_momentum,
    vector_average,
):
    batch, height, width, channels = images.shape
    square = channels * channels
    queries = height * width
    positions = width * width
    factor = channels ** (-0.5)
    weights = lax.all_gather(
        matrix_weight.astype(jnp.bfloat16), ("img", "band"), axis=0, tiled=True
    )
    kernel_one = weights[: 9 * square].reshape(9, channels, channels)
    kernel_two = weights[9 * square : 18 * square].reshape(9, channels, channels)
    attn_in = weights[18 * square : 21 * square].reshape(3, channels, channels)
    attention_output = weights[21 * square :].reshape(channels, channels)
    lines = lax.axis_index("band") * height + jnp.arange(height)
    across = jnp.arange(width)
    limit = sizes[:, None, None]
    inside = (lines[None, :, None] < limit) & (across[None, None, :] < limit)
    mask = jnp.where(inside, 1.0, 0.0).astype(jnp.float32)[..., None]
    count = (sizes * sizes * (channels // GROUPS)).astype(jnp.float32)
    spots = jnp.arange(positions)
    key_valid = ((spots // width)[None, :] < sizes[:, None]) & (
        (spots % width)[None, :] < sizes[:, None]
    )
    start = images.astype(jnp.float32) * mask
    norm_one, sums_one = normalize(start, mask, count, vector_weight[0], vector_weight[1])
    act_one = activate(norm_one, mask).astype(jnp.bfloat16)
    conv_raw, padded_one = conv_forward(act_one, kernel_one)
    conv_out = conv_raw + vector_weight[2]
    norm_two, sums_two = normalize(conv_out, mask, count, vector_weight[3], vector_weight[4])
    act_two = activate(norm_two, mask).astype(jnp.bfloat16)
    conv_raw, padded_two = conv_forward(act_two, kernel_two)
    resid = (start + conv_raw + vector_weight[5]) * mask
    norm_three, sums_three = normalize(resid, mask, count, vector_weight[6], vector_weight[7])
    normed = (norm_three * mask).astype(jnp.bfloat16).reshape(batch, queries, channels)
    projected = jnp.einsum("gqc,jcd->jgqd", normed, attn_in, preferred_element_type=jnp.float32)
    query_low = (projected[0] + vector_weight[8]).astype(jnp.bfloat16)
    key_low = projected[1].astype(jnp.bfloat16)
    value_low = (projected[2] + vector_weight[9]).astype(jnp.bfloat16)
    key_full, value_full = (
        lax.all_gather(key_low, "band", axis=1, tiled=True),
        lax.all_gather(value_low, "band", axis=1, tiled=True),
    )
    probability_rows, row_top, row_total = attend(query_low, key_full, key_valid, factor)
    mixed_values = jnp.einsum(
        "gqk,gkc->gqc",
        probability_rows.astype(jnp.bfloat16),
        value_full,
        preferred_element_type=jnp.float32,
    ).astype(jnp.bfloat16)
    output_rows = (
        jnp.einsum(
            "gqc,cd->gqd", mixed_values, attention_output, preferred_element_type=jnp.float32
        )
        + vector_weight[10]
    )
    block_out = ((resid + output_rows.reshape(images.shape)) * mask).astype(jnp.bfloat16)
    grad_top = cotangent.astype(jnp.float32) * mask
    grad_proj = grad_top.reshape(batch, queries, channels)
    grad_proj_low = grad_proj.astype(jnp.bfloat16)
    grad_out_weight = jnp.einsum(
        "gqc,gqd->cd", mixed_values, grad_proj_low, preferred_element_type=jnp.float32
    )
    grad_mixed = jnp.einsum(
        "gqd,cd->gqc", grad_proj_low, attention_output, preferred_element_type=jnp.float32
    ).astype(jnp.bfloat16)
    back_keys, back_values = (
        lax.all_gather(key_low, "band", axis=1, tiled=True),
        lax.all_gather(value_low, "band", axis=1, tiled=True),
    )
    back_probs = attend(query_low, back_keys, key_valid, factor)[0]
    grad_probs = jnp.einsum(
        "gqc,gkc->gqk", grad_mixed, back_values, preferred_element_type=jnp.float32
    )
    weighted_sum = jnp.sum(back_probs * grad_probs, axis=2, keepdims=True)
    grad_scores = back_probs * (grad_probs - weighted_sum)
    grad_scores_low = (grad_scores * factor).astype(jnp.bfloat16)
    grad_query = jnp.einsum(
        "gqk,gkc->gqc", grad_scores_low, back_keys, preferred_element_type=jnp.float32
    ).astype(jnp.bfloat16)
    key_terms = jnp.einsum(
        "gqk,gqc->gkc", grad_scores_low, query_low, preferred_element_type=jnp.float32
    )
    value_terms = jnp.einsum(
        "gqk,gqc->gkc",
        back_probs.astype(jnp.bfloat16),
        grad_mixed,
        preferred_element_type=jnp.float32,
    )
    grad_key, grad_value = (
        lax.psum_scatter(
            key_terms.astype(jnp.bfloat16), "band", scatter_dimension=1, tiled=True
        ).astype(jnp.float32),
        lax.psum_scatter(
            value_terms.astype(jnp.bfloat16), "band", scatter_dimension=1, tiled=True
        ).astype(jnp.float32),
    )
    grad_value_low = grad_value.astype(jnp.bfloat16)
    grads_low = jnp.stack([grad_query, grad_key.astype(jnp.bfloat16), grad_value_low])
    grad_in_weights = jnp.einsum(
        "gqc,jgqd->jcd", normed, grads_low, preferred_element_type=jnp.float32
    )
    grad_normed = (
        jnp.einsum("jgqd,jcd->gqc", grads_low, attn_in, preferred_element_type=jnp.float32).reshape(
            images.shape
        )
        * mask
    )
    grad_resid_norm, grad_gain_three, grad_shift_three = normalize_back(
        resid, sums_three, mask, count, vector_weight[6], vector_weight[7], grad_normed
    )
    grad_resid = (grad_top + grad_resid_norm) * mask
    grad_act_two, grad_kernel_two = conv_backward(
        grad_resid.astype(jnp.bfloat16), kernel_two, padded_two
    )
    grad_norm_two = activate_back(norm_two, mask, grad_act_two)
    grad_conv_out, grad_gain_two, grad_shift_two = normalize_back(
        conv_out, sums_two, mask, count, vector_weight[3], vector_weight[4], grad_norm_two
    )
    grad_act_one, grad_kernel_one = conv_backward(
        grad_conv_out.astype(jnp.bfloat16), kernel_one, padded_one
    )
    grad_norm_one = activate_back(norm_one, mask, grad_act_one)
    grad_start, grad_gain_one, grad_shift_one = normalize_back(
        start, sums_one, mask, count, vector_weight[0], vector_weight[1], grad_norm_one
    )
    input_grad = (grad_resid + grad_start) * mask
    vector_terms = jnp.stack(
        [
            grad_gain_one,
            grad_shift_one,
            jnp.sum(grad_conv_out, axis=(0, 1, 2)),
            grad_gain_two,
            grad_shift_two,
            jnp.sum(grad_resid, axis=(0, 1, 2)),
            grad_gain_three,
            grad_shift_three,
            jnp.sum(grad_query, axis=(0, 1), dtype=jnp.float32),
            jnp.sum(grad_value_low, axis=(0, 1), dtype=jnp.float32),
            jnp.sum(grad_proj, axis=(0, 1)),
        ]
    )
    vector_grads = lax.psum(vector_terms, ("img", "band"))
    grad_flat = jnp.concatenate(
        [
            grad_kernel_one.reshape(-1),
            grad_kernel_two.reshape(-1),
            grad_in_weights.reshape(-1),
            grad_out_weight.reshape(-1),
        ]
    )
    matrix_grads = lax.psum_scatter(grad_flat, ("img", "band"), scatter_dimension=0, tiled=True)
    matrix_moments = MOMENTUM * matrix_momentum + matrix_grads
    matrix_masters = matrix_weight - LR_MATRIX * (matrix_grads + MOMENTUM * matrix_moments)
    matrix_means = AVERAGE * matrix_average + (1.0 - AVERAGE) * matrix_masters
    vector_moments = MOMENTUM * vector_momentum + vector_grads
    vector_masters = vector_weight - LR_VECTOR * (vector_grads + MOMENTUM * vector_moments)
    vector_means = AVERAGE * vector_average + (1.0 - AVERAGE) * vector_masters
    return (
        block_out,
        input_grad,
        matrix_grads,
        matrix_moments,
        matrix_means,
        matrix_masters,
        vector_grads,
        vector_moments,
        vector_means,
        vector_masters,
    )


F32 = jnp.float32
BF16 = jnp.bfloat16
SIDE = 32
VMEM_LIMIT = 58 * 1024 * 1024


def dot(a, b):
    return lax.dot_general(a, b, (((1,), (0,)), ((), ())), preferred_element_type=F32)


def dot_nt(a, b):
    return lax.dot_general(a, b, (((1,), (1,)), ((), ())), preferred_element_type=F32)


def dot_tn(a, b):
    return lax.dot_general(a, b, (((0,), (0,)), ((), ())), preferred_element_type=F32)


def call(body, outs, ins, scratch=(), flops=0, name=None, aliases=None, vmem=VMEM_LIMIT):
    spaces = {"v": pl.BlockSpec(memory_space=pltpu.VMEM), "s": pl.BlockSpec(memory_space=pltpu.SMEM),
              "a": pl.BlockSpec(memory_space=pl.ANY)}
    return pl.pallas_call(
        body,
        out_shape=[o for o, _ in outs],
        in_specs=[spaces[s] for _, s in ins],
        out_specs=[spaces[s] for _, s in outs],
        scratch_shapes=list(scratch),
        input_output_aliases=aliases or {},
        compiler_params=pltpu.CompilerParams(vmem_limit_bytes=vmem),
        cost_estimate=pl.CostEstimate(flops=flops, bytes_accessed=0, transcendentals=0),
        name=name,
    )(*[a for a, _ in ins])


def shape(dims, dtype):
    return jax.ShapeDtypeStruct(dims, dtype)


def fold(x):
    return jnp.sum(x.reshape(x.shape[0] // 8, 8, x.shape[1]), axis=0)


def group_total(x):
    lane = lax.broadcasted_iota(jnp.int32, x.shape, 1)
    width = x.shape[1]
    for s in (1, 2, 4, 8):
        up = pltpu.roll(x, width - s, 1)
        down = pltpu.roll(x, s, 1)
        x = x + jnp.where((lane & s) == 0, up, down)
    return x


def total_of(*parts):
    rows = [jnp.sum(p, axis=0, keepdims=True) for p in parts]
    pad = jnp.zeros((8 - len(rows), rows[0].shape[1]), F32)
    return jnp.concatenate(rows + [pad], axis=0)


def moments(s1, s2, size):
    count = (size * size * 16).astype(F32)
    both = group_total(total_of(s1, s2)) / count
    mean = both[0:1]
    spread = both[1:2] - mean * mean
    return mean, lax.rsqrt(spread + EPS)


def row_mask(size, channels):
    across = lax.broadcasted_iota(jnp.int32, (SIDE, channels), 0)
    inside = across < size
    return lambda h: inside & (h < size)


def sigmoid(y):
    return 0.5 * jnp.tanh(0.5 * y) + 0.5


def rows(h):
    return pl.ds(pl.multiple_of(h * SIDE, SIDE), SIDE)


def put_shifted(ref, h, r, forward):
    channels = r.shape[1]
    w = lax.broadcasted_iota(jnp.int32, r.shape, 0)
    before = jnp.where(w == 0, 0.0, pltpu.roll(r, 1, 0)).astype(BF16)
    after = jnp.where(w == SIDE - 1, 0.0, pltpu.roll(r, SIDE - 1, 0)).astype(BF16)
    first, last = (before, after) if forward else (after, before)
    at = pl.ds(pl.multiple_of((h + 1) * SIDE, SIDE), SIDE)
    ref[at, 0:channels] = first
    ref[at, channels : 2 * channels] = r.astype(BF16)
    ref[at, 2 * channels :] = last


def clear_border(ref):
    zero = jnp.zeros((SIDE, ref.shape[1]), BF16)
    ref[0:SIDE, :] = zero
    ref[(SIDE + 1) * SIDE :, :] = zero


def put_transposed(ref, src_ref, row0, lane0):
    channels, count = ref.shape
    for j in range(count // 256):
        block = src_ref[row0 + j * 256 : row0 + (j + 1) * 256, lane0 : lane0 + channels]
        ref[:, j * 256 : (j + 1) * 256] = block.T


def act_one_body(size_ref, img_ref, vec_ref, pad_ref, at_ref, stat_ref):
    size = size_ref[0]
    channels = img_ref.shape[1]
    mask = row_mask(size, channels)

    def sums(h, carry):
        x = jnp.where(mask(h), img_ref[rows(h), :].astype(F32), 0.0)
        return carry[0] + fold(x), carry[1] + fold(x * x)

    zero = jnp.zeros((8, channels), F32)
    s1, s2 = lax.fori_loop(0, SIDE, sums, (zero, zero), unroll=2)
    mean, scale = moments(s1, s2, size)
    stat_ref[0:1, :] = mean
    stat_ref[1:2, :] = scale
    stat_ref[2:8, :] = jnp.zeros((6, channels), F32)
    apply_norm(img_ref, mean, scale * vec_ref[0:1, :], vec_ref[1:2, :], mask, pad_ref)
    put_transposed(at_ref, pad_ref, SIDE, 0)


def apply_norm(src_ref, mean, scale, shift, mask, pad_ref):
    clear_border(pad_ref)

    def apply(h, carry):
        y = (src_ref[rows(h), :].astype(F32) - mean) * scale + shift
        at = pl.ds(pl.multiple_of((h + 1) * SIDE, SIDE), SIDE)
        pad_ref[at, :] = jnp.where(mask(h), y * sigmoid(y), 0.0).astype(BF16)
        return carry

    lax.fori_loop(0, SIDE, apply, 0, unroll=4)


def act_one(size, img, vec):
    n, c = img.shape
    return call(act_one_body,
        [(shape((n + 64, c), BF16), "v"), (shape((c, n), BF16), "v"), (shape((8, c), F32), "v")],
        [(size, "s"), (img, "v"), (vec, "v")], name="act_one")


MB = 256


def start_copies(src_ref, dst_ref, sems, parts, offset=0):
    length = dst_ref.shape[0] // parts
    copies = [
        pltpu.make_async_copy(src_ref.at[pl.ds(offset + p * length, length)], dst_ref.at[pl.ds(p * length, length)], sems.at[p])
        for p in range(parts)
    ]
    for copy in copies:
        copy.start()
    return copies


COLUMNS = (1, 0, 2)


def fetch_rows(at_ref, gathered, dst_ref, base, row, count, sem):
    heads, mine, other = gathered
    tail = mine.shape[1]
    head = heads.shape[0] // 32
    block = head + tail
    for owner in range(row // block, (row + count - 1) // block + 1):
        first = owner * block
        lo, hi = max(row, first), min(row + count, first + head)
        if lo < hi:
            inside = pl.ds(base + lo - row, hi - lo)
            pltpu.make_async_copy(heads.at[pl.ds(owner * head + lo - first, hi - lo)], dst_ref.at[inside], sem).start()
        lo, hi = max(row, first + head), min(row + count, first + block)
        if lo >= hi:
            continue
        inside = pl.ds(base + lo - row, hi - lo)
        z, x, y, c = at_ref[4] ^ (owner >> 3), at_ref[1] ^ ((owner >> 2) & 1), at_ref[2] ^ ((owner >> 1) & 1), owner & 1
        slot = jnp.where(z < 2, x * 4 + y * 2 + z, 6 + y * 4 + x * 2 + z)
        place = pl.ds(lo - first - head, hi - lo)
        for far, ref in enumerate((mine, other)):

            @pl.when((at_ref[3] ^ c) == far)
            def _(ref=ref, place=place, inside=inside, slot=slot):
                pltpu.make_async_copy(ref.at[slot, place], dst_ref.at[inside], sem).start()

    whole = dst_ref.at[pl.ds(base, count)]
    return pltpu.make_async_copy(whole, whole, sem)


def start_kernel(at_ref, gathered, dst_ref, sems, row):
    c = dst_ref.shape[1]
    copies = {}
    for dx in COLUMNS:
        for dy in range(3):
            tap = 3 * dy + dx
            copies[tap] = fetch_rows(at_ref, gathered, dst_ref, tap * c, row + tap * c, c, sems.at[tap])
    return copies


def conv(pad_ref, k_ref, copies, out_ref, mb, finish):
    n, c = out_ref.shape
    zero = jnp.zeros((8, c), F32)
    carry = (zero, zero)
    across = lax.broadcasted_iota(jnp.int32, (mb, c), 0) & (SIDE - 1)
    for dx in COLUMNS:
        for dy in range(3):
            copies[3 * dy + dx].wait()

        def block(m, carry, dx=dx):
            first = pl.multiple_of(m * mb, mb)
            at = pl.ds(first, mb)
            value = None
            for dy in range(3):
                tap = 3 * dy + dx
                term = dot(pad_ref[pl.ds(first + dy * SIDE, mb), :], k_ref[tap * c : (tap + 1) * c, :])
                value = term if value is None else value + term
            if dx == 0:
                value = jnp.where(across == 0, 0.0, pltpu.roll(value, 1, 0))
            if dx == 2:
                value = jnp.where(across == SIDE - 1, 0.0, pltpu.roll(value, mb - 1, 0))
            if dx != COLUMNS[0]:
                value = value + out_ref[at, :]
            if dx == COLUMNS[-1]:
                value, carry = finish(first, value, carry)
            out_ref[at, :] = value
            return carry

        carry = lax.fori_loop(0, n // mb, block, carry, unroll=2)
    return carry


def pixel_mask(size, first, count, c):
    place = lax.broadcasted_iota(jnp.int32, (count, c), 0) + first
    return ((place >> 5) < size) & ((place & (SIDE - 1)) < size)


def put_stats(stat_ref, mean, scale):
    stat_ref[...] = jnp.concatenate([mean, scale, jnp.zeros((6, mean.shape[1]), F32)], axis=0)


def pieces_of(row, count, half):
    found = []
    for spot in range(row // half, (row + count - 1) // half + 1):
        found.append((spot, max(row, spot * half), min(row + count, (spot + 1) * half)))
    return found


def send_rows(stage, base, row, count, at_ref, rounds, sem):
    half = rounds[-1][0].shape[1]
    for spot, lo, hi in pieces_of(row, count, half):
        owner, tail = spot // 2, spot % 2
        refs, inner = rounds[owner // 16], owner % 16
        z, x, y, c = inner // 8, (inner >> 2) & 1, (inner >> 1) & 1, inner & 1
        index = ((at_ref[1] ^ x) * 2 + (at_ref[2] ^ y)) * 2 + z
        source = stage.at[pl.ds(base + lo - row, hi - lo)]
        place = pl.ds(lo - spot * half, hi - lo)
        for other in range(2):

            @pl.when((at_ref[3] ^ c) == other)
            def _(ref=refs[2 * other + tail], source=source, place=place):
                pltpu.make_async_copy(source, ref.at[index, place], sem).start()

    return pltpu.make_async_copy(stage.at[pl.ds(base, count)], stage.at[pl.ds(base, count)], sem)


QB = 1024
PB = 512


def forward_body(
    at_ref, pad_one_ref, vec_ref, heads_any, mine_any, other_any, img_any, cot_any,
    weights_any, conv_any, stat_two_ref, mixed_any, resid_any, grad_any, e3_any, vout_ref, *refs,
):
    high, low = refs[0:4], refs[4:8]
    (k_one, k_two, w_ref, img_ref, cot_ref, conv_ref, pad_ref, act_t, resid_ref, normed_ref, normed_t,
     q_ref, k_ref, v_ref, p_ref, ds_ref, mixed_ref, top_ref, gm_ref, gq_ref, gk_ref, gv_ref, grad_ref, e3_ref, gw_ref,
     one_sems, two_sems, w_sems, in_sems, out_sems, gw_sem, gk_sems) = refs[8:]
    n, c = normed_ref.shape
    size = at_ref[0]
    gathered = (heads_any, mine_any, other_any)
    one_copies = start_kernel(at_ref, gathered, k_one, one_sems, 0)
    img_copy = pltpu.make_async_copy(img_any, img_ref, in_sems.at[0])
    cot_copy = pltpu.make_async_copy(cot_any, cot_ref, in_sems.at[1])
    img_copy.start()
    two_copies = start_kernel(at_ref, gathered, k_two, two_sems, 9 * c)
    w_copies = [fetch_rows(at_ref, gathered, w_ref, j * c, (18 + j) * c, c, w_sems.at[j]) for j in range(4)]
    cot_copy.start()
    leaving = []

    def leave(src, dst):
        copy = pltpu.make_async_copy(src, dst, out_sems.at[len(leaving)])
        copy.start()
        leaving.append(copy)

    mask = row_mask(size, c)
    zero = jnp.zeros((8, c), F32)

    bias_one = vec_ref[2:3, :]

    def finish_one(first, v, carry):
        v = v + bias_one
        x = jnp.where(pixel_mask(size, first, MB, c), v, 0.0)
        return v, (carry[0] + fold(x), carry[1] + fold(x * x))

    s1, s2 = conv(pad_one_ref, k_one, one_copies, conv_ref, MB, finish_one)
    leave(conv_ref, conv_any)
    leave(k_one, weights_any.at[pl.ds(0, 9 * c)])
    kept_one = leaving[-1]
    mean, scale = moments(s1, s2, size)
    put_stats(stat_two_ref, mean, scale)
    apply_norm(conv_ref, mean, scale * vec_ref[3:4, :], vec_ref[4:5, :], mask, pad_ref)
    put_transposed(act_t, pad_ref, SIDE, 0)

    bias_two = vec_ref[5:6, :]
    img_copy.wait()

    def finish_two(first, v, carry):
        v = v + bias_two + img_ref[pl.ds(first, MB), :].astype(F32)
        x = jnp.where(pixel_mask(size, first, MB, c), v, 0.0)
        return x, (carry[0] + fold(x), carry[1] + fold(x * x))

    s1, s2 = conv(pad_ref, k_two, two_copies, resid_ref, MB, finish_two)
    leave(resid_ref, resid_any)
    leave(k_two, weights_any.at[pl.ds(9 * c, 9 * c)])
    mean, scale = moments(s1, s2, size)
    gain = vec_ref[6:7, :]
    full_gain, shift = scale * gain, vec_ref[7:8, :]
    cot_copy.wait()

    def apply(h, carry):
        y = (resid_ref[rows(h), :] - mean) * full_gain + shift
        normed_ref[rows(h), :] = jnp.where(mask(h), y, 0.0).astype(BF16)
        t = jnp.where(mask(h), cot_ref[rows(h), :].astype(F32), 0.0)
        top_ref[rows(h), :] = t.astype(BF16)
        return carry + fold(t)

    top_sum = lax.fori_loop(0, SIDE, apply, zero, unroll=4)
    put_transposed(normed_t, normed_ref, 0, 0)

    for copy in w_copies:
        copy.wait()
    leave(w_ref, weights_any.at[pl.ds(18 * c, 4 * c)])
    factor = c ** (-0.5)
    wq, wk, wv, wo = (functools.partial(lambda j: w_ref[j * c : (j + 1) * c, :], j) for j in range(4))
    qb, vb = vec_ref[8:9, :], vec_ref[9:10, :]
    def project(m, carry):
        at = pl.ds(pl.multiple_of(m * PB, PB), PB)
        x = normed_ref[at, :]
        q_ref[at, :] = (dot(x, wq()) + qb).astype(BF16)
        k_ref[at, :] = dot(x, wk()).astype(BF16)
        v_ref[at, :] = (dot(x, wv()) + vb).astype(BF16)
        gm_ref[at, :] = dot_nt(top_ref[at, :], wo()).astype(BF16)
        return carry

    lax.fori_loop(0, n // PB, project, 0, unroll=2)

    spot = lax.broadcasted_iota(jnp.int32, (1, n), 1)
    key_bias = jnp.where(((spot >> 5) < size) & ((spot & (SIDE - 1)) < size), 0.0, -1e30)

    def queries(m, carry):
        at = pl.ds(pl.multiple_of(m * QB, QB), QB)
        s = dot_nt(q_ref[at, :], k_ref[...]) * factor + key_bias
        raised = jnp.exp(s - jnp.max(s, axis=1, keepdims=True))
        p = raised * (1.0 / jnp.sum(raised, axis=1, keepdims=True))
        low_p = p.astype(BF16)
        p_ref[at, :] = low_p
        mixed_ref[at, :] = dot(low_p, v_ref[...]).astype(BF16)
        gp = dot_nt(gm_ref[at, :], v_ref[...])
        weighted = jnp.sum(p * gp, axis=1, keepdims=True)
        ds = (p * ((gp - weighted) * factor)).astype(BF16)
        ds_ref[at, :] = ds
        gq_ref[at, :] = dot(ds, k_ref[...]).astype(BF16)
        return carry

    lax.fori_loop(0, n // QB, queries, 0)
    leave(mixed_ref, mixed_any)

    def keys(m, carry):
        at = pl.ds(pl.multiple_of(m * QB, QB), QB)
        gk_ref[at, :] = dot_tn(ds_ref[:, at], q_ref[...]).astype(BF16)
        gv_ref[at, :] = dot_tn(p_ref[:, at], gm_ref[...]).astype(BF16)
        return carry

    lax.fori_loop(0, n // QB, keys, 0)
    gw_ref[0:c, :] = dot(normed_t[...], gq_ref[...]).astype(BF16)
    gw_ref[c : 2 * c, :] = dot(normed_t[...], gk_ref[...]).astype(BF16)
    gw_ref[2 * c : 3 * c, :] = dot(normed_t[...], gv_ref[...]).astype(BF16)
    gw_ref[3 * c : 4 * c, :] = dot_tn(mixed_ref[...], top_ref[...]).astype(BF16)
    waits = [send_rows(gw_ref, 0, 18 * c, 4 * c, at_ref, (None, high), gw_sem)]

    def normed_grad(m, carry):
        su, sux, sq, sv = carry
        first = pl.multiple_of(m * PB, PB)
        at = pl.ds(first, PB)
        gq, gk, gv = gq_ref[at, :], gk_ref[at, :], gv_ref[at, :]
        u = dot_nt(gq, wq()) + dot_nt(gk, wk()) + dot_nt(gv, wv())
        u = jnp.where(pixel_mask(size, first, PB, c), u, 0.0)
        grad_ref[at, :] = u
        xhat = (resid_ref[at, :] - mean) * scale
        return su + fold(u), sux + fold(u * xhat), sq + fold(gq.astype(F32)), sv + fold(gv.astype(F32))

    su, sux, sq, sv = lax.fori_loop(0, n // PB, normed_grad, (zero, zero, zero, zero), unroll=1)
    count = (size * size * 16).astype(F32)
    both = group_total(total_of(su, sux) * gain) / count
    m1, m2 = both[0:1], both[1:2]
    clear_border(e3_ref)

    def back(h, carry):
        xhat = (resid_ref[rows(h), :] - mean) * scale
        g = (grad_ref[rows(h), :] * gain - m1 - xhat * m2) * scale + top_ref[rows(h), :].astype(F32)
        g = jnp.where(mask(h), g, 0.0)
        grad_ref[rows(h), :] = g
        put_shifted(e3_ref, h, g.astype(BF16).astype(F32), False)
        return carry + fold(g)

    sg = lax.fori_loop(0, SIDE, back, zero, unroll=2)
    leave(e3_ref, e3_any)
    leave(grad_ref, grad_any)
    vout_ref[...] = total_of(sg, sux, su, sq, sv, top_sum)
    still = [v for v in leaving if v is not kept_one]
    kept_one.wait()
    waits += kernel_gradient(act_t, e3_ref, k_one, 9 * c, at_ref, (low, high), gk_sems)
    for wait in waits + still:
        wait.wait()


def forward(at, pad_one, vec, gathered, img, cot):
    n, c = img.shape
    heads, mine, other = gathered
    half = (shape((8, 22 * c // 64, c), BF16), "a")

    def low(*dims):
        return pltpu.VMEM(dims, BF16)

    full = low(n, c)
    found = call(forward_body,
        [(shape((22 * c, c), BF16), "a"), (shape((n, c), F32), "a"), (shape((8, c), F32), "v"), (shape((n, c), BF16), "a"), (shape((n, c), F32), "a"),
         (shape((n, c), F32), "a"), (shape((n + 2 * SIDE, 3 * c), BF16), "a"), (shape((8, c), F32), "v")] + [half] * 8,
        [(at, "s"), (pad_one, "v"), (vec, "v"), (heads, "a"), (mine, "a"), (other, "a"), (img, "a"), (cot, "a")],
        [low(9 * c, c), low(9 * c, c), low(4 * c, c), full, full, pltpu.VMEM((n, c), F32), low(n + 2 * SIDE, c), low(c, n),
         pltpu.VMEM((n, c), F32), full, low(c, n), full, full, full, low(n, n), low(n, n), full, full, full, full, full, full,
         pltpu.VMEM((n, c), F32), low(n + 2 * SIDE, 3 * c), low(4 * c, c),
         pltpu.SemaphoreType.DMA((9,)), pltpu.SemaphoreType.DMA((9,)), pltpu.SemaphoreType.DMA((4,)),
         pltpu.SemaphoreType.DMA((2,)), pltpu.SemaphoreType.DMA((8,)), pltpu.SemaphoreType.DMA, pltpu.SemaphoreType.DMA((9,))],
        name="forward")
    return found[:8], found[8:12], found[12:16]


def kernel_gradient(act_t, e3_ref, stage, row, at_ref, rounds, sems):
    c, n = act_t.shape

    def one_row(dy, carry):
        lo = pl.multiple_of((2 - dy) * SIDE, SIDE)
        for dx in range(3):
            value = dot(act_t[...], e3_ref[pl.ds(lo, n), dx * c : (dx + 1) * c])
            stage[pl.ds(pl.multiple_of((3 * dy + dx) * c, c), c), :] = value.astype(BF16)
        for now in range(3):

            @pl.when(dy == now)
            def _(now=now):
                send_rows(stage, 3 * now * c, row + 3 * now * c, 3 * c, at_ref, rounds, sems.at[now])

        return carry

    lax.fori_loop(0, 3, one_row, 0, unroll=1)
    places = [stage.at[pl.ds(3 * dy * c, 3 * c)] for dy in range(3)]
    return [pltpu.make_async_copy(place, place, sems.at[dy]) for dy, place in enumerate(places)]


def conv_back(e3_ref, k_ref, copies, out_ref):
    n, c = out_ref.shape
    for dy in range(3):
        copies[dy].wait()
        lo = (2 - dy) * SIDE

        def block(m, carry, dy=dy, lo=lo):
            first = pl.multiple_of(m * MB, MB)
            value = None
            for dx in range(3):
                tap = 3 * dy + dx
                term = dot_nt(e3_ref[pl.ds(first + lo, MB), dx * c : (dx + 1) * c], k_ref[tap * c : (tap + 1) * c, :])
                value = term if value is None else value + term
            if dy > 0:
                value = value + out_ref[pl.ds(first, MB), :]
            out_ref[pl.ds(first, MB), :] = value
            return carry

        lax.fori_loop(0, n // MB, block, 0, unroll=4)


def norm_back_sums(src_ref, g_ref, mean, scale, gain, shift, mask, size):
    c = g_ref.shape[1]

    def sums(h, carry):
        xhat = (src_ref[rows(h), :].astype(F32) - mean) * scale
        y = xhat * gain + shift
        s = sigmoid(y)
        u = jnp.where(mask(h), g_ref[rows(h), :] * (s * (1.0 + y * (1.0 - s))), 0.0)
        g_ref[rows(h), :] = u
        return carry[0] + fold(u), carry[1] + fold(u * xhat)

    zero = jnp.zeros((8, c), F32)
    su, sux = lax.fori_loop(0, SIDE, sums, (zero, zero), unroll=2)
    count = (size * size * 16).astype(F32)
    both = group_total(total_of(su, sux) * gain) / count
    return su, sux, both[0:1], both[1:2]


def back_two_body(
    at_ref, e3_ref, vec_ref, stat_ref, k_any, conv_any, act_any, i0, i1, i2, i3,
    e3_any, vout_ref, o0, o1, o2, o3, g_ref, conv_ref, act_t, e3_out, k_vmem, sems, in_sems, out_sem, gk_sems,
):
    n, c = conv_ref.shape
    copies = start_copies(k_any, k_vmem, sems, 3, 9 * c)
    conv_copy = pltpu.make_async_copy(conv_any, conv_ref, in_sems.at[0])
    act_copy = pltpu.make_async_copy(act_any, act_t, in_sems.at[1])
    conv_copy.start()
    act_copy.start()
    size = at_ref[0]
    mask = row_mask(size, c)
    conv_back(e3_ref, k_vmem, copies, g_ref)
    conv_copy.wait()
    mean, scale = stat_ref[0:1, :], stat_ref[1:2, :]
    gain, shift = vec_ref[3:4, :], vec_ref[4:5, :]
    su, sux, m1, m2 = norm_back_sums(conv_ref, g_ref, mean, scale, gain, shift, mask, size)
    clear_border(e3_out)

    def apply(h, carry):
        xhat = (conv_ref[rows(h), :] - mean) * scale
        g = jnp.where(mask(h), (g_ref[rows(h), :] * gain - m1 - xhat * m2) * scale, 0.0)
        put_shifted(e3_out, h, g.astype(BF16).astype(F32), False)
        return carry + fold(g)

    sg = lax.fori_loop(0, SIDE, apply, jnp.zeros((8, c), F32), unroll=2)
    leaving = pltpu.make_async_copy(e3_out, e3_any, out_sem)
    leaving.start()
    vout_ref[...] = total_of(sg, sux, su)
    act_copy.wait()
    for wait in kernel_gradient(act_t, e3_out, k_vmem, 0, at_ref, ((o0, o1, o2, o3),), gk_sems):
        wait.wait()
    leaving.wait()


def back_two(at, e3, weights, vec, conv_out, stat, act, low):
    n, c = conv_out.shape
    half = shape(low[0].shape, BF16)
    e3_out, vout, *low = call(back_two_body,
        [(shape((n + 64, 3 * c), BF16), "a"), (shape((8, c), F32), "v")] + [(half, "a")] * 4,
        [(at, "s"), (e3, "v"), (vec, "v"), (stat, "v"), (weights, "a"), (conv_out, "a"), (act, "a")] + [(v, "a") for v in low],
        [pltpu.VMEM((n, c), F32), pltpu.VMEM((n, c), F32), pltpu.VMEM((c, n), BF16), pltpu.VMEM((n + 64, 3 * c), BF16),
         pltpu.VMEM((9 * c, c), BF16), pltpu.SemaphoreType.DMA((3,)), pltpu.SemaphoreType.DMA((2,)), pltpu.SemaphoreType.DMA,
         pltpu.SemaphoreType.DMA((9,))],
        name="back_two", aliases={7 + i: 2 + i for i in range(4)})
    return e3_out, vout, low


def back_one_body(
    size_ref, e3_ref, k_ref, vec_ref, img_ref, stat_ref, grad_ref, mixed_any, resid_any, both_any, vout_ref,
    g_ref, out_ref, rows_ref, mixed_ref, resid_ref, wo_ref, k_vmem, sems, in_sems, out_sems,
):
    n, c = img_ref.shape
    copies = start_copies(k_ref, k_vmem, sems, 3)
    bands, quarter = both_any.shape[0], both_any.shape[2]
    later = [
        pltpu.make_async_copy(src, dst, in_sems.at[i])
        for i, (src, dst) in enumerate(((mixed_any, mixed_ref), (resid_any, resid_ref), (k_ref.at[pl.ds(21 * c, c)], wo_ref)))
    ]
    for copy in later:
        copy.start()
    leaving = []

    def leave(src_ref, which):
        for j in range(bands):
            copy = pltpu.make_async_copy(src_ref.at[pl.ds(j * quarter, quarter)], both_any.at[j, which], out_sems.at[len(leaving)])
            copy.start()
            leaving.append(copy)

    size = size_ref[0]
    mask = row_mask(size, c)
    conv_back(e3_ref, k_vmem, copies, g_ref)
    for copy in later:
        copy.wait()

    def block_rows(m, carry):
        first = pl.multiple_of(m * MB, MB)
        at = pl.ds(first, MB)
        value = dot(mixed_ref[at, :], wo_ref[...]) + vec_ref[10:11, :] + resid_ref[at, :]
        rows_ref[at, :] = jnp.where(pixel_mask(size, first, MB, c), value, 0.0).astype(BF16)
        return carry

    lax.fori_loop(0, n // MB, block_rows, 0)
    leave(rows_ref, 0)
    mean, scale = stat_ref[0:1, :], stat_ref[1:2, :]
    gain, shift = vec_ref[0:1, :], vec_ref[1:2, :]
    su, sux, m1, m2 = norm_back_sums(img_ref, g_ref, mean, scale, gain, shift, mask, size)

    def apply(h, carry):
        xhat = (img_ref[rows(h), :].astype(F32) - mean) * scale
        g = (g_ref[rows(h), :] * gain - m1 - xhat * m2) * scale + grad_ref[rows(h), :]
        out_ref[rows(h), :] = jnp.where(mask(h), g, 0.0).astype(out_ref.dtype)
        return carry

    lax.fori_loop(0, SIDE, apply, 0, unroll=2)
    leave(out_ref, 1)
    vout_ref[...] = total_of(sux, su)
    for copy in leaving:
        copy.wait()


def back_one(at, e3, weights, vec, img, stat, grad_resid, mixed, resid, bands):
    n, c = img.shape
    low, full = pltpu.VMEM((n, c), BF16), pltpu.VMEM((n, c), F32)
    return call(back_one_body, [(shape((bands, 2, n // bands, c), BF16), "a"), (shape((8, c), F32), "v")],
        [(at, "s"), (e3, "v"), (weights, "a"), (vec, "v"), (img, "v"), (stat, "v"), (grad_resid, "v"), (mixed, "a"), (resid, "a")],
        [full, low, low, low, full, pltpu.VMEM((c, c), BF16), pltpu.VMEM((9 * c, c), BF16), pltpu.SemaphoreType.DMA((3,)),
         pltpu.SemaphoreType.DMA((3,)), pltpu.SemaphoreType.DMA((2 * bands,))],
        name="back_one")


ALL = ("img", "band")
CORE = [(b, b ^ 1) for b in range(4)]
ACROSS_Y = [(b, b ^ 2) for b in range(4)]
ACROSS_X = [(i, i ^ 1) for i in range(8)]

def after(value, *earlier, flops=0):
    def body(*refs):
        pass

    anywhere = pl.BlockSpec(memory_space=pl.ANY)
    return pl.pallas_call(
        body,
        out_shape=shape(value.shape, value.dtype),
        in_specs=[anywhere] * (1 + len(earlier)),
        out_specs=anywhere,
        input_output_aliases={0: 0},
        cost_estimate=pl.CostEstimate(flops=flops, bytes_accessed=0, transcendentals=0),
        name="after",
    )(value, *earlier)


def wide(*parts):
    total = parts[0].astype(F32)
    for part in parts[1:]:
        total = total + part.astype(F32)
    return total


SUMS_VMEM = VMEM_LIMIT


def add_parts(held, ready, terms):
    lead = ready.shape[:-2]

    def one(k, carry):
        spot = (k,) if len(lead) == 1 else (k // lead[1], k % lead[1])
        total = held[(0, *spot)].astype(F32)
        for t in range(1, terms):
            total = total + held[(t, *spot)].astype(F32)
        ready[spot] = total.astype(ready.dtype)
        return carry

    count = lead[0] if len(lead) == 1 else lead[0] * lead[1]
    lax.fori_loop(0, count, one, 0)


def start_terms(ins, terms, held, sems):
    copies = [pltpu.make_async_copy(ins[at].at[index], held.at[t], sems.at[t]) for t, (at, index) in enumerate(terms)]
    for copy in copies:
        copy.start()
    return copies


def sums_body(*refs, arrays, groups):
    count = len(groups)
    ins, outs, rest = refs[:arrays], refs[arrays : arrays + count], refs[arrays + count :]
    held, ready, in_sems, out_sems = rest[:count], rest[count : 2 * count], rest[2 * count : 3 * count], rest[-1]
    copies = [start_terms(ins, terms, held[g], in_sems[g]) for g, terms in enumerate(groups)]
    leaving = []
    for g, terms in enumerate(groups):
        for copy in copies[g]:
            copy.wait()
        add_parts(held[g], ready[g], len(terms))
        leaving.append(pltpu.make_async_copy(ready[g], outs[g], out_sems.at[g]))
        leaving[-1].start()
    for copy in leaving:
        copy.wait()


def indexed(groups):
    arrays, places = [], {}
    for terms in groups:
        for array, _ in terms:
            if id(array) not in places:
                places[id(array)] = len(arrays)
                arrays.append(array)
    return arrays, [[(places[id(array)], index) for array, index in terms] for terms in groups]


def sum_shape(array, index):
    return tuple(array.shape[i] for i in range(array.ndim) if i >= len(index) or index[i] == slice(None))


def block_sums(groups, dtype, name):
    arrays, places = indexed(groups)
    dims = [sum_shape(*terms[0]) for terms in groups]
    return call(functools.partial(sums_body, arrays=len(arrays), groups=places),
        [(shape(d, dtype), "a") for d in dims],
        [(v, "a") for v in arrays],
        [pltpu.VMEM((len(terms), *d), BF16) for terms, d in zip(groups, dims)] + [pltpu.VMEM(d, dtype) for d in dims]
        + [pltpu.SemaphoreType.DMA((len(terms),)) for terms in groups] + [pltpu.SemaphoreType.DMA((len(groups),))],
        name=name, vmem=SUMS_VMEM)


def chip_sends(arrays, *earlier):
    mine_a, mine_b, theirs_a, theirs_b = arrays
    half, c = mine_a.shape[1:]
    dims = (2, 2, 2, half, c)
    if earlier:
        theirs_a, theirs_b = after(theirs_a, *earlier), after(theirs_b, *earlier)
    got = [lax.ppermute(v, "band", CORE) for v in (theirs_a, theirs_b)]
    pair_a = (mine_a.reshape(dims), got[0].reshape(dims))
    pair_b = (mine_b.reshape(dims), got[1].reshape(dims))
    every = slice(None)
    sends = block_sums([[(v, (1,)) for v in pair_a], [(v, (every, 1)) for v in pair_b]], BF16, "chip_sums")
    return pair_a, pair_b, *sends


def plane_swap(send_a, send_b):
    return lax.ppermute(send_a, "img", ACROSS_X), lax.ppermute(send_b, "band", ACROSS_Y)


def plane_sends(pair_a, pair_b, got_a, got_b):
    kept_a = [(v, (0, 0)) for v in pair_a] + [(got_a, (0,))]
    kept_b = [(v, (0, 0)) for v in pair_b] + [(got_b, (0,))]
    sends = block_sums(
        [[(v, (0, 1)) for v in pair_a] + [(got_a, (1,))], [(v, (1, 0)) for v in pair_b] + [(got_b, (1,))]], BF16, "row_sums"
    )
    return kept_a, kept_b, *sends


def plane_parts(kept_a, kept_b, next_a, next_b, *earlier):
    last_a = lax.ppermute(next_a, "band", ACROSS_Y)
    last_b = lax.ppermute(next_b, "img", ACROSS_X)
    if earlier:
        last_a, last_b = after(last_a, *earlier), after(last_b, *earlier)
    return [kept_a + [(last_a, ())], kept_b + [(last_b, ())]]


def owner_body(at_ref, *refs, arrays, groups):
    ins, (own, *sent), rest = refs[:arrays], refs[arrays : arrays + 4], refs[arrays + 4 :]
    high_a, high_b, held_a, held_b, total_a, total_b, sems_a, sems_b, high_sems = rest
    copies = [start_terms(ins, groups[0], held_a, sems_a), start_terms(ins, groups[1], held_b, sems_b)]
    highs = [pltpu.make_async_copy(ins[groups[2 + i][0][0]], ref, high_sems.at[i]) for i, ref in enumerate((high_a, high_b))]
    for copy in highs:
        copy.start()
    for i, (held, total) in enumerate(((held_a, total_a), (held_b, total_b))):
        for copy in copies[i]:
            copy.wait()
        add_parts(held, total, len(groups[i]))
    for copy in highs:
        copy.wait()
    half = total_a.shape[1]
    for step, ref in enumerate((own, *sent)):
        plane = at_ref[4] ^ step
        for upper, pair in enumerate(((total_a, total_b), (high_a, high_b))):

            @pl.when((plane >> 1) == upper)
            def _(ref=ref, pair=pair, plane=plane):
                for tail, part in enumerate(pair):
                    ref[tail * half : (tail + 1) * half, :] = part[plane & 1].astype(ref.dtype)


def owner_parts(at, low, high):
    groups = low + [[(v, ())] for v in high]
    arrays, places = indexed(groups)
    half, c = high[0].shape[1:]
    sums = pltpu.VMEM((2, half, c), F32)
    held = pltpu.VMEM((len(low[0]), 2, half, c), BF16)
    sems = pltpu.SemaphoreType.DMA((len(low[0]),))
    own, *sent = call(functools.partial(owner_body, arrays=len(arrays), groups=places),
        [(shape((2 * half, c), F32), "v")] + [(shape((2 * half, c), BF16), "v")] * 3,
        [(at, "s")] + [(v, "a") for v in arrays],
        [sums, sums, held, held, sums, sums, sems, sems, pltpu.SemaphoreType.DMA((2,))],
        name="owner_sums", vmem=SUMS_VMEM)
    got = [lax.ppermute(v, "img", [(i, i ^ (2 * step)) for i in range(8)]) for v, step in zip(sent, (1, 2, 3))]
    return [own] + got, sent


def plane_gather(own):
    z = [lax.ppermute(own, "img", [(i, i ^ (2 * step)) for i in range(8)]) for step in (1, 2, 3)]
    first, last = jnp.stack([own, z[0]]), jnp.stack([z[1], z[2]])
    first = jnp.concatenate([first, lax.ppermute(first, "band", ACROSS_Y)])
    last = jnp.concatenate([last, lax.ppermute(last, "img", ACROSS_X)])
    mine = jnp.concatenate([first, lax.ppermute(first, "img", ACROSS_X), last, lax.ppermute(last, "band", ACROSS_Y)])
    return mine, lax.ppermute(mine, "band", CORE)


def four_sum(v, axis, steps):
    a, b, c = (lax.ppermute(v, axis, [(i, i ^ step) for i in range(lax.axis_size(axis))]) for step in steps)
    return (v + a) + (b + c)


def whole_image(
    images,
    cotangent,
    sizes,
    matrix_weight,
    matrix_momentum,
    matrix_average,
    vector_weight,
    vector_momentum,
    vector_average,
):
    batch, height, width, c = images.shape
    n = width * width
    mine = lax.axis_index("band")
    place = lax.axis_index("img")
    at = jnp.stack([lax.dynamic_index_in_dim(sizes, mine, 0, False), place % 2, mine // 2, mine % 2, place // 2])

    def to_image(field):
        parts = field.reshape(batch, height * width, c)
        return lax.all_to_all(parts, "band", 0, 0, tiled=True).reshape(n, c)

    own = matrix_weight.astype(BF16).reshape(-1, c)
    head = 288
    gathered = (lax.all_gather(own[:head], ALL, axis=0, tiled=True), *plane_gather(own[head:]))
    img = to_image(images)
    cot = to_image(cotangent)
    pad_one, act_t, stat_one = act_one(at, img, vector_weight)
    (weights, conv_out, stat_two, mixed, resid, grad_resid, e3_two, v3), high, low = forward(
        at, pad_one, vector_weight, gathered, img, cot
    )
    high = chip_sends(high)
    e3_two = after(e3_two, high[2], high[3])
    swapped = plane_swap(high[2], high[3])
    e3_one, v2, low = back_two(at, e3_two, weights, vector_weight, conv_out, stat_two, act_t, low)
    low = chip_sends(low, *swapped)
    high = plane_sends(*high[:2], *swapped)
    low_sends = low[2:4]
    e3_one = after(e3_one, *low_sends)
    swapped = plane_swap(low[2], low[3])
    both, v1 = back_one(at, e3_one, weights, vector_weight, img, stat_one, grad_resid, mixed, resid, batch)
    vecs = jnp.stack([v1[0], v1[1], v2[0], v2[1], v2[2], v3[0], v3[1], v3[2], v3[3], v3[4], v3[5]])
    low = plane_sends(*low[:2], *(after(v, v1) for v in swapped))
    vecs = four_sum(after(vecs, low[2], low[3]), "img", (2, 4, 6))
    high = block_sums(plane_parts(*high, low[2], low[3]), F32, "plane_sums")
    parts, sent = owner_parts(at, plane_parts(*low, vecs), high)
    given = lax.all_to_all(after(both, *sent), "band", 0, 0, tiled=True)
    block_out = given[:, 0].reshape(images.shape)
    input_grad = given[:, 1].reshape(images.shape).astype(F32)
    vecs = after(vecs, parts[1])
    vecs = vecs + lax.ppermute(vecs, "img", ACROSS_X)
    vector_grads = four_sum(vecs, "band", (1, 2, 3))
    vector_moments = MOMENTUM * vector_momentum + vector_grads
    vector_masters = vector_weight - LR_VECTOR * (vector_grads + MOMENTUM * vector_moments)
    vector_means = AVERAGE * vector_average + (1.0 - AVERAGE) * vector_masters
    matrix_grads = wide(*parts).reshape(-1)
    matrix_moments = MOMENTUM * matrix_momentum + matrix_grads
    matrix_masters = matrix_weight - LR_MATRIX * (matrix_grads + MOMENTUM * matrix_moments)
    matrix_means = AVERAGE * matrix_average + (1.0 - AVERAGE) * matrix_masters
    return (
        block_out,
        input_grad,
        matrix_grads,
        matrix_moments,
        matrix_means,
        matrix_masters,
        vector_grads,
        vector_moments,
        vector_means,
        vector_masters,
    )


def solution(mesh):
    fits = mesh.shape["img"] == 8 and mesh.shape["band"] == 4

    def per_device(images, *rest):
        step = whole_image if fits and images.shape[:3] == (4, 8, SIDE) else banded
        return step(images, *rest)

    return jax.shard_map(
            per_device,
        mesh=mesh,
        in_specs=(
            P("img", "band", None, None),
            P("img", "band", None, None),
            P("img"),
            P(("img", "band")),
            P(("img", "band")),
            P(("img", "band")),
            P(),
            P(),
            P(),
        ),
        out_specs=(
            P("img", "band", None, None),
            P("img", "band", None, None),
            P(("img", "band")),
            P(("img", "band")),
            P(("img", "band")),
            P(("img", "band")),
            P(),
            P(),
            P(),
            P(),
        ),
        check_vma=False,
    )
```
